128 devices in a mesh: seq: 32 (over z, y, x_lo), narrow: 2 (over core), wide: 2 (over x_hi).
Axes of the slice: x: 4 (x_hi: 2, x_lo: 2; x = x_hi * 2 + x_lo), y: 4, z: 4, core: 2. Of those that a mesh axis runs over, the one named last changes fastest.
Arguments:
- block_input: bfloat16 [8192, 2048], P(('seq', 'wide'), 'narrow'), may hold values from -6 to 6
- out_grad: bfloat16 [8192, 2048], P(('seq', 'wide'), 'narrow'), may hold values from -6 to 6
- qkv_weight: float32 [2048, 8, 384], P(('narrow', 'seq'), 'wide'), may hold values from -0.0625 to 0.0625
- qkv_moment: float32 [2048, 8, 384], P(('narrow', 'seq'), 'wide'), may hold values from -0.00021362305 to 0.00021362305
- qkv_second: float32 [2048, 8, 384], P(('narrow', 'seq'), 'wide'), may hold values from 4.2748038e-10 to 6.905452e-09
- gate_up_weight: float32 [2048, 2, 8192], P(('narrow', 'seq'), None, 'wide'), may hold values from -0.0625 to 0.0625
- gate_up_moment: float32 [2048, 2, 8192], P(('narrow', 'seq'), None, 'wide'), may hold values from -0.00021362305 to 0.00021362305
- gate_up_second: float32 [2048, 2, 8192], P(('narrow', 'seq'), None, 'wide'), may hold values from 4.2748038e-10 to 6.905452e-09
- out_weight: float32 [2048, 2048], P(('wide', 'seq'), 'narrow')
- out_moment: float32 [2048, 2048], P(('wide', 'seq'), 'narrow'), may hold values from -3.8146973e-06 to 3.8146973e-06
- out_second: float32 [2048, 2048], P(('wide', 'seq'), 'narrow'), may hold values from 3.2883107e-14 to 3.2883107e-13
- down_weight: float32 [8192, 2048], P(('wide', 'seq'), 'narrow')
- down_moment: float32 [8192, 2048], P(('wide', 'seq'), 'narrow'), may hold values from -4.5776367e-05 to 4.5776367e-05
- down_second: float32 [8192, 2048], P(('wide', 'seq'), 'narrow'), may hold values from 4.274804e-12 to 4.2748038e-11
- norm_gains: float32 [2, 2048], P(None, 'narrow')
- gains_moment: float32 [2, 2048], P(None, 'narrow'), may hold values from -0.00012207031 to 0.00012207031
- gains_second: float32 [2, 2048], P(None, 'narrow'), may hold values from 2.9594795e-11 to 2.9594796e-10
- doc_lengths: int32 [4], replicated, may hold values from 1 to 8064, as said below
Outputs:
- layer_output: bfloat16 [8192, 2048], P(('seq', 'wide'), 'narrow')
- input_grad: float32 [8192, 2048], P(('seq', 'wide'), 'narrow')
- grad_norm: float32 [], replicated
- qkv_next: float32 [2048, 8, 384], P(('narrow', 'seq'), 'wide')
- qkv_moment_next: float32 [2048, 8, 384], P(('narrow', 'seq'), 'wide')
- qkv_second_next: float32 [2048, 8, 384], P(('narrow', 'seq'), 'wide')
- gate_up_next: float32 [2048, 2, 8192], P(('narrow', 'seq'), None, 'wide')
- gate_up_moment_next: float32 [2048, 2, 8192], P(('narrow', 'seq'), None, 'wide')
- gate_up_second_next: float32 [2048, 2, 8192], P(('narrow', 'seq'), None, 'wide')
- out_next: float32 [2048, 2048], P(('wide', 'seq'), 'narrow')
- out_moment_next: float32 [2048, 2048], P(('wide', 'seq'), 'narrow')
- out_second_next: float32 [2048, 2048], P(('wide', 'seq'), 'narrow')
- down_next: float32 [8192, 2048], P(('wide', 'seq'), 'narrow')
- down_moment_next: float32 [8192, 2048], P(('wide', 'seq'), 'narrow')
- down_second_next: float32 [8192, 2048], P(('wide', 'seq'), 'narrow')
- gains_next: float32 [2, 2048], P(None, 'narrow')
- gains_moment_next: float32 [2, 2048], P(None, 'narrow')
- gains_second_next: float32 [2, 2048], P(None, 'narrow')
The draws below stay inside these ranges and needn't reach their ends.
Inputs may be any that keep to these rules, and one draw needn't show every extreme that they name: `doc_lengths`: four documents packed in order over the 8192 tokens: the second holds exactly 8064 tokens and runs from the first block of 128 tokens into the last; the first lies in the first block, the third and fourth at the end of the pack, the first, third and fourth together exactly 128; the third and the fourth are shorter than 64 each, and one of them is a single token.
All inputs are finite; a program needn't handle non-finite values.
Results may differ from the reference program's by a relative error of at most 0.04.
Values may be sent and summed in bfloat16 or wider, within the bound.
A program may use at most 192 MiB of HBM per device.

```python
import math
import jax
import jax.numpy as jnp
from jax import lax

D = 2048
HQ = 32
KV = 8
HD = 64
FF = 8192
ADAM_STEP = 10
GROUP = 4
QKV_COLS = 384
TOKENS = 8192
BLOCK = 128
PARAMS = 60821504


def ramp_rows(count, top_value):
    return 1.0 + (top_value - 1.0) * jnp.arange(count, dtype=jnp.float32) / (count - 1)


def draw_out_weight(key, part):
    key = jax.random.fold_in(key, 3)
    spread = 0.3 * (TOKENS / (HQ * HD)) ** 0.5
    noise = jax.random.normal(key, (HQ * HD, D), jnp.float32)
    top_value = 3.0
    return noise * ramp_rows(HQ * HD, top_value)[:, None] * spread


def draw_down_weight(key, part):
    key = jax.random.fold_in(key, 5)
    spread = FF ** (-0.5)
    noise = jax.random.normal(key, (FF, D), jnp.float32)
    top_value = 3.0
    return noise * ramp_rows(FF, top_value)[:, None] * spread


def draw_norm_gains(key, part):
    key = jax.random.fold_in(key, 7)
    top_value = 3.0
    jitter = 0.1
    noise = jax.random.uniform(key, (2, D), jnp.float32, -1.0, 1.0)
    return ramp_rows(D, top_value)[None, :] * (1.0 + jitter * noise)


def draw_doc_lengths(key, part):
    key = jax.random.fold_in(key, 11)
    third_key, fourth_key, pick_key = jax.random.split(key, 3)
    third_doc = jax.random.randint(third_key, (), 1, BLOCK // 2)
    fourth_doc = jax.random.randint(fourth_key, (), 1, BLOCK // 2)
    pick_third = jax.random.randint(pick_key, (), 0, 2)
    third_doc = jnp.where(pick_third == 1, 1, third_doc)
    fourth_doc = jnp.where(pick_third == 1, fourth_doc, 1)
    first_doc = BLOCK - third_doc - fourth_doc
    second_doc = jnp.zeros((), jnp.int32) + (TOKENS - BLOCK)
    return jnp.stack([first_doc, second_doc, third_doc, fourth_doc]).astype(jnp.int32)


def block_levels(rng, dims, shards, low, high):
    def one(dim, blocks):
        heights = jax.random.uniform(jax.random.fold_in(jax.random.fold_in(rng, 6), dim), (blocks,), jnp.float32, low / len(shards), high / len(shards))
        return jnp.repeat(jnp.exp(heights), dims[dim] // blocks).reshape((-1,) + (1,) * (len(dims) - dim - 1))

    gain = one(*shards[0])
    for cut in shards[1:]:
        gain = gain * one(*cut)
    return gain


def centred(own_key, shape, scale, limit, cuts=(), kind=jnp.bfloat16):
    values = scale * jax.random.normal(own_key, shape, jnp.float32)
    if cuts:
        values = values * block_levels(own_key, shape, cuts, -0.22, 0.18)
    return jnp.clip(values, -limit, limit).astype(kind)


def setup_inputs(seed: int = 0) -> dict:
    seeds = jax.random.split(jax.random.key(seed), 19)
    return {
        "block_input": centred(seeds[0], (TOKENS, D), 1.0, 6.0, ((0, 64), (1, 2))),
        "out_grad": centred(seeds[1], (TOKENS, D), 1.0, 6.0, ((0, 64), (1, 2))),
        "qkv_weight": centred(seeds[2], (D, KV, QKV_COLS), (5 * D) ** -0.5, 0.0625, ((0, 64), (1, 2)), jnp.float32),
        "qkv_moment": centred(seeds[3], (D, KV, QKV_COLS), (0.11 / PARAMS ** 0.5), 0.00021362305, ((0, 64), (1, 2)), jnp.float32),
        "qkv_second": jnp.clip(jnp.exp(math.log(6.905452210048679e-09) - 2.7821582 * jax.random.uniform(seeds[4], (D, KV, QKV_COLS), jnp.float32) ** block_levels(seeds[4], (D, KV, QKV_COLS), ((0, 64), (1, 2)), -0.2, 0.2)), 4.2748038442397274e-10, 6.905452210048679e-09),
        "gate_up_weight": centred(seeds[5], (D, 2, FF), (4 * D) ** -0.5, 0.0625, ((0, 64), (2, 2)), jnp.float32),
        "gate_up_moment": centred(seeds[6], (D, 2, FF), (0.11 / PARAMS ** 0.5), 0.00021362305, ((0, 64), (2, 2)), jnp.float32),
        "gate_up_second": jnp.clip(jnp.exp(math.log(6.905452210048679e-09) - 2.7821582 * jax.random.uniform(seeds[7], (D, 2, FF), jnp.float32) ** block_levels(seeds[7], (D, 2, FF), ((0, 64), (2, 2)), -0.2, 0.2)), 4.2748038442397274e-10, 6.905452210048679e-09),
        "out_weight": draw_out_weight(jax.random.fold_in(seeds[18], 71), 0),
        "out_moment": centred(seeds[9], (HQ * HD, D), (0.002 / PARAMS ** 0.5), 3.814697265625e-06, ((0, 64), (1, 2)), jnp.float32),
        "out_second": jnp.clip(jnp.exp(math.log(3.2883106502491766e-13) - 2.3025851 * jax.random.uniform(seeds[10], (HQ * HD, D), jnp.float32) ** block_levels(seeds[10], (HQ * HD, D), ((0, 64), (1, 2)), -0.2, 0.2)), 3.2883106502491766e-14, 3.2883106502491766e-13),
        "down_weight": draw_down_weight(jax.random.fold_in(seeds[18], 71), 0),
        "down_moment": centred(seeds[12], (FF, D), (0.023 / PARAMS ** 0.5), 4.57763671875e-05, ((0, 64), (1, 2)), jnp.float32),
        "down_second": jnp.clip(jnp.exp(math.log(4.2748037748507883e-11) - 2.30258503 * jax.random.uniform(seeds[13], (FF, D), jnp.float32) ** block_levels(seeds[13], (FF, D), ((0, 64), (1, 2)), -0.2, 0.2)), 4.27480403505931e-12, 4.2748037748507883e-11),
        "norm_gains": draw_norm_gains(jax.random.fold_in(seeds[18], 71), 0),
        "gains_moment": centred(seeds[15], (2, D), (0.06 / PARAMS ** 0.5), 0.00012207031, ((1, 2),), jnp.float32),
        "gains_second": jnp.clip(jnp.exp(math.log(2.9594796058241e-10) - 2.3025851 * jax.random.uniform(seeds[16], (2, D), jnp.float32) ** block_levels(seeds[16], (2, D), ((1, 2),), -0.2, 0.2)), 2.959479536435161e-11, 2.9594796058241e-10),
        "doc_lengths": draw_doc_lengths(jax.random.fold_in(seeds[18], 71), 0),
    }


@jax.custom_vjp
def low(v):
    return lax.optimization_barrier(v.astype(jnp.bfloat16)).astype(jnp.float32)

@jax.custom_vjp
def low_back(v):
    return v

def low_keep(v):
    return (low(v), None)

def low_pass(kept, grad):
    return (grad,)

def back_keep(v):
    return (v, None)

def back_low(kept, grad):
    return (low(grad),)
low.defvjp(low_keep, low_pass)
low_back.defvjp(back_keep, back_low)
NORM_EPS = 1e-05
ADAM_EPS = 1e-08
BETA_ONE = 0.9
BETA_TWO = 0.95
WEIGHT_DECAY = 0.1
MATRIX_RATE = 0.01
OUTPUT_RATE = 0.9
DOWN_RATE = 3.0
GAIN_RATE = 2.5
CLIP_NORM = 1.0
ROPE_THETA = 500000.0
ROPE_FACTOR = 32.0
LOW_FREQ = 1.0
HIGH_FREQ = 4.0
OLD_CONTEXT = 8192.0

def doc_tables(doc_lengths, count):
    ends = jnp.cumsum(doc_lengths).astype(jnp.int32)
    places = jnp.arange(count, dtype=jnp.int32)
    passed = (places[:, None] >= ends[None, :]).astype(jnp.int32)
    segment = lax.optimization_barrier(jnp.sum(passed, axis=1)).astype(jnp.int32)
    starts = lax.optimization_barrier(jnp.sum(passed * doc_lengths[None, :], axis=1)).astype(jnp.int32)
    return (places, segment, places - starts)

def rope_tables(position, head_size):
    half_size = head_size // 2
    column = jnp.arange(half_size, dtype=jnp.float32)
    inverse = jnp.exp(-(2.0 * column / head_size) * math.log(ROPE_THETA))
    wavelength = 2.0 * math.pi / inverse
    smooth = (OLD_CONTEXT / wavelength - LOW_FREQ) / (HIGH_FREQ - LOW_FREQ)
    blended = (1.0 - smooth) * inverse / ROPE_FACTOR + smooth * inverse
    inverse = jnp.where(wavelength < OLD_CONTEXT / HIGH_FREQ, inverse, jnp.where(wavelength > OLD_CONTEXT / LOW_FREQ, inverse / ROPE_FACTOR, blended))
    angles = position.astype(jnp.float32)[:, None] * inverse[None, :]
    return (jnp.cos(angles), jnp.sin(angles))

def rotate(values, cosine, sine):
    half_size = values.shape[-1] // 2
    table_shape = (cosine.shape[0],) + (1,) * (values.ndim - 2) + (half_size,)
    cos_part = cosine.reshape(table_shape)
    sin_part = sine.reshape(table_shape)
    first_half = values[..., :half_size]
    second_half = values[..., half_size:]
    return jnp.concatenate([first_half * cos_part - second_half * sin_part, second_half * cos_part + first_half * sin_part], axis=-1)

def rms_norm(values, gain_row):
    return values * lax.rsqrt(lax.optimization_barrier(jnp.mean(values * values, axis=-1, keepdims=True)) + NORM_EPS) * gain_row

def matmul(left, right):
    return jnp.dot(left, right, precision=lax.Precision.HIGHEST, preferred_element_type=jnp.float32)

def attend(queries, keys_all, values_all, places, segment):
    query_rows = BLOCK // 2
    count = TOKENS // query_rows

    def one_block(pieces):
        block_queries, block_segment, block_places = pieces
        scores = jnp.einsum('bkgd,tkd->bkgt', block_queries, keys_all, precision=lax.Precision.HIGHEST) * HD ** (-0.5)
        scores = low_back(scores)
        allowed = (places[None, :] <= block_places[:, None]) & (segment[None, :] == block_segment[:, None])
        scores = jnp.where(allowed[:, None, None, :], scores, -1e+30)
        highest = lax.optimization_barrier(jnp.max(scores, axis=-1, keepdims=True))
        raised = jnp.exp(scores - highest)
        probs = raised / lax.optimization_barrier(jnp.sum(raised, axis=-1, keepdims=True))
        mixed = jnp.einsum('bkgt,tkd->bkgd', low(probs), values_all, precision=lax.Precision.HIGHEST)
        return low(low_back(mixed))
    result = lax.map(jax.checkpoint(one_block), (queries.reshape(count, query_rows, KV, GROUP, HD), segment.reshape(count, query_rows), places.reshape(count, query_rows)))
    return result.reshape(TOKENS, KV * GROUP * HD)

def layer(inputs, qkv_weight, gate_up_weight, out_weight, down_weight, norm_gains, places, segment, cosine, sine):
    normed = low(rms_norm(inputs, norm_gains[0]))
    projected = low_back(matmul(normed, low(qkv_weight).reshape(D, KV * QKV_COLS)))
    projected = projected.reshape(TOKENS, KV, QKV_COLS)
    queries = projected[:, :, :GROUP * HD].reshape(TOKENS, KV, GROUP, HD)
    keys_all = projected[:, :, GROUP * HD:GROUP * HD + HD]
    values_all = low(projected[:, :, GROUP * HD + HD:])
    queries = low(rotate(queries, cosine, sine))
    keys_all = low(rotate(keys_all, cosine, sine))
    attended = attend(queries, keys_all, values_all, places, segment)
    middle = inputs + low_back(matmul(attended, low(out_weight)))
    normed_two = low(rms_norm(middle, norm_gains[1]))
    gate_up = low_back(matmul(normed_two, low(gate_up_weight).reshape(D, 2 * FF)))
    hidden = low(jax.nn.silu(gate_up[:, :FF]) * gate_up[:, FF:])
    return middle + low_back(matmul(hidden, low(down_weight)))

def adam(weight, moment, second, gradient, rate, decay):
    moment_next = BETA_ONE * moment + (1.0 - BETA_ONE) * gradient
    second_next = BETA_TWO * second + (1.0 - BETA_TWO) * gradient * gradient
    unbiased = moment_next / (1.0 - BETA_ONE ** ADAM_STEP)
    divisor = jnp.sqrt(second_next / (1.0 - BETA_TWO ** ADAM_STEP)) + ADAM_EPS
    return (weight - rate * (unbiased / divisor + decay * weight), moment_next, second_next)

def reference(block_input, out_grad, qkv_weight, qkv_moment, qkv_second, gate_up_weight, gate_up_moment, gate_up_second, out_weight, out_moment, out_second, down_weight, down_moment, down_second, norm_gains, gains_moment, gains_second, doc_lengths):
    places, segment, position = doc_tables(doc_lengths, TOKENS)
    cosine, sine = rope_tables(position, HD)

    def forward(inputs, first_weight, second_weight, third_weight, fourth_weight, gains_now):
        return layer(inputs, first_weight, second_weight, third_weight, fourth_weight, gains_now, places, segment, cosine, sine)
    output, pullback = jax.vjp(forward, block_input.astype(jnp.float32), qkv_weight, gate_up_weight, out_weight, down_weight, norm_gains)
    grads = pullback(out_grad.astype(jnp.float32))
    squares = sum((jnp.sum(member * member) for member in grads[1:]))
    grad_norm = jnp.sqrt(squares)
    factor = CLIP_NORM / jnp.maximum(grad_norm, CLIP_NORM)
    out_rate = OUTPUT_RATE * (TOKENS / (HQ * HD)) ** 0.5
    down_rate = DOWN_RATE * FF ** (-0.5)
    qkv_new = adam(qkv_weight, qkv_moment, qkv_second, grads[1] * factor, MATRIX_RATE, WEIGHT_DECAY)
    gate_up_new = adam(gate_up_weight, gate_up_moment, gate_up_second, grads[2] * factor, MATRIX_RATE, WEIGHT_DECAY)
    out_new = adam(out_weight, out_moment, out_second, grads[3] * factor, out_rate, WEIGHT_DECAY)
    down_new = adam(down_weight, down_moment, down_second, grads[4] * factor, down_rate, WEIGHT_DECAY)
    gains_new = adam(norm_gains, gains_moment, gains_second, grads[5] * factor, GAIN_RATE, 0.0)
    return (output.astype(jnp.bfloat16), grads[0], grad_norm, qkv_new[0], qkv_new[1], qkv_new[2], gate_up_new[0], gate_up_new[1], gate_up_new[2], out_new[0], out_new[1], out_new[2], down_new[0], down_new[1], down_new[2], gains_new[0], gains_new[1], gains_new[2])
```

```python
import functools
import math

import jax
import jax.numpy as jnp
from jax import lax
from jax.experimental import pallas as pl
from jax.experimental.pallas import tpu as pltpu
from jax.sharding import PartitionSpec as P

D = 2048
HQ = 32
HD = 64
FF = 8192
ADAM_STEP = 10


NORM_EPS = 1e-05
ADAM_EPS = 1e-08
BETA_ONE = 0.9
BETA_TWO = 0.95
WEIGHT_DECAY = 0.1
MATRIX_RATE = 0.01
OUTPUT_RATE = 0.9
DOWN_RATE = 3.0
GAIN_RATE = 2.5
CLIP_NORM = 1.0
ROPE_THETA = 500000.0
ROPE_FACTOR = 32.0
LOW_FREQ = 1.0
HIGH_FREQ = 4.0
OLD_CONTEXT = 8192.0

TOKENS = 8192
HALF = 256
HALVES = TOKENS // HALF
ROWS = 128
LINE = 512
WIDTH = 1024
GROUP = 4
PIECE = 32
HIDDEN = 1024
MESH = pl.DeviceIdType.MESH
ANY = pl.ANY
BF = jnp.bfloat16
F32 = jnp.float32
VMEM_LIMIT = 56 * 1024 * 1024
NEVER = -1e30


def place():
    seq = lax.axis_index("seq")
    return (
        seq // 8,
        lax.rem(seq // 2, 4),
        lax.rem(seq, 2),
        lax.axis_index("wide"),
        lax.axis_index("narrow"),
    )


def device(z, y, x, c):
    return (lax.rem(z, 4) * 8 + lax.rem(y, 4) * 2 + lax.rem(x, 2), c, x // 2)


def block_of(at):
    spot, x = at // 4, (at % 2) * 2 + (at // 2) % 2
    return 2 * spot + x if x < 2 else 2 * (HALVES - 1 - spot) + x - 2


class Wires:
    def __init__(self, send_sem, recv_sem):
        self.send_sem, self.recv_sem, self.used, self.sent = send_sem, recv_sem, 0, []

    def send(self, src, dst, target, start=True):
        at = self.used
        self.used += 1
        copy = pltpu.make_async_remote_copy(
            src_ref=src,
            dst_ref=dst,
            send_sem=self.send_sem.at[at],
            recv_sem=self.recv_sem.at[at],
            device_id=target,
            device_id_type=MESH,
        )
        if start:
            copy.start()
        self.sent.append(copy)
        return at

    def landed(self, at, region):
        pltpu.make_async_copy(region, region, self.recv_sem.at[at]).wait()

    def close(self):
        for copy in self.sent:
            copy.wait_send()


def greet(targets):
    barrier = pltpu.get_barrier_semaphore()
    for target in targets:
        pl.semaphore_signal(barrier, inc=1, device_id=target, device_id_type=MESH)
    pl.semaphore_wait(barrier, len(targets))


def line_targets(z, y, x, c):
    return [device(z, y, lax.rem(x + o, 4), c) for o in (1, 2, 3)] + [device(z, y, x, 1 - c)]


def plane_targets(z, y, x, c):
    return [device(z + o, y, x, c) for o in (1, 2, 3)] + [device(z, y + o, x, c) for o in (1, 2, 3)]


def wire_scratch(count):
    return [pltpu.SemaphoreType.DMA((count,)), pltpu.SemaphoreType.DMA((count,))]


def comm_params(number):
    return pltpu.CompilerParams(
        collective_id=number, has_side_effects=True, vmem_limit_bytes=VMEM_LIMIT
    )


def row_span(at):
    return pl.ds(pl.multiple_of(at * ROWS, ROWS), ROWS)


def col_span(c):
    return pl.ds(pl.multiple_of(c * WIDTH, WIDTH), WIDTH)


def gather_sends(wires, own, out, here):
    z, y, x, c = here
    spot = out.at[row_span(x), col_span(c)]
    across = {o: wires.send(own, spot, device(z, y, lax.rem(x + o, 4), c)) for o in (2, 1, 3)}
    return across, wires.send(own, spot, device(z, y, x, 1 - c))


def gather_relay(wires, numbers, out, here):
    z, y, x, c = here
    across, direct = numbers
    relays = []
    for o in (1, 3, 2):
        rows = row_span(lax.rem(x + 4 - o, 4))
        spot = out.at[rows, col_span(c)]
        wires.landed(across[o], spot)
        relays.append((wires.send(spot, spot, device(z, y, x, 1 - c)), rows))
    wires.landed(direct, out.at[row_span(x), col_span(1 - c)])
    for at, rows in relays:
        wires.landed(at, out.at[rows, col_span(1 - c)])


FOLD_ORDER = (2, 1, 3, 0)


def fold_sends(wires, part, folded, here):
    z, y, x, c = here
    return [
        wires.send(
            part.at[row_span(lax.rem(x + o, 4)), col_span(1 - c)],
            folded.at[k],
            device(z, y, x, 1 - c),
        )
        for k, o in enumerate(FOLD_ORDER)
    ]


def fold_moves(wires, numbers, part, folded, leaving, arriving, here, total):
    z, y, x, c = here
    moves = []
    for k, o in enumerate(FOLD_ORDER):
        wires.landed(numbers[k], folded.at[k])
        both = part[row_span(lax.rem(x + o, 4)), col_span(c)].astype(F32) + folded[k].astype(F32)
        if o:
            leaving[k] = both.astype(BF)
            moves.append(
                wires.send(leaving.at[k], arriving.at[k], device(z, y, lax.rem(x + o, 4), c))
            )
        else:
            total[...] = both
    return moves


def fold_finish(wires, moves, arriving, total):
    for k, at in enumerate(moves):
        wires.landed(at, arriving.at[k])
    total[...] = (
        total[...]
        + arriving[0].astype(F32)
        + arriving[1].astype(F32)
        + arriving[2].astype(F32)
    )


def fold_scratch():
    return [
        pltpu.VMEM((4, ROWS, WIDTH), BF),
        pltpu.VMEM((3, ROWS, WIDTH), BF),
        pltpu.VMEM((3, ROWS, WIDTH), BF),
        pltpu.VMEM((ROWS, WIDTH), F32),
    ]


def both_cores(wires, mine, theirs, value, here):
    z, y, x, c = here
    mine[...] = jnp.broadcast_to(value, mine.shape)
    at = wires.send(mine, theirs, device(z, y, x, 1 - c))
    wires.landed(at, theirs)
    return value + theirs[:, :1]


def middle_kernel(
    part, inputs, gains, middle_out, scale_out, out,
    folded, leaving, arriving, total, mine, theirs, own, send_sem, recv_sem, local_sem,
):
    z, y, xl, xh, c = place()
    x = xh * 2 + xl
    here = (z, y, x, c)
    greet(line_targets(z, y, x, c))
    wires = Wires(send_sem, recv_sem)
    numbers = fold_sends(wires, part, folded, here)
    moves = fold_moves(wires, numbers, part, folded, leaving, arriving, here, total)
    fold_finish(wires, moves, arriving, total)
    middle = total[...] + inputs[...].astype(F32)
    middle_out[...] = middle
    square = both_cores(
        wires, mine, theirs, jnp.sum(middle * middle, axis=1, keepdims=True), here
    )
    scale = lax.rsqrt(square / D + NORM_EPS)
    scale_out[...] = jnp.broadcast_to(scale, scale_out.shape)
    own[...] = (middle_out[...] * scale * gains[1:2, :]).astype(BF)
    local = pltpu.make_async_copy(own, out.at[row_span(x), col_span(c)], local_sem.at[0])
    local.start()
    gather_relay(wires, gather_sends(wires, own, out, here), out, here)
    local.wait()
    wires.close()


def call_middle(part, inputs, gains):
    vm = pl.BlockSpec(memory_space=pltpu.VMEM)
    return pl.pallas_call(
        middle_kernel,
        out_shape=(
            jax.ShapeDtypeStruct((ROWS, WIDTH), F32),
            jax.ShapeDtypeStruct((ROWS, 128), F32),
            jax.ShapeDtypeStruct((LINE, D), BF),
        ),
        in_specs=[vm] * 3,
        out_specs=(vm, vm, pl.BlockSpec(memory_space=ANY)),
        scratch_shapes=fold_scratch()
        + [
            pltpu.VMEM((ROWS, 128), F32),
            pltpu.VMEM((ROWS, 128), F32),
            pltpu.VMEM((ROWS, WIDTH), BF),
        ]
        + wire_scratch(16)
        + [pltpu.SemaphoreType.DMA((1,))],
        compiler_params=comm_params(2),
        name="line_middle",
    )(part, inputs, gains)


def norm_back(wires, values, scale, gain_row, incoming, mine, theirs, here):
    weighted = incoming * gain_row
    inner = both_cores(
        wires, mine, theirs, jnp.sum(weighted * values, axis=1, keepdims=True), here
    )
    inner = inner / D
    back = scale * (incoming * gain_row) - values * (scale * scale * scale * inner)
    return back, jnp.sum(incoming * values * scale, axis=0, keepdims=True)


def back_kernel(
    part, part_two, middle, scale, gains, cotangent, output, middle_grad, gain_out, out,
    folded, leaving, arriving, total, folded_two, leaving_two, arriving_two, total_two,
    mine, theirs, own, send_sem, recv_sem, local_sem,
):
    z, y, xl, xh, c = place()
    x = xh * 2 + xl
    here = (z, y, x, c)
    greet(line_targets(z, y, x, c))
    wires = Wires(send_sem, recv_sem)
    numbers = fold_sends(wires, part, folded, here)
    moves = fold_moves(wires, numbers, part, folded, leaving, arriving, here, total)
    numbers_two = fold_sends(wires, part_two, folded_two, here)
    moves_two = fold_moves(
        wires, numbers_two, part_two, folded_two, leaving_two, arriving_two, here, total_two
    )
    fold_finish(wires, moves, arriving, total)
    back, gain_sum = norm_back(
        wires, middle[...], scale[:, :1], gains[1:2, :], total[...], mine, theirs, here
    )
    gain_out[...] = jnp.broadcast_to(gain_sum, gain_out.shape)
    grad = cotangent[...].astype(F32) + back
    middle_grad[...] = grad
    own[...] = grad.astype(BF)
    local = pltpu.make_async_copy(own, out.at[row_span(x), col_span(c)], local_sem.at[0])
    local.start()
    sends = gather_sends(wires, own, out, here)
    fold_finish(wires, moves_two, arriving_two, total_two)
    output[...] = (middle[...] + total_two[...]).astype(BF)
    gather_relay(wires, sends, out, here)
    local.wait()
    wires.close()


def call_back(part, part_two, middle, scale, gains, cotangent):
    vm = pl.BlockSpec(memory_space=pltpu.VMEM)
    return pl.pallas_call(
        back_kernel,
        out_shape=(
            jax.ShapeDtypeStruct((ROWS, WIDTH), BF),
            jax.ShapeDtypeStruct((ROWS, WIDTH), F32),
            jax.ShapeDtypeStruct((8, WIDTH), F32),
            jax.ShapeDtypeStruct((LINE, D), BF),
        ),
        in_specs=[vm] * 6,
        out_specs=(vm, vm, vm, pl.BlockSpec(memory_space=ANY)),
        scratch_shapes=fold_scratch()
        + fold_scratch()
        + [
            pltpu.VMEM((ROWS, 128), F32),
            pltpu.VMEM((ROWS, 128), F32),
            pltpu.VMEM((ROWS, WIDTH), BF),
        ]
        + wire_scratch(24)
        + [pltpu.SemaphoreType.DMA((1,))],
        compiler_params=comm_params(3),
        name="line_back",
    )(part, part_two, middle, scale, gains, cotangent)


def last_kernel(
    part, inputs, scale, gains, middle_grad, input_grad, gain_out,
    folded, leaving, arriving, total, mine, theirs, send_sem, recv_sem,
):
    z, y, xl, xh, c = place()
    x = xh * 2 + xl
    here = (z, y, x, c)
    greet(line_targets(z, y, x, c))
    wires = Wires(send_sem, recv_sem)
    numbers = fold_sends(wires, part, folded, here)
    moves = fold_moves(wires, numbers, part, folded, leaving, arriving, here, total)
    fold_finish(wires, moves, arriving, total)
    back, gain_sum = norm_back(
        wires,
        inputs[...].astype(F32),
        scale[:, :1],
        gains[0:1, :],
        total[...],
        mine,
        theirs,
        here,
    )
    gain_out[...] = jnp.broadcast_to(gain_sum, gain_out.shape)
    input_grad[...] = middle_grad[...] + back
    wires.close()


def call_last(part, inputs, scale, gains, middle_grad):
    vm = pl.BlockSpec(memory_space=pltpu.VMEM)
    return pl.pallas_call(
        last_kernel,
        out_shape=(
            jax.ShapeDtypeStruct((ROWS, WIDTH), F32),
            jax.ShapeDtypeStruct((8, WIDTH), F32),
        ),
        in_specs=[vm] * 5,
        out_specs=(vm, vm),
        scratch_shapes=fold_scratch()
        + [pltpu.VMEM((ROWS, 128), F32), pltpu.VMEM((ROWS, 128), F32)]
        + wire_scratch(12),
        compiler_params=comm_params(4),
        name="line_last",
    )(part, inputs, scale, gains, middle_grad)


def whole_piece(ref, order, zi, yi, sub=None):
    if len(ref.shape) == 6:
        return ref.at[order, zi, yi] if sub is None else ref.at[order, zi, yi, sub]
    rows = ref.shape[2] // 2
    if sub is None:
        return ref.at[zi, yi, pl.ds(order * rows, rows)]
    return ref.at[zi, yi, pl.ds(order * rows + sub * (rows // 2), rows // 2)]


def gather_kernel(
    inputs, cotangent, gain_rows, qkv_in, gate_in, down_in, out_in,
    inputs_all, cotangent_all, gains_all, qkv_all, gate_all, down_all, out_all,
    send_sem, recv_sem, out_send, out_recv, local_sem,
):
    z, y, xl, xh, c = place()
    x = xh * 2 + xl
    here = (z, y, x, c)
    mine = xl * 2 + c
    pair = xh * 2 + 1 - xl
    spot = z * 4 + y
    every = slice(None)
    quad = [(x, 1 - c), (pair, c), (pair, 1 - c)]
    near = [(z + 1, y), (z + 3, y), (z, y + 1), (z, y + 3)]
    fixed = (
        line_targets(z, y, x, c)
        + [device(z, y, pair, 1 - c)]
        + [device(a, b, x, c) for a, b in near]
    )
    to_x, to_c = xh * 2 + z // 2, lax.rem(z, 2)
    keeps = z == mine

    barrier = pltpu.get_barrier_semaphore()
    for target in fixed:
        pl.semaphore_signal(barrier, inc=1, device_id=target, device_id_type=MESH)
    for k in range(16):
        from_y, from_x, from_c = k // 4, xh * 2 + (k // 2) % 2, k % 2

        @pl.when(jnp.logical_not(keeps & (y == from_y) & (xl == (k // 2) % 2) & (c == from_c)))
        def _():
            pl.semaphore_signal(
                barrier,
                inc=1,
                device_id=device(mine, jnp.int32(from_y), from_x, jnp.int32(from_c)),
                device_id_type=MESH,
            )

    pl.semaphore_wait(barrier, len(fixed) + 16 - keeps.astype(jnp.int32))

    wires = Wires(send_sem, recv_sem)
    locals_started = []

    def keep(src, dst):
        copy = pltpu.make_async_copy(src, dst, local_sem.at[len(locals_started)])
        copy.start()
        locals_started.append(copy)

    trio = [(qkv_in, qkv_all), (gate_in, gate_all)]
    swaps = []
    for given, whole in trio:
        swaps.append(
            [
                wires.send(
                    given.at[lax.rem(to, 2) * 2 + core],
                    whole.at[c, z, y, xl],
                    device(z, y, to, core),
                )
                for to, core in quad
            ]
        )
        keep(given.at[mine], whole.at[c, z, y, xl])
    down_swap = wires.send(
        down_in.at[1 - c], down_all.at[z, y, :, col_span(c)], device(z, y, x, 1 - c)
    )
    keep(down_in.at[c], down_all.at[z, y, :, col_span(c)])

    keep(inputs, inputs_all.at[row_span(x), col_span(c)])
    keep(cotangent, cotangent_all.at[row_span(x), col_span(c)])
    keep(gain_rows, gains_all.at[:, col_span(c)])
    gain_at = wires.send(gain_rows, gains_all.at[:, col_span(c)], device(z, y, x, 1 - c))
    input_numbers = gather_sends(wires, inputs, inputs_all, here)
    cotangent_numbers = gather_sends(wires, cotangent, cotangent_all, here)

    slot = y * 4 + mine
    out_sends = []
    out_spot = out_all.at[y, xl, :, col_span(c)]
    for k in range(16):
        copy = pltpu.make_async_remote_copy(
            src_ref=out_in,
            dst_ref=out_spot,
            send_sem=out_send.at[k],
            recv_sem=out_recv.at[slot],
            device_id=device(jnp.int32(k // 4), jnp.int32(k % 4), to_x, to_c),
            device_id_type=MESH,
        )
        to_self = keeps & (spot == k)
        out_sends.append((copy, to_self))

        @pl.when(jnp.logical_not(to_self))
        def _():
            copy.start()

        @pl.when(to_self)
        def _():
            pltpu.make_async_copy(out_in, out_spot, out_recv.at[slot]).start()

    for copy in locals_started:
        copy.wait()
    for (given, whole), numbers in zip(trio, swaps):
        for at, (from_x, from_c) in zip(numbers, quad):
            wires.landed(at, whole.at[from_c, z, y, lax.rem(from_x, 2)])
    wires.landed(down_swap, down_all.at[z, y, :, col_span(1 - c)])

    wholes = [qkv_all, gate_all, down_all]

    def step(order, by):
        return (lax.rem(z + by, 4), y) if order == 0 else (z, lax.rem(y + by, 4))

    def other_step(order, by):
        return (z, lax.rem(y + by, 4)) if order == 0 else (lax.rem(z + by, 4), y)

    def run(order, by):
        return (every, lax.rem(y + by, 4)) if order == 0 else (lax.rem(z + by, 4), every)

    first = [
        [[wires.send(whole_piece(w, o, z, y), whole_piece(w, o, z, y), device(*step(o, by), x, c)) for by in (1, 3)] for o in (0, 1)]
        for w in wholes
    ]
    second = []
    for w, numbers in zip(wholes, first):
        per_order = []
        for o in (0, 1):
            sends = []
            for sub, by in enumerate((1, 3)):
                back = 4 - by
                wires.landed(numbers[o][sub], whole_piece(w, o, *step(o, back)))
                part = whole_piece(w, o, *step(o, back), sub)
                sends.append(wires.send(part, part, device(*step(o, by), x, c)))
            per_order.append(sends)
        second.append(per_order)
    third = []
    for w, numbers in zip(wholes, second):
        per_order = []
        for o in (0, 1):
            for sub in (0, 1):
                wires.landed(numbers[o][sub], whole_piece(w, o, *step(o, 2), sub))
            line = whole_piece(w, o, *run(o, 0))
            per_order.append(
                [wires.send(line, line, device(*other_step(o, by), x, c)) for by in (1, 3)]
            )
        third.append(per_order)
    gather_relay(wires, input_numbers, inputs_all, here)
    gather_relay(wires, cotangent_numbers, cotangent_all, here)
    wires.landed(gain_at, gains_all.at[:, col_span(1 - c)])
    fourth = []
    for w, numbers in zip(wholes, third):
        per_order = []
        for o in (0, 1):
            sends = []
            for sub, by in enumerate((1, 3)):
                back = 4 - by
                wires.landed(numbers[o][sub], whole_piece(w, o, *run(o, back)))
                part = whole_piece(w, o, *run(o, back), sub)
                sends.append(wires.send(part, part, device(*other_step(o, by), x, c)))
            per_order.append(sends)
        fourth.append(per_order)
    for w, numbers in zip(wholes, fourth):
        for o in (0, 1):
            for sub in (0, 1):
                wires.landed(numbers[o][sub], whole_piece(w, o, *run(o, 2), sub))
    for k in range(16):
        spot_k = out_all.at[k // 4, (k // 2) % 2, :, pl.ds((k % 2) * WIDTH, WIDTH)]
        pltpu.make_async_copy(spot_k, spot_k, out_recv.at[k]).wait()
    for copy, to_self in out_sends:

        @pl.when(jnp.logical_not(to_self))
        def _():
            copy.wait_send()

    wires.close()


def call_gather(inputs, cotangent, gain_rows, qkv_in, gate_in, down_in, out_in):
    shapes = (
        jax.ShapeDtypeStruct((LINE, D), BF),
        jax.ShapeDtypeStruct((LINE, D), BF),
        jax.ShapeDtypeStruct((8, D), F32),
        jax.ShapeDtypeStruct((2, 4, 4, 2) + qkv_in.shape[1:], BF),
        jax.ShapeDtypeStruct((2, 4, 4, 2) + gate_in.shape[1:], BF),
        jax.ShapeDtypeStruct((4, 4, down_in.shape[1], D), BF),
        jax.ShapeDtypeStruct((4, 2, PIECE, D), BF),
    )
    hbm = pl.BlockSpec(memory_space=ANY)
    return pl.pallas_call(
        gather_kernel,
        out_shape=shapes,
        in_specs=[hbm] * 7,
        out_specs=(hbm,) * 7,
        scratch_shapes=wire_scratch(80)
        + wire_scratch(16)
        + [pltpu.SemaphoreType.DMA((8,))],
        compiler_params=comm_params(1),
        name="gather_weights",
    )(inputs, cotangent, gain_rows, qkv_in, gate_in, down_in, out_in)


def keys_kernel(own, out, send_sem, recv_sem, local_sem):
    z, y, xl, xh, c = place()
    x = xh * 2 + xl
    every = slice(None)
    greet(plane_targets(z, y, x, c))
    wires = Wires(send_sem, recv_sem)
    offsets = (2, 1, 3)
    first = [
        [wires.send(own.at[0], out.at[0, z, y], device(z + o, y, x, c)) for o in offsets],
        [wires.send(own.at[1], out.at[1, z, y], device(z, y + o, x, c)) for o in offsets],
    ]
    keeps = [pltpu.make_async_copy(own.at[s], out.at[s, z, y], local_sem.at[s]) for s in (0, 1)]
    for copy in keeps:
        copy.start()
    for copy in keeps:
        copy.wait()
    for at, o in zip(first[0], offsets):
        wires.landed(at, out.at[0, lax.rem(z + 4 - o, 4), y])
    line = out.at[0, :, y]
    low = [wires.send(line, line, device(z, y + o, x, c)) for o in offsets]
    for at, o in zip(first[1], offsets):
        wires.landed(at, out.at[1, z, lax.rem(y + 4 - o, 4)])
    line = out.at[1, z]
    high = [wires.send(line, line, device(z + o, y, x, c)) for o in offsets]
    for at, o in zip(low, offsets):
        wires.landed(at, out.at[0, :, lax.rem(y + 4 - o, 4)])
    for at, o in zip(high, offsets):
        wires.landed(at, out.at[1, lax.rem(z + 4 - o, 4)])
    wires.close()


def call_keys(own):
    hbm = pl.BlockSpec(memory_space=ANY)
    return pl.pallas_call(
        keys_kernel,
        out_shape=jax.ShapeDtypeStruct((2, 4, 4, HALF, 2 * HD), BF),
        in_specs=[hbm],
        out_specs=hbm,
        scratch_shapes=wire_scratch(12) + [pltpu.SemaphoreType.DMA((2,))],
        compiler_params=comm_params(5),
        name="gather_keys",
    )(own)


def key_grads_kernel(terms, out, rec_one, sums, rec_two, send_sem, recv_sem):
    z, y, xl, xh, c = place()
    x = xh * 2 + xl
    greet(plane_targets(z, y, x, c))
    wires = Wires(send_sem, recv_sem)
    offsets = (2, 1, 3)
    first = [[], []]
    for k, o in enumerate(offsets):
        to_y, to_z = lax.rem(y + o, 4), lax.rem(z + o, 4)
        first[0].append(
            wires.send(terms.at[0, :, to_y], rec_one.at[0, k], device(z, y + o, x, c))
        )
        first[1].append(wires.send(terms.at[1, to_z], rec_one.at[1, k], device(z + o, y, x, c)))
    second = [[], []]
    for s in (0, 1):
        for k in range(3):
            wires.landed(first[s][k], rec_one.at[s, k])
        for i in range(4):
            value = terms[0, i, y] if s == 0 else terms[1, z, i]
            value = value.astype(F32)
            for k in range(3):
                value = value + rec_one[s, k, i].astype(F32)
            sums[s, i] = value.astype(BF)
        for k, o in enumerate(offsets):
            if s == 0:
                src, target = sums.at[0, lax.rem(z + o, 4)], device(z + o, y, x, c)
            else:
                src, target = sums.at[1, lax.rem(y + o, 4)], device(z, y + o, x, c)
            second[s].append(wires.send(src, rec_two.at[s, k], target))
    for s in (0, 1):
        value = sums[s, z if s == 0 else y].astype(F32)
        for k in range(3):
            wires.landed(second[s][k], rec_two.at[s, k])
            value = value + rec_two[s, k].astype(F32)
        out[s] = value
    wires.close()


def call_key_grads(terms):
    vm = pl.BlockSpec(memory_space=pltpu.VMEM)
    return pl.pallas_call(
        key_grads_kernel,
        out_shape=jax.ShapeDtypeStruct((2, HALF, 2 * HD), F32),
        in_specs=[vm],
        out_specs=vm,
        scratch_shapes=[
            pltpu.VMEM((2, 3, 4, HALF, 2 * HD), BF),
            pltpu.VMEM((2, 4, HALF, 2 * HD), BF),
            pltpu.VMEM((2, 3, HALF, 2 * HD), BF),
        ]
        + wire_scratch(12),
        compiler_params=comm_params(6),
        name="sum_key_grads",
    )(terms)


def part_of(ref, order, zi, yi):
    return whole_piece(ref, order, zi, yi)


def grads_kernel(
    qkv, gate, down, out_grad, qkv_out, gate_out, down_out, out_out,
    qkv_rec, qkv_sum, qkv_rec_two, qkv_fin,
    gate_rec, gate_sum, gate_rec_two, gate_fin,
    down_rec, down_sum, down_rec_two, down_fin,
    out_rec, send_sem, recv_sem, out_send, out_recv, local_sem,
):
    z, y, xl, xh, c = place()
    x = xh * 2 + xl
    mine = xl * 2 + c
    pair = xh * 2 + 1 - xl
    spot = z * 4 + y
    every = slice(None)
    quad = [(x, 1 - c), (pair, c), (pair, 1 - c)]
    offsets = (2, 1, 3)
    keeps = z == mine
    from_x, from_c = xh * 2 + z // 2, lax.rem(z, 2)

    fixed = plane_targets(z, y, x, c) + [device(z, y, a, b) for a, b in quad]
    barrier = pltpu.get_barrier_semaphore()
    for target in fixed:
        pl.semaphore_signal(barrier, inc=1, device_id=target, device_id_type=MESH)
    for k in range(16):

        @pl.when(jnp.logical_not(keeps & (spot == k)))
        def _():
            pl.semaphore_signal(
                barrier,
                inc=1,
                device_id=device(jnp.int32(k // 4), jnp.int32(k % 4), from_x, from_c),
                device_id_type=MESH,
            )

    pl.semaphore_wait(barrier, len(fixed) + 16 - keeps.astype(jnp.int32))
    wires = Wires(send_sem, recv_sem)

    def second_axis(order, by):
        return device(z, y + by, x, c) if order == 0 else device(z + by, y, x, c)

    def first_axis(order, by):
        return device(z + by, y, x, c) if order == 0 else device(z, y + by, x, c)

    def run(order, by):
        return (every, lax.rem(y + by, 4)) if order == 0 else (lax.rem(z + by, 4), every)

    sets = [
        (gate, gate_rec, gate_sum, gate_rec_two, gate_fin),
        (down, down_rec, down_sum, down_rec_two, down_fin),
        (qkv, qkv_rec, qkv_sum, qkv_rec_two, qkv_fin),
    ]
    first, own = [], []
    for t, (grad, rec, total, _, _) in enumerate(sets):
        own.append([])
        first.append([])
        for o in (0, 1):
            first[t].append(
                [
                    wires.send(part_of(grad, o, *run(o, by)), rec.at[o, k], second_axis(o, by))
                    for k, by in enumerate(offsets)
                ]
            )
            copy = pltpu.make_async_copy(
                part_of(grad, o, *run(o, 0)), total.at[o], local_sem.at[t * 2 + o]
            )
            copy.start()
            own[t].append(copy)

    out_sends = []
    for k in range(16):
        to_y, to_xl, to_c = k // 4, (k // 2) % 2, k % 2
        src = out_grad.at[to_y, to_xl, :, pl.ds(to_c * WIDTH, WIDTH)]
        to_self = keeps & (y == to_y) & (xl == to_xl) & (c == to_c)
        copy = pltpu.make_async_remote_copy(
            src_ref=src,
            dst_ref=out_rec.at[spot],
            send_sem=out_send.at[k],
            recv_sem=out_recv.at[spot],
            device_id=device(mine, jnp.int32(to_y), xh * 2 + to_xl, jnp.int32(to_c)),
            device_id_type=MESH,
        )
        out_sends.append((copy, to_self))

        @pl.when(jnp.logical_not(to_self))
        def _():
            copy.start()

        @pl.when(to_self)
        def _():
            pltpu.make_async_copy(src, out_rec.at[spot], out_recv.at[spot]).start()

    second = []
    for t, (grad, rec, total, rec_two, _) in enumerate(sets):
        second.append([])
        for o in (0, 1):
            own[t][o].wait()
            for k in range(3):
                wires.landed(first[t][o][k], rec.at[o, k])

            def add(i, carry):
                value = total[o, i].astype(F32)
                for k in range(3):
                    value = value + rec[o, k, i].astype(F32)
                total[o, i] = value.astype(BF)
                return carry

            lax.fori_loop(0, 4, add, 0)
            at = z if o == 0 else y
            second[t].append(
                [
                    wires.send(
                        total.at[o, lax.rem(at + by, 4)], rec_two.at[o, k], first_axis(o, by)
                    )
                    for k, by in enumerate(offsets)
                ]
            )
    last = []
    for t, (_, _, total, rec_two, fin) in enumerate(sets):
        for o in (0, 1):
            for k in range(3):
                wires.landed(second[t][o][k], rec_two.at[o, k])
            value = total[o, z if o == 0 else y].astype(F32)
            for k in range(3):
                value = value + rec_two[o, k].astype(F32)
            fin[o] = value.astype(BF)
        if t == 1:
            to = fin.at[:, :, col_span(1 - c)]
            last.append([wires.send(to, down_out.at[c], device(z, y, x, 1 - c))])
            copy = pltpu.make_async_copy(
                fin.at[:, :, col_span(c)], down_out.at[c], local_sem.at[6]
            )
        else:
            result = gate_out if t == 0 else qkv_out
            last.append(
                [
                    wires.send(fin.at[b, lax.rem(a, 2)], result.at[mine], device(z, y, a, b))
                    for a, b in quad
                ]
            )
            copy = pltpu.make_async_copy(fin.at[c, xl], result.at[mine], local_sem.at[7 + t])
        copy.start()
        own.append(copy)
    total = None
    for k in range(16):
        pltpu.make_async_copy(out_rec.at[k], out_rec.at[k], out_recv.at[k]).wait()
        total = out_rec[k].astype(F32) if total is None else total + out_rec[k].astype(F32)
    out_out[...] = total
    for t, result in ((0, gate_out), (2, qkv_out)):
        for at, (a, b) in zip(last[t], quad):
            wires.landed(at, result.at[lax.rem(a, 2) * 2 + b])
    wires.landed(last[1][0], down_out.at[1 - c])
    for copy in own[3:]:
        copy.wait()
    for copy, to_self in out_sends:

        @pl.when(jnp.logical_not(to_self))
        def _():
            copy.wait_send()

    wires.close()


def call_grads(qkv, gate, down, out_grad):
    hbm = pl.BlockSpec(memory_space=ANY)
    vm = pl.BlockSpec(memory_space=pltpu.VMEM)

    def buffers(cols, depth):
        lead = (2, PIECE) if depth == 0 else (depth,)
        return [
            pltpu.VMEM((2, 3, 4) + lead + (cols,), BF),
            pltpu.VMEM((2, 4) + lead + (cols,), BF),
            pltpu.VMEM((2, 3) + lead + (cols,), BF),
            pltpu.VMEM((2,) + lead + (cols,), BF),
        ]

    qkv_cols, gate_cols = qkv.shape[-1], gate.shape[-1]
    return pl.pallas_call(
        grads_kernel,
        out_shape=(
            jax.ShapeDtypeStruct((4, PIECE, qkv_cols), BF),
            jax.ShapeDtypeStruct((4, PIECE, gate_cols), BF),
            jax.ShapeDtypeStruct((2, 2, PIECE, WIDTH), BF),
            jax.ShapeDtypeStruct((PIECE, WIDTH), F32),
        ),
        in_specs=[hbm] * 4,
        out_specs=(hbm, hbm, hbm, vm),
        scratch_shapes=buffers(qkv_cols, 0)
        + buffers(gate_cols, 0)
        + buffers(D, PIECE)
        + [pltpu.VMEM((16, PIECE, WIDTH), BF)]
        + wire_scratch(48)
        + wire_scratch(16)
        + [pltpu.SemaphoreType.DMA((10,))],
        compiler_params=comm_params(7),
        name="sum_weight_grads",
    )(qkv, gate, down, out_grad)


def total_kernel(terms, out, stage, rec, rec_two, rec_three, last, send_sem, recv_sem):
    z, y, xl, xh, c = place()
    x = xh * 2 + xl
    plane = [(a, b) for a in range(4) for b in range(4) if a or b]
    targets = [device(z + a, y + b, x, c) for a, b in plane] + line_targets(z, y, x, c)
    greet(targets)
    wires = Wires(send_sem, recv_sem)
    first = [
        wires.send(terms, rec.at[k], device(z + a, y + b, x, c)) for k, (a, b) in enumerate(plane)
    ]
    value = terms[...]
    for k, at in enumerate(first):
        wires.landed(at, rec.at[k])
        value = value + rec[k]
    stage[...] = value
    second = [
        wires.send(stage, rec_two.at[k], device(z, y, lax.rem(x + o, 4), c))
        for k, o in enumerate((1, 2, 3))
    ]
    for k, at in enumerate(second):
        wires.landed(at, rec_two.at[k])
        value = value + rec_two[k]
    gains = value[:16]
    square = value[16:] + jnp.sum(gains * gains)
    last[...] = square
    at = wires.send(last, rec_three, device(z, y, x, 1 - c))
    wires.landed(at, rec_three)
    out[:16] = gains
    out[16:] = square + rec_three[...]
    wires.close()


def call_total(terms):
    vm = pl.BlockSpec(memory_space=pltpu.VMEM)
    return pl.pallas_call(
        total_kernel,
        out_shape=jax.ShapeDtypeStruct((24, 128), F32),
        in_specs=[vm],
        out_specs=vm,
        scratch_shapes=[
            pltpu.VMEM((24, 128), F32),
            pltpu.VMEM((15, 24, 128), F32),
            pltpu.VMEM((3, 24, 128), F32),
            pltpu.VMEM((8, 128), F32),
            pltpu.VMEM((8, 128), F32),
        ]
        + wire_scratch(19),
        compiler_params=comm_params(8),
        name="total",
    )(terms)


def slot_of(half):
    return jnp.where(half < HALVES // 2, half, HALVES + HALVES // 2 - 1 - half)


def allowed_pairs(key_half, query_half, ends):
    keys = key_half * HALF + lax.broadcasted_iota(jnp.int32, (HALF, HALF), 0)
    queries = query_half * HALF + lax.broadcasted_iota(jnp.int32, (HALF, HALF), 1)
    same = keys <= queries
    for k in range(3):
        same = same & ((keys >= ends[k]) == (queries >= ends[k]))
    return same


def in_second(query_half, ends):
    queries = query_half * HALF + lax.broadcasted_iota(jnp.int32, (1, HALF), 1)
    return (queries >= ends[0]) & (queries < ends[1])


def forward_kernel(ends, queries, keys, out, log_out, tops, sums, mixed):
    z, y, _, _, _ = place()
    spot = z * 4 + y
    for s in (0, 1):
        half = spot if s == 0 else HALVES - 1 - spot
        tops[...] = jnp.full(tops.shape, NEVER, F32)
        sums[...] = jnp.zeros(sums.shape, F32)
        mixed[...] = jnp.zeros(mixed.shape, F32)

        def step(at, masked):
            pairs = keys[slot_of(at)]
            if masked:
                allowed = allowed_pairs(at, half, ends)
            for g in range(GROUP):
                cols = slice(g * HALF, (g + 1) * HALF)
                scores = jnp.dot(pairs, queries[s, :, cols], preferred_element_type=F32)
                if masked:
                    scores = jnp.where(allowed, scores, NEVER)
                old = tops[:, cols]
                top = jnp.maximum(old, jnp.max(scores, axis=0, keepdims=True))
                weights = jnp.exp(scores - top)
                if masked:
                    weights = jnp.where(allowed, weights, 0.0)
                shrink = jnp.exp(old - top)
                tops[:, cols] = top
                sums[:, cols] = sums[:, cols] * shrink + jnp.sum(weights, axis=0, keepdims=True)
                mixed[:, cols] = mixed[:, cols] * shrink + lax.dot_general(
                    pairs,
                    weights.astype(BF),
                    (((0,), (0,)), ((), ())),
                    preferred_element_type=F32,
                )

        def inner(at, carry):
            step(at, False)
            return carry

        lax.fori_loop(1, half, inner, 0)
        fits = in_second(half, ends)
        for g in range(GROUP):
            cols = slice(g * HALF, (g + 1) * HALF)
            tops[:, cols] = jnp.where(fits, tops[:, cols], NEVER)
            sums[:, cols] = jnp.where(fits, sums[:, cols], 0.0)
            mixed[:, cols] = jnp.where(fits, mixed[:, cols], 0.0)

        def edge(at, carry):
            step(at * half, True)
            return carry

        lax.fori_loop(0, jnp.where(half > 0, 2, 1), edge, 0)
        total = sums[...]
        out[s] = mixed[HD:, :] / total
        log_out[s] = tops[...] + jnp.log(total)


def call_forward(ends, queries, keys):
    vm = pl.BlockSpec(memory_space=pltpu.VMEM)
    cols = GROUP * HALF
    return pl.pallas_call(
        forward_kernel,
        out_shape=(
            jax.ShapeDtypeStruct((2, HD, cols), F32),
            jax.ShapeDtypeStruct((2, 1, cols), F32),
        ),
        in_specs=[pl.BlockSpec(memory_space=pltpu.SMEM), vm, vm],
        out_specs=(vm, vm),
        scratch_shapes=[
            pltpu.VMEM((1, cols), F32),
            pltpu.VMEM((1, cols), F32),
            pltpu.VMEM((2 * HD, cols), F32),
        ],
        compiler_params=pltpu.CompilerParams(vmem_limit_bytes=VMEM_LIMIT),
        name="attention",
    )(ends, queries, keys)


def backward_kernel(
    ends, queries, grads, query_rows, grad_rows, logs, delta, keys, query_back, key_back, terms, sums
):
    z, y, _, _, _ = place()
    spot = z * 4 + y
    terms[...] = jnp.zeros(terms.shape, F32)
    for s in (0, 1):
        half = spot if s == 0 else HALVES - 1 - spot
        sums[...] = jnp.zeros(sums.shape, F32)
        fits = in_second(half, ends)

        def step(at, masked):
            slot = slot_of(at)
            pairs = keys[slot]
            if masked:
                allowed = allowed_pairs(at, half, ends)
            added = None
            for g in range(GROUP):
                cols = slice(g * HALF, (g + 1) * HALF)
                scores = jnp.dot(pairs, queries[s, :, cols], preferred_element_type=F32)
                log_row = logs[s, :, cols]
                if not masked:
                    log_row = jnp.where(fits, log_row, -NEVER)
                probs = jnp.exp(scores - log_row)
                if masked:
                    probs = jnp.where(allowed, probs, 0.0)
                prob_grad = jnp.dot(pairs, grads[s, :, cols], preferred_element_type=F32)
                score_grad = (probs * (prob_grad - delta[s, :, cols])).astype(BF)
                sums[:, cols] += lax.dot_general(
                    pairs, score_grad, (((0,), (0,)), ((), ())), preferred_element_type=F32
                )
                term = jnp.dot(
                    score_grad, query_rows[s, g], preferred_element_type=F32
                ) + jnp.dot(probs.astype(BF), grad_rows[s, g], preferred_element_type=F32)
                added = term if added is None else added + term
            terms[slot] += added

        def inner(at, carry):
            step(at, False)
            return carry

        lax.fori_loop(1, half, inner, 0)

        def edge(at, carry):
            step(at * half, True)
            return carry

        lax.fori_loop(0, jnp.where(half > 0, 2, 1), edge, 0)
        query_back[s] = sums[:HD, :] * HD ** (-0.5)
    key_back[...] = terms[...].astype(BF)


def call_backward(ends, queries, grads, query_rows, grad_rows, logs, delta, keys):
    vm = pl.BlockSpec(memory_space=pltpu.VMEM)
    cols = GROUP * HALF
    return pl.pallas_call(
        backward_kernel,
        out_shape=(
            jax.ShapeDtypeStruct((2, HD, cols), F32),
            jax.ShapeDtypeStruct((HALVES, HALF, 2 * HD), BF),
        ),
        in_specs=[pl.BlockSpec(memory_space=pltpu.SMEM)] + [vm] * 7,
        out_specs=(vm, vm),
        scratch_shapes=[
            pltpu.VMEM((HALVES, HALF, 2 * HD), F32),
            pltpu.VMEM((2 * HD, cols), F32),
        ],
        compiler_params=pltpu.CompilerParams(vmem_limit_bytes=VMEM_LIMIT),
        name="attention_back",
    )(ends, queries, grads, query_rows, grad_rows, logs, delta, keys)


def rope_tables(position, head_size):
    half_size = head_size // 2
    column = jnp.arange(half_size, dtype=jnp.float32)
    inverse = jnp.exp(-(2.0 * column / head_size) * math.log(ROPE_THETA))
    wavelength = 2.0 * math.pi / inverse
    smooth = (OLD_CONTEXT / wavelength - LOW_FREQ) / (HIGH_FREQ - LOW_FREQ)
    blended = (1.0 - smooth) * inverse / ROPE_FACTOR + smooth * inverse
    inverse = jnp.where(
        wavelength < OLD_CONTEXT / HIGH_FREQ,
        inverse,
        jnp.where(wavelength > OLD_CONTEXT / LOW_FREQ, inverse / ROPE_FACTOR, blended),
    )
    angles = position.astype(jnp.float32)[:, None] * inverse[None, :]
    return (jnp.cos(angles), jnp.sin(angles))


def rotate(values, cosine, sine):
    half_size = values.shape[-1] // 2
    table_shape = (cosine.shape[0],) + (1,) * (values.ndim - 2) + (half_size,)
    cos_part = cosine.reshape(table_shape)
    sin_part = sine.reshape(table_shape)
    first_half = values[..., :half_size]
    second_half = values[..., half_size:]
    return jnp.concatenate(
        [
            first_half * cos_part - second_half * sin_part,
            second_half * cos_part + first_half * sin_part,
        ],
        axis=-1,
    )


def times(left, right, kind):
    return jnp.dot(left, right, preferred_element_type=F32).astype(kind)


def times_transpose(left, right, kind):
    return lax.dot_general(
        left, right, (((1,), (1,)), ((), ())), preferred_element_type=F32
    ).astype(kind)


def outer_rows(left, right, kind):
    return lax.dot_general(
        left, right, (((0,), (0,)), ((), ())), preferred_element_type=F32
    ).astype(kind)


def as_columns(rows):
    return rows.reshape(2, HALF, GROUP, HD).transpose(0, 3, 2, 1).reshape(2, HD, GROUP * HALF)


def as_heads(rows):
    return rows.reshape(2, HALF, GROUP, HD).transpose(0, 2, 1, 3)


def from_columns(columns):
    return columns.reshape(2, HD, GROUP, HALF).transpose(0, 3, 2, 1).reshape(LINE, GROUP * HD)


def adam(weight, moment, second, gradient, rate, decay):
    moment_next = BETA_ONE * moment + (1.0 - BETA_ONE) * gradient
    second_next = BETA_TWO * second + (1.0 - BETA_TWO) * gradient * gradient
    unbiased = moment_next / (1.0 - BETA_ONE**ADAM_STEP)
    divisor = jnp.sqrt(second_next / (1.0 - BETA_TWO**ADAM_STEP)) + ADAM_EPS
    return (weight - rate * (unbiased / divisor + decay * weight), moment_next, second_next)


def shards(
    block_input,
    out_grad,
    qkv_weight,
    qkv_moment,
    qkv_second,
    gate_up_weight,
    gate_up_moment,
    gate_up_second,
    out_weight,
    out_moment,
    out_second,
    down_weight,
    down_moment,
    down_second,
    norm_gains,
    gains_moment,
    gains_second,
    doc_lengths,
):
    z, y, xl, xh, c = place()
    x = xh * 2 + xl
    spot = z * 4 + y
    blocks = [block_of(at) for at in range(TOKENS // ROWS)]
    there = [(block, at) for at, block in enumerate(blocks)]
    home = [(at, block) for at, block in enumerate(blocks)]
    inputs = lax.ppermute(block_input, ("seq", "wide"), there)
    cotangent = lax.ppermute(out_grad, ("seq", "wide"), there)

    qkv_in = qkv_weight.astype(BF).transpose(1, 0, 2)
    gate_in = (
        gate_up_weight.astype(BF)
        .reshape(PIECE, 2, 16, 4, HD)
        .transpose(3, 0, 1, 2, 4)
        .reshape(4, PIECE, 2 * HIDDEN)
    )
    down_in = down_weight.astype(BF).reshape(2, ROWS // 2, WIDTH)
    gain_rows = jnp.concatenate([norm_gains, jnp.zeros((6, WIDTH), F32)], axis=0)
    inputs_all, cotangent_all, gains_all, qkv_whole, gate_whole, down_whole, out_whole = (
        call_gather(
            inputs, cotangent, gain_rows, qkv_in, gate_in, down_in, out_weight.astype(BF)
        )
    )
    qkv_low = qkv_whole.reshape(D, (GROUP + 2) * HD)
    gate_low = gate_whole.reshape(D, 2 * HIDDEN)
    down_low = down_whole.reshape(HIDDEN, D)
    out_low = out_whole.reshape(GROUP * HD, D)

    values = inputs_all.astype(F32)
    scale_one = lax.rsqrt(jnp.sum(values * values, axis=1, keepdims=True) / D + NORM_EPS)
    normed = (values * scale_one * gains_all[0:1, :]).astype(BF)
    projected = times(normed, qkv_low, F32)

    ends = jnp.cumsum(doc_lengths)
    local = jnp.arange(LINE, dtype=jnp.int32)
    half = jnp.where(local < HALF, spot, HALVES - 1 - spot)
    places = half * HALF + lax.rem(local, HALF)
    passed = (places[:, None] >= ends[None, :]).astype(jnp.int32)
    position = places - jnp.sum(passed * doc_lengths[None, :], axis=1)
    cosine, sine = rope_tables(position, HD)
    turned = rotate(
        projected[:, : (GROUP + 1) * HD].reshape(LINE, GROUP + 1, HD), cosine, sine
    ).astype(BF)
    queries = turned[:, :GROUP].reshape(LINE, GROUP * HD) * jnp.asarray(HD ** (-0.5), BF)
    own_keys = jnp.concatenate([turned[:, GROUP], projected[:, (GROUP + 1) * HD :].astype(BF)], axis=1)
    keys = call_keys(own_keys.reshape(2, HALF, 2 * HD)).reshape(HALVES, HALF, 2 * HD)

    blank = jnp.zeros((2, HD, GROUP * HALF), BF)
    query_columns = jnp.concatenate([as_columns(queries), blank], axis=1)
    mixed, logs = call_forward(ends, query_columns, keys)
    mixed_rows = from_columns(mixed)
    attended = mixed_rows.astype(BF)
    middle, scale_two, normed_two = call_middle(times(attended, out_low, BF), inputs, norm_gains)

    gate_up = times(normed_two, gate_low, F32)
    gate_part, up_part = gate_up[:, :HIDDEN], gate_up[:, HIDDEN:]
    sigmoid_gate = jax.nn.sigmoid(gate_part)
    hidden = (gate_part * sigmoid_gate * up_part).astype(BF)
    hidden_grad = times_transpose(cotangent_all, down_low, F32)
    gate_back = hidden_grad * up_part * sigmoid_gate * (1.0 + gate_part * (1.0 - sigmoid_gate))
    up_back = hidden_grad * gate_part * sigmoid_gate
    gate_up_back = jnp.concatenate([gate_back, up_back], axis=1).astype(BF)
    output, middle_grad, gain_two, middle_low = call_back(
        times_transpose(gate_up_back, gate_low, BF),
        times(hidden, down_low, BF),
        middle,
        scale_two,
        norm_gains,
        cotangent,
    )
    grad_down = outer_rows(hidden, cotangent_all, BF)
    grad_gate = outer_rows(normed_two, gate_up_back, BF)

    grad_out = outer_rows(attended, middle_low, BF)
    attended_grad = times_transpose(middle_low, out_low, BF)
    delta = jnp.sum(
        (attended_grad.astype(F32) * mixed_rows).reshape(LINE, GROUP, HD), axis=-1
    )
    delta = delta.reshape(2, HALF, GROUP).transpose(0, 2, 1).reshape(2, 1, GROUP * HALF)
    empty = jnp.zeros((2, GROUP, HALF, HD), BF)
    query_back, key_terms = call_backward(
        ends,
        query_columns,
        jnp.concatenate([blank, as_columns(attended_grad)], axis=1),
        jnp.concatenate([as_heads(queries), empty], axis=-1),
        jnp.concatenate([empty, as_heads(attended_grad)], axis=-1),
        logs,
        delta,
        keys,
    )
    key_grads = call_key_grads(key_terms.reshape(2, 4, 4, HALF, 2 * HD)).reshape(LINE, 2 * HD)
    turned_back = jnp.concatenate([from_columns(query_back), key_grads[:, :HD]], axis=1)
    turned_back = rotate(turned_back.reshape(LINE, GROUP + 1, HD), cosine, -sine)
    projected_back = jnp.concatenate(
        [turned_back.reshape(LINE, (GROUP + 1) * HD), key_grads[:, HD:]], axis=1
    ).astype(BF)
    grad_qkv = outer_rows(normed, projected_back, BF)
    scale_rows = lax.dynamic_slice_in_dim(scale_one, x * ROWS, ROWS, 0)
    input_grad, gain_one = call_last(
        times_transpose(projected_back, qkv_low, BF),
        inputs,
        jnp.broadcast_to(scale_rows, (ROWS, 128)),
        norm_gains,
        middle_grad,
    )
    qkv_sum, gate_sum, down_sum, out_sum = call_grads(
        grad_qkv.reshape(qkv_whole.shape),
        grad_gate.reshape(gate_whole.shape),
        grad_down.reshape(down_whole.shape),
        grad_out.reshape(out_whole.shape),
    )
    output = lax.ppermute(output, ("seq", "wide"), home)
    input_grad = lax.ppermute(input_grad, ("seq", "wide"), home)

    shares = (
        qkv_sum.transpose(1, 0, 2).astype(F32),
        gate_sum.reshape(4, PIECE, 2, 16, HD)
        .transpose(1, 2, 3, 0, 4)
        .reshape(gate_up_weight.shape)
        .astype(F32),
        out_sum,
        down_sum.reshape(down_weight.shape).astype(F32),
    )
    square = sum(
        jnp.sum(jnp.square(member.astype(F32))) for member in (qkv_sum, gate_sum, out_sum, down_sum)
    )
    terms = jnp.concatenate(
        [
            jnp.stack([gain_one[0], gain_two[0]]).reshape(16, 128),
            jnp.broadcast_to(square, (8, 128)),
        ],
        axis=0,
    )
    totals = call_total(terms)
    gains_grad = totals[:16].reshape(2, WIDTH)
    grad_norm = jnp.sqrt(totals[16, 0])
    factor = CLIP_NORM / jnp.maximum(grad_norm, CLIP_NORM)
    weights = (qkv_weight, gate_up_weight, out_weight, down_weight)
    moments = (qkv_moment, gate_up_moment, out_moment, down_moment)
    seconds = (qkv_second, gate_up_second, out_second, down_second)
    out_rate = OUTPUT_RATE * (TOKENS / (HQ * HD)) ** 0.5
    down_rate = DOWN_RATE * FF ** (-0.5)
    rates = (MATRIX_RATE, MATRIX_RATE, out_rate, down_rate)
    results = []
    for weight, moment, second, gradient, rate in zip(weights, moments, seconds, shares, rates):
        results.extend(adam(weight, moment, second, gradient * factor, rate, WEIGHT_DECAY))
    gains_new = adam(norm_gains, gains_moment, gains_second, gains_grad * factor, GAIN_RATE, 0.0)
    return (output, input_grad, grad_norm, *results, *gains_new)


def solution(mesh):
    placed = (
        P(("seq", "wide"), "narrow"),
        P(("seq", "wide"), "narrow"),
        P(("narrow", "seq"), "wide", None),
        P(("narrow", "seq"), "wide", None),
        P(("narrow", "seq"), "wide", None),
        P(("narrow", "seq"), None, "wide"),
        P(("narrow", "seq"), None, "wide"),
        P(("narrow", "seq"), None, "wide"),
        P(("wide", "seq"), "narrow"),
        P(("wide", "seq"), "narrow"),
        P(("wide", "seq"), "narrow"),
        P(("wide", "seq"), "narrow"),
        P(("wide", "seq"), "narrow"),
        P(("wide", "seq"), "narrow"),
        P(None, "narrow"),
        P(None, "narrow"),
        P(None, "narrow"),
        P(),
    )
    return jax.shard_map(
        shards,
        mesh=mesh,
        in_specs=placed,
        out_specs=(
            P(("seq", "wide"), "narrow"),
            P(("seq", "wide"), "narrow"),
            P(),
            P(("narrow", "seq"), "wide", None),
            P(("narrow", "seq"), "wide", None),
            P(("narrow", "seq"), "wide", None),
            P(("narrow", "seq"), None, "wide"),
            P(("narrow", "seq"), None, "wide"),
            P(("narrow", "seq"), None, "wide"),
            P(("wide", "seq"), "narrow"),
            P(("wide", "seq"), "narrow"),
            P(("wide", "seq"), "narrow"),
            P(("wide", "seq"), "narrow"),
            P(("wide", "seq"), "narrow"),
            P(("wide", "seq"), "narrow"),
            P(None, "narrow"),
            P(None, "narrow"),
            P(None, "narrow"),
        ),
        check_vma=False,
    )
```

```python
import functools
import math

import jax
import jax.numpy as jnp
from jax import lax
from jax.experimental import pallas as pl
from jax.experimental.pallas import tpu as pltpu
from jax.sharding import PartitionSpec as P

D = 2048
HQ = 32
HD = 64
FF = 8192
ADAM_STEP = 10


NORM_EPS = 1e-05
ADAM_EPS = 1e-08
BETA_ONE = 0.9
BETA_TWO = 0.95
WEIGHT_DECAY = 0.1
MATRIX_RATE = 0.01
OUTPUT_RATE = 0.9
DOWN_RATE = 3.0
GAIN_RATE = 2.5
CLIP_NORM = 1.0
ROPE_THETA = 500000.0
ROPE_FACTOR = 32.0
LOW_FREQ = 1.0
HIGH_FREQ = 4.0
OLD_CONTEXT = 8192.0

TOKENS = 8192
HALF = 256
HALVES = TOKENS // HALF
ROWS = 128
LINE = 512
WIDTH = 1024
GROUP = 4
PIECE = 32
HIDDEN = 1024
MESH = pl.DeviceIdType.MESH
ANY = pl.ANY
BF = jnp.bfloat16
F32 = jnp.float32
VMEM_LIMIT = 56 * 1024 * 1024
NEVER = -1e30


def place():
    seq = lax.axis_index("seq")
    return (
        seq // 8,
        lax.rem(seq // 2, 4),
        lax.rem(seq, 2),
        lax.axis_index("wide"),
        lax.axis_index("narrow"),
    )


def device(z, y, x, c):
    return (lax.rem(z, 4) * 8 + lax.rem(y, 4) * 2 + lax.rem(x, 2), c, x // 2)


class Wires:
    def __init__(self, send_sem, recv_sem):
        self.send_sem, self.recv_sem, self.used, self.sent = send_sem, recv_sem, 0, []

    def send(self, src, dst, target, start=True):
        at = self.used
        self.used += 1
        copy = pltpu.make_async_remote_copy(
            src_ref=src,
            dst_ref=dst,
            send_sem=self.send_sem.at[at],
            recv_sem=self.recv_sem.at[at],
            device_id=target,
            device_id_type=MESH,
        )
        if start:
            copy.start()
        self.sent.append(copy)
        return at

    def landed(self, at, region):
        pltpu.make_async_copy(region, region, self.recv_sem.at[at]).wait()

    def close(self):
        for copy in self.sent:
            copy.wait_send()


def greet(targets):
    barrier = pltpu.get_barrier_semaphore()
    for target in targets:
        pl.semaphore_signal(barrier, inc=1, device_id=target, device_id_type=MESH)
    pl.semaphore_wait(barrier, len(targets))


def line_targets(z, y, x, c):
    return [device(z, y, lax.rem(x + o, 4), c) for o in (1, 2, 3)] + [device(z, y, x, 1 - c)]


def plane_targets(z, y, x, c):
    return [device(z + o, y, x, c) for o in (1, 2, 3)] + [device(z, y + o, x, c) for o in (1, 2, 3)]


def wire_scratch(count):
    return [pltpu.SemaphoreType.DMA((count,)), pltpu.SemaphoreType.DMA((count,))]


def comm_params(number):
    return pltpu.CompilerParams(
        collective_id=number, has_side_effects=True, vmem_limit_bytes=VMEM_LIMIT
    )


def row_span(at):
    return pl.ds(pl.multiple_of(at * ROWS, ROWS), ROWS)


def col_span(c):
    return pl.ds(pl.multiple_of(c * WIDTH, WIDTH), WIDTH)


def gather_sends(wires, own, out, here):
    z, y, x, c = here
    spot = out.at[row_span(x), col_span(c)]
    across = {o: wires.send(own, spot, device(z, y, lax.rem(x + o, 4), c)) for o in (2, 1, 3)}
    return across, wires.send(own, spot, device(z, y, x, 1 - c))


def gather_relay(wires, numbers, out, here):
    z, y, x, c = here
    across, direct = numbers
    relays = []
    for o in (1, 3, 2):
        rows = row_span(lax.rem(x + 4 - o, 4))
        spot = out.at[rows, col_span(c)]
        wires.landed(across[o], spot)
        relays.append((wires.send(spot, spot, device(z, y, x, 1 - c)), rows))
    wires.landed(direct, out.at[row_span(x), col_span(1 - c)])
    for at, rows in relays:
        wires.landed(at, out.at[rows, col_span(1 - c)])


FOLD_ORDER = (2, 1, 3, 0)


def fold_sends(wires, part, folded, here):
    z, y, x, c = here
    return [
        wires.send(
            part.at[row_span(lax.rem(x + o, 4)), col_span(1 - c)],
            folded.at[k],
            device(z, y, x, 1 - c),
        )
        for k, o in enumerate(FOLD_ORDER)
    ]


def fold_moves(wires, numbers, part, folded, leaving, arriving, here, total):
    z, y, x, c = here
    moves = []
    for k, o in enumerate(FOLD_ORDER):
        wires.landed(numbers[k], folded.at[k])
        both = part[row_span(lax.rem(x + o, 4)), col_span(c)].astype(F32) + folded[k].astype(F32)
        if o:
            leaving[k] = both.astype(BF)
            moves.append(
                wires.send(leaving.at[k], arriving.at[k], device(z, y, lax.rem(x + o, 4), c))
            )
        else:
            total[...] = both
    return moves


def fold_finish(wires, moves, arriving, total):
    for k, at in enumerate(moves):
        wires.landed(at, arriving.at[k])
    total[...] = (
        total[...]
        + arriving[0].astype(F32)
        + arriving[1].astype(F32)
        + arriving[2].astype(F32)
    )


def fold_scratch():
    return [
        pltpu.VMEM((4, ROWS, WIDTH), BF),
        pltpu.VMEM((3, ROWS, WIDTH), BF),
        pltpu.VMEM((3, ROWS, WIDTH), BF),
        pltpu.VMEM((ROWS, WIDTH), F32),
    ]


def both_cores(wires, mine, theirs, value, here):
    z, y, x, c = here
    mine[...] = jnp.broadcast_to(value, mine.shape)
    at = wires.send(mine, theirs, device(z, y, x, 1 - c))
    wires.landed(at, theirs)
    return value + theirs[:, :1]


EVERY = slice(None)


def first_device(here, order, by):
    z, y, x, c = here
    return device(z + by, y, x, c) if order == 0 else device(z, y + by, x, c)


def second_device(here, order, by):
    z, y, x, c = here
    return device(z, y + by, x, c) if order == 0 else device(z + by, y, x, c)


def first_at(here, order, by=0):
    return lax.rem((here[0] if order == 0 else here[1]) + by, 4)


def run_of(ref, here, order, by, sub=None):
    z, y, _, _ = here
    zi, yi = (EVERY, lax.rem(y + by, 4)) if order == 0 else (lax.rem(z + by, 4), EVERY)
    if len(ref.shape) == 6:
        return ref.at[order, zi, yi] if sub is None else ref.at[order, zi, yi, sub]
    rows = ref.shape[2] // 2
    if sub is None:
        return ref.at[zi, yi, pl.ds(order * rows, rows)]
    return ref.at[zi, yi, pl.ds(order * rows + sub * (rows // 2), rows // 2)]


def spot_of(line, order, at, sub=None):
    if sub is None:
        return line.at[order, at]
    if len(line.shape) == 5:
        return line.at[order, at, sub]
    rows = line.shape[2] // 2
    return line.at[order, at, pl.ds(sub * rows, rows)]


class LineGather:
    def __init__(self, wires, line, here):
        self.wires, self.line, self.here = wires, line, here

    def start(self):
        self.numbers = []
        for o in (0, 1):
            spot = spot_of(self.line, o, first_at(self.here, o))
            self.numbers.append(
                [self.wires.send(spot, spot, first_device(self.here, o, by)) for by in (1, 3)]
            )

    def relay(self):
        relays = []
        for o in (0, 1):
            sends = []
            for sub, by in enumerate((1, 3)):
                at = first_at(self.here, o, 4 - by)
                self.wires.landed(self.numbers[o][sub], spot_of(self.line, o, at))
                spot = spot_of(self.line, o, at, sub)
                sends.append(self.wires.send(spot, spot, first_device(self.here, o, by)))
            relays.append(sends)
        self.numbers = relays

    def finish(self):
        for o in (0, 1):
            for sub in (0, 1):
                at = first_at(self.here, o, 2)
                self.wires.landed(self.numbers[o][sub], spot_of(self.line, o, at, sub))


class PlaneGather:
    def __init__(self, wires, line, whole, here, local_sem, at):
        self.wires, self.line, self.whole, self.here = wires, line, whole, here
        self.kept = [
            pltpu.make_async_copy(line.at[o], run_of(whole, here, o, 0), local_sem.at[at + o])
            for o in (0, 1)
        ]

    def start(self):
        self.numbers = []
        for o in (0, 1):
            spot = run_of(self.whole, self.here, o, 0)
            self.numbers.append(
                [
                    self.wires.send(self.line.at[o], spot, second_device(self.here, o, by))
                    for by in (1, 3)
                ]
            )
        for copy in self.kept:
            copy.start()

    def relay(self):
        relays = []
        for o in (0, 1):
            sends = []
            for sub, by in enumerate((1, 3)):
                self.wires.landed(self.numbers[o][sub], run_of(self.whole, self.here, o, 4 - by))
                spot = run_of(self.whole, self.here, o, 4 - by, sub)
                sends.append(self.wires.send(spot, spot, second_device(self.here, o, by)))
            relays.append(sends)
        self.numbers = relays

    def finish(self):
        for o in (0, 1):
            for sub in (0, 1):
                self.wires.landed(
                    self.numbers[o][sub], run_of(self.whole, self.here, o, 2, sub)
                )
        for copy in self.kept:
            copy.wait()


OFFSETS = (2, 1, 3)


class PlaneSum:
    def __init__(self, wires, terms, buffers, here, local_sem, at):
        self.wires, self.terms, self.here = wires, terms, here
        self.rec, self.total, self.rec_two, self.fin = buffers
        self.kept = [
            pltpu.make_async_copy(
                run_of(terms, here, o, 0), self.total.at[o], local_sem.at[at + o]
            )
            for o in (0, 1)
        ]

    def start(self):
        self.numbers = []
        for o in (0, 1):
            self.numbers.append(
                [
                    self.wires.send(
                        run_of(self.terms, self.here, o, by),
                        self.rec.at[o, k],
                        second_device(self.here, o, by),
                    )
                    for k, by in enumerate(OFFSETS)
                ]
            )
        for copy in self.kept:
            copy.start()

    def middle(self):
        moves = []
        for o in (0, 1):
            self.kept[o].wait()
            for k in range(3):
                self.wires.landed(self.numbers[o][k], self.rec.at[o, k])

            def add(i, carry):
                value = self.total[o, i].astype(F32)
                for k in range(3):
                    value = value + self.rec[o, k, i].astype(F32)
                self.total[o, i] = value.astype(BF)
                return carry

            lax.fori_loop(0, 4, add, 0)
            moves.append(
                [
                    self.wires.send(
                        self.total.at[o, first_at(self.here, o, by)],
                        self.rec_two.at[o, k],
                        first_device(self.here, o, by),
                    )
                    for k, by in enumerate(OFFSETS)
                ]
            )
        self.numbers = moves

    def finish(self):
        for o in (0, 1):
            for k in range(3):
                self.wires.landed(self.numbers[o][k], self.rec_two.at[o, k])
            value = self.total[o, first_at(self.here, o)].astype(F32)
            for k in range(3):
                value = value + self.rec_two[o, k].astype(F32)
            self.fin[o] = value.astype(self.fin.dtype)


def sum_buffers(piece, kind):
    return [
        pltpu.VMEM((2, 3, 4) + piece, BF),
        pltpu.VMEM((2, 4) + piece, BF),
        pltpu.VMEM((2, 3) + piece, BF),
        pltpu.VMEM((2,) + piece, kind),
    ]


def worked_at(p, x):
    block = p * 4 + lax.rem(x, 2) * 2 + x // 2
    half = block // 2
    low = half < HALVES // 2
    return jnp.where(low, half, HALVES - 1 - half), lax.rem(block, 2) + jnp.where(low, 0, 2)


def lives_at(p, x):
    block = jnp.where(x < 2, 2 * p + x, 2 * (HALVES - 1 - p) + x - 2)
    rest = lax.rem(block, 4)
    return block // 4, lax.rem(rest, 2) * 2 + rest // 2


class Posting:
    def __init__(self, here, to, come, send_sem, recv_sem):
        z, y, x, c = here
        self.here, self.c = here, c
        self.target = device(to[0] // 4, lax.rem(to[0], 4), to[1], c)
        self.source = device(come[0] // 4, lax.rem(come[0], 4), come[1], c)
        self.same = (to[0] == z * 4 + y) & (to[1] == x)
        self.send_sem, self.recv_sem, self.sent = send_sem, recv_sem, []

    def greet(self, barrier):
        @pl.when(jnp.logical_not(self.same))
        def _():
            pl.semaphore_signal(barrier, inc=1, device_id=self.source, device_id_type=MESH)

        return 1 - self.same.astype(jnp.int32)

    def send(self, src, dst):
        at = len(self.sent)
        copy = pltpu.make_async_remote_copy(
            src_ref=src,
            dst_ref=dst,
            send_sem=self.send_sem.at[at],
            recv_sem=self.recv_sem.at[at],
            device_id=self.target,
            device_id_type=MESH,
        )
        self.sent.append(copy)

        @pl.when(jnp.logical_not(self.same))
        def _():
            copy.start()

        @pl.when(self.same)
        def _():
            pltpu.make_async_copy(src, dst, self.recv_sem.at[at]).start()

        return at

    def landed(self, at, region):
        pltpu.make_async_copy(region, region, self.recv_sem.at[at]).wait()

    def close(self):
        @pl.when(jnp.logical_not(self.same))
        def _():
            for copy in self.sent:
                copy.wait_send()


def quad_of(xl, xh, x, c):
    pair = xh * 2 + 1 - xl
    return [(x, 1 - c), (pair, c), (pair, 1 - c)]


def start_kernel(
    block_input, out_grad, gain_rows, qkv_in, gate_in, down_in,
    inputs, cotangent, inputs_all, gains_all, qkv_all, qkv_line, gate_line, down_line,
    send_sem, recv_sem, post_send, post_recv, local_sem,
):
    z, y, xl, xh, c = place()
    x = xh * 2 + xl
    here = (z, y, x, c)
    mine = xl * 2 + c
    quad = quad_of(xl, xh, x, c)
    fixed = line_targets(z, y, x, c) + [device(z, y, *quad[2])]
    fixed += [first_device(here, o, by) for o in (0, 1) for by in (1, 3)]
    barrier = pltpu.get_barrier_semaphore()
    post = Posting(here, worked_at(z * 4 + y, x), lives_at(z * 4 + y, x), post_send, post_recv)
    for target in fixed:
        pl.semaphore_signal(barrier, inc=1, device_id=target, device_id_type=MESH)
    extra = post.greet(barrier)
    pl.semaphore_wait(barrier, len(fixed) + extra)
    wires = Wires(send_sem, recv_sem)
    kept = []

    def keep(src, dst):
        copy = pltpu.make_async_copy(src, dst, local_sem.at[len(kept)])
        copy.start()
        kept.append(copy)

    input_at = post.send(block_input, inputs)
    cotangent_at = post.send(out_grad, cotangent)

    at_here = jnp.where(c == 0, z, y)
    swaps = []
    for given, line in ((qkv_in, qkv_line), (gate_in, gate_line)):
        swaps.append(
            [
                wires.send(
                    given.at[lax.rem(to, 2) * 2 + core],
                    line.at[c, at_here, xl],
                    device(z, y, to, core),
                )
                for to, core in quad
            ]
        )
        keep(given.at[mine], line.at[c, at_here, xl])
    down_swap = [
        wires.send(
            down_in.at[1 - c, pl.ds(o * PIECE, PIECE)],
            down_line.at[o, first_at(here, o), :, col_span(c)],
            device(z, y, x, 1 - c),
        )
        for o in (0, 1)
    ]
    for o in (0, 1):
        keep(
            down_in.at[c, pl.ds(o * PIECE, PIECE)],
            down_line.at[o, first_at(here, o), :, col_span(c)],
        )
    keep(gain_rows, gains_all.at[:, col_span(c)])
    gain_at = wires.send(gain_rows, gains_all.at[:, col_span(c)], device(z, y, x, 1 - c))

    post.landed(input_at, inputs)
    keep(inputs, inputs_all.at[row_span(x), col_span(c)])
    input_numbers = gather_sends(wires, inputs, inputs_all, here)

    def swapped(line, numbers):
        for at, (from_x, from_c) in zip(numbers, quad):
            spot = line.at[from_c, jnp.where(from_c == 0, z, y), lax.rem(from_x, 2)]
            wires.landed(at, spot)

    for copy in kept:
        copy.wait()
    swapped(qkv_line, swaps[0])
    qkv = LineGather(wires, qkv_line, here)
    qkv.start()
    swapped(gate_line, swaps[1])
    gate = LineGather(wires, gate_line, here)
    gate.start()
    for o in (0, 1):
        wires.landed(
            down_swap[o], down_line.at[o, first_at(here, o), :, col_span(1 - c)]
        )
    down = LineGather(wires, down_line, here)
    down.start()
    qkv.relay()
    qkv.finish()
    qkv_plane = PlaneGather(wires, qkv_line, qkv_all, here, local_sem, 8)
    qkv_plane.start()
    gate.relay()
    down.relay()
    qkv_plane.relay()
    gather_relay(wires, input_numbers, inputs_all, here)
    wires.landed(gain_at, gains_all.at[:, col_span(1 - c)])
    qkv_plane.finish()
    gate.finish()
    down.finish()
    post.landed(cotangent_at, cotangent)
    post.close()
    wires.close()


def call_start(block_input, out_grad, gain_rows, qkv_in, gate_in, down_in):
    qkv_cols, gate_cols = qkv_in.shape[2], gate_in.shape[2]
    shapes = (
        jax.ShapeDtypeStruct((ROWS, WIDTH), BF),
        jax.ShapeDtypeStruct((ROWS, WIDTH), BF),
        jax.ShapeDtypeStruct((LINE, D), BF),
        jax.ShapeDtypeStruct((8, D), F32),
        jax.ShapeDtypeStruct((2, 4, 4, 2, PIECE, qkv_cols), BF),
        jax.ShapeDtypeStruct((2, 4, 2, PIECE, qkv_cols), BF),
        jax.ShapeDtypeStruct((2, 4, 2, PIECE, gate_cols), BF),
        jax.ShapeDtypeStruct((2, 4, PIECE, D), BF),
    )
    hbm = pl.BlockSpec(memory_space=ANY)
    return pl.pallas_call(
        start_kernel,
        out_shape=shapes,
        in_specs=[hbm] * 6,
        out_specs=(hbm,) * len(shapes),
        scratch_shapes=wire_scratch(64) + wire_scratch(2) + [pltpu.SemaphoreType.DMA((10,))],
        compiler_params=comm_params(1),
        name="start",
    )(block_input, out_grad, gain_rows, qkv_in, gate_in, down_in)


def middle_kernel(
    part, inputs, gains, down_line, middle_out, scale_out, out, down_all,
    folded, leaving, arriving, total, mine, theirs, own, send_sem, recv_sem, local_sem,
):
    z, y, xl, xh, c = place()
    x = xh * 2 + xl
    here = (z, y, x, c)
    greet(
        line_targets(z, y, x, c)
        + [second_device(here, o, by) for o in (0, 1) for by in (1, 3)]
    )
    wires = Wires(send_sem, recv_sem)
    numbers = fold_sends(wires, part, folded, here)
    down = PlaneGather(wires, down_line, down_all, here, local_sem, 1)
    down.start()
    moves = fold_moves(wires, numbers, part, folded, leaving, arriving, here, total)
    fold_finish(wires, moves, arriving, total)
    middle = total[...] + inputs[...].astype(F32)
    middle_out[...] = middle
    square = both_cores(
        wires, mine, theirs, jnp.sum(middle * middle, axis=1, keepdims=True), here
    )
    scale = lax.rsqrt(square / D + NORM_EPS)
    scale_out[...] = jnp.broadcast_to(scale, scale_out.shape)
    own[...] = (middle_out[...] * scale * gains[1:2, :]).astype(BF)
    local = pltpu.make_async_copy(own, out.at[row_span(x), col_span(c)], local_sem.at[0])
    local.start()
    sends = gather_sends(wires, own, out, here)
    down.relay()
    gather_relay(wires, sends, out, here)
    down.finish()
    local.wait()
    wires.close()


def call_middle(part, inputs, gains, down_line):
    vm = pl.BlockSpec(memory_space=pltpu.VMEM)
    hbm = pl.BlockSpec(memory_space=ANY)
    return pl.pallas_call(
        middle_kernel,
        out_shape=(
            jax.ShapeDtypeStruct((ROWS, WIDTH), F32),
            jax.ShapeDtypeStruct((ROWS, 128), F32),
            jax.ShapeDtypeStruct((LINE, D), BF),
            jax.ShapeDtypeStruct((4, 4, 2 * PIECE, D), BF),
        ),
        in_specs=[vm] * 3 + [hbm],
        out_specs=(vm, vm, hbm, hbm),
        scratch_shapes=fold_scratch()
        + [
            pltpu.VMEM((ROWS, 128), F32),
            pltpu.VMEM((ROWS, 128), F32),
            pltpu.VMEM((ROWS, WIDTH), BF),
        ]
        + wire_scratch(24)
        + [pltpu.SemaphoreType.DMA((3,))],
        compiler_params=comm_params(2),
        name="line_middle",
    )(part, inputs, gains, down_line)


def norm_back(wires, values, scale, gain_row, incoming, mine, theirs, here):
    weighted = incoming * gain_row
    inner = both_cores(
        wires, mine, theirs, jnp.sum(weighted * values, axis=1, keepdims=True), here
    )
    inner = inner / D
    back = scale * (incoming * gain_row) - values * (scale * scale * scale * inner)
    return back, jnp.sum(incoming * values * scale, axis=0, keepdims=True)


def back_kernel(
    part, part_two, middle, scale, gains, cotangent, grad_down,
    output, middle_grad, gain_out, out, down_out,
    folded, leaving, arriving, total, folded_two, leaving_two, arriving_two, total_two,
    mine, theirs, own, rec, rec_sum, rec_two, fin, send_sem, recv_sem, local_sem,
):
    z, y, xl, xh, c = place()
    x = xh * 2 + xl
    here = (z, y, x, c)
    greet(line_targets(z, y, x, c) + plane_targets(z, y, x, c))
    wires = Wires(send_sem, recv_sem)
    numbers = fold_sends(wires, part, folded, here)
    down = PlaneSum(wires, grad_down, (rec, rec_sum, rec_two, fin), here, local_sem, 1)
    down.start()
    moves = fold_moves(wires, numbers, part, folded, leaving, arriving, here, total)
    numbers_two = fold_sends(wires, part_two, folded_two, here)
    moves_two = fold_moves(
        wires, numbers_two, part_two, folded_two, leaving_two, arriving_two, here, total_two
    )
    fold_finish(wires, moves, arriving, total)
    back, gain_sum = norm_back(
        wires, middle[...], scale[:, :1], gains[1:2, :], total[...], mine, theirs, here
    )
    gain_out[...] = jnp.broadcast_to(gain_sum, gain_out.shape)
    grad = cotangent[...].astype(F32) + back
    middle_grad[...] = grad
    own[...] = grad.astype(BF)
    local = pltpu.make_async_copy(own, out.at[row_span(x), col_span(c)], local_sem.at[0])
    local.start()
    sends = gather_sends(wires, own, out, here)
    fold_finish(wires, moves_two, arriving_two, total_two)
    output[...] = (middle[...] + total_two[...]).astype(BF)
    down.middle()
    gather_relay(wires, sends, out, here)
    down.finish()
    swap = wires.send(fin.at[:, :, col_span(1 - c)], down_out.at[c], device(z, y, x, 1 - c))
    kept = pltpu.make_async_copy(fin.at[:, :, col_span(c)], down_out.at[c], local_sem.at[3])
    kept.start()
    wires.landed(swap, down_out.at[1 - c])
    kept.wait()
    local.wait()
    wires.close()


def call_back(part, part_two, middle, scale, gains, cotangent, grad_down):
    vm = pl.BlockSpec(memory_space=pltpu.VMEM)
    hbm = pl.BlockSpec(memory_space=ANY)
    return pl.pallas_call(
        back_kernel,
        out_shape=(
            jax.ShapeDtypeStruct((ROWS, WIDTH), BF),
            jax.ShapeDtypeStruct((ROWS, WIDTH), F32),
            jax.ShapeDtypeStruct((8, WIDTH), F32),
            jax.ShapeDtypeStruct((LINE, D), BF),
            jax.ShapeDtypeStruct((2, 2, PIECE, WIDTH), BF),
        ),
        in_specs=[vm] * 6 + [hbm],
        out_specs=(vm, vm, vm, hbm, hbm),
        scratch_shapes=fold_scratch()
        + fold_scratch()
        + [
            pltpu.VMEM((ROWS, 128), F32),
            pltpu.VMEM((ROWS, 128), F32),
            pltpu.VMEM((ROWS, WIDTH), BF),
        ]
        + sum_buffers((PIECE, D), BF)
        + wire_scratch(40)
        + [pltpu.SemaphoreType.DMA((4,))],
        compiler_params=comm_params(3),
        name="line_back",
    )(part, part_two, middle, scale, gains, cotangent, grad_down)


def last_kernel(
    part, inputs, scale, gains, middle_grad, output, grad_qkv,
    input_home, output_home, gain_out, qkv_out,
    folded, leaving, arriving, total, mine, theirs, rec, rec_sum, rec_two, fin,
    send_sem, recv_sem, post_send, post_recv, local_sem,
):
    z, y, xl, xh, c = place()
    x = xh * 2 + xl
    here = (z, y, x, c)
    quad = quad_of(xl, xh, x, c)
    fixed = line_targets(z, y, x, c) + plane_targets(z, y, x, c) + [device(z, y, *quad[2])]
    barrier = pltpu.get_barrier_semaphore()
    post = Posting(here, lives_at(z * 4 + y, x), worked_at(z * 4 + y, x), post_send, post_recv)
    for target in fixed:
        pl.semaphore_signal(barrier, inc=1, device_id=target, device_id_type=MESH)
    extra = post.greet(barrier)
    pl.semaphore_wait(barrier, len(fixed) + extra)
    wires = Wires(send_sem, recv_sem)
    numbers = fold_sends(wires, part, folded, here)
    qkv = PlaneSum(wires, grad_qkv, (rec, rec_sum, rec_two, fin), here, local_sem, 0)
    qkv.start()
    output_at = post.send(output, output_home)
    moves = fold_moves(wires, numbers, part, folded, leaving, arriving, here, total)
    qkv.middle()
    fold_finish(wires, moves, arriving, total)
    back, gain_sum = norm_back(
        wires,
        inputs[...].astype(F32),
        scale[:, :1],
        gains[0:1, :],
        total[...],
        mine,
        theirs,
        here,
    )
    gain_out[...] = jnp.broadcast_to(gain_sum, gain_out.shape)
    total[...] = middle_grad[...] + back
    input_at = post.send(total, input_home)
    qkv.finish()
    at_mine = xl * 2 + c
    swaps = [
        wires.send(fin.at[b, lax.rem(a, 2)], qkv_out.at[at_mine], device(z, y, a, b))
        for a, b in quad
    ]
    kept = pltpu.make_async_copy(fin.at[c, xl], qkv_out.at[at_mine], local_sem.at[2])
    kept.start()
    for at, (a, b) in zip(swaps, quad):
        wires.landed(at, qkv_out.at[lax.rem(a, 2) * 2 + b])
    kept.wait()
    post.landed(output_at, output_home)
    post.landed(input_at, input_home)
    post.close()
    wires.close()


def call_last(part, inputs, scale, gains, middle_grad, output, grad_qkv):
    vm = pl.BlockSpec(memory_space=pltpu.VMEM)
    hbm = pl.BlockSpec(memory_space=ANY)
    cols = grad_qkv.shape[-1]
    return pl.pallas_call(
        last_kernel,
        out_shape=(
            jax.ShapeDtypeStruct((ROWS, WIDTH), F32),
            jax.ShapeDtypeStruct((ROWS, WIDTH), BF),
            jax.ShapeDtypeStruct((8, WIDTH), F32),
            jax.ShapeDtypeStruct((4, PIECE, cols), BF),
        ),
        in_specs=[vm] * 5 + [hbm, hbm],
        out_specs=(hbm, hbm, vm, hbm),
        scratch_shapes=fold_scratch()
        + [pltpu.VMEM((ROWS, 128), F32), pltpu.VMEM((ROWS, 128), F32)]
        + sum_buffers((2, PIECE, cols), BF)
        + wire_scratch(32)
        + wire_scratch(2)
        + [pltpu.SemaphoreType.DMA((3,))],
        compiler_params=comm_params(4),
        name="line_last",
    )(part, inputs, scale, gains, middle_grad, output, grad_qkv)


def key_at(half):
    low = half < HALVES // 2
    at = jnp.where(low, half, HALVES - 1 - half)
    return jnp.where(low, 0, 1), at // 4, lax.rem(at, 4)


def allowed_pairs(key_half, query_half, ends):
    keys = key_half * HALF + lax.broadcasted_iota(jnp.int32, (HALF, HALF), 0)
    queries = query_half * HALF + lax.broadcasted_iota(jnp.int32, (HALF, HALF), 1)
    same = keys <= queries
    for k in range(3):
        same = same & ((keys >= ends[k]) == (queries >= ends[k]))
    return same


def in_second(query_half, ends):
    queries = query_half * HALF + lax.broadcasted_iota(jnp.int32, (1, HALF), 1)
    return (queries >= ends[0]) & (queries < ends[1])


class Tour:
    def __init__(self, spot):
        self.spot = spot
        self.low = jnp.maximum(spot - 1, 0)
        self.count = self.low + HALVES - 2 - spot

    def half(self, s):
        return jnp.where(s == 0, self.spot, HALVES - 1 - self.spot)

    def inner(self, step, start, stop):
        def body(at, carry):
            s = jnp.where(at >= self.low, 1, 0)
            step(s, 1 + at - s * self.low, False)
            return carry

        lax.fori_loop(start, stop, body, 0)

    def edges(self, step):
        for s in (0, 1):
            half = self.half(s)

            def body(at, carry):
                step(s, at * half, True)
                return carry

            lax.fori_loop(0, jnp.where(half > 0, 2, 1), body, 0)


def head_cols(g):
    return slice(g * HALF, (g + 1) * HALF)


def out_partner(z, y, xl, xh, c):
    return xl * 2 + c, xh * 2 + z // 2, lax.rem(z, 2)


def attention_kernel(
    ends, queries, own_keys, cotangent, gate_line, out_in,
    out, log_out, keys_out, cotangent_all, gate_all, out_all,
    keys, tops, sums, mixed, send_sem, recv_sem, out_send, out_recv, local_sem,
):
    z, y, xl, xh, c = place()
    x = xh * 2 + xl
    here = (z, y, x, c)
    spot = z * 4 + y
    mine, to_x, to_c = out_partner(z, y, xl, xh, c)
    keeps = z == mine
    fixed = plane_targets(z, y, x, c) + line_targets(z, y, x, c)
    barrier = pltpu.get_barrier_semaphore()
    for target in fixed:
        pl.semaphore_signal(barrier, inc=1, device_id=target, device_id_type=MESH)
    for k in range(16):
        from_y, from_xl, from_c = k // 4, (k // 2) % 2, k % 2

        @pl.when(jnp.logical_not(keeps & (y == from_y) & (xl == from_xl) & (c == from_c)))
        def _():
            pl.semaphore_signal(
                barrier,
                inc=1,
                device_id=device(mine, jnp.int32(from_y), xh * 2 + from_xl, jnp.int32(from_c)),
                device_id_type=MESH,
            )

    pl.semaphore_wait(barrier, len(fixed) + 16 - keeps.astype(jnp.int32))
    wires = Wires(send_sem, recv_sem)

    first = [
        [
            wires.send(own_keys.at[s], keys.at[s, z, y], first_device(here, s, by))
            for by in OFFSETS
        ]
        for s in (0, 1)
    ]
    kept = [
        pltpu.make_async_copy(own_keys.at[s], keys.at[s, z, y], local_sem.at[s]) for s in (0, 1)
    ]
    for copy in kept:
        copy.start()
    cotangent_kept = pltpu.make_async_copy(
        cotangent, cotangent_all.at[row_span(x), col_span(c)], local_sem.at[2]
    )
    cotangent_kept.start()
    cotangent_numbers = gather_sends(wires, cotangent, cotangent_all, here)
    for copy in kept:
        copy.wait()
    second = []
    for s in (0, 1):
        for at, by in zip(first[s], OFFSETS):
            back = first_at(here, s, 4 - by)
            wires.landed(at, keys.at[s, back, y] if s == 0 else keys.at[s, z, back])
        line = keys.at[0, :, y] if s == 0 else keys.at[1, z]
        second.append([wires.send(line, line, second_device(here, s, by)) for by in OFFSETS])
    for s in (0, 1):
        for at, by in zip(second[s], OFFSETS):
            if s == 0:
                wires.landed(at, keys.at[0, :, lax.rem(y + 4 - by, 4)])
            else:
                wires.landed(at, keys.at[1, lax.rem(z + 4 - by, 4)])
    keys_kept = pltpu.make_async_copy(keys, keys_out, local_sem.at[3])
    keys_kept.start()

    gate = PlaneGather(wires, gate_line, gate_all, here, local_sem, 4)
    gate.start()
    slot = y * 4 + mine
    out_spot = out_all.at[y, xl, :, col_span(c)]
    out_sends = []
    for k in range(16):
        copy = pltpu.make_async_remote_copy(
            src_ref=out_in,
            dst_ref=out_spot,
            send_sem=out_send.at[k],
            recv_sem=out_recv.at[slot],
            device_id=device(jnp.int32(k // 4), jnp.int32(k % 4), to_x, to_c),
            device_id_type=MESH,
        )
        to_self = keeps & (spot == k)
        out_sends.append((copy, to_self))

        @pl.when(jnp.logical_not(to_self))
        def _():
            copy.start()

        @pl.when(to_self)
        def _():
            pltpu.make_async_copy(out_in, out_spot, out_recv.at[slot]).start()

    tour = Tour(spot)
    tops[...] = jnp.full(tops.shape, NEVER, F32)
    sums[...] = jnp.zeros(sums.shape, F32)
    mixed[...] = jnp.zeros(mixed.shape, F32)

    def step(s, at, masked):
        pairs = keys[key_at(at)]
        if masked:
            allowed = allowed_pairs(at, tour.half(s), ends)
        for g in range(GROUP):
            cols = head_cols(g)
            scores = jnp.dot(pairs, queries[s, :, cols], preferred_element_type=F32)
            if masked:
                scores = jnp.where(allowed, scores, NEVER)
            old = tops[s, :, cols]
            top = jnp.maximum(old, jnp.max(scores, axis=0, keepdims=True))
            weights = jnp.exp(scores - top)
            if masked:
                weights = jnp.where(allowed, weights, 0.0)
            shrink = jnp.exp(old - top)
            tops[s, :, cols] = top
            sums[s, :, cols] = sums[s, :, cols] * shrink + jnp.sum(
                weights, axis=0, keepdims=True
            )
            mixed[s, :, cols] = mixed[s, :, cols] * shrink + lax.dot_general(
                pairs, weights.astype(BF), (((0,), (0,)), ((), ())), preferred_element_type=F32
            )

    tour.inner(step, 0, 10)
    gather_relay(wires, cotangent_numbers, cotangent_all, here)
    tour.inner(step, 10, 22)
    gate.relay()
    tour.inner(step, 22, tour.count)
    for s in (0, 1):
        fits = in_second(tour.half(s), ends)
        for g in range(GROUP):
            cols = head_cols(g)
            tops[s, :, cols] = jnp.where(fits, tops[s, :, cols], NEVER)
            sums[s, :, cols] = jnp.where(fits, sums[s, :, cols], 0.0)
            mixed[s, :, cols] = jnp.where(fits, mixed[s, :, cols], 0.0)
    tour.edges(step)
    for s in (0, 1):
        out[s] = mixed[s, HD:, :] / sums[s]
        log_out[s] = tops[s] + jnp.log(sums[s])
    for k in range(16):
        spot_k = out_all.at[k // 4, (k // 2) % 2, :, pl.ds((k % 2) * WIDTH, WIDTH)]
        pltpu.make_async_copy(spot_k, spot_k, out_recv.at[k]).wait()
    gate.finish()
    cotangent_kept.wait()
    keys_kept.wait()
    for copy, to_self in out_sends:

        @pl.when(jnp.logical_not(to_self))
        def _():
            copy.wait_send()

    wires.close()


def call_attention(ends, queries, own_keys, cotangent, gate_line, out_in):
    vm = pl.BlockSpec(memory_space=pltpu.VMEM)
    hbm = pl.BlockSpec(memory_space=ANY)
    cols = GROUP * HALF
    return pl.pallas_call(
        attention_kernel,
        out_shape=(
            jax.ShapeDtypeStruct((2, HD, cols), F32),
            jax.ShapeDtypeStruct((2, 1, cols), F32),
            jax.ShapeDtypeStruct((2, 4, 4, HALF, 2 * HD), BF),
            jax.ShapeDtypeStruct((LINE, D), BF),
            jax.ShapeDtypeStruct((2, 4, 4, 2, PIECE, gate_line.shape[-1]), BF),
            jax.ShapeDtypeStruct((4, 2, PIECE, D), BF),
        ),
        in_specs=[pl.BlockSpec(memory_space=pltpu.SMEM), vm] + [hbm] * 4,
        out_specs=(vm, vm, hbm, hbm, hbm, hbm),
        scratch_shapes=[
            pltpu.VMEM((2, 4, 4, HALF, 2 * HD), BF),
            pltpu.VMEM((2, 1, cols), F32),
            pltpu.VMEM((2, 1, cols), F32),
            pltpu.VMEM((2, 2 * HD, cols), F32),
        ]
        + wire_scratch(32)
        + wire_scratch(16)
        + [pltpu.SemaphoreType.DMA((6,))],
        compiler_params=comm_params(5),
        name="attention",
    )(ends, queries, own_keys, cotangent, gate_line, out_in)


def attention_back_kernel(
    ends, queries, grads, query_rows, grad_rows, logs, delta, keys, grad_gate, grad_out,
    query_back, key_back, gate_out, out_out,
    terms, sums, rounded, rec, rec_sum, rec_two, fin, key_rec, key_sums, key_rec_two, out_rec,
    send_sem, recv_sem, out_send, out_recv, local_sem,
):
    z, y, xl, xh, c = place()
    x = xh * 2 + xl
    here = (z, y, x, c)
    spot = z * 4 + y
    mine, from_x, from_c = out_partner(z, y, xl, xh, c)
    keeps = z == mine
    quad = quad_of(xl, xh, x, c)
    fixed = plane_targets(z, y, x, c) + [device(z, y, a, b) for a, b in quad]
    barrier = pltpu.get_barrier_semaphore()
    for target in fixed:
        pl.semaphore_signal(barrier, inc=1, device_id=target, device_id_type=MESH)
    for k in range(16):

        @pl.when(jnp.logical_not(keeps & (spot == k)))
        def _():
            pl.semaphore_signal(
                barrier,
                inc=1,
                device_id=device(jnp.int32(k // 4), jnp.int32(k % 4), from_x, from_c),
                device_id_type=MESH,
            )

    pl.semaphore_wait(barrier, len(fixed) + 16 - keeps.astype(jnp.int32))
    wires = Wires(send_sem, recv_sem)
    gate = PlaneSum(wires, grad_gate, (rec, rec_sum, rec_two, fin), here, local_sem, 0)
    gate.start()
    out_sends = []
    for k in range(16):
        to_y, to_xl, to_c = k // 4, (k // 2) % 2, k % 2
        src = grad_out.at[to_y, to_xl, :, pl.ds(to_c * WIDTH, WIDTH)]
        to_self = keeps & (y == to_y) & (xl == to_xl) & (c == to_c)
        copy = pltpu.make_async_remote_copy(
            src_ref=src,
            dst_ref=out_rec.at[spot],
            send_sem=out_send.at[k],
            recv_sem=out_recv.at[spot],
            device_id=device(mine, jnp.int32(to_y), xh * 2 + to_xl, jnp.int32(to_c)),
            device_id_type=MESH,
        )
        out_sends.append((copy, to_self))

        @pl.when(jnp.logical_not(to_self))
        def _():
            copy.start()

        @pl.when(to_self)
        def _():
            pltpu.make_async_copy(src, out_rec.at[spot], out_recv.at[spot]).start()

    tour = Tour(spot)
    terms[...] = jnp.zeros(terms.shape, F32)
    sums[...] = jnp.zeros(sums.shape, F32)

    def step(s, at, masked):
        slot = key_at(at)
        pairs = keys[slot]
        if masked:
            allowed = allowed_pairs(at, tour.half(s), ends)
        else:
            fits = in_second(tour.half(s), ends)
        added = None
        for g in range(GROUP):
            cols = head_cols(g)
            scores = jnp.dot(pairs, queries[s, :, cols], preferred_element_type=F32)
            log_row = logs[s, :, cols]
            if not masked:
                log_row = jnp.where(fits, log_row, -NEVER)
            probs = jnp.exp(scores - log_row)
            if masked:
                probs = jnp.where(allowed, probs, 0.0)
            prob_grad = jnp.dot(pairs, grads[s, :, cols], preferred_element_type=F32)
            score_grad = (probs * (prob_grad - delta[s, :, cols])).astype(BF)
            sums[s, :, cols] += lax.dot_general(
                pairs, score_grad, (((0,), (0,)), ((), ())), preferred_element_type=F32
            )
            term = jnp.dot(score_grad, query_rows[s, g], preferred_element_type=F32) + jnp.dot(
                probs.astype(BF), grad_rows[s, g], preferred_element_type=F32
            )
            added = term if added is None else added + term
        terms[slot] += added

    tour.inner(step, 0, tour.count)
    tour.edges(step)

    for s in (0, 1):
        for i in range(4):
            rounded[s, i] = terms[s, i].astype(BF)
    first = [[], []]
    for k, by in enumerate(OFFSETS):
        first[0].append(
            wires.send(
                rounded.at[0, :, lax.rem(y + by, 4)], key_rec.at[0, k], second_device(here, 0, by)
            )
        )
        first[1].append(
            wires.send(
                rounded.at[1, lax.rem(z + by, 4)], key_rec.at[1, k], second_device(here, 1, by)
            )
        )
    for s in (0, 1):
        query_back[s] = sums[s, :HD, :] * HD ** (-0.5)
    gate.middle()
    second = [[], []]
    for s in (0, 1):
        for k in range(3):
            wires.landed(first[s][k], key_rec.at[s, k])
        for i in range(4):
            value = terms[0, i, y] if s == 0 else terms[1, z, i]
            for k in range(3):
                value = value + key_rec[s, k, i].astype(F32)
            key_sums[s, i] = value.astype(BF)
        for k, by in enumerate(OFFSETS):
            second[s].append(
                wires.send(
                    key_sums.at[s, first_at(here, s, by)],
                    key_rec_two.at[s, k],
                    first_device(here, s, by),
                )
            )
    gate.finish()
    swaps = [
        wires.send(fin.at[b, lax.rem(a, 2)], gate_out.at[mine], device(z, y, a, b))
        for a, b in quad
    ]
    kept = pltpu.make_async_copy(fin.at[c, xl], gate_out.at[mine], local_sem.at[2])
    kept.start()
    total = None
    for k in range(16):
        pltpu.make_async_copy(out_rec.at[k], out_rec.at[k], out_recv.at[k]).wait()
        total = out_rec[k].astype(F32) if total is None else total + out_rec[k].astype(F32)
    out_out[...] = total
    for s in (0, 1):
        value = key_sums[s, first_at(here, s)].astype(F32)
        for k in range(3):
            wires.landed(second[s][k], key_rec_two.at[s, k])
            value = value + key_rec_two[s, k].astype(F32)
        key_back[s] = value
    for at, (a, b) in zip(swaps, quad):
        wires.landed(at, gate_out.at[lax.rem(a, 2) * 2 + b])
    kept.wait()
    for copy, to_self in out_sends:

        @pl.when(jnp.logical_not(to_self))
        def _():
            copy.wait_send()

    wires.close()


def call_attention_back(
    ends, queries, grads, query_rows, grad_rows, logs, delta, keys, grad_gate, grad_out
):
    vm = pl.BlockSpec(memory_space=pltpu.VMEM)
    hbm = pl.BlockSpec(memory_space=ANY)
    cols = GROUP * HALF
    gate_cols = grad_gate.shape[-1]
    return pl.pallas_call(
        attention_back_kernel,
        out_shape=(
            jax.ShapeDtypeStruct((2, HD, cols), F32),
            jax.ShapeDtypeStruct((2, HALF, 2 * HD), F32),
            jax.ShapeDtypeStruct((4, PIECE, gate_cols), BF),
            jax.ShapeDtypeStruct((PIECE, WIDTH), F32),
        ),
        in_specs=[pl.BlockSpec(memory_space=pltpu.SMEM)] + [vm] * 7 + [hbm, hbm],
        out_specs=(vm, vm, hbm, vm),
        scratch_shapes=[
            pltpu.VMEM((2, 4, 4, HALF, 2 * HD), F32),
            pltpu.VMEM((2, 2 * HD, cols), F32),
            pltpu.VMEM((2, 4, 4, HALF, 2 * HD), BF),
        ]
        + sum_buffers((2, PIECE, gate_cols), BF)
        + [
            pltpu.VMEM((2, 3, 4, HALF, 2 * HD), BF),
            pltpu.VMEM((2, 4, HALF, 2 * HD), BF),
            pltpu.VMEM((2, 3, HALF, 2 * HD), BF),
            pltpu.VMEM((16, PIECE, WIDTH), BF),
        ]
        + wire_scratch(40)
        + wire_scratch(16)
        + [pltpu.SemaphoreType.DMA((3,))],
        compiler_params=comm_params(6),
        name="attention_back",
    )(ends, queries, grads, query_rows, grad_rows, logs, delta, keys, grad_gate, grad_out)


def total_kernel(terms, out, stage, rec, rec_two, rec_three, last, send_sem, recv_sem):
    z, y, xl, xh, c = place()
    x = xh * 2 + xl
    plane = [(a, b) for a in range(4) for b in range(4) if a or b]
    targets = [device(z + a, y + b, x, c) for a, b in plane] + line_targets(z, y, x, c)
    greet(targets)
    wires = Wires(send_sem, recv_sem)
    first = [
        wires.send(terms, rec.at[k], device(z + a, y + b, x, c)) for k, (a, b) in enumerate(plane)
    ]
    value = terms[...]
    for k, at in enumerate(first):
        wires.landed(at, rec.at[k])
        value = value + rec[k]
    stage[...] = value
    second = [
        wires.send(stage, rec_two.at[k], device(z, y, lax.rem(x + o, 4), c))
        for k, o in enumerate((1, 2, 3))
    ]
    for k, at in enumerate(second):
        wires.landed(at, rec_two.at[k])
        value = value + rec_two[k]
    gains = value[:16]
    square = value[16:] + jnp.sum(gains * gains)
    last[...] = square
    at = wires.send(last, rec_three, device(z, y, x, 1 - c))
    wires.landed(at, rec_three)
    out[:16] = gains
    out[16:] = square + rec_three[...]
    wires.close()


def call_total(terms):
    vm = pl.BlockSpec(memory_space=pltpu.VMEM)
    return pl.pallas_call(
        total_kernel,
        out_shape=jax.ShapeDtypeStruct((24, 128), F32),
        in_specs=[vm],
        out_specs=vm,
        scratch_shapes=[
            pltpu.VMEM((24, 128), F32),
            pltpu.VMEM((15, 24, 128), F32),
            pltpu.VMEM((3, 24, 128), F32),
            pltpu.VMEM((8, 128), F32),
            pltpu.VMEM((8, 128), F32),
        ]
        + wire_scratch(19),
        compiler_params=comm_params(8),
        name="total",
    )(terms)


def rope_tables(position, head_size):
    half_size = head_size // 2
    column = jnp.arange(half_size, dtype=jnp.float32)
    inverse = jnp.exp(-(2.0 * column / head_size) * math.log(ROPE_THETA))
    wavelength = 2.0 * math.pi / inverse
    smooth = (OLD_CONTEXT / wavelength - LOW_FREQ) / (HIGH_FREQ - LOW_FREQ)
    blended = (1.0 - smooth) * inverse / ROPE_FACTOR + smooth * inverse
    inverse = jnp.where(
        wavelength < OLD_CONTEXT / HIGH_FREQ,
        inverse,
        jnp.where(wavelength > OLD_CONTEXT / LOW_FREQ, inverse / ROPE_FACTOR, blended),
    )
    angles = position.astype(jnp.float32)[:, None] * inverse[None, :]
    return (jnp.cos(angles), jnp.sin(angles))


def rotate(values, cosine, sine):
    half_size = values.shape[-1] // 2
    table_shape = (cosine.shape[0],) + (1,) * (values.ndim - 2) + (half_size,)
    cos_part = cosine.reshape(table_shape)
    sin_part = sine.reshape(table_shape)
    first_half = values[..., :half_size]
    second_half = values[..., half_size:]
    return jnp.concatenate(
        [
            first_half * cos_part - second_half * sin_part,
            second_half * cos_part + first_half * sin_part,
        ],
        axis=-1,
    )


def times(left, right, kind):
    return jnp.dot(left, right, preferred_element_type=F32).astype(kind)


def times_transpose(left, right, kind):
    return lax.dot_general(
        left, right, (((1,), (1,)), ((), ())), preferred_element_type=F32
    ).astype(kind)


def outer_rows(left, right, kind):
    return lax.dot_general(
        left, right, (((0,), (0,)), ((), ())), preferred_element_type=F32
    ).astype(kind)


def as_columns(rows):
    return rows.reshape(2, HALF, GROUP, HD).transpose(0, 3, 2, 1).reshape(2, HD, GROUP * HALF)


def as_heads(rows):
    return rows.reshape(2, HALF, GROUP, HD).transpose(0, 2, 1, 3)


def from_columns(columns):
    return columns.reshape(2, HD, GROUP, HALF).transpose(0, 3, 2, 1).reshape(LINE, GROUP * HD)


def adam(weight, moment, second, gradient, rate, decay):
    moment_next = BETA_ONE * moment + (1.0 - BETA_ONE) * gradient
    second_next = BETA_TWO * second + (1.0 - BETA_TWO) * gradient * gradient
    unbiased = moment_next / (1.0 - BETA_ONE**ADAM_STEP)
    divisor = jnp.sqrt(second_next / (1.0 - BETA_TWO**ADAM_STEP)) + ADAM_EPS
    return (weight - rate * (unbiased / divisor + decay * weight), moment_next, second_next)


def shards(
    block_input,
    out_grad,
    qkv_weight,
    qkv_moment,
    qkv_second,
    gate_up_weight,
    gate_up_moment,
    gate_up_second,
    out_weight,
    out_moment,
    out_second,
    down_weight,
    down_moment,
    down_second,
    norm_gains,
    gains_moment,
    gains_second,
    doc_lengths,
):
    z, y, xl, xh, c = place()
    x = xh * 2 + xl
    spot = z * 4 + y

    qkv_in = qkv_weight.astype(BF).transpose(1, 0, 2)
    gate_in = (
        gate_up_weight.astype(BF)
        .reshape(PIECE, 2, 16, 4, HD)
        .transpose(3, 0, 1, 2, 4)
        .reshape(4, PIECE, 2 * HIDDEN)
    )
    down_in = down_weight.astype(BF).reshape(2, ROWS // 2, WIDTH)
    gain_rows = jnp.concatenate([norm_gains, jnp.zeros((6, WIDTH), F32)], axis=0)
    inputs, cotangent, inputs_all, gains_all, qkv_whole, _, gate_line, down_line = call_start(
        block_input, out_grad, gain_rows, qkv_in, gate_in, down_in
    )
    qkv_low = qkv_whole.reshape(D, (GROUP + 2) * HD)

    values = inputs_all.astype(F32)
    scale_one = lax.rsqrt(jnp.sum(values * values, axis=1, keepdims=True) / D + NORM_EPS)
    normed = (values * scale_one * gains_all[0:1, :]).astype(BF)
    projected = times(normed, qkv_low, F32)

    ends = jnp.cumsum(doc_lengths)
    local = jnp.arange(LINE, dtype=jnp.int32)
    half = jnp.where(local < HALF, spot, HALVES - 1 - spot)
    places = half * HALF + lax.rem(local, HALF)
    passed = (places[:, None] >= ends[None, :]).astype(jnp.int32)
    position = places - jnp.sum(passed * doc_lengths[None, :], axis=1)
    cosine, sine = rope_tables(position, HD)
    turned = rotate(
        projected[:, : (GROUP + 1) * HD].reshape(LINE, GROUP + 1, HD), cosine, sine
    ).astype(BF)
    queries = turned[:, :GROUP].reshape(LINE, GROUP * HD) * jnp.asarray(HD ** (-0.5), BF)
    own_keys = jnp.concatenate([turned[:, GROUP], projected[:, (GROUP + 1) * HD :].astype(BF)], axis=1)

    blank = jnp.zeros((2, HD, GROUP * HALF), BF)
    query_columns = jnp.concatenate([as_columns(queries), blank], axis=1)
    mixed, logs, keys, cotangent_all, gate_whole, out_whole = call_attention(
        ends,
        query_columns,
        own_keys.reshape(2, HALF, 2 * HD),
        cotangent,
        gate_line,
        out_weight.astype(BF),
    )
    gate_low = gate_whole.reshape(D, 2 * HIDDEN)
    out_low = out_whole.reshape(GROUP * HD, D)
    mixed_rows = from_columns(mixed)
    attended = mixed_rows.astype(BF)
    middle, scale_two, normed_two, down_whole = call_middle(
        times(attended, out_low, BF), inputs, norm_gains, down_line
    )
    down_low = down_whole.reshape(HIDDEN, D)

    gate_up = times(normed_two, gate_low, F32)
    gate_part, up_part = gate_up[:, :HIDDEN], gate_up[:, HIDDEN:]
    sigmoid_gate = jax.nn.sigmoid(gate_part)
    hidden = (gate_part * sigmoid_gate * up_part).astype(BF)
    hidden_grad = times_transpose(cotangent_all, down_low, F32)
    gate_back = hidden_grad * up_part * sigmoid_gate * (1.0 + gate_part * (1.0 - sigmoid_gate))
    up_back = hidden_grad * gate_part * sigmoid_gate
    gate_up_back = jnp.concatenate([gate_back, up_back], axis=1).astype(BF)
    grad_down = outer_rows(hidden, cotangent_all, BF)
    output, middle_grad, gain_two, middle_low, down_sum = call_back(
        times_transpose(gate_up_back, gate_low, BF),
        times(hidden, down_low, BF),
        middle,
        scale_two,
        norm_gains,
        cotangent,
        grad_down.reshape(down_whole.shape),
    )
    grad_gate = outer_rows(normed_two, gate_up_back, BF)

    grad_out = outer_rows(attended, middle_low, BF)
    attended_grad = times_transpose(middle_low, out_low, BF)
    delta = jnp.sum(
        (attended_grad.astype(F32) * mixed_rows).reshape(LINE, GROUP, HD), axis=-1
    )
    delta = delta.reshape(2, HALF, GROUP).transpose(0, 2, 1).reshape(2, 1, GROUP * HALF)
    empty = jnp.zeros((2, GROUP, HALF, HD), BF)
    query_back, key_grads, gate_sum, out_sum = call_attention_back(
        ends,
        query_columns,
        jnp.concatenate([blank, as_columns(attended_grad)], axis=1),
        jnp.concatenate([as_heads(queries), empty], axis=-1),
        jnp.concatenate([empty, as_heads(attended_grad)], axis=-1),
        logs,
        delta,
        keys,
        grad_gate.reshape(gate_whole.shape),
        grad_out.reshape(out_whole.shape),
    )
    key_grads = key_grads.reshape(LINE, 2 * HD)
    turned_back = jnp.concatenate([from_columns(query_back), key_grads[:, :HD]], axis=1)
    turned_back = rotate(turned_back.reshape(LINE, GROUP + 1, HD), cosine, -sine)
    projected_back = jnp.concatenate(
        [turned_back.reshape(LINE, (GROUP + 1) * HD), key_grads[:, HD:]], axis=1
    ).astype(BF)
    grad_qkv = outer_rows(normed, projected_back, BF)
    scale_rows = lax.dynamic_slice_in_dim(scale_one, x * ROWS, ROWS, 0)
    input_grad, output, gain_one, qkv_sum = call_last(
        times_transpose(projected_back, qkv_low, BF),
        inputs,
        jnp.broadcast_to(scale_rows, (ROWS, 128)),
        norm_gains,
        middle_grad,
        output,
        grad_qkv.reshape(qkv_whole.shape),
    )

    shares = (
        qkv_sum.transpose(1, 0, 2).astype(F32),
        gate_sum.reshape(4, PIECE, 2, 16, HD)
        .transpose(1, 2, 3, 0, 4)
        .reshape(gate_up_weight.shape)
        .astype(F32),
        out_sum,
        down_sum.reshape(down_weight.shape).astype(F32),
    )
    square = sum(
        jnp.sum(jnp.square(member.astype(F32))) for member in (qkv_sum, gate_sum, out_sum, down_sum)
    )
    terms = jnp.concatenate(
        [
            jnp.stack([gain_one[0], gain_two[0]]).reshape(16, 128),
            jnp.broadcast_to(square, (8, 128)),
        ],
        axis=0,
    )
    totals = call_total(terms)
    gains_grad = totals[:16].reshape(2, WIDTH)
    grad_norm = jnp.sqrt(totals[16, 0])
    factor = CLIP_NORM / jnp.maximum(grad_norm, CLIP_NORM)
    weights = (qkv_weight, gate_up_weight, out_weight, down_weight)
    moments = (qkv_moment, gate_up_moment, out_moment, down_moment)
    seconds = (qkv_second, gate_up_second, out_second, down_second)
    out_rate = OUTPUT_RATE * (TOKENS / (HQ * HD)) ** 0.5
    down_rate = DOWN_RATE * FF ** (-0.5)
    rates = (MATRIX_RATE, MATRIX_RATE, out_rate, down_rate)
    results = []
    for weight, moment, second, gradient, rate in zip(weights, moments, seconds, shares, rates):
        results.extend(adam(weight, moment, second, gradient * factor, rate, WEIGHT_DECAY))
    gains_new = adam(norm_gains, gains_moment, gains_second, gains_grad * factor, GAIN_RATE, 0.0)
    return (output, input_grad, grad_norm, *results, *gains_new)


def solution(mesh):
    placed = (
        P(("seq", "wide"), "narrow"),
        P(("seq", "wide"), "narrow"),
        P(("narrow", "seq"), "wide", None),
        P(("narrow", "seq"), "wide", None),
        P(("narrow", "seq"), "wide", None),
        P(("narrow", "seq"), None, "wide"),
        P(("narrow", "seq"), None, "wide"),
        P(("narrow", "seq"), None, "wide"),
        P(("wide", "seq"), "narrow"),
        P(("wide", "seq"), "narrow"),
        P(("wide", "seq"), "narrow"),
        P(("wide", "seq"), "narrow"),
        P(("wide", "seq"), "narrow"),
        P(("wide", "seq"), "narrow"),
        P(None, "narrow"),
        P(None, "narrow"),
        P(None, "narrow"),
        P(),
    )
    return jax.shard_map(
        shards,
        mesh=mesh,
        in_specs=placed,
        out_specs=(
            P(("seq", "wide"), "narrow"),
            P(("seq", "wide"), "narrow"),
            P(),
            P(("narrow", "seq"), "wide", None),
            P(("narrow", "seq"), "wide", None),
            P(("narrow", "seq"), "wide", None),
            P(("narrow", "seq"), None, "wide"),
            P(("narrow", "seq"), None, "wide"),
            P(("narrow", "seq"), None, "wide"),
            P(("wide", "seq"), "narrow"),
            P(("wide", "seq"), "narrow"),
            P(("wide", "seq"), "narrow"),
            P(("wide", "seq"), "narrow"),
            P(("wide", "seq"), "narrow"),
            P(("wide", "seq"), "narrow"),
            P(None, "narrow"),
            P(None, "narrow"),
            P(None, "narrow"),
        ),
        check_vma=False,
    )
```

```python
import functools
import math

import jax
import jax.numpy as jnp
from jax import lax
from jax.experimental import pallas as pl
from jax.experimental.pallas import tpu as pltpu
from jax.sharding import PartitionSpec as P

D = 2048
HQ = 32
HD = 64
FF = 8192
ADAM_STEP = 10


NORM_EPS = 1e-05
ADAM_EPS = 1e-08
BETA_ONE = 0.9
BETA_TWO = 0.95
WEIGHT_DECAY = 0.1
MATRIX_RATE = 0.01
OUTPUT_RATE = 0.9
DOWN_RATE = 3.0
GAIN_RATE = 2.5
CLIP_NORM = 1.0
ROPE_THETA = 500000.0
ROPE_FACTOR = 32.0
LOW_FREQ = 1.0
HIGH_FREQ = 4.0
OLD_CONTEXT = 8192.0

TOKENS = 8192
HALF = 256
HALVES = TOKENS // HALF
ROWS = 128
LINE = 512
WIDTH = 1024
GROUP = 4
PIECE = 32
HIDDEN = 1024
MESH = pl.DeviceIdType.MESH
ANY = pl.ANY
BF = jnp.bfloat16
F32 = jnp.float32
VMEM_LIMIT = 56 * 1024 * 1024
NEVER = -1e30


def place():
    seq = lax.axis_index("seq")
    return (
        seq // 8,
        lax.rem(seq // 2, 4),
        lax.rem(seq, 2),
        lax.axis_index("wide"),
        lax.axis_index("narrow"),
    )


def device(z, y, x, c):
    return (lax.rem(z, 4) * 8 + lax.rem(y, 4) * 2 + lax.rem(x, 2), c, x // 2)


class Wires:
    def __init__(self, send_sem, recv_sem):
        self.send_sem, self.recv_sem, self.used, self.sent = send_sem, recv_sem, 0, []

    def send(self, src, dst, target, start=True):
        at = self.used
        self.used += 1
        copy = pltpu.make_async_remote_copy(
            src_ref=src,
            dst_ref=dst,
            send_sem=self.send_sem.at[at],
            recv_sem=self.recv_sem.at[at],
            device_id=target,
            device_id_type=MESH,
        )
        if start:
            copy.start()
        self.sent.append(copy)
        return at

    def landed(self, at, region):
        pltpu.make_async_copy(region, region, self.recv_sem.at[at]).wait()

    def close(self):
        for copy in self.sent:
            copy.wait_send()


def greet(targets):
    barrier = pltpu.get_barrier_semaphore()
    for target in targets:
        pl.semaphore_signal(barrier, inc=1, device_id=target, device_id_type=MESH)
    pl.semaphore_wait(barrier, len(targets))


def line_targets(z, y, x, c):
    return [device(z, y, lax.rem(x + o, 4), c) for o in (1, 2, 3)] + [device(z, y, x, 1 - c)]


def plane_targets(z, y, x, c):
    return [device(z + o, y, x, c) for o in (1, 2, 3)] + [device(z, y + o, x, c) for o in (1, 2, 3)]


def wire_scratch(count):
    return [pltpu.SemaphoreType.DMA((count,)), pltpu.SemaphoreType.DMA((count,))]


def comm_params(number):
    return pltpu.CompilerParams(
        collective_id=number, has_side_effects=True, vmem_limit_bytes=VMEM_LIMIT
    )


def rows_of(x):
    return lax.rem(x, 2) * 2 + x // 2


def row_span(x):
    return pl.ds(pl.multiple_of(rows_of(x) * ROWS, ROWS), ROWS)


def col_span(c):
    return pl.ds(pl.multiple_of(c * WIDTH, WIDTH), WIDTH)


def gather_sends(wires, own, out, here):
    z, y, x, c = here
    spot = out.at[row_span(x), col_span(c)]
    across = {o: wires.send(own, spot, device(z, y, lax.rem(x + o, 4), c)) for o in (2, 1, 3)}
    return across, wires.send(own, spot, device(z, y, x, 1 - c))


def gather_relay(wires, numbers, out, here):
    z, y, x, c = here
    across, direct = numbers
    relays = []
    for o in (1, 3, 2):
        rows = row_span(lax.rem(x + 4 - o, 4))
        spot = out.at[rows, col_span(c)]
        wires.landed(across[o], spot)
        relays.append((wires.send(spot, spot, device(z, y, x, 1 - c)), rows))
    wires.landed(direct, out.at[row_span(x), col_span(1 - c)])
    for at, rows in relays:
        wires.landed(at, out.at[rows, col_span(1 - c)])


FOLD_ORDER = (2, 1, 3, 0)


def fold_sends(wires, part, folded, here):
    z, y, x, c = here
    return [
        wires.send(
            part.at[row_span(lax.rem(x + o, 4)), col_span(1 - c)],
            folded.at[k],
            device(z, y, x, 1 - c),
        )
        for k, o in enumerate(FOLD_ORDER)
    ]


def fold_moves(wires, numbers, part, folded, leaving, arriving, here, total):
    z, y, x, c = here
    moves = []
    for k, o in enumerate(FOLD_ORDER):
        wires.landed(numbers[k], folded.at[k])
        both = part[row_span(lax.rem(x + o, 4)), col_span(c)].astype(F32) + folded[k].astype(F32)
        if o:
            leaving[k] = both.astype(BF)
            moves.append(
                wires.send(leaving.at[k], arriving.at[k], device(z, y, lax.rem(x + o, 4), c))
            )
        else:
            total[...] = both
    return moves


def fold_finish(wires, moves, arriving, total):
    for k, at in enumerate(moves):
        wires.landed(at, arriving.at[k])
    total[...] = (
        total[...]
        + arriving[0].astype(F32)
        + arriving[1].astype(F32)
        + arriving[2].astype(F32)
    )


def fold_scratch():
    return [
        pltpu.VMEM((4, ROWS, WIDTH), BF),
        pltpu.VMEM((3, ROWS, WIDTH), BF),
        pltpu.VMEM((3, ROWS, WIDTH), BF),
        pltpu.VMEM((ROWS, WIDTH), F32),
    ]


def both_cores(wires, mine, theirs, value, here):
    z, y, x, c = here
    mine[...] = jnp.broadcast_to(value, mine.shape)
    at = wires.send(mine, theirs, device(z, y, x, 1 - c))
    wires.landed(at, theirs)
    return value + theirs[:, :1]


EVERY = slice(None)


def first_device(here, order, by):
    z, y, x, c = here
    return device(z + by, y, x, c) if order == 0 else device(z, y + by, x, c)


def second_device(here, order, by):
    z, y, x, c = here
    return device(z, y + by, x, c) if order == 0 else device(z + by, y, x, c)


def first_at(here, order, by=0):
    return lax.rem((here[0] if order == 0 else here[1]) + by, 4)


def run_of(ref, here, order, by, sub=None):
    z, y, _, _ = here
    zi, yi = (EVERY, lax.rem(y + by, 4)) if order == 0 else (lax.rem(z + by, 4), EVERY)
    if len(ref.shape) == 6:
        return ref.at[order, zi, yi] if sub is None else ref.at[order, zi, yi, sub]
    rows = ref.shape[2] // 2
    if sub is None:
        return ref.at[zi, yi, pl.ds(order * rows, rows)]
    return ref.at[zi, yi, pl.ds(order * rows + sub * (rows // 2), rows // 2)]


def spot_of(ref, here, order, at, sub=None):
    z, y, _, _ = here
    zi, yi = (at, y) if order == 0 else (z, at)
    if len(ref.shape) == 6:
        return ref.at[order, zi, yi] if sub is None else ref.at[order, zi, yi, sub]
    rows = ref.shape[2] // 2
    if sub is None:
        return ref.at[zi, yi, pl.ds(order * rows, rows)]
    return ref.at[zi, yi, pl.ds(order * rows + sub * (rows // 2), rows // 2)]


class PlaneGather:
    def __init__(self, wires, whole, here):
        self.wires, self.whole, self.here = wires, whole, here

    def start(self):
        self.numbers = []
        for o in (0, 1):
            spot = spot_of(self.whole, self.here, o, first_at(self.here, o))
            self.numbers.append(
                [self.wires.send(spot, spot, first_device(self.here, o, by)) for by in (1, 3)]
            )

    def relay(self):
        relays = []
        for o in (0, 1):
            sends = []
            for sub, by in enumerate((1, 3)):
                at = first_at(self.here, o, 4 - by)
                self.wires.landed(self.numbers[o][sub], spot_of(self.whole, self.here, o, at))
                spot = spot_of(self.whole, self.here, o, at, sub)
                sends.append(self.wires.send(spot, spot, first_device(self.here, o, by)))
            relays.append(sends)
        self.numbers = relays

    def turn(self):
        lines = []
        for o in (0, 1):
            for sub in (0, 1):
                at = first_at(self.here, o, 2)
                self.wires.landed(
                    self.numbers[o][sub], spot_of(self.whole, self.here, o, at, sub)
                )
            spot = run_of(self.whole, self.here, o, 0)
            lines.append(
                [self.wires.send(spot, spot, second_device(self.here, o, by)) for by in (1, 3)]
            )
        self.numbers = lines

    def relay_two(self):
        relays = []
        for o in (0, 1):
            sends = []
            for sub, by in enumerate((1, 3)):
                self.wires.landed(self.numbers[o][sub], run_of(self.whole, self.here, o, 4 - by))
                spot = run_of(self.whole, self.here, o, 4 - by, sub)
                sends.append(self.wires.send(spot, spot, second_device(self.here, o, by)))
            relays.append(sends)
        self.numbers = relays

    def finish(self):
        for o in (0, 1):
            for sub in (0, 1):
                self.wires.landed(
                    self.numbers[o][sub], run_of(self.whole, self.here, o, 2, sub)
                )


OFFSETS = (2, 1, 3)


class PlaneSum:
    def __init__(self, wires, terms, buffers, here, local_sem, at):
        self.wires, self.terms, self.here = wires, terms, here
        self.far, self.joined, self.rec, self.total, self.rec_two, self.fin = buffers
        self.kept, self.added = [], []
        for o in (0, 1):
            self.kept.append(
                pltpu.make_async_copy(
                    run_of(terms, here, o, 0), self.total.at[o], local_sem.at[at + 3 * o]
                )
            )
            self.added.append(
                [
                    pltpu.make_async_copy(
                        run_of(terms, here, o, by, sub),
                        self.joined.at[o, sub],
                        local_sem.at[at + 3 * o + 1 + sub],
                    )
                    for sub, by in enumerate((1, 3))
                ]
            )

    def start(self):
        self.numbers = []
        for o in (0, 1):
            self.numbers.append(
                [
                    self.wires.send(
                        run_of(self.terms, self.here, o, 2, sub),
                        self.far.at[o, sub],
                        second_device(self.here, o, by),
                    )
                    for sub, by in enumerate((1, 3))
                ]
            )
        for o in (0, 1):
            for copy in self.added[o]:
                copy.start()
        self.direct = []
        for o in (0, 1):
            self.direct.append(
                [
                    self.wires.send(
                        run_of(self.terms, self.here, o, by, 1 - sub),
                        half_of(self.rec.at[o, sub], 1 - sub),
                        second_device(self.here, o, by),
                    )
                    for sub, by in enumerate((1, 3))
                ]
            )
        for copy in self.kept:
            copy.start()

    def relay(self):
        self.passed = []
        for o in (0, 1):
            moves = []
            for sub, by in enumerate((1, 3)):
                self.added[o][sub].wait()
                self.wires.landed(self.numbers[o][sub], self.far.at[o, sub])

                def add(i, carry):
                    value = self.joined[o, sub, i].astype(F32) + self.far[o, sub, i].astype(F32)
                    self.joined[o, sub, i] = value.astype(BF)
                    return carry

                lax.fori_loop(0, 4, add, 0)
                moves.append(
                    self.wires.send(
                        self.joined.at[o, sub],
                        half_of(self.rec.at[o, sub], sub),
                        second_device(self.here, o, by),
                    )
                )
            self.passed.append(moves)

    def middle(self):
        self.moves = []
        for o in (0, 1):
            self.kept[o].wait()
            for sub in (0, 1):
                self.wires.landed(self.direct[o][sub], half_of(self.rec.at[o, sub], 1 - sub))
                self.wires.landed(self.passed[o][sub], half_of(self.rec.at[o, sub], sub))

            def add(i, carry):
                value = self.total[o, i].astype(F32)
                for sub in (0, 1):
                    value = value + self.rec[o, sub, i].astype(F32)
                self.total[o, i] = value.astype(BF)
                return carry

            lax.fori_loop(0, 4, add, 0)
            self.moves.append(
                [
                    self.wires.send(
                        self.total.at[o, first_at(self.here, o, by)],
                        self.rec_two.at[o, k],
                        first_device(self.here, o, by),
                    )
                    for k, by in enumerate(OFFSETS)
                ]
            )

    def finish(self):
        for o in (0, 1):
            for k in range(3):
                self.wires.landed(self.moves[o][k], self.rec_two.at[o, k])
            value = self.total[o, first_at(self.here, o)].astype(F32)
            for k in range(3):
                value = value + self.rec_two[o, k].astype(F32)
            self.fin[o] = value.astype(self.fin.dtype)


def half_of(line, sub):
    if len(line.shape) == 4:
        return line.at[:, sub]
    rows = line.shape[1] // 2
    return line.at[:, pl.ds(sub * rows, rows)]


def sum_buffers(piece, kind):
    half = piece[1:] if len(piece) == 3 else (piece[0] // 2,) + piece[1:]
    return [
        pltpu.VMEM((2, 2, 4) + half, BF),
        pltpu.VMEM((2, 2, 4) + half, BF),
        pltpu.VMEM((2, 2, 4) + piece, BF),
        pltpu.VMEM((2, 4) + piece, BF),
        pltpu.VMEM((2, 3) + piece, BF),
        pltpu.VMEM((2,) + piece, kind),
    ]


class OutGather:
    def __init__(self, wires, stage, whole, here, mine, send_sem, recv_sem, local_sem, at):
        z, y, x, c = here
        self.wires, self.stage, self.whole, self.here = wires, stage, whole, here
        self.off = lax.rem(z - mine + 4, 4)
        self.recv_sem = recv_sem
        spot = whole.at[y]
        self.kept = pltpu.make_async_copy(stage, spot, local_sem.at[at])

        def copy(k, src, dst, by):
            return pltpu.make_async_remote_copy(
                src_ref=src,
                dst_ref=dst,
                send_sem=send_sem.at[k],
                recv_sem=recv_sem.at[k],
                device_id=device(z + by, y, x, c),
                device_id_type=MESH,
            )

        self.first = [copy(0, stage, spot, 1), copy(1, stage, spot, 3)]
        self.onward = [
            copy(2, spot.at[0], spot.at[0], 1),
            copy(3, spot.at[1], spot.at[1], 3),
        ]

    def landed(self, k, region):
        pltpu.make_async_copy(region, region, self.recv_sem.at[k]).wait()

    def start(self):
        @pl.when(self.off == 0)
        def _():
            self.kept.start()
            for copy in self.first:
                copy.start()

    def relay(self):
        spot = self.whole.at[self.here[1]]
        for k, off in ((0, 1), (1, 3)):

            @pl.when(self.off == off)
            def _():
                self.landed(k, spot)
                self.onward[k].start()

    def turn(self):
        z, y, x, c = self.here
        spot = self.whole.at[y]

        @pl.when(self.off == 0)
        def _():
            self.kept.wait()

        @pl.when(self.off == 2)
        def _():
            self.landed(2, spot.at[0])
            self.landed(3, spot.at[1])

        self.numbers = [self.wires.send(spot, spot, device(z, y + by, x, c)) for by in (1, 3)]

    def relay_two(self):
        z, y, x, c = self.here
        relays = []
        for sub, by in enumerate((1, 3)):
            spot = self.whole.at[lax.rem(y + 4 - by, 4)]
            self.wires.landed(self.numbers[sub], spot)
            relays.append(
                self.wires.send(spot.at[sub], spot.at[sub], device(z, y + by, x, c))
            )
        self.numbers = relays

    def finish(self):
        spot = self.whole.at[lax.rem(self.here[1] + 2, 4)]
        for sub in (0, 1):
            self.wires.landed(self.numbers[sub], spot.at[sub])

        @pl.when(self.off == 0)
        def _():
            for copy in self.first:
                copy.wait_send()

        for k, off in ((0, 1), (1, 3)):

            @pl.when(self.off == off)
            def _():
                self.onward[k].wait_send()


class OutSum:
    def __init__(self, wires, terms, buffers, piece, here, mine, quad, sems, local_sem, at):
        self.wires, self.terms, self.here, self.mine, self.quad = wires, terms, here, mine, quad
        self.rec, self.total, self.rec_two = buffers
        self.piece, self.local_sem, self.at = piece, local_sem, at
        self.send_sem, self.recv_sem = sems
        self.off = lax.rem(here[0] - mine + 4, 4)
        self.kept = pltpu.make_async_copy(
            terms.at[here[1]], self.total, local_sem.at[at]
        )

    def start(self):
        z, y, x, c = self.here
        self.kept.start()
        self.numbers = [
            self.wires.send(
                self.terms.at[lax.rem(y + by, 4)], self.rec.at[k], device(z, y + by, x, c)
            )
            for k, by in enumerate(OFFSETS)
        ]

    def copy(self, k, src, dst, target):
        return pltpu.make_async_remote_copy(
            src_ref=src,
            dst_ref=dst,
            send_sem=self.send_sem.at[k],
            recv_sem=self.recv_sem.at[k],
            device_id=target,
            device_id_type=MESH,
        )

    def middle(self):
        z, y, x, c = self.here
        self.kept.wait()
        value = self.total[...].astype(F32)
        for k in range(3):
            self.wires.landed(self.numbers[k], self.rec.at[k])
            value = value + self.rec[k].astype(F32)
        self.total[...] = value.astype(BF)
        self.moves = []
        for off in (1, 2, 3):
            move = self.copy(
                off - 1, self.total, self.rec_two.at[off - 1], device(self.mine, y, x, c)
            )
            self.moves.append(move)

            @pl.when(self.off == off)
            def _():
                move.start()

    def deal(self):
        z, y, x, c = self.here
        self.deals = []
        xl = lax.rem(x, 2)
        for k, (a, b) in enumerate(self.quad):
            self.deals.append(
                self.copy(
                    3 + k, self.total.at[lax.rem(a, 2), :, col_span(b)], self.piece, device(z, y, a, b)
                )
            )

        @pl.when(self.off == 0)
        def _():
            value = self.total[...].astype(F32)
            for k in range(3):
                region = self.rec_two.at[k]
                pltpu.make_async_copy(region, region, self.recv_sem.at[k]).wait()
                value = value + self.rec_two[k].astype(F32)
            self.total[...] = value.astype(BF)
            for copy in self.deals:
                copy.start()
            own = pltpu.make_async_copy(
                self.total.at[xl, :, col_span(c)], self.piece, self.local_sem.at[self.at]
            )
            own.start()
            own.wait()

    def finish(self):
        z, y, x, c = self.here
        xl = lax.rem(x, 2)
        holder_xl, holder_c = z // 2, lax.rem(z, 2)
        for k, (dx, dc) in enumerate(((0, 1), (1, 0), (1, 1))):

            @pl.when(
                (holder_xl == lax.rem(xl + dx, 2)) & (holder_c == lax.rem(c + dc, 2))
            )
            def _():
                pltpu.make_async_copy(self.piece, self.piece, self.recv_sem.at[3 + k]).wait()

        for off in (1, 2, 3):

            @pl.when(self.off == off)
            def _():
                self.moves[off - 1].wait_send()

        @pl.when(self.off == 0)
        def _():
            for copy in self.deals:
                copy.wait_send()


class Posting:
    def __init__(self, here, send_sem, recv_sem):
        z, y, x, c = here
        self.target = device(3 - z, 3 - y, x, c)
        self.away = lax.rem(x, 2) == 1
        self.send_sem, self.recv_sem, self.sent = send_sem, recv_sem, []

    def greet(self, barrier):
        @pl.when(self.away)
        def _():
            pl.semaphore_signal(barrier, inc=1, device_id=self.target, device_id_type=MESH)

        return self.away.astype(jnp.int32)

    def send(self, src, dst):
        at = len(self.sent)
        copy = pltpu.make_async_remote_copy(
            src_ref=src,
            dst_ref=dst,
            send_sem=self.send_sem.at[at],
            recv_sem=self.recv_sem.at[at],
            device_id=self.target,
            device_id_type=MESH,
        )
        self.sent.append(copy)

        @pl.when(self.away)
        def _():
            copy.start()

        @pl.when(jnp.logical_not(self.away))
        def _():
            pltpu.make_async_copy(src, dst, self.recv_sem.at[at]).start()

        return at

    def landed(self, at, region):
        pltpu.make_async_copy(region, region, self.recv_sem.at[at]).wait()

    def close(self):
        @pl.when(self.away)
        def _():
            for copy in self.sent:
                copy.wait_send()


def quad_of(xl, xh, x, c):
    pair = xh * 2 + 1 - xl
    return [(x, 1 - c), (pair, c), (pair, 1 - c)]


def norm_back(wires, values, scale, gain_row, incoming, mine, theirs, here):
    weighted = incoming * gain_row
    inner = both_cores(
        wires, mine, theirs, jnp.sum(weighted * values, axis=1, keepdims=True), here
    )
    inner = inner / D
    back = scale * (incoming * gain_row) - values * (scale * scale * scale * inner)
    return back, jnp.sum(incoming * values * scale, axis=0, keepdims=True)


def back_kernel(
    part, middle, scale, gains, cotangent, grad_down, grad_up,
    middle_grad, gain_out, out, down_out, up_out,
    folded, leaving, arriving, total, mine, theirs, own, *rest,
):
    down_buffers, up_buffers, (send_sem, recv_sem, local_sem) = rest[:6], rest[6:12], rest[12:]
    z, y, xl, xh, c = place()
    x = xh * 2 + xl
    here = (z, y, x, c)
    greet(line_targets(z, y, x, c) + plane_targets(z, y, x, c))
    wires = Wires(send_sem, recv_sem)
    numbers = fold_sends(wires, part, folded, here)
    down = PlaneSum(wires, grad_down, down_buffers, here, local_sem, 0)
    up = PlaneSum(wires, grad_up, up_buffers, here, local_sem, 6)
    down.start()
    up.start()
    moves = fold_moves(wires, numbers, part, folded, leaving, arriving, here, total)
    down.relay()
    up.relay()
    fold_finish(wires, moves, arriving, total)
    back, gain_sum = norm_back(
        wires, middle[...], scale[:, :1], gains[1:2, :], total[...], mine, theirs, here
    )
    gain_out[...] = jnp.broadcast_to(gain_sum, gain_out.shape)
    grad = cotangent[...].astype(F32) + back
    middle_grad[...] = grad
    own[...] = grad.astype(BF)
    local = pltpu.make_async_copy(own, out.at[row_span(x), col_span(c)], local_sem.at[12])
    local.start()
    sends = gather_sends(wires, own, out, here)
    down.middle()
    gather_relay(wires, sends, out, here)
    up.middle()
    down.finish()
    up.finish()
    kept = [
        pltpu.make_async_copy(down_buffers[5], down_out, local_sem.at[13]),
        pltpu.make_async_copy(up_buffers[5], up_out, local_sem.at[14]),
        local,
    ]
    for copy in kept[:2]:
        copy.start()
    for copy in kept:
        copy.wait()
    wires.close()


def call_back(part, middle, scale, gains, cotangent, grad_down, grad_up):
    vm = pl.BlockSpec(memory_space=pltpu.VMEM)
    hbm = pl.BlockSpec(memory_space=ANY)
    return pl.pallas_call(
        back_kernel,
        out_shape=(
            jax.ShapeDtypeStruct((ROWS, WIDTH), F32),
            jax.ShapeDtypeStruct((8, WIDTH), F32),
            jax.ShapeDtypeStruct((LINE, D), BF),
            jax.ShapeDtypeStruct((2, PIECE, D), BF),
            jax.ShapeDtypeStruct((2, 2, PIECE, HIDDEN), BF),
        ),
        in_specs=[vm] * 5 + [hbm] * 2,
        out_specs=(vm, vm, hbm, hbm, hbm),
        scratch_shapes=fold_scratch()
        + [
            pltpu.VMEM((ROWS, 128), F32),
            pltpu.VMEM((ROWS, 128), F32),
            pltpu.VMEM((ROWS, WIDTH), BF),
        ]
        + sum_buffers((PIECE, D), BF)
        + sum_buffers((2, PIECE, HIDDEN), BF)
        + wire_scratch(56)
        + [pltpu.SemaphoreType.DMA((15,))],
        compiler_params=comm_params(3),
        name="line_back",
    )(part, middle, scale, gains, cotangent, grad_down, grad_up)


PLANE = [(a, b) for a in range(4) for b in range(4) if a or b]


def last_kernel(
    part, inputs, scale, gains, middle_grad, gain_two, squares, output, grad_qkv,
    input_home, output_home, qkv_out, totals,
    folded, leaving, arriving, total, mine, theirs, *rest,
):
    buffers, rest = rest[:6], rest[6:]
    landing, terms, stage, rec_one, rec_two = rest[:5]
    send_sem, recv_sem, post_send, post_recv, local_sem = rest[5:]
    fin = buffers[5]
    z, y, xl, xh, c = place()
    x = xh * 2 + xl
    here = (z, y, x, c)
    quad = quad_of(xl, xh, x, c)
    line = [(o, b) for b in (0, 1) for o in range(4) if o or b]
    fixed = [device(z + a, y + b, x, c) for a, b in PLANE]
    fixed += [device(z, y, lax.rem(x + o, 4), lax.rem(c + b, 2)) for o, b in line]
    barrier = pltpu.get_barrier_semaphore()
    post = Posting(here, post_send, post_recv)
    for target in fixed:
        pl.semaphore_signal(barrier, inc=1, device_id=target, device_id_type=MESH)
    extra = post.greet(barrier)
    pl.semaphore_wait(barrier, len(fixed) + extra)
    wires = Wires(send_sem, recv_sem)
    numbers = fold_sends(wires, part, folded, here)
    qkv = PlaneSum(wires, grad_qkv, buffers, here, local_sem, 0)
    qkv.start()
    output_at = post.send(output, output_home)
    moves = fold_moves(wires, numbers, part, folded, leaving, arriving, here, total)
    qkv.relay()
    qkv.middle()
    fold_finish(wires, moves, arriving, total)
    back, gain_one = norm_back(
        wires,
        inputs[...].astype(F32),
        scale[:, :1],
        gains[0:1, :],
        total[...],
        mine,
        theirs,
        here,
    )
    total[...] = middle_grad[...] + back
    input_at = post.send(total, input_home)
    qkv.finish()
    at_mine = xl * 2 + c
    swaps = [
        wires.send(fin.at[b, lax.rem(a, 2)], landing.at[at_mine], device(z, y, a, b))
        for a, b in quad
    ]
    landing[at_mine] = fin[c, xl]
    for at, (a, b) in zip(swaps, quad):
        wires.landed(at, landing.at[lax.rem(a, 2) * 2 + b])
    square = squares[...]
    for k in range(4):
        value = landing[k].astype(F32)
        square = square + jnp.sum(value * value)
    qkv_out[...] = landing[...]

    for k in range(8):
        cols = slice(k * 128, (k + 1) * 128)
        terms[k : k + 1] = gain_one[:, cols]
        terms[8 + k : 9 + k] = gain_two[0:1, cols]
    terms[16:] = square
    first = [
        wires.send(terms, rec_one.at[k], device(z + a, y + b, x, c))
        for k, (a, b) in enumerate(PLANE)
    ]
    value = terms[...]
    for k, at in enumerate(first):
        wires.landed(at, rec_one.at[k])
        value = value + rec_one[k]
    stage[...] = value
    second = [
        wires.send(stage, rec_two.at[k], device(z, y, lax.rem(x + o, 4), lax.rem(c + b, 2)))
        for k, (o, b) in enumerate(line)
    ]
    both = [value, None]
    for k, (o, b) in enumerate(line):
        wires.landed(second[k], rec_two.at[k])
        both[b] = rec_two[k] if both[b] is None else both[b] + rec_two[k]
    totals[:16] = both[0][:16]
    totals[16:] = (
        both[0][16:]
        + both[1][16:]
        + jnp.sum(both[0][:16] * both[0][:16])
        + jnp.sum(both[1][:16] * both[1][:16])
    )
    post.landed(output_at, output_home)
    post.landed(input_at, input_home)
    post.close()
    wires.close()


def call_last(part, inputs, scale, gains, middle_grad, gain_two, squares, output, grad_qkv):
    vm = pl.BlockSpec(memory_space=pltpu.VMEM)
    hbm = pl.BlockSpec(memory_space=ANY)
    cols = grad_qkv.shape[-1]
    return pl.pallas_call(
        last_kernel,
        out_shape=(
            jax.ShapeDtypeStruct((ROWS, WIDTH), F32),
            jax.ShapeDtypeStruct((ROWS, WIDTH), BF),
            jax.ShapeDtypeStruct((4, PIECE, cols), BF),
            jax.ShapeDtypeStruct((24, 128), F32),
        ),
        in_specs=[vm] * 7 + [hbm, hbm],
        out_specs=(hbm, hbm, vm, vm),
        scratch_shapes=fold_scratch()
        + [pltpu.VMEM((ROWS, 128), F32), pltpu.VMEM((ROWS, 128), F32)]
        + sum_buffers((2, PIECE, cols), BF)
        + [
            pltpu.VMEM((4, PIECE, cols), BF),
            pltpu.VMEM((24, 128), F32),
            pltpu.VMEM((24, 128), F32),
            pltpu.VMEM((15, 24, 128), F32),
            pltpu.VMEM((7, 24, 128), F32),
        ]
        + wire_scratch(64)
        + wire_scratch(2)
        + [pltpu.SemaphoreType.DMA((6,))],
        compiler_params=comm_params(4),
        name="line_last",
    )(part, inputs, scale, gains, middle_grad, gain_two, squares, output, grad_qkv)


def key_at(half):
    odd = lax.rem(half, 2)
    at = jnp.where(odd == 1, HALVES - 1 - half, half) // 2
    return odd, at // 4, lax.rem(at, 4)


def allowed_pairs(key_half, query_half, ends):
    keys = key_half * HALF + lax.broadcasted_iota(jnp.int32, (HALF, HALF), 0)
    queries = query_half * HALF + lax.broadcasted_iota(jnp.int32, (HALF, HALF), 1)
    same = keys <= queries
    for k in range(3):
        same = same & ((keys >= ends[k]) == (queries >= ends[k]))
    return same


def in_second(query_half, ends):
    queries = query_half * HALF + lax.broadcasted_iota(jnp.int32, (1, HALF), 1)
    return (queries >= ends[0]) & (queries < ends[1])


class Tour:
    def __init__(self, spot):
        self.spot = spot
        self.low = jnp.maximum(2 * spot - 1, 0)
        self.count = self.low + HALVES - 2 - 2 * spot

    def half(self, s):
        return jnp.where(s == 0, 2 * self.spot, HALVES - 1 - 2 * self.spot)

    def inner(self, step, start, stop):
        def body(at, carry):
            s = jnp.where(at >= self.low, 1, 0)
            step(s, 1 + at - s * self.low, False)
            return carry

        lax.fori_loop(start, stop, body, 0)

    def edges(self, step):
        for s in (0, 1):
            half = self.half(s)

            def body(at, carry):
                step(s, at * half, True)
                return carry

            lax.fori_loop(0, jnp.where(half > 0, 2, 1), body, 0)


def head_cols(g):
    return slice(g * HALF, (g + 1) * HALF)


def rope(columns, at, cosine, sine):
    first = columns[at : at + HD // 2]
    second = columns[at + HD // 2 : at + HD]
    return first * cosine - second * sine, second * cosine + first * sine


def forward_kernel(
    ends, cosine, sine, block_input, out_grad, gain_rows, qkv_in, gate_in, up_in, down_in, out_in,
    inputs, scale_one, normed_out, qkv_out, queries, mixed_out, log_out, attended, keys_out,
    cotangent, cotangent_all, out_out, gate_all, up_all, down_all, middle_out, scale_two, out,
    inputs_all, gains_all, qkv_all, normed, columns, own_keys, keys, tops, sums, mixed,
    out_stage, out_all, part, folded, leaving, arriving, total, mine_row, their_row, own,
    send_sem, recv_sem, post_send, post_recv, stage_send, stage_recv, out_send, out_recv, local_sem,
):
    z, y, xl, xh, c = place()
    x = xh * 2 + xl
    here = (z, y, x, c)
    mine = xl * 2 + c
    quad = quad_of(xl, xh, x, c)
    fixed = line_targets(z, y, x, c) + [device(z, y, *quad[2])] + plane_targets(z, y, x, c)
    barrier = pltpu.get_barrier_semaphore()
    post = Posting(here, post_send, post_recv)
    for target in fixed:
        pl.semaphore_signal(barrier, inc=1, device_id=target, device_id_type=MESH)
    extra = post.greet(barrier)
    pl.semaphore_wait(barrier, len(fixed) + extra)
    wires = Wires(send_sem, recv_sem)
    kept = {}

    def keep(name, src, dst):
        copy = pltpu.make_async_copy(src, dst, local_sem.at[len(kept)])
        copy.start()
        kept[name] = copy

    def swap(given, whole):
        numbers = [
            wires.send(
                given.at[lax.rem(to, 2) * 2 + core], whole.at[c, z, y, xl], device(z, y, to, core)
            )
            for to, core in quad
        ]
        return numbers

    def swapped(numbers, whole):
        for at, (from_x, from_c) in zip(numbers, quad):
            wires.landed(at, whole.at[from_c, z, y, lax.rem(from_x, 2)])

    input_at = post.send(block_input, inputs)
    keep("qkv", qkv_in.at[mine], qkv_all.at[c, z, y, xl])
    qkv_swap = swap(qkv_in, qkv_all)
    keep("gains", gain_rows, gains_all.at[:, col_span(c)])
    gain_at = wires.send(gain_rows, gains_all.at[:, col_span(c)], device(z, y, x, 1 - c))
    keep("gate", gate_in.at[mine], gate_all.at[c, z, y, xl])
    keep("up", up_in.at[mine], up_all.at[c, z, y, xl])
    keep("down", down_in.at[c], down_all.at[z, y, :, col_span(c)])
    down_swap = wires.send(
        down_in.at[1 - c], down_all.at[z, y, :, col_span(c)], device(z, y, x, 1 - c)
    )
    holds = z == mine
    stage_spot = out_stage.at[xl, :, col_span(c)]
    stage_copy = pltpu.make_async_remote_copy(
        src_ref=out_in,
        dst_ref=stage_spot,
        send_sem=stage_send.at[0],
        recv_sem=stage_recv.at[mine],
        device_id=device(z, y, xh * 2 + z // 2, lax.rem(z, 2)),
        device_id_type=MESH,
    )

    @pl.when(jnp.logical_not(holds))
    def _():
        stage_copy.start()

    @pl.when(holds)
    def _():
        pltpu.make_async_copy(out_in, stage_spot, stage_recv.at[mine]).start()

    qkv = PlaneGather(wires, qkv_all, here)
    gate = PlaneGather(wires, gate_all, here)
    up = PlaneGather(wires, up_all, here)
    down = PlaneGather(wires, down_all, here)
    out_gather = OutGather(
        wires, out_stage, out_all, here, mine, out_send, out_recv, local_sem, 12
    )

    kept["qkv"].wait()
    swapped(qkv_swap, qkv_all)
    qkv.start()
    post.landed(input_at, inputs)
    keep("inputs", inputs, inputs_all.at[row_span(x), col_span(c)])
    input_numbers = gather_sends(wires, inputs, inputs_all, here)
    gate_swap = swap(gate_in, gate_all)
    up_swap = swap(up_in, up_all)
    cotangent_at = post.send(out_grad, cotangent)
    qkv.relay()
    qkv.turn()
    gather_relay(wires, input_numbers, inputs_all, here)
    qkv.relay_two()
    kept["inputs"].wait()
    kept["gains"].wait()
    wires.landed(gain_at, gains_all.at[:, col_span(1 - c)])
    gain_one = gains_all[0:1, :]

    def norm_rows(i, carry):
        rows = pl.ds(pl.multiple_of(i * ROWS, ROWS), ROWS)
        values = inputs_all[rows, :].astype(F32)
        scale = lax.rsqrt(jnp.sum(values * values, axis=1, keepdims=True) / D + NORM_EPS)
        normed[rows, :] = (values * scale * gain_one).astype(BF)

        @pl.when(i == rows_of(x))
        def _():
            scale_one[...] = jnp.broadcast_to(scale, scale_one.shape)

        return carry

    lax.fori_loop(0, 4, norm_rows, 0)
    keep("normed", normed, normed_out)
    swapped(gate_swap, gate_all)
    kept["gate"].wait()
    gate.start()
    swapped(up_swap, up_all)
    kept["up"].wait()
    up.start()
    qkv.finish()
    keep("qkv_out", qkv_all, qkv_out)
    weight = qkv_all[...].reshape(D, columns.shape[0])

    def project_rows(i, carry):
        rows = pl.ds(pl.multiple_of(i * ROWS, ROWS), ROWS)
        product = jnp.dot(normed[rows, :], weight, preferred_element_type=F32)
        columns[:, rows] = product.T
        return carry

    lax.fori_loop(0, 4, project_rows, 0)
    queries[:, HD:, :] = jnp.zeros((2, HD, GROUP * HALF), BF)
    for g in range(GROUP):
        first, second = rope(columns, g * HD, cosine[...], sine[...])
        for s in (0, 1):
            tokens = slice(s * HALF, (s + 1) * HALF)
            queries[s, : HD // 2, head_cols(g)] = (first[:, tokens] * HD ** (-0.5)).astype(BF)
            queries[s, HD // 2 : HD, head_cols(g)] = (second[:, tokens] * HD ** (-0.5)).astype(BF)
    first, second = rope(columns, GROUP * HD, cosine[...], sine[...])
    pair_columns = jnp.concatenate([first, second, columns[(GROUP + 1) * HD :]], axis=0)
    for s in (0, 1):
        own_keys[s] = pair_columns[:, s * HALF : (s + 1) * HALF].T.astype(BF)

    numbers = [
        [
            wires.send(own_keys.at[s], keys.at[s, z, y], first_device(here, s, by))
            for by in OFFSETS
        ]
        for s in (0, 1)
    ]
    for s in (0, 1):
        keys[s, z, y] = own_keys[s]
    second_numbers = []
    for s in (0, 1):
        for at, by in zip(numbers[s], OFFSETS):
            back = first_at(here, s, 4 - by)
            wires.landed(at, keys.at[s, back, y] if s == 0 else keys.at[s, z, back])
        line = keys.at[0, :, y] if s == 0 else keys.at[1, z]
        second_numbers.append(
            [wires.send(line, line, second_device(here, s, by)) for by in OFFSETS]
        )

    @pl.when(holds)
    def _():
        for k in range(4):
            spot = out_stage.at[k // 2, :, pl.ds((k % 2) * WIDTH, WIDTH)]
            pltpu.make_async_copy(spot, spot, stage_recv.at[k]).wait()

    out_gather.start()
    gate.relay()
    up.relay()
    post.landed(cotangent_at, cotangent)
    keep("cotangent", cotangent, cotangent_all.at[row_span(x), col_span(c)])
    cotangent_numbers = gather_sends(wires, cotangent, cotangent_all, here)
    for s in (0, 1):
        for at, by in zip(second_numbers[s], OFFSETS):
            if s == 0:
                wires.landed(at, keys.at[0, :, lax.rem(y + 4 - by, 4)])
            else:
                wires.landed(at, keys.at[1, lax.rem(z + 4 - by, 4)])
    keep("keys", keys, keys_out)
    out_gather.relay()
    gate.turn()
    up.turn()

    tour = Tour(spot=z * 4 + y)
    tops[...] = jnp.full(tops.shape, NEVER, F32)
    sums[...] = jnp.zeros(sums.shape, F32)
    mixed[...] = jnp.zeros(mixed.shape, F32)
    heads = range(GROUP)

    def step(s, at, masked):
        pairs = keys[key_at(at)]
        old = [tops[s, :, head_cols(g)] for g in heads]
        old_sums = [sums[s, :, head_cols(g)] for g in heads]
        scores = [
            jnp.dot(pairs, queries[s, :, head_cols(g)], preferred_element_type=F32) for g in heads
        ]
        if masked:
            allowed = allowed_pairs(at, tour.half(s), ends)
            scores = [jnp.where(allowed, value, NEVER) for value in scores]
        top = [jnp.maximum(old[g], jnp.max(scores[g], axis=0, keepdims=True)) for g in heads]
        weights = [jnp.exp(scores[g] - top[g]) for g in heads]
        if masked:
            weights = [jnp.where(allowed, value, 0.0) for value in weights]
        shrink = [jnp.exp(old[g] - top[g]) for g in heads]
        new_sums = [
            old_sums[g] * shrink[g] + jnp.sum(weights[g], axis=0, keepdims=True) for g in heads
        ]
        new = [
            lax.dot_general(
                pairs, weights[g].astype(BF), (((0,), (0,)), ((), ())), preferred_element_type=F32
            )
            for g in heads
        ]
        for g in heads:
            cols = head_cols(g)
            tops[s, :, cols] = top[g]
            sums[s, :, cols] = new_sums[g]
            mixed[s, :, cols] = mixed[s, :, cols] * shrink[g] + new[g]

    tour.inner(step, 0, 6)
    out_gather.turn()
    gather_relay(wires, cotangent_numbers, cotangent_all, here)
    kept["down"].wait()
    wires.landed(down_swap, down_all.at[z, y, :, col_span(1 - c)])
    down.start()
    tour.inner(step, 6, 20)
    out_gather.relay_two()
    down.relay()
    tour.inner(step, 20, tour.count)
    for s in (0, 1):
        fits = in_second(tour.half(s), ends)
        for g in heads:
            cols = head_cols(g)
            tops[s, :, cols] = jnp.where(fits, tops[s, :, cols], NEVER)
            sums[s, :, cols] = jnp.where(fits, sums[s, :, cols], 0.0)
            mixed[s, :, cols] = jnp.where(fits, mixed[s, :, cols], 0.0)
    tour.edges(step)
    gate.relay_two()
    up.relay_two()
    down.turn()
    for s in (0, 1):
        tokens = slice(s * HALF, (s + 1) * HALF)
        log_out[s] = tops[s] + jnp.log(sums[s])
        mixed_out[s] = mixed[s, HD:, :] / sums[s]
        for g in range(0, GROUP, 2):
            two = jnp.concatenate(
                [mixed_out[s, :, head_cols(g)], mixed_out[s, :, head_cols(g + 1)]], axis=0
            )
            attended[tokens, g * HD : (g + 2) * HD] = two.T.astype(BF)

    out_gather.finish()
    keep("out", out_all, out_out)
    out_low = out_all[...].reshape(GROUP * HD, D)
    fold_numbers = []
    for k, o in enumerate(FOLD_ORDER):
        rows = row_span(lax.rem(x + o, 4))
        part[rows, :] = jnp.dot(
            attended[rows, :], out_low, preferred_element_type=F32
        ).astype(BF)
        fold_numbers.append(
            wires.send(part.at[rows, col_span(1 - c)], folded.at[k], device(z, y, x, 1 - c))
        )
    moves = fold_moves(wires, fold_numbers, part, folded, leaving, arriving, here, total)
    fold_finish(wires, moves, arriving, total)
    middle = total[...] + inputs[...].astype(F32)
    middle_out[...] = middle
    square = both_cores(
        wires, mine_row, their_row, jnp.sum(middle * middle, axis=1, keepdims=True), here
    )
    scale = lax.rsqrt(square / D + NORM_EPS)
    scale_two[...] = jnp.broadcast_to(scale, scale_two.shape)
    own[...] = (
        middle_out[...] * scale * gains_all[1:2, col_span(c)]
    ).astype(BF)
    keep("own", own, out.at[row_span(x), col_span(c)])
    sends = gather_sends(wires, own, out, here)
    down.relay_two()
    gather_relay(wires, sends, out, here)
    gate.finish()
    up.finish()
    down.finish()
    for name in ("normed", "qkv_out", "cotangent", "keys", "out", "own"):
        kept[name].wait()

    @pl.when(jnp.logical_not(holds))
    def _():
        stage_copy.wait_send()

    post.close()
    wires.close()


def call_forward(ends, cosine, sine, block_input, out_grad, gain_rows, qkv_in, gate_in, up_in, down_in, out_in):
    vm = pl.BlockSpec(memory_space=pltpu.VMEM)
    hbm = pl.BlockSpec(memory_space=ANY)
    cols = GROUP * HALF
    qkv_cols = qkv_in.shape[2]
    share = (ROWS, WIDTH)
    whole = (2, 4, 4, 2, PIECE)
    outs = [
        (share, BF, vm),
        ((ROWS, 128), F32, vm),
        ((LINE, D), BF, hbm),
        (whole + (qkv_cols,), BF, hbm),
        ((2, 2 * HD, cols), BF, vm),
        ((2, HD, cols), F32, vm),
        ((2, 1, cols), F32, vm),
        ((LINE, GROUP * HD), BF, vm),
        ((2, 4, 4, HALF, 2 * HD), BF, hbm),
        (share, BF, hbm),
        ((LINE, D), BF, hbm),
        ((4, 2, PIECE, D), BF, hbm),
        (whole + (HIDDEN,), BF, hbm),
        (whole + (HIDDEN,), BF, hbm),
        ((4, 4, 2 * PIECE, D), BF, hbm),
        (share, F32, vm),
        ((ROWS, 128), F32, vm),
        ((LINE, D), BF, hbm),
    ]
    return pl.pallas_call(
        forward_kernel,
        out_shape=tuple(jax.ShapeDtypeStruct(shape, kind) for shape, kind, _ in outs),
        in_specs=[pl.BlockSpec(memory_space=pltpu.SMEM), vm, vm] + [hbm] * 8,
        out_specs=tuple(spec for _, _, spec in outs),
        scratch_shapes=[
            pltpu.VMEM((LINE, D), BF),
            pltpu.VMEM((8, D), F32),
            pltpu.VMEM(whole + (qkv_cols,), BF),
            pltpu.VMEM((LINE, D), BF),
            pltpu.VMEM((qkv_cols, LINE), F32),
            pltpu.VMEM((2, HALF, 2 * HD), BF),
            pltpu.VMEM((2, 4, 4, HALF, 2 * HD), BF),
            pltpu.VMEM((2, 1, cols), F32),
            pltpu.VMEM((2, 1, cols), F32),
            pltpu.VMEM((2, 2 * HD, cols), F32),
            pltpu.VMEM((2, PIECE, D), BF),
            pltpu.VMEM((4, 2, PIECE, D), BF),
            pltpu.VMEM((LINE, D), BF),
        ]
        + fold_scratch()
        + [
            pltpu.VMEM((ROWS, 128), F32),
            pltpu.VMEM((ROWS, 128), F32),
            pltpu.VMEM((ROWS, WIDTH), BF),
        ]
        + wire_scratch(128)
        + wire_scratch(2)
        + wire_scratch(4)
        + wire_scratch(4)
        + [pltpu.SemaphoreType.DMA((13,))],
        compiler_params=comm_params(1),
        name="forward",
    )(ends, cosine, sine, block_input, out_grad, gain_rows, qkv_in, gate_in, up_in, down_in, out_in)


def attention_back_kernel(
    ends, queries, grads, query_rows, grad_rows, logs, delta, keys, output_part, middle,
    grad_gate, grad_out, down_fin, up_fin,
    query_back, key_back, output, gate_out, up_out, down_out, out_out,
    terms, sums, rounded, folded, leaving, arriving, total, *rest,
):
    buffers, key_buffers, out_buffers = rest[:6], rest[6:9], rest[9:12]
    send_sem, recv_sem, out_send, out_recv, local_sem = rest[12:]
    key_rec, key_sums, key_rec_two = key_buffers
    fin = buffers[5]
    z, y, xl, xh, c = place()
    x = xh * 2 + xl
    here = (z, y, x, c)
    mine = xl * 2 + c
    quad = quad_of(xl, xh, x, c)
    greet(plane_targets(z, y, x, c) + line_targets(z, y, x, c) + [device(z, y, *quad[2])])
    wires = Wires(send_sem, recv_sem)
    gate = PlaneSum(wires, grad_gate, buffers, here, local_sem, 0)
    out_sum = OutSum(
        wires, grad_out, out_buffers, out_out, here, mine, quad, (out_send, out_recv), local_sem, 6
    )
    numbers = fold_sends(wires, output_part, folded, here)
    gate.start()
    out_sum.start()
    up_swaps = [
        wires.send(up_fin.at[b, lax.rem(a, 2)], up_out.at[mine], device(z, y, a, b))
        for a, b in quad
    ]
    down_swap = wires.send(
        down_fin.at[:, :, col_span(1 - c)], down_out.at[c], device(z, y, x, 1 - c)
    )
    kept = [
        pltpu.make_async_copy(up_fin.at[c, xl], up_out.at[mine], local_sem.at[7]),
        pltpu.make_async_copy(down_fin.at[:, :, col_span(c)], down_out.at[c], local_sem.at[8]),
    ]
    for copy in kept:
        copy.start()

    tour = Tour(z * 4 + y)
    terms[...] = jnp.zeros(terms.shape, F32)
    sums[...] = jnp.zeros(sums.shape, F32)
    heads = range(GROUP)

    def step(s, at, masked):
        slot = key_at(at)
        pairs = keys[slot]
        columns = [queries[s, :, head_cols(g)] for g in heads]
        grad_columns = [grads[s, :, head_cols(g)] for g in heads]
        log_rows = [logs[s, :, head_cols(g)] for g in heads]
        deltas = [delta[s, :, head_cols(g)] for g in heads]
        rows = [query_rows[s, g] for g in heads]
        outer = [grad_rows[s, g] for g in heads]
        if not masked:
            fits = in_second(tour.half(s), ends)
            log_rows = [jnp.where(fits, value, -NEVER) for value in log_rows]
        scores = [jnp.dot(pairs, value, preferred_element_type=F32) for value in columns]
        prob_grads = [jnp.dot(pairs, value, preferred_element_type=F32) for value in grad_columns]
        probs = [jnp.exp(scores[g] - log_rows[g]) for g in heads]
        if masked:
            allowed = allowed_pairs(at, tour.half(s), ends)
            probs = [jnp.where(allowed, value, 0.0) for value in probs]
        score_grads = [(probs[g] * (prob_grads[g] - deltas[g])).astype(BF) for g in heads]
        probs_low = [value.astype(BF) for value in probs]
        back = [
            lax.dot_general(
                pairs, value, (((0,), (0,)), ((), ())), preferred_element_type=F32
            )
            for value in score_grads
        ]
        added = [
            jnp.dot(score_grads[g], rows[g], preferred_element_type=F32)
            + jnp.dot(probs_low[g], outer[g], preferred_element_type=F32)
            for g in heads
        ]
        terms[slot] += (added[0] + added[1]) + (added[2] + added[3])
        for g in heads:
            sums[s, :, head_cols(g)] += back[g]

    tour.inner(step, 0, 8)
    gate.relay()
    moves = fold_moves(wires, numbers, output_part, folded, leaving, arriving, here, total)
    out_sum.middle()
    tour.inner(step, 8, 20)
    fold_finish(wires, moves, arriving, total)
    output[...] = (middle[...] + total[...]).astype(BF)
    out_sum.deal()
    gate.middle()
    tour.inner(step, 20, tour.count)
    tour.edges(step)

    for s in (0, 1):
        for i in range(4):
            rounded[s, i] = terms[s, i].astype(BF)
    first = [[], []]
    for k, by in enumerate(OFFSETS):
        first[0].append(
            wires.send(
                rounded.at[0, :, lax.rem(y + by, 4)], key_rec.at[0, k], second_device(here, 0, by)
            )
        )
        first[1].append(
            wires.send(
                rounded.at[1, lax.rem(z + by, 4)], key_rec.at[1, k], second_device(here, 1, by)
            )
        )
    for s in (0, 1):
        query_back[s] = sums[s, :HD, :] * HD ** (-0.5)
    gate.finish()
    swaps = [
        wires.send(fin.at[b, lax.rem(a, 2)], gate_out.at[mine], device(z, y, a, b))
        for a, b in quad
    ]
    kept.append(pltpu.make_async_copy(fin.at[c, xl], gate_out.at[mine], local_sem.at[9]))
    kept[-1].start()
    second = [[], []]
    for s in (0, 1):
        for k in range(3):
            wires.landed(first[s][k], key_rec.at[s, k])
        for i in range(4):
            value = terms[0, i, y] if s == 0 else terms[1, z, i]
            for k in range(3):
                value = value + key_rec[s, k, i].astype(F32)
            key_sums[s, i] = value.astype(BF)
        for k, by in enumerate(OFFSETS):
            second[s].append(
                wires.send(
                    key_sums.at[s, first_at(here, s, by)],
                    key_rec_two.at[s, k],
                    first_device(here, s, by),
                )
            )
    out_sum.finish()
    for s in (0, 1):
        value = key_sums[s, first_at(here, s)].astype(F32)
        for k in range(3):
            wires.landed(second[s][k], key_rec_two.at[s, k])
            value = value + key_rec_two[s, k].astype(F32)
        key_back[s] = value
    for at, (a, b) in zip(up_swaps, quad):
        wires.landed(at, up_out.at[lax.rem(a, 2) * 2 + b])
    wires.landed(down_swap, down_out.at[1 - c])
    for at, (a, b) in zip(swaps, quad):
        wires.landed(at, gate_out.at[lax.rem(a, 2) * 2 + b])
    for copy in kept:
        copy.wait()
    wires.close()


def call_attention_back(
    ends, queries, grads, query_rows, grad_rows, logs, delta, keys, output_part, middle,
    grad_gate, grad_out, down_fin, up_fin,
):
    vm = pl.BlockSpec(memory_space=pltpu.VMEM)
    hbm = pl.BlockSpec(memory_space=ANY)
    cols = GROUP * HALF
    return pl.pallas_call(
        attention_back_kernel,
        out_shape=(
            jax.ShapeDtypeStruct((2, HD, cols), F32),
            jax.ShapeDtypeStruct((2, HALF, 2 * HD), F32),
            jax.ShapeDtypeStruct((ROWS, WIDTH), BF),
            jax.ShapeDtypeStruct((4, PIECE, HIDDEN), BF),
            jax.ShapeDtypeStruct((4, PIECE, HIDDEN), BF),
            jax.ShapeDtypeStruct((2, 2, PIECE, WIDTH), BF),
            jax.ShapeDtypeStruct((PIECE, WIDTH), BF),
        ),
        in_specs=[pl.BlockSpec(memory_space=pltpu.SMEM)] + [vm] * 9 + [hbm] * 4,
        out_specs=(vm, vm, vm, hbm, hbm, hbm, hbm),
        scratch_shapes=[
            pltpu.VMEM((2, 4, 4, HALF, 2 * HD), F32),
            pltpu.VMEM((2, 2 * HD, cols), F32),
            pltpu.VMEM((2, 4, 4, HALF, 2 * HD), BF),
        ]
        + fold_scratch()
        + sum_buffers((2, PIECE, HIDDEN), BF)
        + [
            pltpu.VMEM((2, 3, 4, HALF, 2 * HD), BF),
            pltpu.VMEM((2, 4, HALF, 2 * HD), BF),
            pltpu.VMEM((2, 3, HALF, 2 * HD), BF),
            pltpu.VMEM((3, 2, PIECE, D), BF),
            pltpu.VMEM((2, PIECE, D), BF),
            pltpu.VMEM((3, 2, PIECE, D), BF),
        ]
        + wire_scratch(56)
        + wire_scratch(6)
        + [pltpu.SemaphoreType.DMA((10,))],
        compiler_params=comm_params(6),
        name="attention_back",
    )(
        ends, queries, grads, query_rows, grad_rows, logs, delta, keys, output_part, middle,
        grad_gate, grad_out, down_fin, up_fin,
    )


def rope_tables(position, head_size):
    half_size = head_size // 2
    column = jnp.arange(half_size, dtype=jnp.float32)
    inverse = jnp.exp(-(2.0 * column / head_size) * math.log(ROPE_THETA))
    wavelength = 2.0 * math.pi / inverse
    smooth = (OLD_CONTEXT / wavelength - LOW_FREQ) / (HIGH_FREQ - LOW_FREQ)
    blended = (1.0 - smooth) * inverse / ROPE_FACTOR + smooth * inverse
    inverse = jnp.where(
        wavelength < OLD_CONTEXT / HIGH_FREQ,
        inverse,
        jnp.where(wavelength > OLD_CONTEXT / LOW_FREQ, inverse / ROPE_FACTOR, blended),
    )
    angles = position.astype(jnp.float32)[:, None] * inverse[None, :]
    return (jnp.cos(angles), jnp.sin(angles))


def rotate(values, cosine, sine):
    half_size = values.shape[-1] // 2
    table_shape = (cosine.shape[0],) + (1,) * (values.ndim - 2) + (half_size,)
    cos_part = cosine.reshape(table_shape)
    sin_part = sine.reshape(table_shape)
    first_half = values[..., :half_size]
    second_half = values[..., half_size:]
    return jnp.concatenate(
        [
            first_half * cos_part - second_half * sin_part,
            second_half * cos_part + first_half * sin_part,
        ],
        axis=-1,
    )


def times(left, right, kind):
    return jnp.dot(left, right, preferred_element_type=F32).astype(kind)


def times_transpose(left, right, kind):
    return lax.dot_general(
        left, right, (((1,), (1,)), ((), ())), preferred_element_type=F32
    ).astype(kind)


def outer_rows(left, right, kind):
    return lax.dot_general(
        left, right, (((0,), (0,)), ((), ())), preferred_element_type=F32
    ).astype(kind)


def as_columns(rows):
    return rows.reshape(2, HALF, GROUP, HD).transpose(0, 3, 2, 1).reshape(2, HD, GROUP * HALF)


def as_heads(rows):
    return rows.reshape(2, HALF, GROUP, HD).transpose(0, 2, 1, 3)


def from_columns(columns):
    return columns.reshape(2, HD, GROUP, HALF).transpose(0, 3, 2, 1).reshape(LINE, GROUP * HD)


def adam(weight, moment, second, gradient, rate, decay):
    moment_next = BETA_ONE * moment + (1.0 - BETA_ONE) * gradient
    second_next = BETA_TWO * second + (1.0 - BETA_TWO) * gradient * gradient
    unbiased = moment_next / (1.0 - BETA_ONE**ADAM_STEP)
    divisor = jnp.sqrt(second_next / (1.0 - BETA_TWO**ADAM_STEP)) + ADAM_EPS
    return (weight - rate * (unbiased / divisor + decay * weight), moment_next, second_next)


def shards(
    block_input,
    out_grad,
    qkv_weight,
    qkv_moment,
    qkv_second,
    gate_up_weight,
    gate_up_moment,
    gate_up_second,
    out_weight,
    out_moment,
    out_second,
    down_weight,
    down_moment,
    down_second,
    norm_gains,
    gains_moment,
    gains_second,
    doc_lengths,
):
    z, y, xl, xh, c = place()
    x = xh * 2 + xl
    spot = z * 4 + y

    ends = jnp.cumsum(doc_lengths)
    local = jnp.arange(LINE, dtype=jnp.int32)
    half = jnp.where(local < HALF, 2 * spot, HALVES - 1 - 2 * spot)
    places = half * HALF + lax.rem(local, HALF)
    passed = (places[:, None] >= ends[None, :]).astype(jnp.int32)
    position = places - jnp.sum(passed * doc_lengths[None, :], axis=1)
    cosine, sine = rope_tables(position, HD)

    def dealt(half_weight):
        return (
            half_weight.astype(BF)
            .reshape(PIECE, 16, 4, HD)
            .transpose(2, 0, 1, 3)
            .reshape(4, PIECE, HIDDEN)
        )

    (
        inputs,
        scale_one,
        normed,
        qkv_whole,
        query_columns,
        mixed,
        logs,
        attended,
        keys,
        cotangent,
        cotangent_all,
        out_whole,
        gate_whole,
        up_whole,
        down_whole,
        middle,
        scale_two,
        normed_two,
    ) = call_forward(
        ends,
        cosine.T,
        sine.T,
        block_input,
        out_grad,
        jnp.concatenate([norm_gains, jnp.zeros((6, WIDTH), F32)], axis=0),
        qkv_weight.astype(BF).transpose(1, 0, 2),
        dealt(gate_up_weight[:, 0]),
        dealt(gate_up_weight[:, 1]),
        down_weight.astype(BF).reshape(2, ROWS // 2, WIDTH),
        out_weight.astype(BF),
    )
    qkv_low = qkv_whole.reshape(D, (GROUP + 2) * HD)
    gate_low = gate_whole.reshape(D, HIDDEN)
    up_low = up_whole.reshape(D, HIDDEN)
    down_low = down_whole.reshape(HIDDEN, D)
    out_low = out_whole.reshape(GROUP * HD, D)

    gate_part = times(normed_two, gate_low, F32)
    up_part = times(normed_two, up_low, F32)
    sigmoid_gate = jax.nn.sigmoid(gate_part)
    hidden = (gate_part * sigmoid_gate * up_part).astype(BF)
    hidden_grad = times_transpose(cotangent_all, down_low, F32)
    gate_back = hidden_grad * up_part * sigmoid_gate * (1.0 + gate_part * (1.0 - sigmoid_gate))
    up_back = hidden_grad * gate_part * sigmoid_gate
    gate_back, up_back = gate_back.astype(BF), up_back.astype(BF)
    grad_down = outer_rows(hidden, cotangent_all, BF)
    grad_up = outer_rows(normed_two, up_back, BF)
    half_shape = gate_whole.shape
    middle_grad, gain_two, middle_low, down_fin, up_fin = call_back(
        (
            times_transpose(gate_back, gate_low, F32) + times_transpose(up_back, up_low, F32)
        ).astype(BF),
        middle,
        scale_two,
        norm_gains,
        cotangent,
        grad_down.reshape(down_whole.shape),
        grad_up.reshape(half_shape),
    )
    output_part = times(hidden, down_low, BF)
    grad_gate = outer_rows(normed_two, gate_back, BF)

    grad_out = outer_rows(attended, middle_low, BF)
    attended_grad = times_transpose(middle_low, out_low, BF)
    delta = jnp.sum(
        (attended_grad.astype(F32) * from_columns(mixed)).reshape(LINE, GROUP, HD), axis=-1
    )
    delta = delta.reshape(2, HALF, GROUP).transpose(0, 2, 1).reshape(2, 1, GROUP * HALF)
    blank = jnp.zeros((2, HD, GROUP * HALF), BF)
    empty = jnp.zeros((2, GROUP, HALF, HD), BF)
    query_back, key_grads, output, gate_sum, up_sum, down_sum, out_sum = call_attention_back(
        ends,
        query_columns,
        jnp.concatenate([blank, as_columns(attended_grad)], axis=1),
        query_columns.reshape(2, 2 * HD, GROUP, HALF).transpose(0, 2, 3, 1),
        jnp.concatenate([empty, as_heads(attended_grad)], axis=-1),
        logs,
        delta,
        keys,
        output_part,
        middle,
        grad_gate.reshape(half_shape),
        grad_out.reshape(out_whole.shape),
        down_fin,
        up_fin,
    )
    key_grads = key_grads.reshape(LINE, 2 * HD)
    turned_back = jnp.concatenate([from_columns(query_back), key_grads[:, :HD]], axis=1)
    turned_back = rotate(turned_back.reshape(LINE, GROUP + 1, HD), cosine, -sine)
    projected_back = jnp.concatenate(
        [turned_back.reshape(LINE, (GROUP + 1) * HD), key_grads[:, HD:]], axis=1
    ).astype(BF)
    grad_qkv = outer_rows(normed, projected_back, BF)
    square = sum(
        jnp.sum(jnp.square(member.astype(F32))) for member in (gate_sum, up_sum, out_sum, down_sum)
    )
    input_grad, output, qkv_sum, totals = call_last(
        times_transpose(projected_back, qkv_low, BF),
        inputs,
        scale_one,
        norm_gains,
        middle_grad,
        gain_two,
        jnp.broadcast_to(square, (8, 128)),
        output,
        grad_qkv.reshape(qkv_whole.shape),
    )
    gate_both = jnp.stack([gate_sum, up_sum], axis=2).reshape(4, PIECE, 2, 16, HD)
    shares = (
        qkv_sum.transpose(1, 0, 2).astype(F32),
        gate_both.transpose(1, 2, 3, 0, 4).reshape(gate_up_weight.shape).astype(F32),
        out_sum.astype(F32),
        down_sum.reshape(down_weight.shape).astype(F32),
    )
    gains_grad = totals[:16].reshape(2, WIDTH)
    grad_norm = jnp.sqrt(totals[16, 0])
    factor = CLIP_NORM / jnp.maximum(grad_norm, CLIP_NORM)
    weights = (qkv_weight, gate_up_weight, out_weight, down_weight)
    moments = (qkv_moment, gate_up_moment, out_moment, down_moment)
    seconds = (qkv_second, gate_up_second, out_second, down_second)
    out_rate = OUTPUT_RATE * (TOKENS / (HQ * HD)) ** 0.5
    down_rate = DOWN_RATE * FF ** (-0.5)
    rates = (MATRIX_RATE, MATRIX_RATE, out_rate, down_rate)
    results = []
    for weight, moment, second, gradient, rate in zip(weights, moments, seconds, shares, rates):
        results.extend(adam(weight, moment, second, gradient * factor, rate, WEIGHT_DECAY))
    gains_new = adam(norm_gains, gains_moment, gains_second, gains_grad * factor, GAIN_RATE, 0.0)
    return (output, input_grad, grad_norm, *results, *gains_new)


def solution(mesh):
    placed = (
        P(("seq", "wide"), "narrow"),
        P(("seq", "wide"), "narrow"),
        P(("narrow", "seq"), "wide", None),
        P(("narrow", "seq"), "wide", None),
        P(("narrow", "seq"), "wide", None),
        P(("narrow", "seq"), None, "wide"),
        P(("narrow", "seq"), None, "wide"),
        P(("narrow", "seq"), None, "wide"),
        P(("wide", "seq"), "narrow"),
        P(("wide", "seq"), "narrow"),
        P(("wide", "seq"), "narrow"),
        P(("wide", "seq"), "narrow"),
        P(("wide", "seq"), "narrow"),
        P(("wide", "seq"), "narrow"),
        P(None, "narrow"),
        P(None, "narrow"),
        P(None, "narrow"),
        P(),
    )
    return jax.shard_map(
        shards,
        mesh=mesh,
        in_specs=placed,
        out_specs=(
            P(("seq", "wide"), "narrow"),
            P(("seq", "wide"), "narrow"),
            P(),
            P(("narrow", "seq"), "wide", None),
            P(("narrow", "seq"), "wide", None),
            P(("narrow", "seq"), "wide", None),
            P(("narrow", "seq"), None, "wide"),
            P(("narrow", "seq"), None, "wide"),
            P(("narrow", "seq"), None, "wide"),
            P(("wide", "seq"), "narrow"),
            P(("wide", "seq"), "narrow"),
            P(("wide", "seq"), "narrow"),
            P(("wide", "seq"), "narrow"),
            P(("wide", "seq"), "narrow"),
            P(("wide", "seq"), "narrow"),
            P(None, "narrow"),
            P(None, "narrow"),
            P(None, "narrow"),
        ),
        check_vma=False,
    )
```

```python
import functools
import math

import jax
import jax.numpy as jnp
from jax import lax
from jax.experimental import pallas as pl
from jax.experimental.pallas import tpu as pltpu
from jax.sharding import PartitionSpec as P

D = 2048
HQ = 32
HD = 64
FF = 8192
ADAM_STEP = 10


NORM_EPS = 1e-05
ADAM_EPS = 1e-08
BETA_ONE = 0.9
BETA_TWO = 0.95
WEIGHT_DECAY = 0.1
MATRIX_RATE = 0.01
OUTPUT_RATE = 0.9
DOWN_RATE = 3.0
GAIN_RATE = 2.5
CLIP_NORM = 1.0
ROPE_THETA = 500000.0
ROPE_FACTOR = 32.0
LOW_FREQ = 1.0
HIGH_FREQ = 4.0
OLD_CONTEXT = 8192.0

TOKENS = 8192
HALF = 256
HALVES = TOKENS // HALF
ROWS = 128
LINE = 512
WIDTH = 1024
GROUP = 4
PIECE = 32
HIDDEN = 1024
MESH = pl.DeviceIdType.MESH
ANY = pl.ANY
BF = jnp.bfloat16
F32 = jnp.float32
VMEM_LIMIT = 60 * 1024 * 1024
NEVER = -1e30


def place():
    seq = lax.axis_index("seq")
    return (
        seq // 8,
        lax.rem(seq // 2, 4),
        lax.rem(seq, 2),
        lax.axis_index("wide"),
        lax.axis_index("narrow"),
    )


def device(z, y, x, c):
    return (lax.rem(z, 4) * 8 + lax.rem(y, 4) * 2 + lax.rem(x, 2), c, x // 2)


class Wires:
    def __init__(self, send_sem, recv_sem):
        self.send_sem, self.recv_sem, self.used, self.sent = send_sem, recv_sem, 0, []
        self.settled = set()

    def send(self, src, dst, target, start=True):
        at = self.used
        self.used += 1
        copy = pltpu.make_async_remote_copy(
            src_ref=src,
            dst_ref=dst,
            send_sem=self.send_sem.at[at],
            recv_sem=self.recv_sem.at[at],
            device_id=target,
            device_id_type=MESH,
        )
        if start:
            copy.start()
        self.sent.append(copy)
        return at

    def landed(self, at, region):
        pltpu.make_async_copy(region, region, self.recv_sem.at[at]).wait()

    def settle(self, numbers):
        for at in numbers:
            self.sent[at].wait_send()
            self.settled.add(at)

    def close(self):
        self.settle([at for at in range(self.used) if at not in self.settled])


def greet(targets):
    barrier = pltpu.get_barrier_semaphore()
    for target in targets:
        pl.semaphore_signal(barrier, inc=1, device_id=target, device_id_type=MESH)
    pl.semaphore_wait(barrier, len(targets))


def line_targets(z, y, x, c):
    return [device(z, y, lax.rem(x + o, 4), c) for o in (1, 2, 3)] + [device(z, y, x, 1 - c)]


def plane_targets(z, y, x, c):
    return [device(z + o, y, x, c) for o in (1, 2, 3)] + [device(z, y + o, x, c) for o in (1, 2, 3)]


def wire_scratch(count):
    return [pltpu.SemaphoreType.DMA((count,)), pltpu.SemaphoreType.DMA((count,))]


def comm_params(number):
    return pltpu.CompilerParams(
        collective_id=number, has_side_effects=True, vmem_limit_bytes=VMEM_LIMIT
    )


def rows_of(x):
    return lax.rem(x, 2) * 2 + x // 2


def row_span(x):
    return pl.ds(pl.multiple_of(rows_of(x) * ROWS, ROWS), ROWS)


def col_span(c):
    return pl.ds(pl.multiple_of(c * WIDTH, WIDTH), WIDTH)


def gather_sends(wires, own, out, here):
    z, y, x, c = here
    spot = out.at[row_span(x), col_span(c)]
    across = {o: wires.send(own, spot, device(z, y, lax.rem(x + o, 4), c)) for o in (2, 1, 3)}
    return across, wires.send(own, spot, device(z, y, x, 1 - c))


def gather_relay(wires, numbers, out, here):
    z, y, x, c = here
    across, direct = numbers
    relays = []
    for o in (1, 3, 2):
        rows = row_span(lax.rem(x + 4 - o, 4))
        spot = out.at[rows, col_span(c)]
        wires.landed(across[o], spot)
        relays.append((wires.send(spot, spot, device(z, y, x, 1 - c)), rows))
    wires.landed(direct, out.at[row_span(x), col_span(1 - c)])
    for at, rows in relays:
        wires.landed(at, out.at[rows, col_span(1 - c)])
    return [at for at, _ in relays]


FOLD_ORDER = (2, 1, 3, 0)
EVERY = slice(None)


def fold_sends(wires, part, folded, here):
    z, y, x, c = here
    return [
        wires.send(
            part.at[row_span(lax.rem(x + o, 4)), col_span(1 - c)],
            folded.at[k],
            device(z, y, x, 1 - c),
        )
        for k, o in enumerate(FOLD_ORDER)
    ]


def fold_moves(wires, numbers, part, folded, leaving, arriving, here, total, cols=EVERY):
    z, y, x, c = here
    moves = []
    for k, o in enumerate(FOLD_ORDER):
        wires.landed(numbers[k], folded.at[k])
        both = part[row_span(lax.rem(x + o, 4)), cols].astype(F32) + folded[k].astype(F32)
        if o:
            leaving[k] = both.astype(BF)
            moves.append(
                wires.send(leaving.at[k], arriving.at[k], device(z, y, lax.rem(x + o, 4), c))
            )
        else:
            total[...] = both
    return moves


def fold_finish(wires, moves, arriving, total):
    for k, at in enumerate(moves):
        wires.landed(at, arriving.at[k])
    total[...] = (
        total[...]
        + arriving[0].astype(F32)
        + arriving[1].astype(F32)
        + arriving[2].astype(F32)
    )


def fold_scratch():
    return [
        pltpu.VMEM((4, ROWS, WIDTH), BF),
        pltpu.VMEM((3, ROWS, WIDTH), BF),
        pltpu.VMEM((3, ROWS, WIDTH), BF),
        pltpu.VMEM((ROWS, WIDTH), F32),
    ]


def both_cores(wires, mine, theirs, value, here):
    z, y, x, c = here
    mine[...] = jnp.broadcast_to(value, mine.shape)
    at = wires.send(mine, theirs, device(z, y, x, 1 - c))
    wires.landed(at, theirs)
    return value + theirs[:, :1]


def first_device(here, order, by):
    z, y, x, c = here
    return device(z + by, y, x, c) if order == 0 else device(z, y + by, x, c)


def second_device(here, order, by):
    z, y, x, c = here
    return device(z, y + by, x, c) if order == 0 else device(z + by, y, x, c)


def first_at(here, order, by=0):
    return lax.rem((here[0] if order == 0 else here[1]) + by, 4)


def run_of(ref, here, order, by, sub=None):
    z, y, _, _ = here
    zi, yi = (EVERY, lax.rem(y + by, 4)) if order == 0 else (lax.rem(z + by, 4), EVERY)
    if len(ref.shape) == 6:
        return ref.at[order, zi, yi] if sub is None else ref.at[order, zi, yi, sub]
    rows = ref.shape[2] // 2
    if sub is None:
        return ref.at[zi, yi, pl.ds(order * rows, rows)]
    return ref.at[zi, yi, pl.ds(order * rows + sub * (rows // 2), rows // 2)]


def spot_of(ref, here, order, at, sub=None):
    z, y, _, _ = here
    zi, yi = (at, y) if order == 0 else (z, at)
    if len(ref.shape) == 6:
        return ref.at[order, zi, yi] if sub is None else ref.at[order, zi, yi, sub]
    rows = ref.shape[2] // 2
    if sub is None:
        return ref.at[zi, yi, pl.ds(order * rows, rows)]
    return ref.at[zi, yi, pl.ds(order * rows + sub * (rows // 2), rows // 2)]


class PlaneGather:
    def __init__(self, wires, whole, here):
        self.wires, self.whole, self.here = wires, whole, here

    def start(self):
        self.numbers = []
        for o in (0, 1):
            spot = spot_of(self.whole, self.here, o, first_at(self.here, o))
            self.numbers.append(
                [self.wires.send(spot, spot, first_device(self.here, o, by)) for by in (1, 3)]
            )

    def relay(self):
        relays = []
        for o in (0, 1):
            sends = []
            for sub, by in enumerate((1, 3)):
                at = first_at(self.here, o, 4 - by)
                self.wires.landed(self.numbers[o][sub], spot_of(self.whole, self.here, o, at))
                spot = spot_of(self.whole, self.here, o, at, sub)
                sends.append(self.wires.send(spot, spot, first_device(self.here, o, by)))
            relays.append(sends)
        self.numbers = relays

    def turn(self):
        lines = []
        for o in (0, 1):
            for sub in (0, 1):
                at = first_at(self.here, o, 2)
                self.wires.landed(
                    self.numbers[o][sub], spot_of(self.whole, self.here, o, at, sub)
                )
            spot = run_of(self.whole, self.here, o, 0)
            lines.append(
                [self.wires.send(spot, spot, second_device(self.here, o, by)) for by in (1, 3)]
            )
        self.numbers = lines

    def relay_two(self):
        relays = []
        for o in (0, 1):
            sends = []
            for sub, by in enumerate((1, 3)):
                self.wires.landed(self.numbers[o][sub], run_of(self.whole, self.here, o, 4 - by))
                spot = run_of(self.whole, self.here, o, 4 - by, sub)
                sends.append(self.wires.send(spot, spot, second_device(self.here, o, by)))
            relays.append(sends)
        self.numbers = relays

    def finish(self):
        for o in (0, 1):
            for sub in (0, 1):
                self.wires.landed(
                    self.numbers[o][sub], run_of(self.whole, self.here, o, 2, sub)
                )


OFFSETS = (2, 1, 3)


class PlaneSum:
    def __init__(self, wires, terms, buffers, here, local_sem, at):
        self.wires, self.terms, self.here = wires, terms, here
        self.far, self.joined, self.rec, self.total, self.rec_two, self.fin = buffers
        self.kept, self.added = [], []
        for o in (0, 1):
            self.kept.append(
                pltpu.make_async_copy(
                    run_of(terms, here, o, 0), self.total.at[o], local_sem.at[at + 3 * o]
                )
            )
            self.added.append(
                [
                    pltpu.make_async_copy(
                        run_of(terms, here, o, by, sub),
                        self.joined.at[o, sub],
                        local_sem.at[at + 3 * o + 1 + sub],
                    )
                    for sub, by in enumerate((1, 3))
                ]
            )

    def start(self):
        self.numbers = []
        for o in (0, 1):
            self.numbers.append(
                [
                    self.wires.send(
                        run_of(self.terms, self.here, o, 2, sub),
                        self.far.at[o, sub],
                        second_device(self.here, o, by),
                    )
                    for sub, by in enumerate((1, 3))
                ]
            )
        for o in (0, 1):
            for copy in self.added[o]:
                copy.start()
        self.direct = []
        for o in (0, 1):
            self.direct.append(
                [
                    self.wires.send(
                        run_of(self.terms, self.here, o, by, 1 - sub),
                        half_of(self.rec.at[o, sub], 1 - sub),
                        second_device(self.here, o, by),
                    )
                    for sub, by in enumerate((1, 3))
                ]
            )
        for copy in self.kept:
            copy.start()

    def relay(self):
        self.passed = []
        for o in (0, 1):
            moves = []
            for sub, by in enumerate((1, 3)):
                self.added[o][sub].wait()
                self.wires.landed(self.numbers[o][sub], self.far.at[o, sub])

                def add(i, carry):
                    value = self.joined[o, sub, i].astype(F32) + self.far[o, sub, i].astype(F32)
                    self.joined[o, sub, i] = value.astype(BF)
                    return carry

                lax.fori_loop(0, 4, add, 0)
                moves.append(
                    self.wires.send(
                        self.joined.at[o, sub],
                        half_of(self.rec.at[o, sub], sub),
                        second_device(self.here, o, by),
                    )
                )
            self.passed.append(moves)

    def middle(self):
        self.moves = []
        for o in (0, 1):
            self.kept[o].wait()
            for sub in (0, 1):
                self.wires.landed(self.direct[o][sub], half_of(self.rec.at[o, sub], 1 - sub))
                self.wires.landed(self.passed[o][sub], half_of(self.rec.at[o, sub], sub))

            def add(i, carry):
                value = self.total[o, i].astype(F32)
                for sub in (0, 1):
                    value = value + self.rec[o, sub, i].astype(F32)
                self.total[o, i] = value.astype(BF)
                return carry

            lax.fori_loop(0, 4, add, 0)
            self.moves.append(
                [
                    self.wires.send(
                        self.total.at[o, first_at(self.here, o, by)],
                        self.rec_two.at[o, k],
                        first_device(self.here, o, by),
                    )
                    for k, by in enumerate(OFFSETS)
                ]
            )

    def finish(self):
        for o in (0, 1):
            for k in range(3):
                self.wires.landed(self.moves[o][k], self.rec_two.at[o, k])
            value = self.total[o, first_at(self.here, o)].astype(F32)
            for k in range(3):
                value = value + self.rec_two[o, k].astype(F32)
            self.fin[o] = value.astype(self.fin.dtype)


def half_of(line, sub):
    if len(line.shape) == 4:
        return line.at[:, sub]
    rows = line.shape[1] // 2
    return line.at[:, pl.ds(sub * rows, rows)]


def sum_buffers(piece, kind):
    half = piece[1:] if len(piece) == 3 else (piece[0] // 2,) + piece[1:]
    return [
        pltpu.VMEM((2, 2, 4) + half, BF),
        pltpu.VMEM((2, 2, 4) + half, BF),
        pltpu.VMEM((2, 2, 4) + piece, BF),
        pltpu.VMEM((2, 4) + piece, BF),
        pltpu.VMEM((2, 3) + piece, BF),
        pltpu.VMEM((2,) + piece, kind),
    ]


class OutGather:
    def __init__(self, wires, stage, whole, here, mine, send_sem, recv_sem, local_sem, at):
        z, y, x, c = here
        self.wires, self.stage, self.whole, self.here = wires, stage, whole, here
        self.off = lax.rem(z - mine + 4, 4)
        self.recv_sem = recv_sem
        spot = whole.at[y]
        self.kept = pltpu.make_async_copy(stage, spot, local_sem.at[at])

        def copy(k, src, dst, by):
            return pltpu.make_async_remote_copy(
                src_ref=src,
                dst_ref=dst,
                send_sem=send_sem.at[k],
                recv_sem=recv_sem.at[k],
                device_id=device(z + by, y, x, c),
                device_id_type=MESH,
            )

        self.first = [copy(0, stage, spot, 1), copy(1, stage, spot, 3)]
        self.onward = [
            copy(2, spot.at[0], spot.at[0], 1),
            copy(3, spot.at[1], spot.at[1], 3),
        ]

    def landed(self, k, region):
        pltpu.make_async_copy(region, region, self.recv_sem.at[k]).wait()

    def start(self):
        @pl.when(self.off == 0)
        def _():
            self.kept.start()
            for copy in self.first:
                copy.start()

    def relay(self):
        spot = self.whole.at[self.here[1]]
        for k, off in ((0, 1), (1, 3)):

            @pl.when(self.off == off)
            def _():
                self.landed(k, spot)
                self.onward[k].start()

    def turn(self):
        z, y, x, c = self.here
        spot = self.whole.at[y]

        @pl.when(self.off == 0)
        def _():
            self.kept.wait()

        @pl.when(self.off == 2)
        def _():
            self.landed(2, spot.at[0])
            self.landed(3, spot.at[1])

        self.numbers = [self.wires.send(spot, spot, device(z, y + by, x, c)) for by in (1, 3)]

    def relay_two(self):
        z, y, x, c = self.here
        relays = []
        for sub, by in enumerate((1, 3)):
            spot = self.whole.at[lax.rem(y + 4 - by, 4)]
            self.wires.landed(self.numbers[sub], spot)
            relays.append(
                self.wires.send(spot.at[sub], spot.at[sub], device(z, y + by, x, c))
            )
        self.numbers = relays

    def finish(self):
        spot = self.whole.at[lax.rem(self.here[1] + 2, 4)]
        for sub in (0, 1):
            self.wires.landed(self.numbers[sub], spot.at[sub])

        @pl.when(self.off == 0)
        def _():
            for copy in self.first:
                copy.wait_send()

        for k, off in ((0, 1), (1, 3)):

            @pl.when(self.off == off)
            def _():
                self.onward[k].wait_send()


class OutSum:
    def __init__(self, wires, terms, buffers, piece, here, mine, quad, sems, local_sem, at):
        self.wires, self.terms, self.here, self.mine, self.quad = wires, terms, here, mine, quad
        self.rec, self.total, self.rec_two = buffers
        self.piece, self.local_sem, self.at = piece, local_sem, at
        self.send_sem, self.recv_sem = sems
        self.off = lax.rem(here[0] - mine + 4, 4)
        self.kept = pltpu.make_async_copy(
            terms.at[here[1]], self.total, local_sem.at[at]
        )

    def start(self):
        z, y, x, c = self.here
        self.kept.start()
        self.numbers = [
            self.wires.send(
                self.terms.at[lax.rem(y + by, 4)], self.rec.at[k], device(z, y + by, x, c)
            )
            for k, by in enumerate(OFFSETS)
        ]

    def copy(self, k, src, dst, target):
        return pltpu.make_async_remote_copy(
            src_ref=src,
            dst_ref=dst,
            send_sem=self.send_sem.at[k],
            recv_sem=self.recv_sem.at[k],
            device_id=target,
            device_id_type=MESH,
        )

    def middle(self):
        z, y, x, c = self.here
        self.kept.wait()
        value = self.total[...].astype(F32)
        for k in range(3):
            self.wires.landed(self.numbers[k], self.rec.at[k])
            value = value + self.rec[k].astype(F32)
        self.total[...] = value.astype(BF)
        self.moves = []
        for off in (1, 2, 3):
            move = self.copy(
                off - 1, self.total, self.rec_two.at[off - 1], device(self.mine, y, x, c)
            )
            self.moves.append(move)

            @pl.when(self.off == off)
            def _():
                move.start()

    def deal(self):
        z, y, x, c = self.here
        self.deals = []
        xl = lax.rem(x, 2)
        for k, (a, b) in enumerate(self.quad):
            self.deals.append(
                self.copy(
                    3 + k, self.total.at[lax.rem(a, 2), :, col_span(b)], self.piece, device(z, y, a, b)
                )
            )

        @pl.when(self.off == 0)
        def _():
            value = self.total[...].astype(F32)
            for k in range(3):
                region = self.rec_two.at[k]
                pltpu.make_async_copy(region, region, self.recv_sem.at[k]).wait()
                value = value + self.rec_two[k].astype(F32)
            self.total[...] = value.astype(BF)
            for copy in self.deals:
                copy.start()
            own = pltpu.make_async_copy(
                self.total.at[xl, :, col_span(c)], self.piece, self.local_sem.at[self.at]
            )
            own.start()
            own.wait()

    def finish(self):
        z, y, x, c = self.here
        xl = lax.rem(x, 2)
        holder_xl, holder_c = z // 2, lax.rem(z, 2)
        for k, (dx, dc) in enumerate(((0, 1), (1, 0), (1, 1))):

            @pl.when(
                (holder_xl == lax.rem(xl + dx, 2)) & (holder_c == lax.rem(c + dc, 2))
            )
            def _():
                pltpu.make_async_copy(self.piece, self.piece, self.recv_sem.at[3 + k]).wait()

        for off in (1, 2, 3):

            @pl.when(self.off == off)
            def _():
                self.moves[off - 1].wait_send()

        @pl.when(self.off == 0)
        def _():
            for copy in self.deals:
                copy.wait_send()


class Posting:
    def __init__(self, here, send_sem, recv_sem):
        z, y, x, c = here
        self.target = device(3 - z, 3 - y, x, c)
        self.away = lax.rem(x, 2) == 1
        self.send_sem, self.recv_sem, self.sent = send_sem, recv_sem, []

    def greet(self, barrier):
        @pl.when(self.away)
        def _():
            pl.semaphore_signal(barrier, inc=1, device_id=self.target, device_id_type=MESH)

        return self.away.astype(jnp.int32)

    def send(self, src, dst):
        at = len(self.sent)
        copy = pltpu.make_async_remote_copy(
            src_ref=src,
            dst_ref=dst,
            send_sem=self.send_sem.at[at],
            recv_sem=self.recv_sem.at[at],
            device_id=self.target,
            device_id_type=MESH,
        )
        self.sent.append(copy)

        @pl.when(self.away)
        def _():
            copy.start()

        @pl.when(jnp.logical_not(self.away))
        def _():
            pltpu.make_async_copy(src, dst, self.recv_sem.at[at]).start()

        return at

    def landed(self, at, region):
        pltpu.make_async_copy(region, region, self.recv_sem.at[at]).wait()

    def close(self):
        @pl.when(self.away)
        def _():
            for copy in self.sent:
                copy.wait_send()


def quad_of(xl, xh, x, c):
    pair = xh * 2 + 1 - xl
    return [(x, 1 - c), (pair, c), (pair, 1 - c)]


def norm_back(wires, values, scale, gain_row, incoming, mine, theirs, here):
    weighted = incoming * gain_row
    inner = both_cores(
        wires, mine, theirs, jnp.sum(weighted * values, axis=1, keepdims=True), here
    )
    inner = inner / D
    back = scale * (incoming * gain_row) - values * (scale * scale * scale * inner)
    return back, jnp.sum(incoming * values * scale, axis=0, keepdims=True)


PLANE = [(a, b) for a in range(4) for b in range(4) if a or b]


def key_at(half):
    odd = lax.rem(half, 2)
    at = jnp.where(odd == 1, HALVES - 1 - half, half) // 2
    return odd, at // 4, lax.rem(at, 4)


def allowed_pairs(key_half, query_half, ends):
    keys = key_half * HALF + lax.broadcasted_iota(jnp.int32, (HALF, HALF), 0)
    queries = query_half * HALF + lax.broadcasted_iota(jnp.int32, (HALF, HALF), 1)
    same = keys <= queries
    for k in range(3):
        same = same & ((keys >= ends[k]) == (queries >= ends[k]))
    return same


def in_second(query_half, ends):
    queries = query_half * HALF + lax.broadcasted_iota(jnp.int32, (1, HALF), 1)
    return (queries >= ends[0]) & (queries < ends[1])


class Tour:
    def __init__(self, spot):
        self.spot = spot
        self.low = jnp.maximum(2 * spot - 1, 0)
        self.count = self.low + HALVES - 2 - 2 * spot

    def half(self, s):
        return jnp.where(s == 0, 2 * self.spot, HALVES - 1 - 2 * self.spot)

    def inner(self, step, start, stop):
        def body(at, carry):
            s = jnp.where(at >= self.low, 1, 0)
            step(s, 1 + at - s * self.low, False)
            return carry

        lax.fori_loop(start, stop, body, 0)

    def edges(self, step):
        for s in (0, 1):
            half = self.half(s)

            def body(at, carry):
                step(s, at * half, True)
                return carry

            lax.fori_loop(0, jnp.where(half > 0, 2, 1), body, 0)


def head_cols(g):
    return slice(g * HALF, (g + 1) * HALF)


def rope(columns, at, cosine, sine):
    first = columns[at : at + HD // 2]
    second = columns[at + HD // 2 : at + HD]
    return first * cosine - second * sine, second * cosine + first * sine


def forward_kernel(
    ends, cosine, sine, block_input, out_grad, gain_rows, qkv_in, gate_in, up_in, down_in, out_in,
    inputs, scale_one, normed_out, qkv_out, queries, mixed_out, log_out, attended_out, keys_out,
    cotangent, cotangent_all, out_out, gate_all, up_all, down_all, middle_out, scale_two, out,
    inputs_all, gains_all, qkv_all, normed, columns, own_keys, keys, tops, sums, mixed,
    attended, out_stage, out_all, part, folded, leaving, arriving, total, mine_row, their_row, own,
    send_sem, recv_sem, post_send, post_recv, stage_send, stage_recv, out_send, out_recv, local_sem,
):
    z, y, xl, xh, c = place()
    x = xh * 2 + xl
    here = (z, y, x, c)
    mine = xl * 2 + c
    quad = quad_of(xl, xh, x, c)
    fixed = line_targets(z, y, x, c) + [device(z, y, *quad[2])] + plane_targets(z, y, x, c)
    barrier = pltpu.get_barrier_semaphore()
    post = Posting(here, post_send, post_recv)
    for target in fixed:
        pl.semaphore_signal(barrier, inc=1, device_id=target, device_id_type=MESH)
    extra = post.greet(barrier)
    pl.semaphore_wait(barrier, len(fixed) + extra)
    wires = Wires(send_sem, recv_sem)
    kept = {}

    def keep(name, src, dst):
        copy = pltpu.make_async_copy(src, dst, local_sem.at[len(kept)])
        copy.start()
        kept[name] = copy

    def swap(given, whole):
        numbers = [
            wires.send(
                given.at[lax.rem(to, 2) * 2 + core], whole.at[c, z, y, xl], device(z, y, to, core)
            )
            for to, core in quad
        ]
        return numbers

    def swapped(numbers, whole):
        for at, (from_x, from_c) in zip(numbers, quad):
            wires.landed(at, whole.at[from_c, z, y, lax.rem(from_x, 2)])

    input_at = post.send(block_input, inputs)
    keep("qkv", qkv_in.at[mine], qkv_all.at[c, z, y, xl])
    qkv_swap = swap(qkv_in, qkv_all)
    keep("gains", gain_rows, gains_all.at[:, col_span(c)])
    gain_at = wires.send(gain_rows, gains_all.at[:, col_span(c)], device(z, y, x, 1 - c))
    keep("gate", gate_in.at[mine], gate_all.at[c, z, y, xl])
    keep("up", up_in.at[mine], up_all.at[c, z, y, xl])
    keep("down", down_in.at[c], down_all.at[z, y, :, col_span(c)])
    down_swap = wires.send(
        down_in.at[1 - c], down_all.at[z, y, :, col_span(c)], device(z, y, x, 1 - c)
    )
    holds = z == mine
    stage_spot = out_stage.at[xl, :, col_span(c)]
    stage_copy = pltpu.make_async_remote_copy(
        src_ref=out_in,
        dst_ref=stage_spot,
        send_sem=stage_send.at[0],
        recv_sem=stage_recv.at[mine],
        device_id=device(z, y, xh * 2 + z // 2, lax.rem(z, 2)),
        device_id_type=MESH,
    )

    @pl.when(jnp.logical_not(holds))
    def _():
        stage_copy.start()

    @pl.when(holds)
    def _():
        pltpu.make_async_copy(out_in, stage_spot, stage_recv.at[mine]).start()

    qkv = PlaneGather(wires, qkv_all, here)
    gate = PlaneGather(wires, gate_all, here)
    up = PlaneGather(wires, up_all, here)
    down = PlaneGather(wires, down_all, here)
    out_gather = OutGather(
        wires, out_stage, out_all, here, mine, out_send, out_recv, local_sem, 12
    )

    kept["qkv"].wait()
    swapped(qkv_swap, qkv_all)
    qkv.start()
    post.landed(input_at, inputs)
    keep("inputs", inputs, inputs_all.at[row_span(x), col_span(c)])
    input_numbers = gather_sends(wires, inputs, inputs_all, here)
    gate_swap = swap(gate_in, gate_all)
    up_swap = swap(up_in, up_all)
    cotangent_at = post.send(out_grad, cotangent)
    qkv.relay()
    qkv.turn()
    gather_relay(wires, input_numbers, inputs_all, here)
    qkv.relay_two()
    kept["inputs"].wait()
    kept["gains"].wait()
    wires.landed(gain_at, gains_all.at[:, col_span(1 - c)])
    gain_one = gains_all[0:1, :]

    def norm_rows(i, carry):
        rows = pl.ds(pl.multiple_of(i * ROWS, ROWS), ROWS)
        values = inputs_all[rows, :].astype(F32)
        scale = lax.rsqrt(jnp.sum(values * values, axis=1, keepdims=True) / D + NORM_EPS)
        normed[rows, :] = (values * scale * gain_one).astype(BF)

        @pl.when(i == rows_of(x))
        def _():
            scale_one[...] = jnp.broadcast_to(scale, scale_one.shape)

        return carry

    lax.fori_loop(0, 4, norm_rows, 0)
    keep("normed", normed, normed_out)
    swapped(gate_swap, gate_all)
    kept["gate"].wait()
    gate.start()
    swapped(up_swap, up_all)
    kept["up"].wait()
    up.start()
    qkv.finish()
    keep("qkv_out", qkv_all, qkv_out)
    weight = qkv_all[...].reshape(D, columns.shape[0])

    def project_rows(i, carry):
        rows = pl.ds(pl.multiple_of(i * ROWS, ROWS), ROWS)
        product = jnp.dot(normed[rows, :], weight, preferred_element_type=F32)
        columns[:, rows] = product.T
        return carry

    lax.fori_loop(0, 4, project_rows, 0)
    queries[:, HD:, :] = jnp.zeros((2, HD, GROUP * HALF), BF)
    for g in range(GROUP):
        first, second = rope(columns, g * HD, cosine[...], sine[...])
        for s in (0, 1):
            tokens = slice(s * HALF, (s + 1) * HALF)
            queries[s, : HD // 2, head_cols(g)] = (first[:, tokens] * HD ** (-0.5)).astype(BF)
            queries[s, HD // 2 : HD, head_cols(g)] = (second[:, tokens] * HD ** (-0.5)).astype(BF)
    first, second = rope(columns, GROUP * HD, cosine[...], sine[...])
    pair_columns = jnp.concatenate([first, second, columns[(GROUP + 1) * HD :]], axis=0)
    for s in (0, 1):
        own_keys[s] = pair_columns[:, s * HALF : (s + 1) * HALF].T.astype(BF)

    numbers = [
        [
            wires.send(own_keys.at[s], keys.at[s, z, y], first_device(here, s, by))
            for by in OFFSETS
        ]
        for s in (0, 1)
    ]
    for s in (0, 1):
        keys[s, z, y] = own_keys[s]
    second_numbers = []
    for s in (0, 1):
        for at, by in zip(numbers[s], OFFSETS):
            back = first_at(here, s, 4 - by)
            wires.landed(at, keys.at[s, back, y] if s == 0 else keys.at[s, z, back])
        line = keys.at[0, :, y] if s == 0 else keys.at[1, z]
        second_numbers.append(
            [wires.send(line, line, second_device(here, s, by)) for by in OFFSETS]
        )

    @pl.when(holds)
    def _():
        for k in range(4):
            spot = out_stage.at[k // 2, :, pl.ds((k % 2) * WIDTH, WIDTH)]
            pltpu.make_async_copy(spot, spot, stage_recv.at[k]).wait()

    out_gather.start()
    gate.relay()
    up.relay()
    post.landed(cotangent_at, cotangent)
    keep("cotangent", cotangent, cotangent_all.at[row_span(x), col_span(c)])
    cotangent_numbers = gather_sends(wires, cotangent, cotangent_all, here)
    for s in (0, 1):
        for at, by in zip(second_numbers[s], OFFSETS):
            if s == 0:
                wires.landed(at, keys.at[0, :, lax.rem(y + 4 - by, 4)])
            else:
                wires.landed(at, keys.at[1, lax.rem(z + 4 - by, 4)])
    keep("keys", keys, keys_out)
    out_gather.relay()
    gate.turn()
    up.turn()

    tour = Tour(spot=z * 4 + y)
    tops[...] = jnp.full(tops.shape, NEVER, F32)
    sums[...] = jnp.zeros(sums.shape, F32)
    mixed[...] = jnp.zeros(mixed.shape, F32)
    heads = range(GROUP)

    def step(s, at, masked):
        pairs = keys[key_at(at)]
        old = [tops[s, :, head_cols(g)] for g in heads]
        old_sums = [sums[s, :, head_cols(g)] for g in heads]
        scores = [
            jnp.dot(pairs, queries[s, :, head_cols(g)], preferred_element_type=F32) for g in heads
        ]
        if masked:
            allowed = allowed_pairs(at, tour.half(s), ends)
            scores = [jnp.where(allowed, value, NEVER) for value in scores]
        top = [jnp.maximum(old[g], jnp.max(scores[g], axis=0, keepdims=True)) for g in heads]
        weights = [jnp.exp(scores[g] - top[g]) for g in heads]
        if masked:
            weights = [jnp.where(allowed, value, 0.0) for value in weights]
        shrink = [jnp.exp(old[g] - top[g]) for g in heads]
        new_sums = [
            old_sums[g] * shrink[g] + jnp.sum(weights[g], axis=0, keepdims=True) for g in heads
        ]
        new = [
            lax.dot_general(
                pairs, weights[g].astype(BF), (((0,), (0,)), ((), ())), preferred_element_type=F32
            )
            for g in heads
        ]
        for g in heads:
            cols = head_cols(g)
            tops[s, :, cols] = top[g]
            sums[s, :, cols] = new_sums[g]
            mixed[s, :, cols] = mixed[s, :, cols] * shrink[g] + new[g]

    tour.inner(step, 0, 6)
    out_gather.turn()
    gather_relay(wires, cotangent_numbers, cotangent_all, here)
    kept["down"].wait()
    wires.landed(down_swap, down_all.at[z, y, :, col_span(1 - c)])
    down.start()
    tour.inner(step, 6, 20)
    out_gather.relay_two()
    down.relay()
    tour.inner(step, 20, tour.count)
    for s in (0, 1):
        fits = in_second(tour.half(s), ends)
        for g in heads:
            cols = head_cols(g)
            tops[s, :, cols] = jnp.where(fits, tops[s, :, cols], NEVER)
            sums[s, :, cols] = jnp.where(fits, sums[s, :, cols], 0.0)
            mixed[s, :, cols] = jnp.where(fits, mixed[s, :, cols], 0.0)
    tour.edges(step)
    gate.relay_two()
    up.relay_two()
    down.turn()
    for s in (0, 1):
        tokens = slice(s * HALF, (s + 1) * HALF)
        log_out[s] = tops[s] + jnp.log(sums[s])
        mixed_out[s] = mixed[s, HD:, :] / sums[s]
        for g in range(0, GROUP, 2):
            two = jnp.concatenate(
                [mixed_out[s, :, head_cols(g)], mixed_out[s, :, head_cols(g + 1)]], axis=0
            )
            attended_out[g * HD : (g + 2) * HD, tokens] = two.astype(BF)
            attended[tokens, g * HD : (g + 2) * HD] = two.T.astype(BF)

    out_gather.finish()
    keep("out", out_all, out_out)
    out_low = out_all[...].reshape(GROUP * HD, D)
    fold_numbers = []
    for k, o in enumerate(FOLD_ORDER):
        rows = row_span(lax.rem(x + o, 4))
        part[rows, :] = jnp.dot(
            attended[rows, :], out_low, preferred_element_type=F32
        ).astype(BF)
        fold_numbers.append(
            wires.send(part.at[rows, col_span(1 - c)], folded.at[k], device(z, y, x, 1 - c))
        )
    moves = fold_moves(
        wires, fold_numbers, part, folded, leaving, arriving, here, total, col_span(c)
    )
    fold_finish(wires, moves, arriving, total)
    middle = total[...] + inputs[...].astype(F32)
    middle_out[...] = middle
    square = both_cores(
        wires, mine_row, their_row, jnp.sum(middle * middle, axis=1, keepdims=True), here
    )
    scale = lax.rsqrt(square / D + NORM_EPS)
    scale_two[...] = jnp.broadcast_to(scale, scale_two.shape)
    own[...] = (
        middle_out[...] * scale * gains_all[1:2, col_span(c)]
    ).astype(BF)
    keep("own", own, out.at[row_span(x), col_span(c)])
    sends = gather_sends(wires, own, out, here)
    down.relay_two()
    gather_relay(wires, sends, out, here)
    gate.finish()
    up.finish()
    down.finish()
    for name in ("normed", "qkv_out", "cotangent", "keys", "out", "own"):
        kept[name].wait()

    @pl.when(jnp.logical_not(holds))
    def _():
        stage_copy.wait_send()

    post.close()
    wires.close()


def call_forward(ends, cosine, sine, block_input, out_grad, gain_rows, qkv_in, gate_in, up_in, down_in, out_in):
    vm = pl.BlockSpec(memory_space=pltpu.VMEM)
    hbm = pl.BlockSpec(memory_space=ANY)
    cols = GROUP * HALF
    qkv_cols = qkv_in.shape[2]
    share = (ROWS, WIDTH)
    whole = (2, 4, 4, 2, PIECE)
    outs = [
        (share, BF, vm),
        ((ROWS, 128), F32, vm),
        ((LINE, D), BF, hbm),
        (whole + (qkv_cols,), BF, hbm),
        ((2, 2 * HD, cols), BF, vm),
        ((2, HD, cols), F32, vm),
        ((2, 1, cols), F32, vm),
        ((GROUP * HD, LINE), BF, vm),
        ((2, 4, 4, HALF, 2 * HD), BF, hbm),
        (share, BF, hbm),
        ((LINE, D), BF, hbm),
        ((4, 2, PIECE, D), BF, hbm),
        (whole + (HIDDEN,), BF, hbm),
        (whole + (HIDDEN,), BF, hbm),
        ((4, 4, 2 * PIECE, D), BF, hbm),
        (share, F32, vm),
        ((ROWS, 128), F32, vm),
        ((LINE, D), BF, hbm),
    ]
    return pl.pallas_call(
        forward_kernel,
        out_shape=tuple(jax.ShapeDtypeStruct(shape, kind) for shape, kind, _ in outs),
        in_specs=[pl.BlockSpec(memory_space=pltpu.SMEM), vm, vm] + [hbm] * 8,
        out_specs=tuple(spec for _, _, spec in outs),
        scratch_shapes=[
            pltpu.VMEM((LINE, D), BF),
            pltpu.VMEM((8, D), F32),
            pltpu.VMEM(whole + (qkv_cols,), BF),
            pltpu.VMEM((LINE, D), BF),
            pltpu.VMEM((qkv_cols, LINE), F32),
            pltpu.VMEM((2, HALF, 2 * HD), BF),
            pltpu.VMEM((2, 4, 4, HALF, 2 * HD), BF),
            pltpu.VMEM((2, 1, cols), F32),
            pltpu.VMEM((2, 1, cols), F32),
            pltpu.VMEM((2, 2 * HD, cols), F32),
            pltpu.VMEM((LINE, GROUP * HD), BF),
            pltpu.VMEM((2, PIECE, D), BF),
            pltpu.VMEM((4, 2, PIECE, D), BF),
            pltpu.VMEM((LINE, D), BF),
        ]
        + fold_scratch()
        + [
            pltpu.VMEM((ROWS, 128), F32),
            pltpu.VMEM((ROWS, 128), F32),
            pltpu.VMEM((ROWS, WIDTH), BF),
        ]
        + wire_scratch(128)
        + wire_scratch(2)
        + wire_scratch(4)
        + wire_scratch(4)
        + [pltpu.SemaphoreType.DMA((13,))],
        compiler_params=comm_params(1),
        name="forward",
    )(ends, cosine, sine, block_input, out_grad, gain_rows, qkv_in, gate_in, up_in, down_in, out_in)


def backward_kernel(
    ends, cosine, sine, part, output_part, middle, scale_two, scale_one, gains, inputs, cotangent,
    queries, mixed, logs, attended, keys, out_low, qkv_low, normed, grad_down, grad_up, grad_gate,
    input_home, output_home, qkv_out, gate_out, up_out, down_out, out_out, totals,
    middle_grad, middle_all, grads, delta, query_rows, grad_rows, out_terms, output,
    terms, sums, rounded, columns, rows_back, qkv_terms, key_rec, key_sums, key_rec_two,
    *rest,
):
    rest = list(rest)

    def take(count):
        taken = rest[:count]
        del rest[:count]
        return taken

    first_fold, output_fold, (part_own, output_own) = take(4), take(4), take(2)
    last_fold = first_fold
    first_rows, last_rows, (own,) = take(2), take(2), take(1)
    down_buffers, up_buffers, gate_buffers, qkv_buffers = take(6), take(6), take(6), take(6)
    out_buffers, (total_terms, stage, rec_one, rec_two) = take(3), take(4)
    send_sem, recv_sem, post_send, post_recv, out_send, out_recv, local_sem = rest
    z, y, xl, xh, c = place()
    x = xh * 2 + xl
    here = (z, y, x, c)
    mine = xl * 2 + c
    quad = quad_of(xl, xh, x, c)
    line = [(o, b) for b in (0, 1) for o in range(4) if o or b]
    fixed = [device(z + a, y + b, x, c) for a, b in PLANE]
    fixed += [device(z, y, lax.rem(x + o, 4), lax.rem(c + b, 2)) for o, b in line]
    barrier = pltpu.get_barrier_semaphore()
    post = Posting(here, post_send, post_recv)
    for target in fixed:
        pl.semaphore_signal(barrier, inc=1, device_id=target, device_id_type=MESH)
    extra = post.greet(barrier)
    pl.semaphore_wait(barrier, len(fixed) + extra)
    wires = Wires(send_sem, recv_sem)
    kept = []

    def keep(src, dst):
        copy = pltpu.make_async_copy(src, dst, local_sem.at[25 + len(kept)])
        copy.start()
        kept.append(copy)

    def deal(fin, result):
        keep(fin.at[c, xl], result.at[mine])
        return [
            wires.send(fin.at[b, lax.rem(a, 2)], result.at[mine], device(z, y, a, b))
            for a, b in quad
        ]

    def dealt(numbers, result):
        for at, (a, b) in zip(numbers, quad):
            wires.landed(at, result.at[lax.rem(a, 2) * 2 + b])

    numbers = fold_sends(wires, part, first_fold[0], here)
    own_parts = [
        pltpu.make_async_copy(part.at[:, col_span(c)], part_own, local_sem.at[36]),
        pltpu.make_async_copy(output_part.at[:, col_span(c)], output_own, local_sem.at[37]),
        pltpu.make_async_copy(out_low, out_terms, local_sem.at[38]),
        pltpu.make_async_copy(qkv_low, qkv_terms, local_sem.at[39]),
    ]
    for copy in own_parts:
        copy.start()
    down = PlaneSum(wires, grad_down, down_buffers, here, local_sem, 0)
    up = PlaneSum(wires, grad_up, up_buffers, here, local_sem, 6)
    gate = PlaneSum(wires, grad_gate, gate_buffers, here, local_sem, 12)
    qkv = PlaneSum(wires, qkv_terms, qkv_buffers, here, local_sem, 18)
    out_sum = OutSum(
        wires, out_terms, out_buffers, out_out, here, mine, quad, (out_send, out_recv), local_sem, 24
    )
    down.start()
    up.start()
    own_parts[0].wait()
    moves = fold_moves(wires, numbers, part_own, *first_fold[:3], here, first_fold[3])
    down.relay()
    up.relay()
    gate.start()
    fold_finish(wires, moves, first_fold[2], first_fold[3])
    back, gain_two = norm_back(
        wires, middle[...], scale_two[:, :1], gains[1:2, :], first_fold[3][...], *first_rows, here
    )
    grad = cotangent[...].astype(F32) + back
    middle_grad[...] = grad
    own[...] = grad.astype(BF)
    keep(own, middle_all.at[row_span(x), col_span(c)])
    sends = gather_sends(wires, own, middle_all, here)
    for s in (0, 1):
        for g in range(GROUP):
            query_rows[s, g] = queries[s, :, head_cols(g)].astype(F32).T.astype(BF)
    grads[:, :HD, :] = jnp.zeros((2, HD, GROUP * HALF), BF)
    terms[...] = jnp.zeros(terms.shape, F32)
    sums[...] = jnp.zeros(sums.shape, F32)
    down.middle()
    relayed = gather_relay(wires, sends, middle_all, here)
    kept[0].wait()

    own_parts[2].wait()
    shared = out_terms[...].reshape(GROUP * HD, D)

    def attended_rows(i, carry):
        rows = pl.ds(pl.multiple_of(i * ROWS, ROWS), ROWS)
        value = lax.dot_general(
            middle_all[rows, :], shared, (((1,), (1,)), ((), ())), preferred_element_type=F32
        )
        columns[: GROUP * HD, rows] = value.astype(BF).astype(F32).T
        return carry

    lax.fori_loop(0, 4, attended_rows, 0)
    for s in (0, 1):
        for g in range(GROUP):
            cols = head_cols(g)
            value = columns[g * HD : (g + 1) * HD, s * HALF : (s + 1) * HALF]
            grads[s, HD:, cols] = value.astype(BF)
            delta[s, :, cols] = jnp.sum(value * mixed[s, :, cols], axis=0, keepdims=True)
            grad_rows[s, g] = (
                jnp.concatenate([jnp.zeros_like(value), value], axis=0).T.astype(BF)
            )

    def out_columns(i, carry):
        cols = pl.ds(pl.multiple_of(i * HALF, HALF), HALF)
        value = jnp.dot(attended[...], middle_all[:, cols], preferred_element_type=F32)
        out_terms[:, :, :, cols] = value.astype(BF).reshape(4, 2, PIECE, HALF)
        return carry

    lax.fori_loop(0, D // HALF, out_columns, 0)
    out_sum.start()
    gate.relay()
    output_numbers = fold_sends(wires, output_part, output_fold[0], here)

    tour = Tour(z * 4 + y)
    heads = range(GROUP)

    def step(s, at, masked):
        slot = key_at(at)
        pairs = keys[slot]
        query_columns = [queries[s, :, head_cols(g)] for g in heads]
        grad_columns = [grads[s, :, head_cols(g)] for g in heads]
        log_rows = [logs[s, :, head_cols(g)] for g in heads]
        deltas = [delta[s, :, head_cols(g)] for g in heads]
        rows = [query_rows[s, g] for g in heads]
        outer = [grad_rows[s, g] for g in heads]
        if not masked:
            fits = in_second(tour.half(s), ends)
            log_rows = [jnp.where(fits, value, -NEVER) for value in log_rows]
        scores = [jnp.dot(pairs, value, preferred_element_type=F32) for value in query_columns]
        prob_grads = [jnp.dot(pairs, value, preferred_element_type=F32) for value in grad_columns]
        probs = [jnp.exp(scores[g] - log_rows[g]) for g in heads]
        if masked:
            allowed = allowed_pairs(at, tour.half(s), ends)
            probs = [jnp.where(allowed, value, 0.0) for value in probs]
        score_grads = [(probs[g] * (prob_grads[g] - deltas[g])).astype(BF) for g in heads]
        probs_low = [value.astype(BF) for value in probs]
        back = [
            lax.dot_general(pairs, value, (((0,), (0,)), ((), ())), preferred_element_type=F32)
            for value in score_grads
        ]
        added = [
            jnp.dot(score_grads[g], rows[g], preferred_element_type=F32)
            + jnp.dot(probs_low[g], outer[g], preferred_element_type=F32)
            for g in heads
        ]
        terms[slot] += (added[0] + added[1]) + (added[2] + added[3])
        for g in heads:
            sums[s, :, head_cols(g)] += back[g]

    tour.inner(step, 0, 8)
    own_parts[1].wait()
    output_moves = fold_moves(
        wires, output_numbers, output_own, *output_fold[:3], here, output_fold[3]
    )
    out_sum.middle()
    up.middle()
    tour.inner(step, 8, 20)
    fold_finish(wires, output_moves, output_fold[2], output_fold[3])
    output[...] = (middle[...] + output_fold[3][...]).astype(BF)
    output_at = post.send(output, output_home)
    normed_parts = [
        pltpu.make_async_copy(normed.at[:, pl.ds(n * WIDTH, WIDTH)], value, local_sem.at[40 + n])
        for n, value in enumerate((part_own, output_own))
    ]
    for copy in normed_parts:
        copy.start()
    out_sum.deal()
    down.finish()
    down_fin = down_buffers[5]
    down_swap = wires.send(
        down_fin.at[:, :, col_span(1 - c)], down_out.at[c], device(z, y, x, 1 - c)
    )
    keep(down_fin.at[:, :, col_span(c)], down_out.at[c])
    gate.middle()
    tour.inner(step, 20, tour.count)
    tour.edges(step)

    for s in (0, 1):
        for i in range(4):
            rounded[s, i] = terms[s, i].astype(BF)
    first = [[], []]
    for k, by in enumerate(OFFSETS):
        first[0].append(
            wires.send(
                rounded.at[0, :, lax.rem(y + by, 4)], key_rec.at[0, k], second_device(here, 0, by)
            )
        )
        first[1].append(
            wires.send(
                rounded.at[1, lax.rem(z + by, 4)], key_rec.at[1, k], second_device(here, 1, by)
            )
        )
    for s in (0, 1):
        tokens = slice(s * HALF, (s + 1) * HALF)
        for g in range(GROUP):
            turned = rope(
                sums.at[s, :, head_cols(g)], 0, cosine[:, tokens], -sine[:, tokens]
            )
            for i, value in enumerate(turned):
                at = g * HD + i * (HD // 2)
                columns[at : at + HD // 2, tokens] = value * HD ** (-0.5)
    up.finish()
    up_swap = deal(up_buffers[5], up_out)
    gate.finish()
    gate_swap = deal(gate_buffers[5], gate_out)
    second = [[], []]
    for s in (0, 1):
        for k in range(3):
            wires.landed(first[s][k], key_rec.at[s, k])
        for i in range(4):
            value = terms[0, i, y] if s == 0 else terms[1, z, i]
            for k in range(3):
                value = value + key_rec[s, k, i].astype(F32)
            key_sums[s, i] = value.astype(BF)
        for k, by in enumerate(OFFSETS):
            second[s].append(
                wires.send(
                    key_sums.at[s, first_at(here, s, by)],
                    key_rec_two.at[s, k],
                    first_device(here, s, by),
                )
            )
    for s in (0, 1):
        tokens = slice(s * HALF, (s + 1) * HALF)
        value = key_sums[s, first_at(here, s)].astype(F32)
        for k in range(3):
            wires.landed(second[s][k], key_rec_two.at[s, k])
            value = value + key_rec_two[s, k].astype(F32)
        pair_columns = value.T
        turned = rope(pair_columns, 0, cosine[:, tokens], -sine[:, tokens])
        for i, value in enumerate(turned):
            at = GROUP * HD + i * (HD // 2)
            columns[at : at + HD // 2, tokens] = value
        columns[(GROUP + 1) * HD :, tokens] = pair_columns[HD:]

    own_parts[3].wait()
    wires.settle(relayed)
    weight = qkv_terms[...].reshape(D, columns.shape[0])
    last_numbers = []
    for k, o in enumerate(FOLD_ORDER):
        rows = row_span(lax.rem(x + o, 4))
        back_rows = columns[:, rows].T.astype(BF)
        rows_back[rows, :] = back_rows
        middle_all[rows, :] = lax.dot_general(
            back_rows, weight, (((1,), (1,)), ((), ())), preferred_element_type=F32
        ).astype(BF)
        last_numbers.append(
            wires.send(
                middle_all.at[rows, col_span(1 - c)], last_fold[0].at[k], device(z, y, x, 1 - c)
            )
        )
    wires.settle(moves)
    back_all = rows_back[...]
    for n, half in enumerate((part_own, output_own)):
        normed_parts[n].wait()

        def outer_rows_of(i, carry):
            cols = pl.ds(pl.multiple_of(i * 256, 256), 256)
            value = lax.dot_general(
                half[:, cols], back_all, (((0,), (0,)), ((), ())), preferred_element_type=F32
            )
            qkv_terms[n, i] = value.astype(BF).reshape(qkv_terms.shape[2:])
            return carry

        lax.fori_loop(0, 4, outer_rows_of, 0)
    qkv.start()
    last_moves = fold_moves(
        wires, last_numbers, middle_all, *last_fold[:3], here, last_fold[3], col_span(c)
    )
    qkv.relay()
    qkv.middle()
    fold_finish(wires, last_moves, last_fold[2], last_fold[3])
    back, gain_one = norm_back(
        wires,
        inputs[...].astype(F32),
        scale_one[:, :1],
        gains[0:1, :],
        last_fold[3][...],
        *last_rows,
        here,
    )
    middle_grad[...] = middle_grad[...] + back
    input_at = post.send(middle_grad, input_home)
    qkv.finish()
    qkv_swap = deal(qkv_buffers[5], qkv_out)
    out_sum.finish()
    wires.landed(down_swap, down_out.at[1 - c])
    dealt(up_swap, up_out)
    dealt(gate_swap, gate_out)
    for copy in kept[1:]:
        copy.wait()
    squares = jnp.zeros((), F32)
    for result in (gate_out, up_out, down_out):
        for k in range(result.shape[0]):
            value = result[k].astype(F32)
            squares = squares + jnp.sum(value * value)
    value = out_out[...].astype(F32)
    squares = squares + jnp.sum(value * value)
    dealt(qkv_swap, qkv_out)
    for k in range(4):
        value = qkv_out[k].astype(F32)
        squares = squares + jnp.sum(value * value)

    for k in range(8):
        cols = slice(k * 128, (k + 1) * 128)
        total_terms[k : k + 1] = gain_one[:, cols]
        total_terms[8 + k : 9 + k] = gain_two[:, cols]
    total_terms[16:] = jnp.broadcast_to(squares, (8, 128))
    first = [
        wires.send(total_terms, rec_one.at[k], device(z + a, y + b, x, c))
        for k, (a, b) in enumerate(PLANE)
    ]
    value = total_terms[...]
    for k, at in enumerate(first):
        wires.landed(at, rec_one.at[k])
        value = value + rec_one[k]
    stage[...] = value
    second = [
        wires.send(stage, rec_two.at[k], device(z, y, lax.rem(x + o, 4), lax.rem(c + b, 2)))
        for k, (o, b) in enumerate(line)
    ]
    both = [value, None]
    for k, (o, b) in enumerate(line):
        wires.landed(second[k], rec_two.at[k])
        both[b] = rec_two[k] if both[b] is None else both[b] + rec_two[k]
    totals[:16] = both[0][:16]
    totals[16:] = (
        both[0][16:]
        + both[1][16:]
        + jnp.sum(both[0][:16] * both[0][:16])
        + jnp.sum(both[1][:16] * both[1][:16])
    )
    post.landed(output_at, output_home)
    post.landed(input_at, input_home)
    post.close()
    wires.close()


def call_backward(*operands):
    vm = pl.BlockSpec(memory_space=pltpu.VMEM)
    hbm = pl.BlockSpec(memory_space=ANY)
    cols = GROUP * HALF
    qkv_cols = (GROUP + 2) * HD
    share = (ROWS, WIDTH)
    outs = [
        (share, F32, hbm),
        (share, BF, hbm),
        ((4, PIECE, qkv_cols), BF, vm),
        ((4, PIECE, HIDDEN), BF, vm),
        ((4, PIECE, HIDDEN), BF, vm),
        ((2, 2, PIECE, WIDTH), BF, vm),
        ((PIECE, WIDTH), BF, vm),
        ((24, 128), F32, vm),
    ]
    return pl.pallas_call(
        backward_kernel,
        out_shape=tuple(jax.ShapeDtypeStruct(shape, kind) for shape, kind, _ in outs),
        in_specs=[pl.BlockSpec(memory_space=pltpu.SMEM)] + [vm] * 2 + [hbm] * 2 + [vm] * 11 + [hbm] * 6,
        out_specs=tuple(spec for _, _, spec in outs),
        scratch_shapes=[
            pltpu.VMEM(share, F32),
            pltpu.VMEM((LINE, D), BF),
            pltpu.VMEM((2, 2 * HD, cols), BF),
            pltpu.VMEM((2, 1, cols), F32),
            pltpu.VMEM((2, GROUP, HALF, 2 * HD), BF),
            pltpu.VMEM((2, GROUP, HALF, 2 * HD), BF),
            pltpu.VMEM((4, 2, PIECE, D), BF),
            pltpu.VMEM(share, BF),
            pltpu.VMEM((2, 4, 4, HALF, 2 * HD), F32),
            pltpu.VMEM((2, 2 * HD, cols), F32),
            pltpu.VMEM((2, 4, 4, HALF, 2 * HD), BF),
            pltpu.VMEM((qkv_cols, LINE), F32),
            pltpu.VMEM((LINE, qkv_cols), BF),
            pltpu.VMEM((2, 4, 4, 2, PIECE, qkv_cols), BF),
            pltpu.VMEM((2, 3, 4, HALF, 2 * HD), BF),
            pltpu.VMEM((2, 4, HALF, 2 * HD), BF),
            pltpu.VMEM((2, 3, HALF, 2 * HD), BF),
        ]
        + fold_scratch() * 2
        + [pltpu.VMEM((LINE, WIDTH), BF)] * 2
        + [pltpu.VMEM((ROWS, 128), F32)] * 4
        + [pltpu.VMEM(share, BF)]
        + sum_buffers((PIECE, D), BF)
        + sum_buffers((2, PIECE, HIDDEN), BF) * 2
        + sum_buffers((2, PIECE, qkv_cols), BF)
        + [
            pltpu.VMEM((3, 2, PIECE, D), BF),
            pltpu.VMEM((2, PIECE, D), BF),
            pltpu.VMEM((3, 2, PIECE, D), BF),
            pltpu.VMEM((24, 128), F32),
            pltpu.VMEM((24, 128), F32),
            pltpu.VMEM((15, 24, 128), F32),
            pltpu.VMEM((7, 24, 128), F32),
        ]
        + wire_scratch(160)
        + wire_scratch(2)
        + wire_scratch(6)
        + [pltpu.SemaphoreType.DMA((42,))],
        compiler_params=comm_params(2),
        name="backward",
    )(*operands)


def rope_tables(position, head_size):
    half_size = head_size // 2
    column = jnp.arange(half_size, dtype=jnp.float32)
    inverse = jnp.exp(-(2.0 * column / head_size) * math.log(ROPE_THETA))
    wavelength = 2.0 * math.pi / inverse
    smooth = (OLD_CONTEXT / wavelength - LOW_FREQ) / (HIGH_FREQ - LOW_FREQ)
    blended = (1.0 - smooth) * inverse / ROPE_FACTOR + smooth * inverse
    inverse = jnp.where(
        wavelength < OLD_CONTEXT / HIGH_FREQ,
        inverse,
        jnp.where(wavelength > OLD_CONTEXT / LOW_FREQ, inverse / ROPE_FACTOR, blended),
    )
    angles = position.astype(jnp.float32)[:, None] * inverse[None, :]
    return (jnp.cos(angles), jnp.sin(angles))


def times(left, right, kind):
    return jnp.dot(left, right, preferred_element_type=F32).astype(kind)


def times_transpose(left, right, kind):
    return lax.dot_general(
        left, right, (((1,), (1,)), ((), ())), preferred_element_type=F32
    ).astype(kind)


def outer_rows(left, right, kind):
    return lax.dot_general(
        left, right, (((0,), (0,)), ((), ())), preferred_element_type=F32
    ).astype(kind)


def adam(weight, moment, second, gradient, rate, decay):
    moment_next = BETA_ONE * moment + (1.0 - BETA_ONE) * gradient
    second_next = BETA_TWO * second + (1.0 - BETA_TWO) * gradient * gradient
    unbiased = moment_next / (1.0 - BETA_ONE**ADAM_STEP)
    divisor = jnp.sqrt(second_next / (1.0 - BETA_TWO**ADAM_STEP)) + ADAM_EPS
    return (weight - rate * (unbiased / divisor + decay * weight), moment_next, second_next)


def shards(
    block_input,
    out_grad,
    qkv_weight,
    qkv_moment,
    qkv_second,
    gate_up_weight,
    gate_up_moment,
    gate_up_second,
    out_weight,
    out_moment,
    out_second,
    down_weight,
    down_moment,
    down_second,
    norm_gains,
    gains_moment,
    gains_second,
    doc_lengths,
):
    z, y, xl, xh, c = place()
    x = xh * 2 + xl
    spot = z * 4 + y

    ends = jnp.cumsum(doc_lengths)
    local = jnp.arange(LINE, dtype=jnp.int32)
    half = jnp.where(local < HALF, 2 * spot, HALVES - 1 - 2 * spot)
    places = half * HALF + lax.rem(local, HALF)
    passed = (places[:, None] >= ends[None, :]).astype(jnp.int32)
    position = places - jnp.sum(passed * doc_lengths[None, :], axis=1)
    cosine, sine = rope_tables(position, HD)
    cosine, sine = cosine.T, sine.T

    def dealt(half_weight):
        return (
            half_weight.astype(BF)
            .reshape(PIECE, 16, 4, HD)
            .transpose(2, 0, 1, 3)
            .reshape(4, PIECE, HIDDEN)
        )

    (
        inputs,
        scale_one,
        normed,
        qkv_whole,
        query_columns,
        mixed,
        logs,
        attended,
        keys,
        cotangent,
        cotangent_all,
        out_whole,
        gate_whole,
        up_whole,
        down_whole,
        middle,
        scale_two,
        normed_two,
    ) = call_forward(
        ends,
        cosine,
        sine,
        block_input,
        out_grad,
        jnp.concatenate([norm_gains, jnp.zeros((6, WIDTH), F32)], axis=0),
        qkv_weight.astype(BF).transpose(1, 0, 2),
        dealt(gate_up_weight[:, 0]),
        dealt(gate_up_weight[:, 1]),
        down_weight.astype(BF).reshape(2, ROWS // 2, WIDTH),
        out_weight.astype(BF),
    )
    gate_low = gate_whole.reshape(D, HIDDEN)
    up_low = up_whole.reshape(D, HIDDEN)
    down_low = down_whole.reshape(HIDDEN, D)

    gate_part = times(normed_two, gate_low, F32)
    up_part = times(normed_two, up_low, F32)
    sigmoid_gate = jax.nn.sigmoid(gate_part)
    hidden = (gate_part * sigmoid_gate * up_part).astype(BF)
    hidden_grad = times_transpose(cotangent_all, down_low, F32)
    gate_back = hidden_grad * up_part * sigmoid_gate * (1.0 + gate_part * (1.0 - sigmoid_gate))
    up_back = hidden_grad * gate_part * sigmoid_gate
    gate_back, up_back = gate_back.astype(BF), up_back.astype(BF)
    grad_down = outer_rows(hidden, cotangent_all, BF)
    grad_up = outer_rows(normed_two, up_back, BF)
    grad_gate = outer_rows(normed_two, gate_back, BF)
    part = times_transpose(gate_back, gate_low, F32) + times_transpose(up_back, up_low, F32)
    input_grad, output, qkv_sum, gate_sum, up_sum, down_sum, out_sum, totals = call_backward(
        ends,
        cosine,
        sine,
        part.astype(BF),
        times(hidden, down_low, BF),
        middle,
        scale_two,
        scale_one,
        norm_gains,
        inputs,
        cotangent,
        query_columns,
        mixed,
        logs,
        attended,
        keys,
        out_whole,
        qkv_whole,
        normed,
        grad_down.reshape(down_whole.shape),
        grad_up.reshape(up_whole.shape),
        grad_gate.reshape(gate_whole.shape),
    )
    gate_both = jnp.stack([gate_sum, up_sum], axis=2).reshape(4, PIECE, 2, 16, HD)
    shares = (
        qkv_sum.transpose(1, 0, 2).astype(F32),
        gate_both.transpose(1, 2, 3, 0, 4).reshape(gate_up_weight.shape).astype(F32),
        out_sum.astype(F32),
        down_sum.reshape(down_weight.shape).astype(F32),
    )
    gains_grad = totals[:16].reshape(2, WIDTH)
    grad_norm = jnp.sqrt(totals[16, 0])
    factor = CLIP_NORM / jnp.maximum(grad_norm, CLIP_NORM)
    weights = (qkv_weight, gate_up_weight, out_weight, down_weight)
    moments = (qkv_moment, gate_up_moment, out_moment, down_moment)
    seconds = (qkv_second, gate_up_second, out_second, down_second)
    out_rate = OUTPUT_RATE * (TOKENS / (HQ * HD)) ** 0.5
    down_rate = DOWN_RATE * FF ** (-0.5)
    rates = (MATRIX_RATE, MATRIX_RATE, out_rate, down_rate)
    results = []
    for weight, moment, second, gradient, rate in zip(weights, moments, seconds, shares, rates):
        results.extend(adam(weight, moment, second, gradient * factor, rate, WEIGHT_DECAY))
    gains_new = adam(norm_gains, gains_moment, gains_second, gains_grad * factor, GAIN_RATE, 0.0)
    return (output, input_grad, grad_norm, *results, *gains_new)


def solution(mesh):
    placed = (
        P(("seq", "wide"), "narrow"),
        P(("seq", "wide"), "narrow"),
        P(("narrow", "seq"), "wide", None),
        P(("narrow", "seq"), "wide", None),
        P(("narrow", "seq"), "wide", None),
        P(("narrow", "seq"), None, "wide"),
        P(("narrow", "seq"), None, "wide"),
        P(("narrow", "seq"), None, "wide"),
        P(("wide", "seq"), "narrow"),
        P(("wide", "seq"), "narrow"),
        P(("wide", "seq"), "narrow"),
        P(("wide", "seq"), "narrow"),
        P(("wide", "seq"), "narrow"),
        P(("wide", "seq"), "narrow"),
        P(None, "narrow"),
        P(None, "narrow"),
        P(None, "narrow"),
        P(),
    )
    return jax.shard_map(
        shards,
        mesh=mesh,
        in_specs=placed,
        out_specs=(
            P(("seq", "wide"), "narrow"),
            P(("seq", "wide"), "narrow"),
            P(),
            P(("narrow", "seq"), "wide", None),
            P(("narrow", "seq"), "wide", None),
            P(("narrow", "seq"), "wide", None),
            P(("narrow", "seq"), None, "wide"),
            P(("narrow", "seq"), None, "wide"),
            P(("narrow", "seq"), None, "wide"),
            P(("wide", "seq"), "narrow"),
            P(("wide", "seq"), "narrow"),
            P(("wide", "seq"), "narrow"),
            P(("wide", "seq"), "narrow"),
            P(("wide", "seq"), "narrow"),
            P(("wide", "seq"), "narrow"),
            P(None, "narrow"),
            P(None, "narrow"),
            P(None, "narrow"),
        ),
        check_vma=False,
    )
```

```python
import functools
import math

import jax
import jax.numpy as jnp
import numpy as np
from jax import lax
from jax.experimental import pallas as pl
from jax.experimental.pallas import tpu as pltpu
from jax.sharding import PartitionSpec as P

D = 2048
HQ = 32
HD = 64
FF = 8192
ADAM_STEP = 10


NORM_EPS = 1e-05
ADAM_EPS = 1e-08
BETA_ONE = 0.9
BETA_TWO = 0.95
WEIGHT_DECAY = 0.1
MATRIX_RATE = 0.01
OUTPUT_RATE = 0.9
DOWN_RATE = 3.0
GAIN_RATE = 2.5
CLIP_NORM = 1.0
ROPE_THETA = 500000.0
ROPE_FACTOR = 32.0
LOW_FREQ = 1.0
HIGH_FREQ = 4.0
OLD_CONTEXT = 8192.0

TOKENS = 8192
HALF = 256
HALVES = TOKENS // HALF
ROWS = 128
LINE = 512
WIDTH = 1024
GROUP = 4
PIECE = 32
HIDDEN = 1024
MESH = pl.DeviceIdType.MESH
ANY = pl.ANY
BF = jnp.bfloat16
F32 = jnp.float32
VMEM_LIMIT = 60 * 1024 * 1024
NEVER = -1e30


def place():
    seq = lax.axis_index("seq")
    return (
        seq // 8,
        lax.rem(seq // 2, 4),
        lax.rem(seq, 2),
        lax.axis_index("wide"),
        lax.axis_index("narrow"),
    )


def device(z, y, x, c):
    return (lax.rem(z, 4) * 8 + lax.rem(y, 4) * 2 + lax.rem(x, 2), c, x // 2)


class Wires:
    def __init__(self, send_sem, recv_sem):
        self.send_sem, self.recv_sem, self.used, self.sent = send_sem, recv_sem, 0, []
        self.settled = set()

    def reserve(self):
        self.used += 1
        self.sent.append(None)
        return self.used - 1

    def send(self, src, dst, target, start=True, at=None):
        held = at is None
        if held:
            at = self.reserve()
        copy = pltpu.make_async_remote_copy(
            src_ref=src,
            dst_ref=dst,
            send_sem=self.send_sem.at[at],
            recv_sem=self.recv_sem.at[at],
            device_id=target,
            device_id_type=MESH,
        )
        if start:
            copy.start()
        if held:
            self.sent[at] = copy
        return at

    def left(self, at, region):
        pltpu.make_async_copy(region, region, self.send_sem.at[at]).wait()

    def landed(self, at, region):
        pltpu.make_async_copy(region, region, self.recv_sem.at[at]).wait()

    def settle(self, numbers):
        for at in numbers:
            self.sent[at].wait_send()
            self.settled.add(at)

    def close(self):
        held = [at for at in range(self.used) if self.sent[at] is not None]
        self.settle([at for at in held if at not in self.settled])


def greet(targets):
    barrier = pltpu.get_barrier_semaphore()
    for target in targets:
        pl.semaphore_signal(barrier, inc=1, device_id=target, device_id_type=MESH)
    pl.semaphore_wait(barrier, len(targets))


def line_targets(z, y, x, c):
    return [device(z, y, lax.rem(x + o, 4), c) for o in (1, 2, 3)] + [device(z, y, x, 1 - c)]


def plane_targets(z, y, x, c):
    return [device(z + o, y, x, c) for o in (1, 2, 3)] + [device(z, y + o, x, c) for o in (1, 2, 3)]


def wire_scratch(count):
    return [pltpu.SemaphoreType.DMA((count,)), pltpu.SemaphoreType.DMA((count,))]


def comm_params(number):
    return pltpu.CompilerParams(
        collective_id=number, has_side_effects=True, vmem_limit_bytes=VMEM_LIMIT
    )


def rows_of(x):
    return lax.rem(x, 2) * 2 + x // 2


def row_span(x):
    return pl.ds(pl.multiple_of(rows_of(x) * ROWS, ROWS), ROWS)


def col_span(c):
    return pl.ds(pl.multiple_of(c * WIDTH, WIDTH), WIDTH)


def half_span(x, half):
    return pl.ds(pl.multiple_of(rows_of(x) * ROWS + half * (ROWS // 2), ROWS // 2), ROWS // 2)


def chip(x, by):
    return lax.rem(x + by, 4)


def gather_sends(wires, own, out, here):
    z, y, x, c = here
    numbers = {}
    for first in (0, 1):
        for by, half in ((1, first), (3, 1 - first)):
            src = own.at[pl.ds(half * (ROWS // 2), ROWS // 2)]
            spot = out.at[half_span(x, half), col_span(c)]
            numbers[by, half] = wires.send(src, spot, device(z, y, chip(x, by), c))
    spot = out.at[row_span(x), col_span(c)]
    numbers["core"] = wires.send(own, spot, device(z, y, x, 1 - c))
    return numbers


def gather_hand(wires, numbers, out, here):
    z, y, x, c = here
    for by, half in ((1, 0), (3, 1)):
        spot = out.at[half_span(chip(x, 4 - by), half), col_span(c)]
        wires.landed(numbers[by, half], spot)
        numbers["far", half] = wires.send(spot, spot, device(z, y, chip(x, by), c))
    relays = []
    for by, half in ((1, 1), (3, 0)):
        from_x = chip(x, 4 - by)
        wires.landed(numbers[by, half], out.at[half_span(from_x, half), col_span(c)])
        spot = out.at[row_span(from_x), col_span(c)]
        relays.append((wires.send(spot, spot, device(z, y, x, 1 - c)), from_x))
    return relays


def gather_take(wires, numbers, relays, out, here):
    z, y, x, c = here
    far = chip(x, 2)
    for half in (0, 1):
        wires.landed(numbers["far", half], out.at[half_span(far, half), col_span(c)])
    spot = out.at[row_span(far), col_span(c)]
    relays = relays + [(wires.send(spot, spot, device(z, y, x, 1 - c)), far)]
    wires.landed(numbers["core"], out.at[row_span(x), col_span(1 - c)])
    for at, from_x in relays:
        wires.landed(at, out.at[row_span(from_x), col_span(1 - c)])
    return [at for at, _ in relays] + [numbers["far", 0], numbers["far", 1]]


def gather_relay(wires, numbers, out, here):
    relays = gather_hand(wires, numbers, out, here)
    return gather_take(wires, numbers, relays, out, here)


FOLD_ORDER = (2, 1, 3, 0)
EVERY = slice(None)


def fold_sends(wires, part, folded, here):
    z, y, x, c = here
    return [
        wires.send(
            part.at[row_span(lax.rem(x + o, 4)), col_span(1 - c)],
            folded.at[k],
            device(z, y, x, 1 - c),
        )
        for k, o in enumerate(FOLD_ORDER)
    ]


def fold_moves(wires, numbers, part, folded, leaving, arriving, here, total, cols=EVERY):
    z, y, x, c = here
    halves = [pl.ds(half * (ROWS // 2), ROWS // 2) for half in (0, 1)]
    near = [device(z, y, chip(x, by), c) for by in (1, 3)]
    far, direct, passed = [], [], []
    for k, o in enumerate(FOLD_ORDER):
        wires.landed(numbers[k], folded.at[k])
        both = part[row_span(chip(x, o)), cols].astype(F32) + folded[k].astype(F32)
        if o == 0:
            total[...] = both
            continue
        leaving[k] = both.astype(BF)
        if o == 2:
            for half in (0, 1):
                src = leaving.at[k, halves[half]]
                far.append(wires.send(src, arriving.at[2, halves[half]], near[half]))
        else:
            side = k - 1
            spot = halves[1 - side]
            direct.append(wires.send(leaving.at[k, spot], arriving.at[side, spot], near[side]))
    for side in (0, 1):
        spot = halves[side]
        wires.landed(far[side], arriving.at[2, spot])
        both = leaving[side + 1, spot].astype(F32) + arriving[2, spot].astype(F32)
        leaving[side + 1, spot] = both.astype(BF)
        passed.append(wires.send(leaving.at[side + 1, spot], arriving.at[side, spot], near[side]))
    return direct + passed + far


def fold_finish(wires, moves, arriving, total):
    for side in (0, 1):
        for at, half in ((moves[side], 1 - side), (moves[2 + side], side)):
            wires.landed(at, arriving.at[side, pl.ds(half * (ROWS // 2), ROWS // 2)])
    total[...] = total[...] + arriving[0].astype(F32) + arriving[1].astype(F32)


def fold_scratch():
    return [
        pltpu.VMEM((4, ROWS, WIDTH), BF),
        pltpu.VMEM((3, ROWS, WIDTH), BF),
        pltpu.VMEM((3, ROWS, WIDTH), BF),
        pltpu.VMEM((ROWS, WIDTH), F32),
    ]


def both_cores(wires, mine, theirs, value, here):
    z, y, x, c = here
    mine[...] = jnp.broadcast_to(value, mine.shape)
    at = wires.send(mine, theirs, device(z, y, x, 1 - c))
    wires.landed(at, theirs)
    return value + theirs[:, :1]


def first_device(here, order, by):
    z, y, x, c = here
    return device(z + by, y, x, c) if order == 0 else device(z, y + by, x, c)


def second_device(here, order, by):
    z, y, x, c = here
    return device(z, y + by, x, c) if order == 0 else device(z + by, y, x, c)


def first_at(here, order, by=0):
    return lax.rem((here[0] if order == 0 else here[1]) + by, 4)


def run_of(ref, here, order, by, sub=None):
    z, y, _, _ = here
    zi, yi = (EVERY, lax.rem(y + by, 4)) if order == 0 else (lax.rem(z + by, 4), EVERY)
    if len(ref.shape) > 4:
        return ref.at[order, zi, yi] if sub is None else ref.at[order, zi, yi, sub]
    rows = ref.shape[2] // 2
    if sub is None:
        return ref.at[zi, yi, pl.ds(order * rows, rows)]
    return ref.at[zi, yi, pl.ds(order * rows + sub * (rows // 2), rows // 2)]


def spot_of(ref, here, order, at, sub=None):
    z, y, _, _ = here
    zi, yi = (at, y) if order == 0 else (z, at)
    if len(ref.shape) > 4:
        return ref.at[order, zi, yi] if sub is None else ref.at[order, zi, yi, sub]
    rows = ref.shape[2] // 2
    if sub is None:
        return ref.at[zi, yi, pl.ds(order * rows, rows)]
    return ref.at[zi, yi, pl.ds(order * rows + sub * (rows // 2), rows // 2)]


class PlaneGather:
    def __init__(self, wires, whole, here):
        self.wires, self.whole, self.here, self.numbers = wires, whole, here, {}

    def send(self, key, spot, target):
        if key not in self.numbers:
            self.numbers[key] = self.wires.reserve()
        self.wires.send(spot, spot, target, at=self.numbers[key])

    def start(self, o):
        spot = spot_of(self.whole, self.here, o, first_at(self.here, o))
        for by in (1, 3):
            self.send(("first", o, by), spot, first_device(self.here, o, by))

    def relay(self, o):
        for sub, by in enumerate((1, 3)):
            at = first_at(self.here, o, 4 - by)
            self.wires.landed(self.numbers["first", o, by], spot_of(self.whole, self.here, o, at))
            spot = spot_of(self.whole, self.here, o, at, sub)
            self.send(("onward", o, by), spot, first_device(self.here, o, by))

    def turn(self, o):
        at = first_at(self.here, o, 2)
        for sub, by in enumerate((1, 3)):
            spot = spot_of(self.whole, self.here, o, at, sub)
            self.wires.landed(self.numbers["onward", o, by], spot)
        spot = run_of(self.whole, self.here, o, 0)
        for by in (1, 3):
            self.send(("second", o, by), spot, second_device(self.here, o, by))

    def relay_two(self, o):
        for sub, by in enumerate((1, 3)):
            spot = run_of(self.whole, self.here, o, 4 - by)
            self.wires.landed(self.numbers["second", o, by], spot)
            spot = run_of(self.whole, self.here, o, 4 - by, sub)
            self.send(("last", o, by), spot, second_device(self.here, o, by))

    def finish(self, o):
        for sub, by in enumerate((1, 3)):
            spot = run_of(self.whole, self.here, o, 2, sub)
            self.wires.landed(self.numbers["last", o, by], spot)

    def leave(self):
        for o in (0, 1):
            spot = spot_of(self.whole, self.here, o, first_at(self.here, o))
            half = spot_of(self.whole, self.here, o, first_at(self.here, o), 0)
            for by in (1, 3):
                self.wires.left(self.numbers["first", o, by], spot)
                self.wires.left(self.numbers["onward", o, by], half)
                self.wires.left(self.numbers["second", o, by], run_of(self.whole, self.here, o, 0))
                self.wires.left(self.numbers["last", o, by], run_of(self.whole, self.here, o, 0, 0))


def in_turn(c, members, first):
    def run(*steps):
        for core in (0, 1):

            @pl.when(c == core)
            def _():
                for step in steps:
                    for member in members:
                        getattr(member, step)(core if first else 1 - core)

    return run


OFFSETS = (2, 1, 3)


class DirectGather:
    def __init__(self, wires, whole, here):
        self.wires, self.whole, self.here = wires, whole, here

    def start(self):
        self.numbers = []
        for o in (0, 1):
            spot = spot_of(self.whole, self.here, o, first_at(self.here, o))
            self.numbers.append(
                [self.wires.send(spot, spot, first_device(self.here, o, by)) for by in OFFSETS]
            )

    def turn(self):
        lines = []
        for o in (0, 1):
            for at, by in zip(self.numbers[o], OFFSETS):
                back = first_at(self.here, o, 4 - by)
                self.wires.landed(at, spot_of(self.whole, self.here, o, back))
            spot = run_of(self.whole, self.here, o, 0)
            lines.append(
                [self.wires.send(spot, spot, second_device(self.here, o, by)) for by in OFFSETS]
            )
        self.numbers = lines

    def finish(self):
        for o in (0, 1):
            for at, by in zip(self.numbers[o], OFFSETS):
                self.wires.landed(at, run_of(self.whole, self.here, o, 4 - by))


class PlaneSum:
    def __init__(self, wires, terms, buffers, here, local_sem, at):
        self.wires, self.terms, self.here, self.numbers = wires, terms, here, {}
        self.far, self.joined, self.rec, self.total, self.rec_two, self.fin = buffers
        self.kept, self.added = [], []
        for o in (0, 1):
            self.kept.append(
                pltpu.make_async_copy(
                    run_of(terms, here, o, 0), self.total.at[o], local_sem.at[at + 3 * o]
                )
            )
            self.added.append(
                [
                    pltpu.make_async_copy(
                        run_of(terms, here, o, by, sub),
                        self.joined.at[o, sub],
                        local_sem.at[at + 3 * o + 1 + sub],
                    )
                    for sub, by in enumerate((1, 3))
                ]
            )

    def send(self, key, src, dst, target):
        if key not in self.numbers:
            self.numbers[key] = self.wires.reserve()
        self.wires.send(src, dst, target, at=self.numbers[key])

    def start(self, o):
        for sub, by in enumerate((1, 3)):
            self.send(
                ("far", o, sub),
                run_of(self.terms, self.here, o, 2, sub),
                self.far.at[o, sub],
                second_device(self.here, o, by),
            )
        for copy in self.added[o]:
            copy.start()
        self.kept[o].start()

    def direct(self, o):
        for sub, by in enumerate((1, 3)):
            self.send(
                ("direct", o, sub),
                run_of(self.terms, self.here, o, by, 1 - sub),
                half_of(self.rec.at[o, sub], 1 - sub),
                second_device(self.here, o, by),
            )

    def relay(self, o):
        for sub, by in enumerate((1, 3)):
            self.added[o][sub].wait()
            self.wires.landed(self.numbers["far", o, sub], self.far.at[o, sub])

            def add(i, carry):
                value = self.joined[o, sub, i].astype(F32) + self.far[o, sub, i].astype(F32)
                self.joined[o, sub, i] = value.astype(BF)
                return carry

            lax.fori_loop(0, 4, add, 0)
            self.send(
                ("passed", o, sub),
                self.joined.at[o, sub],
                half_of(self.rec.at[o, sub], sub),
                second_device(self.here, o, by),
            )

    def middle(self, o):
        self.kept[o].wait()
        for sub in (0, 1):
            rec = self.rec.at[o, sub]
            self.wires.landed(self.numbers["direct", o, sub], half_of(rec, 1 - sub))
            self.wires.landed(self.numbers["passed", o, sub], half_of(rec, sub))

        def add(i, carry):
            value = self.total[o, i].astype(F32)
            for sub in (0, 1):
                value = value + self.rec[o, sub, i].astype(F32)
            self.total[o, i] = value.astype(BF)
            return carry

        lax.fori_loop(0, 4, add, 0)
        for k, by in enumerate(OFFSETS):
            self.send(
                ("last", o, k),
                self.total.at[o, first_at(self.here, o, by)],
                self.rec_two.at[o, k],
                first_device(self.here, o, by),
            )

    def finish(self, o):
        value = self.total[o, first_at(self.here, o)].astype(F32)
        for k in range(3):
            self.wires.landed(self.numbers["last", o, k], self.rec_two.at[o, k])
            value = value + self.rec_two[o, k].astype(F32)
        self.fin[o] = value.astype(self.fin.dtype)

    def leave(self):
        for o in (0, 1):
            for sub in (0, 1):
                self.wires.left(self.numbers["far", o, sub], self.far.at[o, sub])
                self.wires.left(self.numbers["passed", o, sub], self.joined.at[o, sub])
                half = half_of(self.rec.at[o, sub], 1 - sub)
                self.wires.left(self.numbers["direct", o, sub], half)
            for k in range(3):
                self.wires.left(self.numbers["last", o, k], self.rec_two.at[o, k])


def run_bulk(members, steps):
    for step in steps:
        for o in (0, 1):
            for member in members:
                getattr(member, step)(o)


def half_of(line, sub):
    if len(line.shape) == 4:
        return line.at[:, sub]
    rows = line.shape[1] // 2
    return line.at[:, pl.ds(sub * rows, rows)]


def sum_buffers(piece, kind):
    half = piece[1:] if len(piece) == 3 else (piece[0] // 2,) + piece[1:]
    return [
        pltpu.VMEM((2, 2, 4) + half, BF),
        pltpu.VMEM((2, 2, 4) + half, BF),
        pltpu.VMEM((2, 2, 4) + piece, BF),
        pltpu.VMEM((2, 4) + piece, BF),
        pltpu.VMEM((2, 3) + piece, BF),
        pltpu.VMEM((2,) + piece, kind),
    ]


class OutGather:
    def __init__(self, wires, stage, whole, here, mine, send_sem, recv_sem, local_sem, at):
        z, y, x, c = here
        self.wires, self.stage, self.whole, self.here = wires, stage, whole, here
        self.off = lax.rem(z - mine + 4, 4)
        self.recv_sem = recv_sem
        spot = whole.at[y]
        self.kept = pltpu.make_async_copy(stage, spot, local_sem.at[at])

        def copy(k, src, dst, by):
            return pltpu.make_async_remote_copy(
                src_ref=src,
                dst_ref=dst,
                send_sem=send_sem.at[k],
                recv_sem=recv_sem.at[k],
                device_id=device(z + by, y, x, c),
                device_id_type=MESH,
            )

        self.first = [copy(0, stage, spot, 1), copy(1, stage, spot, 3)]
        self.onward = [
            copy(2, spot.at[0], spot.at[0], 1),
            copy(3, spot.at[1], spot.at[1], 3),
        ]

    def landed(self, k, region):
        pltpu.make_async_copy(region, region, self.recv_sem.at[k]).wait()

    def start(self):
        @pl.when(self.off == 0)
        def _():
            self.kept.start()
            for copy in self.first:
                copy.start()

    def relay(self):
        spot = self.whole.at[self.here[1]]
        for k, off in ((0, 1), (1, 3)):

            @pl.when(self.off == off)
            def _():
                self.landed(k, spot)
                self.onward[k].start()

    def turn(self):
        z, y, x, c = self.here
        spot = self.whole.at[y]

        @pl.when(self.off == 0)
        def _():
            self.kept.wait()

        @pl.when(self.off == 2)
        def _():
            self.landed(2, spot.at[0])
            self.landed(3, spot.at[1])

        self.numbers = [self.wires.send(spot, spot, device(z, y + by, x, c)) for by in (1, 3)]

    def relay_two(self):
        z, y, x, c = self.here
        relays = []
        for sub, by in enumerate((1, 3)):
            spot = self.whole.at[lax.rem(y + 4 - by, 4)]
            self.wires.landed(self.numbers[sub], spot)
            relays.append(
                self.wires.send(spot.at[sub], spot.at[sub], device(z, y + by, x, c))
            )
        self.numbers = relays

    def finish(self):
        spot = self.whole.at[lax.rem(self.here[1] + 2, 4)]
        for sub in (0, 1):
            self.wires.landed(self.numbers[sub], spot.at[sub])

        @pl.when(self.off == 0)
        def _():
            for copy in self.first:
                copy.wait_send()

        for k, off in ((0, 1), (1, 3)):

            @pl.when(self.off == off)
            def _():
                self.onward[k].wait_send()


class OutSum:
    def __init__(self, wires, terms, buffers, piece, here, mine, quad, sems, local_sem, at):
        self.wires, self.terms, self.here, self.mine, self.quad = wires, terms, here, mine, quad
        self.rec, self.total, self.rec_two = buffers
        self.piece, self.local_sem, self.at = piece, local_sem, at
        self.send_sem, self.recv_sem = sems
        self.off = lax.rem(here[0] - mine + 4, 4)
        self.kept = pltpu.make_async_copy(
            terms.at[here[1]], self.total, local_sem.at[at]
        )

    def start(self):
        z, y, x, c = self.here
        self.kept.start()
        self.numbers = [
            self.wires.send(
                self.terms.at[lax.rem(y + by, 4)], self.rec.at[k], device(z, y + by, x, c)
            )
            for k, by in enumerate(OFFSETS)
        ]

    def copy(self, k, src, dst, target):
        return pltpu.make_async_remote_copy(
            src_ref=src,
            dst_ref=dst,
            send_sem=self.send_sem.at[k],
            recv_sem=self.recv_sem.at[k],
            device_id=target,
            device_id_type=MESH,
        )

    def middle(self):
        z, y, x, c = self.here
        self.kept.wait()
        value = self.total[...].astype(F32)
        for k in range(3):
            self.wires.landed(self.numbers[k], self.rec.at[k])
            value = value + self.rec[k].astype(F32)
        self.total[...] = value.astype(BF)
        self.moves = []
        for off in (1, 2, 3):
            move = self.copy(
                off - 1, self.total, self.rec_two.at[off - 1], device(self.mine, y, x, c)
            )
            self.moves.append(move)

            @pl.when(self.off == off)
            def _():
                move.start()

    def deal(self):
        z, y, x, c = self.here
        self.deals = []
        xl = lax.rem(x, 2)
        for k, (a, b) in enumerate(self.quad):
            self.deals.append(
                self.copy(
                    3 + k, self.total.at[lax.rem(a, 2), :, col_span(b)], self.piece, device(z, y, a, b)
                )
            )

        @pl.when(self.off == 0)
        def _():
            value = self.total[...].astype(F32)
            for k in range(3):
                region = self.rec_two.at[k]
                pltpu.make_async_copy(region, region, self.recv_sem.at[k]).wait()
                value = value + self.rec_two[k].astype(F32)
            self.total[...] = value.astype(BF)
            for copy in self.deals:
                copy.start()
            own = pltpu.make_async_copy(
                self.total.at[xl, :, col_span(c)], self.piece, self.local_sem.at[self.at]
            )
            own.start()
            own.wait()

    def finish(self):
        z, y, x, c = self.here
        xl = lax.rem(x, 2)
        holder_xl, holder_c = z // 2, lax.rem(z, 2)
        for k, (dx, dc) in enumerate(((0, 1), (1, 0), (1, 1))):

            @pl.when(
                (holder_xl == lax.rem(xl + dx, 2)) & (holder_c == lax.rem(c + dc, 2))
            )
            def _():
                pltpu.make_async_copy(self.piece, self.piece, self.recv_sem.at[3 + k]).wait()

        for off in (1, 2, 3):

            @pl.when(self.off == off)
            def _():
                self.moves[off - 1].wait_send()

        @pl.when(self.off == 0)
        def _():
            for copy in self.deals:
                copy.wait_send()


def quad_of(xl, xh, x, c):
    pair = xh * 2 + 1 - xl
    return [(x, 1 - c), (pair, c), (pair, 1 - c)]


def norm_back(wires, values, scale, gain_row, incoming, mine, theirs, here):
    weighted = incoming * gain_row
    inner = both_cores(
        wires, mine, theirs, jnp.sum(weighted * values, axis=1, keepdims=True), here
    )
    inner = inner / D
    back = scale * (incoming * gain_row) - values * (scale * scale * scale * inner)
    return back, jnp.sum(incoming * values * scale, axis=0, keepdims=True)


PLANE = [(a, b) for a in range(4) for b in range(4) if a or b]


def key_at(half):
    at = half // 2
    return lax.rem(half, 2), at // 4, lax.rem(at, 4)


def ends_of(lengths):
    ends = [lengths[0]]
    for k in range(1, 4):
        ends.append(ends[-1] + lengths[k])
    return ends


def allowed_pairs(key_half, query_half, ends):
    keys = key_half * HALF + lax.broadcasted_iota(jnp.int32, (HALF, HALF), 0)
    queries = query_half * HALF + lax.broadcasted_iota(jnp.int32, (HALF, HALF), 1)
    same = keys <= queries
    for k in range(3):
        same = same & ((keys >= ends[k]) == (queries >= ends[k]))
    return same


def in_second(query_half, ends):
    queries = query_half * HALF + lax.broadcasted_iota(jnp.int32, (1, HALF), 1)
    return (queries >= ends[0]) & (queries < ends[1])


class Tour:
    def __init__(self, spot, order):
        self.spot, self.order = spot, order
        halves = [2 * spot, HALVES - 1 - 2 * spot]
        self.first, self.last = halves[order[0]], halves[order[1]]
        self.turn = self.first + 1

    def half(self, s):
        return jnp.where(s == 0, 2 * self.spot, HALVES - 1 - 2 * self.spot)

    def run(self, step, between, start, stop):
        def body(t, carry):
            late = t >= self.turn

            @pl.when(t == self.turn)
            def _():
                between()

            half = jnp.where(late, self.last, self.first)
            s = jnp.where(late, self.order[1], self.order[0])
            u = t - jnp.where(late, self.turn, 0)
            inner = jnp.maximum(half - 1, 0)

            @pl.when(u < inner)
            def _():
                step(s, 1 + u, False)

            @pl.when(u >= inner)
            def _():
                step(s, (u - inner) * half, True)

            return carry

        lax.fori_loop(start, stop, body, 0)


def head_cols(g):
    return slice(g * HALF, (g + 1) * HALF)


def rope(columns, at, cosine, sine):
    first = columns[at : at + HD // 2]
    second = columns[at + HD // 2 : at + HD]
    return first * cosine - second * sine, second * cosine + first * sine


def forward_kernel(
    lengths, inverse, block_input, qkv_weight, gate_up_weight, down_weight, out_weight, gains, out_grad,
    cosine, sine, scale_one, normed_out, qkv_out, queries, mixed_out, log_out, attended_out, keys_out,
    cotangent_all, out_out, gate_all, up_all, down_all, middle_out, scale_two, out,
    qkv_in, gate_in, up_in, down_in, out_in, gain_rows,
    inputs_all, gains_all, qkv_all, normed, columns, across_queries, attended_here, across,
    keys, tops, sums, mixed,
    attended, out_stage, out_all, part, folded, leaving, arriving, total, mine_row, their_row, own,
    send_sem, recv_sem, stage_send, stage_recv, out_send, out_recv, local_sem,
):
    z, y, xl, xh, c = place()
    x = xh * 2 + xl
    here = (z, y, x, c)
    mine = xl * 2 + c
    quad = quad_of(xl, xh, x, c)
    opposite = device(3 - z, 3 - y, x, c)
    greet(
        line_targets(z, y, x, c)
        + [device(z, y, *quad[2]), opposite]
        + plane_targets(z, y, x, c)
    )
    wires = Wires(send_sem, recv_sem)
    kept = {}

    def keep(name, src, dst):
        copy = pltpu.make_async_copy(src, dst, local_sem.at[len(kept)])
        copy.start()
        kept[name] = copy

    def swap(given, whole):
        numbers = [
            wires.send(
                given.at[lax.rem(to, 2) * 2 + core], whole.at[c, z, y, xl], device(z, y, to, core)
            )
            for to, core in quad
        ]
        return numbers

    def swapped(numbers, whole):
        for at, (from_x, from_c) in zip(numbers, quad):
            wires.landed(at, whole.at[from_c, z, y, lax.rem(from_x, 2)])

    keep("inputs", block_input, inputs_all.at[row_span(x), col_span(c)])
    input_numbers = gather_sends(wires, block_input, inputs_all, here)
    for k in range(4):
        qkv_in[k] = qkv_weight[:, k, :].astype(BF)
    qkv_swap = swap(qkv_in, qkv_all)
    qkv_all[c, z, y, xl] = qkv_in[mine]
    gain_rows[...] = jnp.zeros(gain_rows.shape, F32)
    gain_rows[0:2, :] = gains[...]
    gains_all[:, col_span(c)] = gain_rows[...]
    gain_at = wires.send(gain_rows, gains_all.at[:, col_span(c)], device(z, y, x, 1 - c))
    for k in (0, 1):
        down_in[k] = down_weight[k * 2 * PIECE : (k + 1) * 2 * PIECE, :].astype(BF)
    keep("down", down_in.at[c], down_all.at[z, y, :, col_span(c)])
    down_swap = wires.send(
        down_in.at[1 - c], down_all.at[z, y, :, col_span(c)], device(z, y, x, 1 - c)
    )
    out_in[...] = out_weight[...].astype(BF)
    holds = z == mine
    stage_spot = out_stage.at[xl, :, col_span(c)]
    stage_copy = pltpu.make_async_remote_copy(
        src_ref=out_in,
        dst_ref=stage_spot,
        send_sem=stage_send.at[0],
        recv_sem=stage_recv.at[mine],
        device_id=device(z, y, xh * 2 + z // 2, lax.rem(z, 2)),
        device_id_type=MESH,
    )

    @pl.when(jnp.logical_not(holds))
    def _():
        stage_copy.start()

    @pl.when(holds)
    def _():
        pltpu.make_async_copy(out_in, stage_spot, stage_recv.at[mine]).start()

    qkv = DirectGather(wires, qkv_all, here)
    pairs_gather = DirectGather(wires, keys, here)
    gate = PlaneGather(wires, gate_all, here)
    up = PlaneGather(wires, up_all, here)
    down = PlaneGather(wires, down_all, here)
    bulk = (gate, up, down)
    out_gather = OutGather(
        wires, out_stage, out_all, here, mine, out_send, out_recv, local_sem, 12
    )

    def down_ready():
        wires.landed(down_swap, down_all.at[z, y, :, col_span(1 - c)])
        kept["down"].wait()

    swapped(qkv_swap, qkv_all)
    qkv.start()
    down_ready()
    run_bulk((down,), ('start',))
    left = lax.broadcasted_iota(jnp.int32, (PIECE, 2 * HD), 1) < HD
    for u, dealt in enumerate((gate_in, up_in)):
        for side in (0, 1):
            for j in range(HIDDEN // (2 * HD)):
                cols = slice(j * 2 * HD, (j + 1) * 2 * HD)
                even, odd = (
                    gate_up_weight[:, u, ((2 * j + i) * 2 + side) * 2 * HD :][:, : 2 * HD]
                    for i in (0, 1)
                )
                dealt[side * 2, :, cols] = jnp.where(left, even, pltpu.roll(odd, HD, 1)).astype(BF)
                dealt[side * 2 + 1, :, cols] = jnp.where(
                    left, pltpu.roll(even, HD, 1), odd
                ).astype(BF)
    keep("gate", gate_in.at[mine], gate_all.at[c, z, y, xl])
    keep("up", up_in.at[mine], up_all.at[c, z, y, xl])
    gate_swap = swap(gate_in, gate_all)
    up_swap = swap(up_in, up_all)
    ends = ends_of(lengths)
    tokens = (z * 4 + y) * LINE + lax.broadcasted_iota(jnp.int32, (HD // 2, LINE), 1)
    position = tokens
    for k in range(4):
        position = position - jnp.where(tokens >= ends[k], lengths[k], 0)
    angles = position.astype(F32) * inverse[:, :1]
    cosine[...] = jnp.cos(angles)
    sine[...] = jnp.sin(angles)
    input_relays = gather_hand(wires, input_numbers, inputs_all, here)
    qkv.turn()
    run_bulk((down,), ('relay',))
    gather_take(wires, input_numbers, input_relays, inputs_all, here)
    kept["inputs"].wait()
    wires.landed(gain_at, gains_all.at[:, col_span(1 - c)])
    gain_one = gains_all[0:1, :]

    def norm_rows(i, carry):
        rows = pl.ds(pl.multiple_of(i * ROWS, ROWS), ROWS)
        values = inputs_all[rows, :].astype(F32)
        scale = lax.rsqrt(jnp.sum(values * values, axis=1, keepdims=True) / D + NORM_EPS)
        normed[rows, :] = (values * scale * gain_one).astype(BF)

        @pl.when(i == rows_of(x))
        def _():
            scale_one[...] = jnp.broadcast_to(scale, scale_one.shape)

        return carry

    lax.fori_loop(0, 4, norm_rows, 0)
    keep("normed", normed, normed_out)
    swapped(gate_swap, gate_all)
    swapped(up_swap, up_all)
    for name in ("gate", "up"):
        kept[name].wait()
    run_bulk((gate, up), ('start',))
    qkv.finish()
    keep("qkv_out", qkv_all, qkv_out)
    weight = qkv_all[...].reshape(D, columns.shape[0])

    def project(cols):
        def body(i, carry):
            rows = pl.ds(pl.multiple_of(i * ROWS, ROWS), ROWS)
            product = jnp.dot(normed[rows, :], weight[:, cols], preferred_element_type=F32)
            columns[cols, rows] = product.T
            return carry

        lax.fori_loop(0, 4, body, 0)

    project(slice(GROUP * HD, (GROUP + 2) * HD))
    first, second = rope(columns, GROUP * HD, cosine[...], sine[...])
    pair_columns = jnp.concatenate([first, second, columns[(GROUP + 1) * HD :]], axis=0)
    for s in (0, 1):
        keys[s, z, y] = pair_columns[:, s * HALF : (s + 1) * HALF].T.astype(BF)

    pairs_gather.start()
    project(slice(0, GROUP * HD))
    queries[:, HD:, :] = jnp.zeros((2, HD, GROUP * HALF), BF)
    for g in range(GROUP):
        turned = rope(columns, g * HD, cosine[...], sine[...])
        for i, value in enumerate(turned):
            rows = slice(i * (HD // 2), (i + 1) * (HD // 2))
            value = (value * HD ** (-0.5)).astype(BF)
            queries[0, rows, head_cols(g)] = value[:, :HALF]
            across_queries[rows, head_cols(g)] = value[:, HALF:]
    query_at = wires.send(across_queries, queries.at[1, pl.ds(0, HD)], opposite)
    pairs_gather.turn()
    run_bulk((gate, up), ('relay',))

    @pl.when(holds)
    def _():
        for k in range(4):
            spot = out_stage.at[k // 2, :, pl.ds((k % 2) * WIDTH, WIDTH)]
            pltpu.make_async_copy(spot, spot, stage_recv.at[k]).wait()

    out_gather.start()
    keep("cotangent", out_grad, cotangent_all.at[row_span(x), col_span(c)])
    cotangent_numbers = gather_sends(wires, out_grad, cotangent_all, here)
    pairs_gather.finish()
    keep("keys", keys, keys_out)
    out_gather.relay()
    run_bulk((gate,), ('turn',))

    wires.landed(query_at, queries.at[1, pl.ds(0, HD)])
    tour = Tour(z * 4 + y, (1, 0))
    tops[...] = jnp.full(tops.shape, NEVER, F32)
    sums[...] = jnp.zeros(sums.shape, F32)
    mixed[...] = jnp.zeros(mixed.shape, F32)
    heads = range(GROUP)

    def step(s, at, masked):
        pairs = keys[key_at(at)]
        old = [tops[s, :, head_cols(g)] for g in heads]
        old_sums = [sums[s, :, head_cols(g)] for g in heads]
        scores = [
            jnp.dot(pairs, queries[s, :, head_cols(g)], preferred_element_type=F32) for g in heads
        ]
        if masked:
            counts = in_second(tour.half(s), ends) | (at > 0)
            old = [jnp.where(counts, value, NEVER) for value in old]
            old_sums = [jnp.where(counts, value, 0.0) for value in old_sums]
            allowed = allowed_pairs(at, tour.half(s), ends)
            scores = [jnp.where(allowed, value, NEVER) for value in scores]
        top = [jnp.maximum(old[g], jnp.max(scores[g], axis=0, keepdims=True)) for g in heads]
        weights = [jnp.exp(scores[g] - top[g]) for g in heads]
        if masked:
            weights = [jnp.where(allowed, value, 0.0) for value in weights]
        shrink = [jnp.exp(old[g] - top[g]) for g in heads]
        if masked:
            shrink = [jnp.where(counts, value, 0.0) for value in shrink]
        new_sums = [
            old_sums[g] * shrink[g] + jnp.sum(weights[g], axis=0, keepdims=True) for g in heads
        ]
        new = [
            lax.dot_general(
                pairs, weights[g].astype(BF), (((0,), (0,)), ((), ())), preferred_element_type=F32
            )
            for g in heads
        ]
        for g in heads:
            cols = head_cols(g)
            tops[s, :, cols] = top[g]
            sums[s, :, cols] = new_sums[g]
            mixed[s, :, cols] = mixed[s, :, cols] * shrink[g] + new[g]

    def settle(s, rows):
        log_out[s] = tops[s] + jnp.log(sums[s])
        mixed_out[s] = mixed[s, HD:, :] / sums[s]
        for g in heads:
            rows[g * HD : (g + 1) * HD, :] = mixed_out[s, :, head_cols(g)].astype(BF)

    across_at = wires.send(attended_here, across, opposite, start=False)

    def between():
        settle(1, attended_here)
        wires.sent[across_at].start()

    tour.run(step, between, 0, 5)
    out_gather.turn()
    tour.run(step, between, 5, 9)
    gather_relay(wires, cotangent_numbers, cotangent_all, here)
    run_bulk((up,), ('turn',))
    tour.run(step, between, 9, 17)
    out_gather.relay_two()
    run_bulk((gate,), ('relay_two',))
    tour.run(step, between, 17, 21)
    tour.run(step, between, 21, 27)
    run_bulk((down,), ('turn',))
    tour.run(step, between, 27, 33)
    run_bulk((up,), ('relay_two',))
    settle(0, attended_out.at[:, pl.ds(0, HALF)])
    wires.landed(across_at, across)
    attended_out[:, HALF:] = across[...]
    for g in range(0, GROUP, 2):
        rows = slice(g * HD, (g + 2) * HD)
        attended[:, rows] = attended_out[rows, :].astype(F32).T.astype(BF)

    out_gather.finish()
    keep("out", out_all, out_out)
    out_low = out_all[...].reshape(GROUP * HD, D)
    fold_numbers = []
    for k, o in enumerate(FOLD_ORDER):
        rows = row_span(lax.rem(x + o, 4))
        part[rows, :] = jnp.dot(
            attended[rows, :], out_low, preferred_element_type=F32
        ).astype(BF)
        fold_numbers.append(
            wires.send(part.at[rows, col_span(1 - c)], folded.at[k], device(z, y, x, 1 - c))
        )
    moves = fold_moves(
        wires, fold_numbers, part, folded, leaving, arriving, here, total, col_span(c)
    )
    fold_finish(wires, moves, arriving, total)
    run_bulk((down,), ('relay_two',))
    middle = total[...] + block_input[...].astype(F32)
    middle_out[...] = middle
    square = both_cores(
        wires, mine_row, their_row, jnp.sum(middle * middle, axis=1, keepdims=True), here
    )
    scale = lax.rsqrt(square / D + NORM_EPS)
    scale_two[...] = jnp.broadcast_to(scale, scale_two.shape)
    own[...] = (
        middle_out[...] * scale * gains_all[1:2, col_span(c)]
    ).astype(BF)
    keep("own", own, out.at[row_span(x), col_span(c)])
    sends = gather_sends(wires, own, out, here)
    gather_relay(wires, sends, out, here)
    run_bulk(bulk, ('finish',))
    for member in bulk:
        member.leave()
    for name in ("normed", "qkv_out", "cotangent", "keys", "out", "own"):
        kept[name].wait()

    @pl.when(jnp.logical_not(holds))
    def _():
        stage_copy.wait_send()

    wires.close()


def call_forward(*operands):
    vm = pl.BlockSpec(memory_space=pltpu.VMEM)
    hbm = pl.BlockSpec(memory_space=ANY)
    cols = GROUP * HALF
    qkv_cols = (GROUP + 2) * HD
    share = (ROWS, WIDTH)
    whole = (2, 4, 4, 2, PIECE)
    outs = [
        ((HD // 2, LINE), F32, vm),
        ((HD // 2, LINE), F32, vm),
        ((ROWS, 128), F32, vm),
        ((LINE, D), BF, hbm),
        (whole + (qkv_cols,), BF, hbm),
        ((2, 2 * HD, cols), BF, vm),
        ((2, HD, cols), F32, vm),
        ((2, 1, cols), F32, vm),
        ((GROUP * HD, LINE), BF, vm),
        ((2, 4, 4, HALF, 2 * HD), BF, hbm),
        ((LINE, D), BF, hbm),
        ((4, 2, PIECE, D), BF, hbm),
        (whole + (HIDDEN,), BF, hbm),
        (whole + (HIDDEN,), BF, hbm),
        ((4, 4, 2 * PIECE, D), BF, hbm),
        (share, F32, vm),
        ((ROWS, 128), F32, vm),
        ((LINE, D), BF, hbm),
    ]
    return pl.pallas_call(
        forward_kernel,
        out_shape=tuple(jax.ShapeDtypeStruct(shape, kind) for shape, kind, _ in outs),
        in_specs=[pl.BlockSpec(memory_space=pltpu.SMEM)] + [vm] * 7 + [hbm],
        out_specs=tuple(spec for _, _, spec in outs),
        scratch_shapes=[
            pltpu.VMEM((4, PIECE, qkv_cols), BF),
            pltpu.VMEM((4, PIECE, HIDDEN), BF),
            pltpu.VMEM((4, PIECE, HIDDEN), BF),
            pltpu.VMEM((2, ROWS // 2, WIDTH), BF),
            pltpu.VMEM((PIECE, WIDTH), BF),
            pltpu.VMEM((8, WIDTH), F32),
            pltpu.VMEM((LINE, D), BF),
            pltpu.VMEM((8, D), F32),
            pltpu.VMEM(whole + (qkv_cols,), BF),
            pltpu.VMEM((LINE, D), BF),
            pltpu.VMEM((qkv_cols, LINE), F32),
            pltpu.VMEM((HD, cols), BF),
            pltpu.VMEM((GROUP * HD, HALF), BF),
            pltpu.VMEM((GROUP * HD, HALF), BF),
            pltpu.VMEM((2, 4, 4, HALF, 2 * HD), BF),
            pltpu.VMEM((2, 1, cols), F32),
            pltpu.VMEM((2, 1, cols), F32),
            pltpu.VMEM((2, 2 * HD, cols), F32),
            pltpu.VMEM((LINE, GROUP * HD), BF),
            pltpu.VMEM((2, PIECE, D), BF),
            pltpu.VMEM((4, 2, PIECE, D), BF),
            pltpu.VMEM((LINE, D), BF),
        ]
        + fold_scratch()
        + [
            pltpu.VMEM((ROWS, 128), F32),
            pltpu.VMEM((ROWS, 128), F32),
            pltpu.VMEM((ROWS, WIDTH), BF),
        ]
        + wire_scratch(144)
        + wire_scratch(4)
        + wire_scratch(4)
        + [pltpu.SemaphoreType.DMA((13,))],
        compiler_params=comm_params(1),
        name="forward",
    )(*operands)


def backward_kernel(
    lengths, cosine, sine, part, output_part, middle, scale_two, scale_one, gains, inputs, cotangent,
    queries, mixed, logs, attended, keys, out_low, qkv_low, normed, grad_down, grad_up, grad_gate,
    input_grad, output, qkv_grad, gate_up_grad, down_grad, out_grad, totals,
    q_out, kv_out, gate_out, up_out, down_out, out_out, across_grads, across_back, across,
    middle_all, grads, delta, query_rows, grad_rows, out_terms,
    terms, sums, rounded, columns, rows_back, q_terms, kv_terms, key_rec, key_sums, key_rec_two,
    *rest,
):
    rest = list(rest)

    def take(count):
        taken = rest[:count]
        del rest[:count]
        return taken

    first_fold, output_fold, (part_own, output_own) = take(4), take(4), take(2)
    last_fold = first_fold
    first_rows, last_rows, (own,) = take(2), take(2), take(1)
    down_buffers, up_buffers, gate_buffers = take(6), take(6), take(6)
    q_buffers, kv_buffers = take(6), take(6)
    out_buffers, (total_terms, stage, rec_one, rec_two) = take(3), take(4)
    send_sem, recv_sem, out_send, out_recv, local_sem = rest
    z, y, xl, xh, c = place()
    x = xh * 2 + xl
    here = (z, y, x, c)
    mine = xl * 2 + c
    quad = quad_of(xl, xh, x, c)
    line = [(o, b) for b in (0, 1) for o in range(4) if o or b]
    fixed = [device(z + a, y + b, x, c) for a, b in PLANE]
    fixed += [device(z, y, lax.rem(x + o, 4), lax.rem(c + b, 2)) for o, b in line]
    opposite = device(3 - z, 3 - y, x, c)
    greet(fixed)
    wires = Wires(send_sem, recv_sem)
    kept = []

    def keep(src, dst):
        copy = pltpu.make_async_copy(src, dst, local_sem.at[31 + len(kept)])
        copy.start()
        kept.append(copy)

    def deal(fin, result):
        keep(fin.at[c, xl], result.at[mine])
        return [
            wires.send(fin.at[b, lax.rem(a, 2)], result.at[mine], device(z, y, a, b))
            for a, b in quad
        ]

    def dealt(numbers, result):
        for at, (a, b) in zip(numbers, quad):
            wires.landed(at, result.at[lax.rem(a, 2) * 2 + b])

    numbers = fold_sends(wires, part, first_fold[0], here)
    own_parts = [
        pltpu.make_async_copy(part.at[:, col_span(c)], part_own, local_sem.at[42]),
        pltpu.make_async_copy(output_part.at[:, col_span(c)], output_own, local_sem.at[43]),
        pltpu.make_async_copy(out_low, out_terms, local_sem.at[44]),
        pltpu.make_async_copy(
            qkv_low.at[:, :, :, :, :, pl.ds(0, GROUP * HD)], q_terms, local_sem.at[45]
        ),
        pltpu.make_async_copy(
            qkv_low.at[:, :, :, :, :, pl.ds(GROUP * HD, 2 * HD)], kv_terms, local_sem.at[48]
        ),
    ]
    for copy in own_parts:
        copy.start()
    down = PlaneSum(wires, grad_down, down_buffers, here, local_sem, 0)
    up = PlaneSum(wires, grad_up, up_buffers, here, local_sem, 6)
    gate = PlaneSum(wires, grad_gate, gate_buffers, here, local_sem, 12)
    q_sum = PlaneSum(wires, q_terms, q_buffers, here, local_sem, 18)
    kv_sum = PlaneSum(wires, kv_terms, kv_buffers, here, local_sem, 24)
    out_sum = OutSum(
        wires, out_terms, out_buffers, out_out, here, mine, quad, (out_send, out_recv), local_sem, 30
    )
    bulk = (down, up, gate)
    in_turn(c, bulk, True)(*('start', 'direct'))
    own_parts[0].wait()
    moves = fold_moves(wires, numbers, part_own, *first_fold[:3], here, first_fold[3])
    in_turn(c, bulk, True)(*('relay',))
    fold_finish(wires, moves, first_fold[2], first_fold[3])
    back, gain_two = norm_back(
        wires, middle[...], scale_two[:, :1], gains[1:2, :], first_fold[3][...], *first_rows, here
    )
    grad = cotangent[...].astype(F32) + back
    input_grad[...] = grad
    own[...] = grad.astype(BF)
    keep(own, middle_all.at[row_span(x), col_span(c)])
    sends = gather_sends(wires, own, middle_all, here)
    for s in (0, 1):
        for g in range(GROUP):
            query_rows[s, g] = queries[s, :, head_cols(g)].astype(F32).T.astype(BF)
    grads[:, :HD, :] = jnp.zeros((2, HD, GROUP * HALF), BF)
    terms[...] = jnp.zeros(terms.shape, F32)
    sums[...] = jnp.zeros(sums.shape, F32)
    in_turn(c, bulk, True)(*('middle',))
    in_turn(c, bulk, False)(*('start', 'direct'))
    relayed = gather_relay(wires, sends, middle_all, here)
    kept[0].wait()

    own_parts[2].wait()
    shared = out_terms[...].reshape(GROUP * HD, D)

    def attended_rows(i, carry):
        rows = pl.ds(pl.multiple_of(i * ROWS, ROWS), ROWS)
        value = lax.dot_general(
            middle_all[rows, :], shared, (((1,), (1,)), ((), ())), preferred_element_type=F32
        )
        columns[: GROUP * HD, rows] = value.astype(BF).astype(F32).T
        return carry

    lax.fori_loop(0, 4, attended_rows, 0)
    for g in range(GROUP):
        rows = slice(g * HD, (g + 1) * HD)
        grads[0, HD:, head_cols(g)] = columns[rows, :HALF].astype(BF)
        across_grads[:, head_cols(g)] = columns[rows, HALF:].astype(BF)
    grad_at = wires.send(across_grads, grads.at[1, pl.ds(HD, HD)], opposite)

    def prepare(s):
        for g in range(GROUP):
            cols = head_cols(g)
            value = grads[s, :, cols].astype(F32)
            delta[s, :, cols] = jnp.sum(value[HD:] * mixed[s, :, cols], axis=0, keepdims=True)
            grad_rows[s, g] = value.T.astype(BF)

    prepare(0)

    def out_columns(i, carry):
        cols = pl.ds(pl.multiple_of(i * HALF, HALF), HALF)
        value = jnp.dot(attended[...], middle_all[:, cols], preferred_element_type=F32)
        out_terms[:, :, :, cols] = value.astype(BF).reshape(4, 2, PIECE, HALF)
        return carry

    lax.fori_loop(0, D // HALF, out_columns, 0)
    out_sum.start()
    in_turn(c, bulk, False)(*('relay',))
    output_numbers = fold_sends(wires, output_part, output_fold[0], here)

    ends = ends_of(lengths)
    tour = Tour(z * 4 + y, (0, 1))
    heads = range(GROUP)

    def step(s, at, masked):
        slot = key_at(at)
        pairs = keys[slot]
        query_columns = [queries[s, :, head_cols(g)] for g in heads]
        grad_columns = [grads[s, :, head_cols(g)] for g in heads]
        log_rows = [logs[s, :, head_cols(g)] for g in heads]
        deltas = [delta[s, :, head_cols(g)] for g in heads]
        rows = [query_rows[s, g] for g in heads]
        outer = [grad_rows[s, g] for g in heads]
        if not masked:
            fits = in_second(tour.half(s), ends)
            log_rows = [jnp.where(fits, value, -NEVER) for value in log_rows]
        scores = [jnp.dot(pairs, value, preferred_element_type=F32) for value in query_columns]
        prob_grads = [jnp.dot(pairs, value, preferred_element_type=F32) for value in grad_columns]
        probs = [jnp.exp(scores[g] - log_rows[g]) for g in heads]
        if masked:
            allowed = allowed_pairs(at, tour.half(s), ends)
            probs = [jnp.where(allowed, value, 0.0) for value in probs]
        score_grads = [(probs[g] * (prob_grads[g] - deltas[g])).astype(BF) for g in heads]
        probs_low = [value.astype(BF) for value in probs]
        back = [
            lax.dot_general(pairs, value, (((0,), (0,)), ((), ())), preferred_element_type=F32)
            for value in score_grads
        ]
        added = [
            jnp.dot(score_grads[g], rows[g], preferred_element_type=F32)
            + jnp.dot(probs_low[g], outer[g], preferred_element_type=F32)
            for g in heads
        ]
        terms[slot] += (added[0] + added[1]) + (added[2] + added[3])
        for g in heads:
            sums[s, :, head_cols(g)] += back[g]

    def between():
        wires.landed(grad_at, grads.at[1, pl.ds(HD, HD)])
        prepare(1)

    tour.run(step, between, 0, 4)
    tour.run(step, between, 4, 8)
    own_parts[1].wait()
    output_moves = fold_moves(
        wires, output_numbers, output_own, *output_fold[:3], here, output_fold[3]
    )
    out_sum.middle()
    tour.run(step, between, 8, 14)
    tour.run(step, between, 14, 20)
    fold_finish(wires, output_moves, output_fold[2], output_fold[3])
    output[...] = (middle[...] + output_fold[3][...]).astype(BF)
    normed_parts = [
        pltpu.make_async_copy(normed.at[:, pl.ds(n * WIDTH, WIDTH)], value, local_sem.at[46 + n])
        for n, value in enumerate((part_own, output_own))
    ]
    for copy in normed_parts:
        copy.start()
    out_sum.deal()
    in_turn(c, bulk, True)(*('finish',))
    in_turn(c, bulk, False)(*('middle',))
    tour.run(step, between, 20, 26)
    tour.run(step, between, 26, 33)

    for s in (0, 1):
        for i in range(4):
            rounded[s, i] = terms[s, i].astype(BF)
    first = [[], []]
    for k, by in enumerate(OFFSETS):
        first[0].append(
            wires.send(
                rounded.at[0, :, lax.rem(y + by, 4)], key_rec.at[0, k], second_device(here, 0, by)
            )
        )
        first[1].append(
            wires.send(
                rounded.at[1, lax.rem(z + by, 4)], key_rec.at[1, k], second_device(here, 1, by)
            )
        )
    across_back[...] = (sums[1, :HD, :] * HD ** (-0.5)).astype(BF)
    back_at = wires.send(across_back, across, opposite)
    in_turn(c, bulk, False)(*('finish',))
    down_fin = down_buffers[5]
    down_swap = wires.send(
        down_fin.at[:, :, col_span(1 - c)], down_out.at[c], device(z, y, x, 1 - c)
    )
    keep(down_fin.at[:, :, col_span(c)], down_out.at[c])
    up_swap = deal(up_buffers[5], up_out)
    gate_swap = deal(gate_buffers[5], gate_out)

    def turn_back(values, tokens, scale):
        for g in range(GROUP):
            turned = rope(values.at[:, head_cols(g)], 0, cosine[:, tokens], -sine[:, tokens])
            for i, value in enumerate(turned):
                at = g * HD + i * (HD // 2)
                columns[at : at + HD // 2, tokens] = value * scale

    turn_back(sums.at[0], slice(0, HALF), HD ** (-0.5))
    wires.landed(back_at, across)
    turn_back(across, slice(HALF, LINE), 1.0)

    def take_rows(cols):
        for r in range(4):
            rows = slice(r * ROWS, (r + 1) * ROWS)
            rows_back[rows, cols] = columns[cols, rows].T.astype(BF)

    def weight_terms(cols, result):
        back_part = rows_back[:, cols]
        for n, half in enumerate((part_own, output_own)):

            def body(i, carry):
                at = pl.ds(pl.multiple_of(i * 256, 256), 256)
                value = lax.dot_general(
                    half[:, at], back_part, (((0,), (0,)), ((), ())), preferred_element_type=F32
                )
                result[n, i] = value.astype(BF).reshape(result.shape[2:])
                return carry

            lax.fori_loop(0, 4, body, 0)

    q_cols, kv_cols = slice(0, GROUP * HD), slice(GROUP * HD, (GROUP + 2) * HD)
    take_rows(q_cols)
    own_parts[3].wait()
    wires.settle(relayed)
    weight = q_terms[...].reshape(D, GROUP * HD)
    for r in range(4):
        rows = slice(r * ROWS, (r + 1) * ROWS)
        middle_all[rows, :] = lax.dot_general(
            rows_back[rows, q_cols], weight, (((1,), (1,)), ((), ())), preferred_element_type=F32
        ).astype(BF)
    for copy in normed_parts:
        copy.wait()
    weight_terms(q_cols, q_terms)
    run_bulk((q_sum,), ('start', 'direct'))
    second = [[], []]
    for s in (0, 1):
        for k in range(3):
            wires.landed(first[s][k], key_rec.at[s, k])
        for i in range(4):
            value = terms[0, i, y] if s == 0 else terms[1, z, i]
            for k in range(3):
                value = value + key_rec[s, k, i].astype(F32)
            key_sums[s, i] = value.astype(BF)
        for k, by in enumerate(OFFSETS):
            second[s].append(
                wires.send(
                    key_sums.at[s, first_at(here, s, by)],
                    key_rec_two.at[s, k],
                    first_device(here, s, by),
                )
            )
    run_bulk((q_sum,), ('relay',))
    for s in (0, 1):
        tokens = slice(s * HALF, (s + 1) * HALF)
        value = key_sums[s, first_at(here, s)].astype(F32)
        for k in range(3):
            wires.landed(second[s][k], key_rec_two.at[s, k])
            value = value + key_rec_two[s, k].astype(F32)
        pair_columns = value.T
        turned = rope(pair_columns, 0, cosine[:, tokens], -sine[:, tokens])
        for i, value in enumerate(turned):
            at = GROUP * HD + i * (HD // 2)
            columns[at : at + HD // 2, tokens] = value
        columns[(GROUP + 1) * HD :, tokens] = pair_columns[HD:]

    take_rows(kv_cols)
    own_parts[4].wait()
    weight = kv_terms[...].reshape(D, 2 * HD)
    last_numbers = []
    for k, o in enumerate(FOLD_ORDER):
        rows = row_span(lax.rem(x + o, 4))
        value = lax.dot_general(
            rows_back[rows, kv_cols], weight, (((1,), (1,)), ((), ())), preferred_element_type=F32
        )
        middle_all[rows, :] = (middle_all[rows, :].astype(F32) + value).astype(BF)
        last_numbers.append(
            wires.send(
                middle_all.at[rows, col_span(1 - c)], last_fold[0].at[k], device(z, y, x, 1 - c)
            )
        )
    weight_terms(kv_cols, kv_terms)
    run_bulk((kv_sum,), ('start', 'direct'))
    wires.settle(moves)
    last_moves = fold_moves(
        wires, last_numbers, middle_all, *last_fold[:3], here, last_fold[3], col_span(c)
    )

    run_bulk((kv_sum,), ('relay',))
    run_bulk((q_sum,), ('middle',))
    out_sum.finish()
    wires.landed(down_swap, down_out.at[1 - c])
    dealt(up_swap, up_out)
    dealt(gate_swap, gate_out)
    for copy in kept[1:]:
        copy.wait()
    left = lax.broadcasted_iota(jnp.int32, (PIECE, 2 * HD), 1) < HD
    squares = jnp.zeros((PIECE, 2 * HD), F32)
    for u, result in enumerate((gate_out, up_out)):
        for side in (0, 1):
            for j in range(HIDDEN // (2 * HD)):
                cols = slice(j * 2 * HD, (j + 1) * 2 * HD)
                one = result[side * 2, :, cols].astype(F32)
                two = result[side * 2 + 1, :, cols].astype(F32)
                squares = squares + one * one + two * two
                even = jnp.where(left, one, pltpu.roll(two, HD, 1))
                odd = jnp.where(left, pltpu.roll(one, HD, 1), two)
                for i, value in enumerate((even, odd)):
                    at = ((2 * j + i) * 2 + side) * 2 * HD
                    gate_up_grad[:, u, at : at + 2 * HD] = value
    square = jnp.sum(squares)
    for k in range(2):
        for o in range(2):
            value = down_out[k, o].astype(F32)
            down_grad[(2 * k + o) * PIECE : (2 * k + o + 1) * PIECE, :] = value
            square = square + jnp.sum(value * value)
    value = out_out[...].astype(F32)
    out_grad[...] = value
    square = square + jnp.sum(value * value)
    run_bulk((kv_sum,), ('middle',))
    run_bulk((q_sum,), ('finish',))
    q_swap = deal(q_buffers[5], q_out)
    fold_finish(wires, last_moves, last_fold[2], last_fold[3])
    back, gain_one = norm_back(
        wires,
        inputs[...].astype(F32),
        scale_one[:, :1],
        gains[0:1, :],
        last_fold[3][...],
        *last_rows,
        here,
    )
    input_grad[...] = input_grad[...] + back
    run_bulk((kv_sum,), ('finish',))
    kv_swap = deal(kv_buffers[5], kv_out)
    dealt(q_swap, q_out)
    dealt(kv_swap, kv_out)
    for copy in kept[-2:]:
        copy.wait()
    for k in range(4):
        for result, at in ((q_out, 0), (kv_out, GROUP * HD)):
            value = result[k].astype(F32)
            qkv_grad[:, k, at : at + value.shape[1]] = value
            square = square + jnp.sum(value * value)

    for k in range(8):
        cols = slice(k * 128, (k + 1) * 128)
        total_terms[k : k + 1] = gain_one[:, cols]
        total_terms[8 + k : 9 + k] = gain_two[:, cols]
    total_terms[16:] = jnp.broadcast_to(square, (8, 128))
    first = [
        wires.send(total_terms, rec_one.at[k], device(z + a, y + b, x, c))
        for k, (a, b) in enumerate(PLANE)
    ]
    value = total_terms[...]
    for k, at in enumerate(first):
        wires.landed(at, rec_one.at[k])
        value = value + rec_one[k]
    stage[...] = value
    second = [
        wires.send(stage, rec_two.at[k], device(z, y, lax.rem(x + o, 4), lax.rem(c + b, 2)))
        for k, (o, b) in enumerate(line)
    ]
    both = [value, None]
    for k, (o, b) in enumerate(line):
        wires.landed(second[k], rec_two.at[k])
        both[b] = rec_two[k] if both[b] is None else both[b] + rec_two[k]
    totals[:16] = both[0][:16]
    totals[16:] = (
        both[0][16:]
        + both[1][16:]
        + jnp.sum(both[0][:16] * both[0][:16])
        + jnp.sum(both[1][:16] * both[1][:16])
    )
    for member in bulk + (q_sum, kv_sum):
        member.leave()
    wires.close()


def call_backward(*operands):
    vm = pl.BlockSpec(memory_space=pltpu.VMEM)
    hbm = pl.BlockSpec(memory_space=ANY)
    cols = GROUP * HALF
    qkv_cols = (GROUP + 2) * HD
    share = (ROWS, WIDTH)
    outs = [
        (share, F32, vm),
        (share, BF, vm),
        ((PIECE, 4, qkv_cols), F32, vm),
        ((PIECE, 2, 4 * HIDDEN), F32, vm),
        (share, F32, vm),
        ((PIECE, WIDTH), F32, vm),
        ((24, 128), F32, vm),
    ]
    return pl.pallas_call(
        backward_kernel,
        out_shape=tuple(jax.ShapeDtypeStruct(shape, kind) for shape, kind, _ in outs),
        in_specs=[pl.BlockSpec(memory_space=pltpu.SMEM)] + [vm] * 2 + [hbm] * 2 + [vm] * 11 + [hbm] * 6,
        out_specs=tuple(spec for _, _, spec in outs),
        scratch_shapes=[
            pltpu.VMEM((4, PIECE, GROUP * HD), BF),
            pltpu.VMEM((4, PIECE, 2 * HD), BF),
            pltpu.VMEM((4, PIECE, HIDDEN), BF),
            pltpu.VMEM((4, PIECE, HIDDEN), BF),
            pltpu.VMEM((2, 2, PIECE, WIDTH), BF),
            pltpu.VMEM((PIECE, WIDTH), BF),
            pltpu.VMEM((HD, cols), BF),
            pltpu.VMEM((HD, cols), BF),
            pltpu.VMEM((HD, cols), BF),
            pltpu.VMEM((LINE, D), BF),
            pltpu.VMEM((2, 2 * HD, cols), BF),
            pltpu.VMEM((2, 1, cols), F32),
            pltpu.VMEM((2, GROUP, HALF, 2 * HD), BF),
            pltpu.VMEM((2, GROUP, HALF, 2 * HD), BF),
            pltpu.VMEM((4, 2, PIECE, D), BF),
            pltpu.VMEM((2, 4, 4, HALF, 2 * HD), F32),
            pltpu.VMEM((2, 2 * HD, cols), F32),
            pltpu.VMEM((2, 4, 4, HALF, 2 * HD), BF),
            pltpu.VMEM((qkv_cols, LINE), F32),
            pltpu.VMEM((LINE, qkv_cols), BF),
            pltpu.VMEM((2, 4, 4, 2, PIECE, GROUP * HD), BF),
            pltpu.VMEM((2, 4, 4, 2, PIECE, 2 * HD), BF),
            pltpu.VMEM((2, 3, 4, HALF, 2 * HD), BF),
            pltpu.VMEM((2, 4, HALF, 2 * HD), BF),
            pltpu.VMEM((2, 3, HALF, 2 * HD), BF),
        ]
        + fold_scratch() * 2
        + [pltpu.VMEM((LINE, WIDTH), BF)] * 2
        + [pltpu.VMEM((ROWS, 128), F32)] * 4
        + [pltpu.VMEM(share, BF)]
        + sum_buffers((PIECE, D), BF)
        + sum_buffers((2, PIECE, HIDDEN), BF) * 2
        + sum_buffers((2, PIECE, GROUP * HD), BF)
        + sum_buffers((2, PIECE, 2 * HD), BF)
        + [
            pltpu.VMEM((3, 2, PIECE, D), BF),
            pltpu.VMEM((2, PIECE, D), BF),
            pltpu.VMEM((3, 2, PIECE, D), BF),
            pltpu.VMEM((24, 128), F32),
            pltpu.VMEM((24, 128), F32),
            pltpu.VMEM((15, 24, 128), F32),
            pltpu.VMEM((7, 24, 128), F32),
        ]
        + wire_scratch(200)
        + wire_scratch(6)
        + [pltpu.SemaphoreType.DMA((49,))],
        compiler_params=comm_params(2),
        name="backward",
    )(*operands)


CHUNK = 256


def feed_kernel(
    normed_two, cotangent, gate_low, up_low, down_low,
    output_part, back_part, grad_gate, grad_up, grad_down, output_sum, back_sum,
):
    at = pl.program_id(0)

    @pl.when(at == 0)
    def _():
        output_sum[...] = jnp.zeros(output_sum.shape, F32)
        back_sum[...] = jnp.zeros(back_sum.shape, F32)

    inputs, incoming = normed_two[...], cotangent[...]
    gate = jnp.dot(inputs, gate_low[...], preferred_element_type=F32)
    up = jnp.dot(inputs, up_low[...], preferred_element_type=F32)
    hidden_grad = lax.dot_general(
        incoming, down_low[...], (((1,), (1,)), ((), ())), preferred_element_type=F32
    )
    sigmoid = jax.nn.sigmoid(gate)
    silu = gate * sigmoid
    hidden = (silu * up).astype(BF)
    gate_back = (hidden_grad * up * sigmoid * (1.0 + gate * (1.0 - sigmoid))).astype(BF)
    up_back = (hidden_grad * silu).astype(BF)
    both_back = jnp.concatenate([gate_back, up_back], axis=1)
    for k in range(4):
        cols = slice(k * D // 4, (k + 1) * D // 4)
        output_sum[:, cols] += jnp.dot(hidden, down_low[:, cols], preferred_element_type=F32)
        back_sum[:, cols] += lax.dot_general(
            gate_back, gate_low[cols, :], (((1,), (1,)), ((), ())), preferred_element_type=F32
        ) + lax.dot_general(
            up_back, up_low[cols, :], (((1,), (1,)), ((), ())), preferred_element_type=F32
        )
        grad_down[:, cols] = outer_rows(hidden, incoming[:, cols], BF)
        both = outer_rows(inputs[:, cols], both_back, BF)
        grad_gate[cols, :] = both[:, :CHUNK]
        grad_up[cols, :] = both[:, CHUNK:]

    @pl.when(at == HIDDEN // CHUNK - 1)
    def _():
        output_part[...] = output_sum[...].astype(BF)
        back_part[...] = back_sum[...].astype(BF)


def call_feed(normed_two, cotangent, gate_low, up_low, down_low):
    rows = pl.BlockSpec((LINE, D), lambda j: (0, 0))
    tall = pl.BlockSpec((D, CHUNK), lambda j: (0, j))
    wide = pl.BlockSpec((CHUNK, D), lambda j: (j, 0))
    return pl.pallas_call(
        feed_kernel,
        out_shape=(
            jax.ShapeDtypeStruct((LINE, D), BF),
            jax.ShapeDtypeStruct((LINE, D), BF),
            jax.ShapeDtypeStruct((D, HIDDEN), BF),
            jax.ShapeDtypeStruct((D, HIDDEN), BF),
            jax.ShapeDtypeStruct((HIDDEN, D), BF),
        ),
        grid=(HIDDEN // CHUNK,),
        in_specs=[rows, rows, tall, tall, wide],
        out_specs=(rows, rows, tall, tall, wide),
        scratch_shapes=[pltpu.VMEM((LINE, D), F32), pltpu.VMEM((LINE, D), F32)],
        compiler_params=pltpu.CompilerParams(vmem_limit_bytes=VMEM_LIMIT),
        name="feed_forward",
    )(normed_two, cotangent, gate_low, up_low, down_low)


def rope_inverse():
    half_size = HD // 2
    column = np.arange(half_size, dtype=np.float32)
    inverse = np.exp(-(np.float32(2.0) * column / HD) * np.float32(math.log(ROPE_THETA)))
    wavelength = np.float32(2.0 * math.pi) / inverse
    smooth = (np.float32(OLD_CONTEXT) / wavelength - LOW_FREQ) / (HIGH_FREQ - LOW_FREQ)
    blended = (1.0 - smooth) * inverse / ROPE_FACTOR + smooth * inverse
    inverse = np.where(
        wavelength < OLD_CONTEXT / HIGH_FREQ,
        inverse,
        np.where(wavelength > OLD_CONTEXT / LOW_FREQ, inverse / ROPE_FACTOR, blended),
    )
    return np.broadcast_to(inverse.astype(np.float32)[:, None], (half_size, 128))


def outer_rows(left, right, kind):
    return lax.dot_general(
        left, right, (((0,), (0,)), ((), ())), preferred_element_type=F32
    ).astype(kind)


def adam(weight, moment, second, gradient, rate, decay):
    moment_next = BETA_ONE * moment + (1.0 - BETA_ONE) * gradient
    second_next = BETA_TWO * second + (1.0 - BETA_TWO) * gradient * gradient
    unbiased = moment_next / (1.0 - BETA_ONE**ADAM_STEP)
    divisor = jnp.sqrt(second_next / (1.0 - BETA_TWO**ADAM_STEP)) + ADAM_EPS
    return (weight - rate * (unbiased / divisor + decay * weight), moment_next, second_next)


def shards(
    block_input,
    out_grad,
    qkv_weight,
    qkv_moment,
    qkv_second,
    gate_up_weight,
    gate_up_moment,
    gate_up_second,
    out_weight,
    out_moment,
    out_second,
    down_weight,
    down_moment,
    down_second,
    norm_gains,
    gains_moment,
    gains_second,
    doc_lengths,
):
    (
        cosine,
        sine,
        scale_one,
        normed,
        qkv_whole,
        query_columns,
        mixed,
        logs,
        attended,
        keys,
        cotangent_all,
        out_whole,
        gate_whole,
        up_whole,
        down_whole,
        middle,
        scale_two,
        normed_two,
    ) = call_forward(
        doc_lengths,
        jnp.asarray(rope_inverse()),
        block_input,
        qkv_weight,
        gate_up_weight,
        down_weight,
        out_weight,
        norm_gains,
        out_grad,
    )
    output_part, back_part, grad_gate, grad_up, grad_down = call_feed(
        normed_two,
        cotangent_all,
        gate_whole.reshape(D, HIDDEN),
        up_whole.reshape(D, HIDDEN),
        down_whole.reshape(HIDDEN, D),
    )
    input_grad, output, grad_qkv, grad_gate_up, grad_down, grad_out, totals = call_backward(
        doc_lengths,
        cosine,
        sine,
        back_part,
        output_part,
        middle,
        scale_two,
        scale_one,
        norm_gains,
        block_input,
        out_grad,
        query_columns,
        mixed,
        logs,
        attended,
        keys,
        out_whole,
        qkv_whole,
        normed,
        grad_down.reshape(down_whole.shape),
        grad_up.reshape(up_whole.shape),
        grad_gate.reshape(gate_whole.shape),
    )
    shares = (grad_qkv, grad_gate_up, grad_out, grad_down)
    gains_grad = totals[:16].reshape(2, WIDTH)
    grad_norm = jnp.sqrt(totals[16, 0])
    factor = CLIP_NORM / jnp.maximum(grad_norm, CLIP_NORM)
    weights = (qkv_weight, gate_up_weight, out_weight, down_weight)
    moments = (qkv_moment, gate_up_moment, out_moment, down_moment)
    seconds = (qkv_second, gate_up_second, out_second, down_second)
    out_rate = OUTPUT_RATE * (TOKENS / (HQ * HD)) ** 0.5
    down_rate = DOWN_RATE * FF ** (-0.5)
    rates = (MATRIX_RATE, MATRIX_RATE, out_rate, down_rate)
    results = []
    for weight, moment, second, gradient, rate in zip(weights, moments, seconds, shares, rates):
        results.extend(adam(weight, moment, second, gradient * factor, rate, WEIGHT_DECAY))
    gains_new = adam(norm_gains, gains_moment, gains_second, gains_grad * factor, GAIN_RATE, 0.0)
    return (output, input_grad, grad_norm, *results, *gains_new)


def solution(mesh):
    placed = (
        P(("seq", "wide"), "narrow"),
        P(("seq", "wide"), "narrow"),
        P(("narrow", "seq"), "wide", None),
        P(("narrow", "seq"), "wide", None),
        P(("narrow", "seq"), "wide", None),
        P(("narrow", "seq"), None, "wide"),
        P(("narrow", "seq"), None, "wide"),
        P(("narrow", "seq"), None, "wide"),
        P(("wide", "seq"), "narrow"),
        P(("wide", "seq"), "narrow"),
        P(("wide", "seq"), "narrow"),
        P(("wide", "seq"), "narrow"),
        P(("wide", "seq"), "narrow"),
        P(("wide", "seq"), "narrow"),
        P(None, "narrow"),
        P(None, "narrow"),
        P(None, "narrow"),
        P(),
    )
    return jax.shard_map(
        shards,
        mesh=mesh,
        in_specs=placed,
        out_specs=(
            P(("seq", "wide"), "narrow"),
            P(("seq", "wide"), "narrow"),
            P(),
            P(("narrow", "seq"), "wide", None),
            P(("narrow", "seq"), "wide", None),
            P(("narrow", "seq"), "wide", None),
            P(("narrow", "seq"), None, "wide"),
            P(("narrow", "seq"), None, "wide"),
            P(("narrow", "seq"), None, "wide"),
            P(("wide", "seq"), "narrow"),
            P(("wide", "seq"), "narrow"),
            P(("wide", "seq"), "narrow"),
            P(("wide", "seq"), "narrow"),
            P(("wide", "seq"), "narrow"),
            P(("wide", "seq"), "narrow"),
            P(None, "narrow"),
            P(None, "narrow"),
            P(None, "narrow"),
        ),
        check_vma=False,
    )
```

```python
import functools
import math

import jax
import jax.numpy as jnp
import numpy as np
from jax import lax
from jax.experimental import pallas as pl
from jax.experimental.pallas import tpu as pltpu
from jax.sharding import PartitionSpec as P

D = 2048
HQ = 32
HD = 64
FF = 8192
ADAM_STEP = 10


NORM_EPS = 1e-05
ADAM_EPS = 1e-08
BETA_ONE = 0.9
BETA_TWO = 0.95
WEIGHT_DECAY = 0.1
MATRIX_RATE = 0.01
OUTPUT_RATE = 0.9
DOWN_RATE = 3.0
GAIN_RATE = 2.5
CLIP_NORM = 1.0
ROPE_THETA = 500000.0
ROPE_FACTOR = 32.0
LOW_FREQ = 1.0
HIGH_FREQ = 4.0
OLD_CONTEXT = 8192.0

TOKENS = 8192
HALF = 256
HALVES = TOKENS // HALF
ROWS = 128
LINE = 512
WIDTH = 1024
GROUP = 4
PIECE = 32
HIDDEN = 1024
MESH = pl.DeviceIdType.MESH
ANY = pl.ANY
BF = jnp.bfloat16
F32 = jnp.float32
VMEM_LIMIT = 60 * 1024 * 1024
NEVER = -1e30


def place():
    seq = lax.axis_index("seq")
    return (
        seq // 8,
        lax.rem(seq // 2, 4),
        lax.rem(seq, 2),
        lax.axis_index("wide"),
        lax.axis_index("narrow"),
    )


def device(z, y, x, c):
    return (lax.rem(z, 4) * 8 + lax.rem(y, 4) * 2 + lax.rem(x, 2), c, x // 2)


class Wires:
    def __init__(self, send_sem, recv_sem):
        self.send_sem, self.recv_sem, self.used, self.sent = send_sem, recv_sem, 0, []
        self.settled = set()

    def reserve(self):
        self.used += 1
        self.sent.append(None)
        return self.used - 1

    def send(self, src, dst, target, start=True, at=None):
        held = at is None
        if held:
            at = self.reserve()
        copy = pltpu.make_async_remote_copy(
            src_ref=src,
            dst_ref=dst,
            send_sem=self.send_sem.at[at],
            recv_sem=self.recv_sem.at[at],
            device_id=target,
            device_id_type=MESH,
        )
        if start:
            copy.start()
        if held:
            self.sent[at] = copy
        return at

    def left(self, at, region):
        pltpu.make_async_copy(region, region, self.send_sem.at[at]).wait()

    def landed(self, at, region):
        pltpu.make_async_copy(region, region, self.recv_sem.at[at]).wait()

    def settle(self, numbers):
        for at in numbers:
            self.sent[at].wait_send()
            self.settled.add(at)

    def close(self):
        held = [at for at in range(self.used) if self.sent[at] is not None]
        self.settle([at for at in held if at not in self.settled])


def greet(targets):
    barrier = pltpu.get_barrier_semaphore()
    for target in targets:
        pl.semaphore_signal(barrier, inc=1, device_id=target, device_id_type=MESH)
    pl.semaphore_wait(barrier, len(targets))


def line_targets(z, y, x, c):
    return [device(z, y, lax.rem(x + o, 4), c) for o in (1, 2, 3)] + [device(z, y, x, 1 - c)]


def plane_targets(z, y, x, c):
    return [device(z + o, y, x, c) for o in (1, 2, 3)] + [device(z, y + o, x, c) for o in (1, 2, 3)]


def wire_scratch(count):
    return [pltpu.SemaphoreType.DMA((count,)), pltpu.SemaphoreType.DMA((count,))]


def comm_params(number):
    return pltpu.CompilerParams(
        collective_id=number, has_side_effects=True, vmem_limit_bytes=VMEM_LIMIT
    )


def rows_of(x):
    return lax.rem(x, 2) * 2 + x // 2


def row_span(x):
    return pl.ds(pl.multiple_of(rows_of(x) * ROWS, ROWS), ROWS)


def col_span(c):
    return pl.ds(pl.multiple_of(c * WIDTH, WIDTH), WIDTH)


def half_span(x, half):
    return pl.ds(pl.multiple_of(rows_of(x) * ROWS + half * (ROWS // 2), ROWS // 2), ROWS // 2)


def chip(x, by):
    return lax.rem(x + by, 4)


def gather_sends(wires, own, out, here):
    z, y, x, c = here
    numbers = {}
    for first in (0, 1):
        for by, half in ((1, first), (3, 1 - first)):
            src = own.at[pl.ds(half * (ROWS // 2), ROWS // 2)]
            spot = out.at[half_span(x, half), col_span(c)]
            numbers[by, half] = wires.send(src, spot, device(z, y, chip(x, by), c))
    spot = out.at[row_span(x), col_span(c)]
    numbers["core"] = wires.send(own, spot, device(z, y, x, 1 - c))
    return numbers


def gather_hand(wires, numbers, out, here):
    z, y, x, c = here
    for by, half in ((1, 0), (3, 1)):
        spot = out.at[half_span(chip(x, 4 - by), half), col_span(c)]
        wires.landed(numbers[by, half], spot)
        numbers["far", half] = wires.send(spot, spot, device(z, y, chip(x, by), c))
    relays = []
    for by, half in ((1, 1), (3, 0)):
        from_x = chip(x, 4 - by)
        wires.landed(numbers[by, half], out.at[half_span(from_x, half), col_span(c)])
        spot = out.at[row_span(from_x), col_span(c)]
        relays.append((wires.send(spot, spot, device(z, y, x, 1 - c)), from_x))
    return relays


def gather_take(wires, numbers, relays, out, here):
    z, y, x, c = here
    far = chip(x, 2)
    for half in (0, 1):
        wires.landed(numbers["far", half], out.at[half_span(far, half), col_span(c)])
    spot = out.at[row_span(far), col_span(c)]
    relays = relays + [(wires.send(spot, spot, device(z, y, x, 1 - c)), far)]
    wires.landed(numbers["core"], out.at[row_span(x), col_span(1 - c)])
    for at, from_x in relays:
        wires.landed(at, out.at[row_span(from_x), col_span(1 - c)])
    return [at for at, _ in relays] + [numbers["far", 0], numbers["far", 1]]


def gather_relay(wires, numbers, out, here):
    relays = gather_hand(wires, numbers, out, here)
    return gather_take(wires, numbers, relays, out, here)


FOLD_ORDER = (2, 1, 3, 0)
EVERY = slice(None)


def fold_sends(wires, part, folded, here):
    z, y, x, c = here
    return [
        wires.send(
            part.at[row_span(lax.rem(x + o, 4)), col_span(1 - c)],
            folded.at[k],
            device(z, y, x, 1 - c),
        )
        for k, o in enumerate(FOLD_ORDER)
    ]


def fold_moves(wires, numbers, part, folded, leaving, arriving, here, total, cols=EVERY):
    z, y, x, c = here
    halves = [pl.ds(half * (ROWS // 2), ROWS // 2) for half in (0, 1)]
    near = [device(z, y, chip(x, by), c) for by in (1, 3)]
    far, direct, passed = [], [], []
    for k, o in enumerate(FOLD_ORDER):
        wires.landed(numbers[k], folded.at[k])
        both = part[row_span(chip(x, o)), cols].astype(F32) + folded[k].astype(F32)
        if o == 0:
            total[...] = both
            continue
        leaving[k] = both.astype(BF)
        if o == 2:
            for half in (0, 1):
                src = leaving.at[k, halves[half]]
                far.append(wires.send(src, arriving.at[2, halves[half]], near[half]))
        else:
            side = k - 1
            spot = halves[1 - side]
            direct.append(wires.send(leaving.at[k, spot], arriving.at[side, spot], near[side]))
    for side in (0, 1):
        spot = halves[side]
        wires.landed(far[side], arriving.at[2, spot])
        both = leaving[side + 1, spot].astype(F32) + arriving[2, spot].astype(F32)
        leaving[side + 1, spot] = both.astype(BF)
        passed.append(wires.send(leaving.at[side + 1, spot], arriving.at[side, spot], near[side]))
    return direct + passed + far


def fold_finish(wires, moves, arriving, total):
    for side in (0, 1):
        for at, half in ((moves[side], 1 - side), (moves[2 + side], side)):
            wires.landed(at, arriving.at[side, pl.ds(half * (ROWS // 2), ROWS // 2)])
    total[...] = total[...] + arriving[0].astype(F32) + arriving[1].astype(F32)


def fold_scratch():
    return [
        pltpu.VMEM((4, ROWS, WIDTH), BF),
        pltpu.VMEM((3, ROWS, WIDTH), BF),
        pltpu.VMEM((3, ROWS, WIDTH), BF),
        pltpu.VMEM((ROWS, WIDTH), F32),
    ]


def both_cores(wires, mine, theirs, value, here):
    z, y, x, c = here
    mine[...] = jnp.broadcast_to(value, mine.shape)
    at = wires.send(mine, theirs, device(z, y, x, 1 - c))
    wires.landed(at, theirs)
    return value + theirs[:, :1]


def first_device(here, order, by):
    z, y, x, c = here
    return device(z + by, y, x, c) if order == 0 else device(z, y + by, x, c)


def second_device(here, order, by):
    z, y, x, c = here
    return device(z, y + by, x, c) if order == 0 else device(z + by, y, x, c)


def first_at(here, order, by=0):
    return lax.rem((here[0] if order == 0 else here[1]) + by, 4)


def run_of(ref, here, order, by, sub=None):
    z, y, _, _ = here
    zi, yi = (EVERY, lax.rem(y + by, 4)) if order == 0 else (lax.rem(z + by, 4), EVERY)
    if len(ref.shape) > 4:
        return ref.at[order, zi, yi] if sub is None else ref.at[order, zi, yi, sub]
    rows = ref.shape[2] // 2
    if sub is None:
        return ref.at[zi, yi, pl.ds(order * rows, rows)]
    return ref.at[zi, yi, pl.ds(order * rows + sub * (rows // 2), rows // 2)]


def spot_of(ref, here, order, at, sub=None):
    z, y, _, _ = here
    zi, yi = (at, y) if order == 0 else (z, at)
    if len(ref.shape) > 4:
        return ref.at[order, zi, yi] if sub is None else ref.at[order, zi, yi, sub]
    rows = ref.shape[2] // 2
    if sub is None:
        return ref.at[zi, yi, pl.ds(order * rows, rows)]
    return ref.at[zi, yi, pl.ds(order * rows + sub * (rows // 2), rows // 2)]


class PlaneGather:
    def __init__(self, wires, whole, here):
        self.wires, self.whole, self.here, self.numbers = wires, whole, here, {}

    def send(self, key, spot, target):
        if key not in self.numbers:
            self.numbers[key] = self.wires.reserve()
        self.wires.send(spot, spot, target, at=self.numbers[key])

    def start(self, o):
        spot = spot_of(self.whole, self.here, o, first_at(self.here, o))
        for by in (1, 3):
            self.send(("first", o, by), spot, first_device(self.here, o, by))

    def relay(self, o):
        for sub, by in enumerate((1, 3)):
            at = first_at(self.here, o, 4 - by)
            self.wires.landed(self.numbers["first", o, by], spot_of(self.whole, self.here, o, at))
            spot = spot_of(self.whole, self.here, o, at, sub)
            self.send(("onward", o, by), spot, first_device(self.here, o, by))

    def turn(self, o):
        at = first_at(self.here, o, 2)
        for sub, by in enumerate((1, 3)):
            spot = spot_of(self.whole, self.here, o, at, sub)
            self.wires.landed(self.numbers["onward", o, by], spot)
        spot = run_of(self.whole, self.here, o, 0)
        for by in (1, 3):
            self.send(("second", o, by), spot, second_device(self.here, o, by))

    def relay_two(self, o):
        for sub, by in enumerate((1, 3)):
            spot = run_of(self.whole, self.here, o, 4 - by)
            self.wires.landed(self.numbers["second", o, by], spot)
            spot = run_of(self.whole, self.here, o, 4 - by, sub)
            self.send(("last", o, by), spot, second_device(self.here, o, by))

    def finish(self, o):
        for sub, by in enumerate((1, 3)):
            spot = run_of(self.whole, self.here, o, 2, sub)
            self.wires.landed(self.numbers["last", o, by], spot)

    def leave(self):
        for o in (0, 1):
            spot = spot_of(self.whole, self.here, o, first_at(self.here, o))
            half = spot_of(self.whole, self.here, o, first_at(self.here, o), 0)
            for by in (1, 3):
                self.wires.left(self.numbers["first", o, by], spot)
                self.wires.left(self.numbers["onward", o, by], half)
                self.wires.left(self.numbers["second", o, by], run_of(self.whole, self.here, o, 0))
                self.wires.left(self.numbers["last", o, by], run_of(self.whole, self.here, o, 0, 0))


def in_turn(c, members, first):
    def run(*steps):
        for core in (0, 1):

            @pl.when(c == core)
            def _():
                for step in steps:
                    for member in members:
                        getattr(member, step)(core if first else 1 - core)

    return run


OFFSETS = (2, 1, 3)


class DirectGather:
    def __init__(self, wires, whole, here):
        self.wires, self.whole, self.here = wires, whole, here

    def start(self):
        self.numbers = []
        for o in (0, 1):
            spot = spot_of(self.whole, self.here, o, first_at(self.here, o))
            self.numbers.append(
                [self.wires.send(spot, spot, first_device(self.here, o, by)) for by in OFFSETS]
            )

    def turn(self):
        lines = []
        for o in (0, 1):
            for at, by in zip(self.numbers[o], OFFSETS):
                back = first_at(self.here, o, 4 - by)
                self.wires.landed(at, spot_of(self.whole, self.here, o, back))
            spot = run_of(self.whole, self.here, o, 0)
            lines.append(
                [self.wires.send(spot, spot, second_device(self.here, o, by)) for by in OFFSETS]
            )
        self.numbers = lines

    def finish(self):
        for o in (0, 1):
            for at, by in zip(self.numbers[o], OFFSETS):
                self.wires.landed(at, run_of(self.whole, self.here, o, 4 - by))


class PlaneSum:
    def __init__(self, wires, terms, buffers, here, local_sem, at):
        self.wires, self.terms, self.here, self.numbers = wires, terms, here, {}
        self.far, self.joined, self.rec, self.total, self.rec_two, self.fin = buffers
        self.kept, self.added = [], []
        for o in (0, 1):
            self.kept.append(
                pltpu.make_async_copy(
                    run_of(terms, here, o, 0), self.total.at[o], local_sem.at[at + 3 * o]
                )
            )
            self.added.append(
                [
                    pltpu.make_async_copy(
                        run_of(terms, here, o, by, sub),
                        self.joined.at[o, sub],
                        local_sem.at[at + 3 * o + 1 + sub],
                    )
                    for sub, by in enumerate((1, 3))
                ]
            )

    def send(self, key, src, dst, target):
        if key not in self.numbers:
            self.numbers[key] = self.wires.reserve()
        self.wires.send(src, dst, target, at=self.numbers[key])

    def start(self, o):
        for sub, by in enumerate((1, 3)):
            self.send(
                ("far", o, sub),
                run_of(self.terms, self.here, o, 2, sub),
                self.far.at[o, sub],
                second_device(self.here, o, by),
            )
        for copy in self.added[o]:
            copy.start()
        self.kept[o].start()

    def direct(self, o):
        for sub, by in enumerate((1, 3)):
            self.send(
                ("direct", o, sub),
                run_of(self.terms, self.here, o, by, 1 - sub),
                half_of(self.rec.at[o, sub], 1 - sub),
                second_device(self.here, o, by),
            )

    def relay(self, o):
        for sub, by in enumerate((1, 3)):
            self.added[o][sub].wait()
            self.wires.landed(self.numbers["far", o, sub], self.far.at[o, sub])

            def add(i, carry):
                value = self.joined[o, sub, i].astype(F32) + self.far[o, sub, i].astype(F32)
                self.joined[o, sub, i] = value.astype(BF)
                return carry

            lax.fori_loop(0, 4, add, 0)
            self.send(
                ("passed", o, sub),
                self.joined.at[o, sub],
                half_of(self.rec.at[o, sub], sub),
                second_device(self.here, o, by),
            )

    def middle(self, o):
        self.kept[o].wait()
        for sub in (0, 1):
            rec = self.rec.at[o, sub]
            self.wires.landed(self.numbers["direct", o, sub], half_of(rec, 1 - sub))
            self.wires.landed(self.numbers["passed", o, sub], half_of(rec, sub))

        def add(i, carry):
            value = self.total[o, i].astype(F32)
            for sub in (0, 1):
                value = value + self.rec[o, sub, i].astype(F32)
            self.total[o, i] = value.astype(BF)
            return carry

        lax.fori_loop(0, 4, add, 0)
        for k, by in enumerate(OFFSETS):
            self.send(
                ("last", o, k),
                self.total.at[o, first_at(self.here, o, by)],
                self.rec_two.at[o, k],
                first_device(self.here, o, by),
            )

    def finish(self, o):
        value = self.total[o, first_at(self.here, o)].astype(F32)
        for k in range(3):
            self.wires.landed(self.numbers["last", o, k], self.rec_two.at[o, k])
            value = value + self.rec_two[o, k].astype(F32)
        self.fin[o] = value.astype(self.fin.dtype)

    def leave(self):
        for o in (0, 1):
            for sub in (0, 1):
                self.wires.left(self.numbers["far", o, sub], self.far.at[o, sub])
                self.wires.left(self.numbers["passed", o, sub], self.joined.at[o, sub])
                half = half_of(self.rec.at[o, sub], 1 - sub)
                self.wires.left(self.numbers["direct", o, sub], half)
            for k in range(3):
                self.wires.left(self.numbers["last", o, k], self.rec_two.at[o, k])


def run_bulk(members, steps):
    for step in steps:
        for o in (0, 1):
            for member in members:
                getattr(member, step)(o)


def half_of(line, sub):
    if len(line.shape) == 4:
        return line.at[:, sub]
    rows = line.shape[1] // 2
    return line.at[:, pl.ds(sub * rows, rows)]


def sum_buffers(piece, kind):
    half = piece[1:] if len(piece) == 3 else (piece[0] // 2,) + piece[1:]
    return [
        pltpu.VMEM((2, 2, 4) + half, BF),
        pltpu.VMEM((2, 2, 4) + half, BF),
        pltpu.VMEM((2, 2, 4) + piece, BF),
        pltpu.VMEM((2, 4) + piece, BF),
        pltpu.VMEM((2, 3) + piece, BF),
        pltpu.VMEM((2,) + piece, kind),
    ]


class OutGather:
    def __init__(self, wires, stage, whole, here, mine, send_sem, recv_sem, local_sem, at):
        z, y, x, c = here
        self.wires, self.stage, self.whole, self.here = wires, stage, whole, here
        self.off = lax.rem(z - mine + 4, 4)
        self.recv_sem = recv_sem
        spot = whole.at[y]
        self.kept = pltpu.make_async_copy(stage, spot, local_sem.at[at])

        def copy(k, src, dst, by):
            return pltpu.make_async_remote_copy(
                src_ref=src,
                dst_ref=dst,
                send_sem=send_sem.at[k],
                recv_sem=recv_sem.at[k],
                device_id=device(z + by, y, x, c),
                device_id_type=MESH,
            )

        self.first = [copy(0, stage, spot, 1), copy(1, stage, spot, 3)]
        self.onward = [
            copy(2, spot.at[0], spot.at[0], 1),
            copy(3, spot.at[1], spot.at[1], 3),
        ]

    def landed(self, k, region):
        pltpu.make_async_copy(region, region, self.recv_sem.at[k]).wait()

    def start(self):
        @pl.when(self.off == 0)
        def _():
            self.kept.start()
            for copy in self.first:
                copy.start()

    def relay(self):
        spot = self.whole.at[self.here[1]]
        for k, off in ((0, 1), (1, 3)):

            @pl.when(self.off == off)
            def _():
                self.landed(k, spot)
                self.onward[k].start()

    def turn(self):
        z, y, x, c = self.here
        spot = self.whole.at[y]

        @pl.when(self.off == 0)
        def _():
            self.kept.wait()

        @pl.when(self.off == 2)
        def _():
            self.landed(2, spot.at[0])
            self.landed(3, spot.at[1])

        self.numbers = [self.wires.send(spot, spot, device(z, y + by, x, c)) for by in (1, 3)]

    def relay_two(self):
        z, y, x, c = self.here
        relays = []
        for sub, by in enumerate((1, 3)):
            spot = self.whole.at[lax.rem(y + 4 - by, 4)]
            self.wires.landed(self.numbers[sub], spot)
            relays.append(
                self.wires.send(spot.at[sub], spot.at[sub], device(z, y + by, x, c))
            )
        self.numbers = relays

    def finish(self):
        spot = self.whole.at[lax.rem(self.here[1] + 2, 4)]
        for sub in (0, 1):
            self.wires.landed(self.numbers[sub], spot.at[sub])

        @pl.when(self.off == 0)
        def _():
            for copy in self.first:
                copy.wait_send()

        for k, off in ((0, 1), (1, 3)):

            @pl.when(self.off == off)
            def _():
                self.onward[k].wait_send()


class OutSum:
    def __init__(self, wires, terms, buffers, piece, here, mine, quad, sems, local_sem, at):
        self.wires, self.terms, self.here, self.mine, self.quad = wires, terms, here, mine, quad
        self.rec, self.total, self.rec_two = buffers
        self.piece, self.local_sem, self.at = piece, local_sem, at
        self.send_sem, self.recv_sem = sems
        self.off = lax.rem(here[0] - mine + 4, 4)
        self.kept = pltpu.make_async_copy(
            terms.at[here[1]], self.total, local_sem.at[at]
        )

    def start(self):
        z, y, x, c = self.here
        self.kept.start()
        self.numbers = [
            self.wires.send(
                self.terms.at[lax.rem(y + by, 4)], self.rec.at[k], device(z, y + by, x, c)
            )
            for k, by in enumerate(OFFSETS)
        ]

    def copy(self, k, src, dst, target):
        return pltpu.make_async_remote_copy(
            src_ref=src,
            dst_ref=dst,
            send_sem=self.send_sem.at[k],
            recv_sem=self.recv_sem.at[k],
            device_id=target,
            device_id_type=MESH,
        )

    def middle(self):
        z, y, x, c = self.here
        self.kept.wait()
        value = self.total[...].astype(F32)
        for k in range(3):
            self.wires.landed(self.numbers[k], self.rec.at[k])
            value = value + self.rec[k].astype(F32)
        self.total[...] = value.astype(BF)
        self.moves = []
        for off in (1, 2, 3):
            move = self.copy(
                off - 1, self.total, self.rec_two.at[off - 1], device(self.mine, y, x, c)
            )
            self.moves.append(move)

            @pl.when(self.off == off)
            def _():
                move.start()

    def deal(self):
        z, y, x, c = self.here
        self.deals = []
        xl = lax.rem(x, 2)
        for k, (a, b) in enumerate(self.quad):
            self.deals.append(
                self.copy(
                    3 + k, self.total.at[lax.rem(a, 2), :, col_span(b)], self.piece, device(z, y, a, b)
                )
            )

        @pl.when(self.off == 0)
        def _():
            value = self.total[...].astype(F32)
            for k in range(3):
                region = self.rec_two.at[k]
                pltpu.make_async_copy(region, region, self.recv_sem.at[k]).wait()
                value = value + self.rec_two[k].astype(F32)
            self.total[...] = value.astype(BF)
            for copy in self.deals:
                copy.start()
            own = pltpu.make_async_copy(
                self.total.at[xl, :, col_span(c)], self.piece, self.local_sem.at[self.at]
            )
            own.start()
            own.wait()

    def finish(self):
        z, y, x, c = self.here
        xl = lax.rem(x, 2)
        holder_xl, holder_c = z // 2, lax.rem(z, 2)
        for k, (dx, dc) in enumerate(((0, 1), (1, 0), (1, 1))):

            @pl.when(
                (holder_xl == lax.rem(xl + dx, 2)) & (holder_c == lax.rem(c + dc, 2))
            )
            def _():
                pltpu.make_async_copy(self.piece, self.piece, self.recv_sem.at[3 + k]).wait()

        for off in (1, 2, 3):

            @pl.when(self.off == off)
            def _():
                self.moves[off - 1].wait_send()

        @pl.when(self.off == 0)
        def _():
            for copy in self.deals:
                copy.wait_send()


def quad_of(xl, xh, x, c):
    pair = xh * 2 + 1 - xl
    return [(x, 1 - c), (pair, c), (pair, 1 - c)]


def norm_back(wires, values, scale, gain_row, incoming, mine, theirs, here):
    weighted = incoming * gain_row
    inner = both_cores(
        wires, mine, theirs, jnp.sum(weighted * values, axis=1, keepdims=True), here
    )
    inner = inner / D
    back = scale * (incoming * gain_row) - values * (scale * scale * scale * inner)
    return back, jnp.sum(incoming * values * scale, axis=0, keepdims=True)


PLANE = [(a, b) for a in range(4) for b in range(4) if a or b]


def key_at(half):
    at = half // 2
    return lax.rem(half, 2), at // 4, lax.rem(at, 4)


def ends_of(lengths):
    ends = [lengths[0]]
    for k in range(1, 4):
        ends.append(ends[-1] + lengths[k])
    return ends


def allowed_pairs(key_half, query_half, ends):
    keys = key_half * HALF + lax.broadcasted_iota(jnp.int32, (HALF, HALF), 0)
    queries = query_half * HALF + lax.broadcasted_iota(jnp.int32, (HALF, HALF), 1)
    same = keys <= queries
    for k in range(3):
        same = same & ((keys >= ends[k]) == (queries >= ends[k]))
    return same


def in_second(query_half, ends):
    queries = query_half * HALF + lax.broadcasted_iota(jnp.int32, (1, HALF), 1)
    return (queries >= ends[0]) & (queries < ends[1])


class Tour:
    def __init__(self, spot, order):
        self.spot, self.order = spot, order
        halves = [2 * spot, HALVES - 1 - 2 * spot]
        self.first, self.last = halves[order[0]], halves[order[1]]
        self.turn = self.first + 1

    def half(self, s):
        return jnp.where(s == 0, 2 * self.spot, HALVES - 1 - 2 * self.spot)

    def run(self, step, between, start, stop):
        def body(t, carry):
            late = t >= self.turn

            @pl.when(t == self.turn)
            def _():
                between()

            half = jnp.where(late, self.last, self.first)
            s = jnp.where(late, self.order[1], self.order[0])
            u = t - jnp.where(late, self.turn, 0)
            inner = jnp.maximum(half - 1, 0)

            @pl.when(u < inner)
            def _():
                step(s, 1 + u, False)

            @pl.when(u >= inner)
            def _():
                step(s, (u - inner) * half, True)

            return carry

        lax.fori_loop(start, stop, body, 0)


def head_cols(g):
    return slice(g * HALF, (g + 1) * HALF)


def rope(columns, at, cosine, sine):
    first = columns[at : at + HD // 2]
    second = columns[at + HD // 2 : at + HD]
    return first * cosine - second * sine, second * cosine + first * sine


def forward_kernel(
    lengths, inverse, block_input, qkv_weight, gate_up_weight, down_weight, out_weight, gains, out_grad,
    cosine, sine, scale_one, normed_out, qkv_out, queries, mixed_out, log_out, attended_out, keys_out,
    cotangent_all, out_out, gate_all, up_all, down_all, middle_out, scale_two, out,
    qkv_in, gate_in, up_in, down_in, out_in, gain_rows,
    inputs_all, gains_all, qkv_all, normed, columns, across_queries, attended_here, across,
    keys, tops, sums, mixed,
    attended, out_stage, out_all, part, folded, leaving, arriving, total, mine_row, their_row, own,
    send_sem, recv_sem, stage_send, stage_recv, out_send, out_recv, local_sem,
):
    z, y, xl, xh, c = place()
    x = xh * 2 + xl
    here = (z, y, x, c)
    mine = xl * 2 + c
    quad = quad_of(xl, xh, x, c)
    opposite = device(3 - z, 3 - y, x, c)
    greet(
        line_targets(z, y, x, c)
        + [device(z, y, *quad[2]), opposite]
        + plane_targets(z, y, x, c)
    )
    wires = Wires(send_sem, recv_sem)
    kept = {}

    def keep(name, src, dst):
        copy = pltpu.make_async_copy(src, dst, local_sem.at[len(kept)])
        copy.start()
        kept[name] = copy

    def swap(given, whole):
        numbers = [
            wires.send(
                given.at[lax.rem(to, 2) * 2 + core], whole.at[c, z, y, xl], device(z, y, to, core)
            )
            for to, core in quad
        ]
        return numbers

    def swapped(numbers, whole):
        for at, (from_x, from_c) in zip(numbers, quad):
            wires.landed(at, whole.at[from_c, z, y, lax.rem(from_x, 2)])

    keep("inputs", block_input, inputs_all.at[row_span(x), col_span(c)])
    input_numbers = gather_sends(wires, block_input, inputs_all, here)
    for k in range(4):
        qkv_in[k] = qkv_weight[:, k, :].astype(BF)
    qkv_swap = swap(qkv_in, qkv_all)
    qkv_all[c, z, y, xl] = qkv_in[mine]
    gain_rows[...] = jnp.zeros(gain_rows.shape, F32)
    gain_rows[0:2, :] = gains[...]
    gains_all[:, col_span(c)] = gain_rows[...]
    gain_at = wires.send(gain_rows, gains_all.at[:, col_span(c)], device(z, y, x, 1 - c))
    for k in (0, 1):
        down_in[k] = down_weight[k * 2 * PIECE : (k + 1) * 2 * PIECE, :].astype(BF)
    keep("down", down_in.at[c], down_all.at[z, y, :, col_span(c)])
    down_swap = wires.send(
        down_in.at[1 - c], down_all.at[z, y, :, col_span(c)], device(z, y, x, 1 - c)
    )
    out_in[...] = out_weight[...].astype(BF)
    holds = z == mine
    stage_spot = out_stage.at[xl, :, col_span(c)]
    stage_copy = pltpu.make_async_remote_copy(
        src_ref=out_in,
        dst_ref=stage_spot,
        send_sem=stage_send.at[0],
        recv_sem=stage_recv.at[mine],
        device_id=device(z, y, xh * 2 + z // 2, lax.rem(z, 2)),
        device_id_type=MESH,
    )

    @pl.when(jnp.logical_not(holds))
    def _():
        stage_copy.start()

    @pl.when(holds)
    def _():
        pltpu.make_async_copy(out_in, stage_spot, stage_recv.at[mine]).start()

    qkv = DirectGather(wires, qkv_all, here)
    pairs_gather = DirectGather(wires, keys, here)
    gate = PlaneGather(wires, gate_all, here)
    up = PlaneGather(wires, up_all, here)
    down = PlaneGather(wires, down_all, here)
    bulk = (gate, up, down)
    out_gather = OutGather(
        wires, out_stage, out_all, here, mine, out_send, out_recv, local_sem, 12
    )

    def down_ready():
        wires.landed(down_swap, down_all.at[z, y, :, col_span(1 - c)])
        kept["down"].wait()

    swapped(qkv_swap, qkv_all)
    qkv.start()
    down_ready()
    run_bulk((down,), ('start',))
    left = lax.broadcasted_iota(jnp.int32, (PIECE, 2 * HD), 1) < HD
    for u, dealt in enumerate((gate_in, up_in)):
        for side in (0, 1):
            for j in range(HIDDEN // (2 * HD)):
                cols = slice(j * 2 * HD, (j + 1) * 2 * HD)
                even, odd = (
                    gate_up_weight[:, u, ((2 * j + i) * 2 + side) * 2 * HD :][:, : 2 * HD]
                    for i in (0, 1)
                )
                dealt[side * 2, :, cols] = jnp.where(left, even, pltpu.roll(odd, HD, 1)).astype(BF)
                dealt[side * 2 + 1, :, cols] = jnp.where(
                    left, pltpu.roll(even, HD, 1), odd
                ).astype(BF)
    keep("gate", gate_in.at[mine], gate_all.at[c, z, y, xl])
    keep("up", up_in.at[mine], up_all.at[c, z, y, xl])
    gate_swap = swap(gate_in, gate_all)
    up_swap = swap(up_in, up_all)
    ends = ends_of(lengths)
    tokens = (z * 4 + y) * LINE + lax.broadcasted_iota(jnp.int32, (HD // 2, LINE), 1)
    position = tokens
    for k in range(4):
        position = position - jnp.where(tokens >= ends[k], lengths[k], 0)
    angles = position.astype(F32) * inverse[:, :1]
    cosine[...] = jnp.cos(angles)
    sine[...] = jnp.sin(angles)
    input_relays = gather_hand(wires, input_numbers, inputs_all, here)
    qkv.turn()
    run_bulk((down,), ('relay',))
    gather_take(wires, input_numbers, input_relays, inputs_all, here)
    kept["inputs"].wait()
    wires.landed(gain_at, gains_all.at[:, col_span(1 - c)])
    gain_one = gains_all[0:1, :]

    def norm_rows(i, carry):
        rows = pl.ds(pl.multiple_of(i * ROWS, ROWS), ROWS)
        values = inputs_all[rows, :].astype(F32)
        scale = lax.rsqrt(jnp.sum(values * values, axis=1, keepdims=True) / D + NORM_EPS)
        normed[rows, :] = (values * scale * gain_one).astype(BF)

        @pl.when(i == rows_of(x))
        def _():
            scale_one[...] = jnp.broadcast_to(scale, scale_one.shape)

        return carry

    lax.fori_loop(0, 4, norm_rows, 0)
    keep("normed", normed, normed_out)
    swapped(gate_swap, gate_all)
    swapped(up_swap, up_all)
    for name in ("gate", "up"):
        kept[name].wait()
    run_bulk((gate, up), ('start',))
    qkv.finish()
    keep("qkv_out", qkv_all, qkv_out)
    weight = qkv_all[...].reshape(D, columns.shape[0])

    def project(cols):
        def body(i, carry):
            rows = pl.ds(pl.multiple_of(i * ROWS, ROWS), ROWS)
            product = jnp.dot(normed[rows, :], weight[:, cols], preferred_element_type=F32)
            columns[cols, rows] = product.T
            return carry

        lax.fori_loop(0, 4, body, 0)

    project(slice(GROUP * HD, (GROUP + 2) * HD))
    first, second = rope(columns, GROUP * HD, cosine[...], sine[...])
    pair_columns = jnp.concatenate([first, second, columns[(GROUP + 1) * HD :]], axis=0)
    for s in (0, 1):
        keys[s, z, y] = pair_columns[:, s * HALF : (s + 1) * HALF].T.astype(BF)

    pairs_gather.start()
    project(slice(0, GROUP * HD))
    queries[:, HD:, :] = jnp.zeros((2, HD, GROUP * HALF), BF)
    for g in range(GROUP):
        turned = rope(columns, g * HD, cosine[...], sine[...])
        for i, value in enumerate(turned):
            rows = slice(i * (HD // 2), (i + 1) * (HD // 2))
            value = (value * HD ** (-0.5)).astype(BF)
            queries[0, rows, head_cols(g)] = value[:, :HALF]
            across_queries[rows, head_cols(g)] = value[:, HALF:]
    query_at = wires.send(across_queries, queries.at[1, pl.ds(0, HD)], opposite)
    pairs_gather.turn()
    run_bulk((gate, up), ('relay',))

    @pl.when(holds)
    def _():
        for k in range(4):
            spot = out_stage.at[k // 2, :, pl.ds((k % 2) * WIDTH, WIDTH)]
            pltpu.make_async_copy(spot, spot, stage_recv.at[k]).wait()

    out_gather.start()
    keep("cotangent", out_grad, cotangent_all.at[row_span(x), col_span(c)])
    cotangent_numbers = gather_sends(wires, out_grad, cotangent_all, here)
    pairs_gather.finish()
    keep("keys", keys, keys_out)
    out_gather.relay()
    run_bulk((gate,), ('turn',))

    wires.landed(query_at, queries.at[1, pl.ds(0, HD)])
    tour = Tour(z * 4 + y, (1, 0))
    tops[...] = jnp.full(tops.shape, NEVER, F32)
    sums[...] = jnp.zeros(sums.shape, F32)
    mixed[...] = jnp.zeros(mixed.shape, F32)
    heads = range(GROUP)

    def step(s, at, masked):
        pairs = keys[key_at(at)]
        old = [tops[s, :, head_cols(g)] for g in heads]
        old_sums = [sums[s, :, head_cols(g)] for g in heads]
        scores = [
            jnp.dot(pairs, queries[s, :, head_cols(g)], preferred_element_type=F32) for g in heads
        ]
        if masked:
            counts = in_second(tour.half(s), ends) | (at > 0)
            old = [jnp.where(counts, value, NEVER) for value in old]
            old_sums = [jnp.where(counts, value, 0.0) for value in old_sums]
            allowed = allowed_pairs(at, tour.half(s), ends)
            scores = [jnp.where(allowed, value, NEVER) for value in scores]
        top = [jnp.maximum(old[g], jnp.max(scores[g], axis=0, keepdims=True)) for g in heads]
        weights = [jnp.exp(scores[g] - top[g]) for g in heads]
        if masked:
            weights = [jnp.where(allowed, value, 0.0) for value in weights]
        shrink = [jnp.exp(old[g] - top[g]) for g in heads]
        if masked:
            shrink = [jnp.where(counts, value, 0.0) for value in shrink]
        new_sums = [
            old_sums[g] * shrink[g] + jnp.sum(weights[g], axis=0, keepdims=True) for g in heads
        ]
        new = [
            lax.dot_general(
                pairs, weights[g].astype(BF), (((0,), (0,)), ((), ())), preferred_element_type=F32
            )
            for g in heads
        ]
        for g in heads:
            cols = head_cols(g)
            tops[s, :, cols] = top[g]
            sums[s, :, cols] = new_sums[g]
            mixed[s, :, cols] = mixed[s, :, cols] * shrink[g] + new[g]

    def settle(s, rows):
        log_out[s] = tops[s] + jnp.log(sums[s])
        mixed_out[s] = mixed[s, HD:, :] / sums[s]
        for g in heads:
            rows[g * HD : (g + 1) * HD, :] = mixed_out[s, :, head_cols(g)].astype(BF)

    across_at = wires.send(attended_here, across, opposite, start=False)

    def between():
        settle(1, attended_here)
        wires.sent[across_at].start()

    tour.run(step, between, 0, 5)
    out_gather.turn()
    tour.run(step, between, 5, 9)
    gather_relay(wires, cotangent_numbers, cotangent_all, here)
    run_bulk((up,), ('turn',))
    tour.run(step, between, 9, 17)
    out_gather.relay_two()
    run_bulk((gate,), ('relay_two',))
    tour.run(step, between, 17, 21)
    tour.run(step, between, 21, 27)
    run_bulk((down,), ('turn',))
    tour.run(step, between, 27, 33)
    run_bulk((up,), ('relay_two',))
    settle(0, attended_out.at[:, pl.ds(0, HALF)])
    wires.landed(across_at, across)
    attended_out[:, HALF:] = across[...]
    for g in range(0, GROUP, 2):
        rows = slice(g * HD, (g + 2) * HD)
        attended[:, rows] = attended_out[rows, :].astype(F32).T.astype(BF)

    out_gather.finish()
    keep("out", out_all, out_out)
    out_low = out_all[...].reshape(GROUP * HD, D)
    fold_numbers = []
    for k, o in enumerate(FOLD_ORDER):
        rows = row_span(lax.rem(x + o, 4))
        part[rows, :] = jnp.dot(
            attended[rows, :], out_low, preferred_element_type=F32
        ).astype(BF)
        fold_numbers.append(
            wires.send(part.at[rows, col_span(1 - c)], folded.at[k], device(z, y, x, 1 - c))
        )
    moves = fold_moves(
        wires, fold_numbers, part, folded, leaving, arriving, here, total, col_span(c)
    )
    fold_finish(wires, moves, arriving, total)
    run_bulk((down,), ('relay_two',))
    middle = total[...] + block_input[...].astype(F32)
    middle_out[...] = middle
    square = both_cores(
        wires, mine_row, their_row, jnp.sum(middle * middle, axis=1, keepdims=True), here
    )
    scale = lax.rsqrt(square / D + NORM_EPS)
    scale_two[...] = jnp.broadcast_to(scale, scale_two.shape)
    own[...] = (
        middle_out[...] * scale * gains_all[1:2, col_span(c)]
    ).astype(BF)
    keep("own", own, out.at[row_span(x), col_span(c)])
    sends = gather_sends(wires, own, out, here)
    gather_relay(wires, sends, out, here)
    run_bulk(bulk, ('finish',))
    for member in bulk:
        member.leave()
    for name in ("normed", "qkv_out", "cotangent", "keys", "out", "own"):
        kept[name].wait()

    @pl.when(jnp.logical_not(holds))
    def _():
        stage_copy.wait_send()

    wires.close()


def call_forward(*operands):
    vm = pl.BlockSpec(memory_space=pltpu.VMEM)
    hbm = pl.BlockSpec(memory_space=ANY)
    cols = GROUP * HALF
    qkv_cols = (GROUP + 2) * HD
    share = (ROWS, WIDTH)
    whole = (2, 4, 4, 2, PIECE)
    outs = [
        ((HD // 2, LINE), F32, vm),
        ((HD // 2, LINE), F32, vm),
        ((ROWS, 128), F32, vm),
        ((LINE, D), BF, hbm),
        (whole + (qkv_cols,), BF, hbm),
        ((2, 2 * HD, cols), BF, vm),
        ((2, HD, cols), F32, vm),
        ((2, 1, cols), F32, vm),
        ((GROUP * HD, LINE), BF, vm),
        ((2, 4, 4, HALF, 2 * HD), BF, hbm),
        ((LINE, D), BF, hbm),
        ((4, 2, PIECE, D), BF, hbm),
        (whole + (HIDDEN,), BF, hbm),
        (whole + (HIDDEN,), BF, hbm),
        ((4, 4, 2 * PIECE, D), BF, hbm),
        (share, F32, vm),
        ((ROWS, 128), F32, vm),
        ((LINE, D), BF, hbm),
    ]
    return pl.pallas_call(
        forward_kernel,
        out_shape=tuple(jax.ShapeDtypeStruct(shape, kind) for shape, kind, _ in outs),
        in_specs=[pl.BlockSpec(memory_space=pltpu.SMEM)] + [vm] * 7 + [hbm],
        out_specs=tuple(spec for _, _, spec in outs),
        scratch_shapes=[
            pltpu.VMEM((4, PIECE, qkv_cols), BF),
            pltpu.VMEM((4, PIECE, HIDDEN), BF),
            pltpu.VMEM((4, PIECE, HIDDEN), BF),
            pltpu.VMEM((2, ROWS // 2, WIDTH), BF),
            pltpu.VMEM((PIECE, WIDTH), BF),
            pltpu.VMEM((8, WIDTH), F32),
            pltpu.VMEM((LINE, D), BF),
            pltpu.VMEM((8, D), F32),
            pltpu.VMEM(whole + (qkv_cols,), BF),
            pltpu.VMEM((LINE, D), BF),
            pltpu.VMEM((qkv_cols, LINE), F32),
            pltpu.VMEM((HD, cols), BF),
            pltpu.VMEM((GROUP * HD, HALF), BF),
            pltpu.VMEM((GROUP * HD, HALF), BF),
            pltpu.VMEM((2, 4, 4, HALF, 2 * HD), BF),
            pltpu.VMEM((2, 1, cols), F32),
            pltpu.VMEM((2, 1, cols), F32),
            pltpu.VMEM((2, 2 * HD, cols), F32),
            pltpu.VMEM((LINE, GROUP * HD), BF),
            pltpu.VMEM((2, PIECE, D), BF),
            pltpu.VMEM((4, 2, PIECE, D), BF),
            pltpu.VMEM((LINE, D), BF),
        ]
        + fold_scratch()
        + [
            pltpu.VMEM((ROWS, 128), F32),
            pltpu.VMEM((ROWS, 128), F32),
            pltpu.VMEM((ROWS, WIDTH), BF),
        ]
        + wire_scratch(144)
        + wire_scratch(4)
        + wire_scratch(4)
        + [pltpu.SemaphoreType.DMA((13,))],
        compiler_params=comm_params(1),
        name="forward",
    )(*operands)


def backward_kernel(
    lengths, cosine, sine, part, output_part, middle, scale_two, scale_one, gains, inputs, cotangent,
    queries, mixed, logs, attended, keys, out_low, qkv_low, normed, grad_down, grad_up, grad_gate,
    input_grad, output, qkv_grad, gate_up_grad, down_grad, out_grad, totals,
    q_out, kv_out, gate_out, up_out, down_out, out_out, across_grads, across_back, across,
    middle_all, grads, delta, query_rows, grad_rows, out_terms,
    terms, sums, rounded, columns, rows_back, q_terms, kv_terms, key_rec, key_sums, key_rec_two,
    *rest,
):
    rest = list(rest)

    def take(count):
        taken = rest[:count]
        del rest[:count]
        return taken

    first_fold, output_fold, (part_own, output_own) = take(4), take(4), take(2)
    last_fold = first_fold
    first_rows, last_rows, (own,) = take(2), take(2), take(1)
    down_buffers, up_buffers, gate_buffers = take(6), take(6), take(6)
    q_buffers, kv_buffers = take(6), take(6)
    out_buffers, (total_terms, stage, rec_one, rec_two) = take(3), take(4)
    send_sem, recv_sem, out_send, out_recv, local_sem = rest
    z, y, xl, xh, c = place()
    x = xh * 2 + xl
    here = (z, y, x, c)
    mine = xl * 2 + c
    quad = quad_of(xl, xh, x, c)
    line = [(o, b) for b in (0, 1) for o in range(4) if o or b]
    fixed = [device(z + a, y + b, x, c) for a, b in PLANE]
    fixed += [device(z, y, lax.rem(x + o, 4), lax.rem(c + b, 2)) for o, b in line]
    opposite = device(3 - z, 3 - y, x, c)
    greet(fixed)
    wires = Wires(send_sem, recv_sem)
    kept = []

    def keep(src, dst):
        copy = pltpu.make_async_copy(src, dst, local_sem.at[31 + len(kept)])
        copy.start()
        kept.append(copy)

    def deal(fin, result):
        keep(fin.at[c, xl], result.at[mine])
        return [
            wires.send(fin.at[b, lax.rem(a, 2)], result.at[mine], device(z, y, a, b))
            for a, b in quad
        ]

    def dealt(numbers, result):
        for at, (a, b) in zip(numbers, quad):
            wires.landed(at, result.at[lax.rem(a, 2) * 2 + b])

    numbers = fold_sends(wires, part, first_fold[0], here)
    own_parts = [
        pltpu.make_async_copy(part.at[:, col_span(c)], part_own, local_sem.at[42]),
        pltpu.make_async_copy(output_part.at[:, col_span(c)], output_own, local_sem.at[43]),
        pltpu.make_async_copy(out_low, out_terms, local_sem.at[44]),
        pltpu.make_async_copy(
            qkv_low.at[:, :, :, :, :, pl.ds(0, GROUP * HD)], q_terms, local_sem.at[45]
        ),
        pltpu.make_async_copy(
            qkv_low.at[:, :, :, :, :, pl.ds(GROUP * HD, 2 * HD)], kv_terms, local_sem.at[48]
        ),
    ]
    for copy in own_parts:
        copy.start()
    down = PlaneSum(wires, grad_down, down_buffers, here, local_sem, 0)
    up = PlaneSum(wires, grad_up, up_buffers, here, local_sem, 6)
    gate = PlaneSum(wires, grad_gate, gate_buffers, here, local_sem, 12)
    q_sum = PlaneSum(wires, q_terms, q_buffers, here, local_sem, 18)
    kv_sum = PlaneSum(wires, kv_terms, kv_buffers, here, local_sem, 24)
    out_sum = OutSum(
        wires, out_terms, out_buffers, out_out, here, mine, quad, (out_send, out_recv), local_sem, 30
    )
    bulk = (down, up, gate)
    in_turn(c, bulk, True)(*('start', 'direct'))
    own_parts[0].wait()
    moves = fold_moves(wires, numbers, part_own, *first_fold[:3], here, first_fold[3])
    in_turn(c, bulk, True)(*('relay',))
    fold_finish(wires, moves, first_fold[2], first_fold[3])
    back, gain_two = norm_back(
        wires, middle[...], scale_two[:, :1], gains[1:2, :], first_fold[3][...], *first_rows, here
    )
    grad = cotangent[...].astype(F32) + back
    input_grad[...] = grad
    own[...] = grad.astype(BF)
    keep(own, middle_all.at[row_span(x), col_span(c)])
    sends = gather_sends(wires, own, middle_all, here)
    for s in (0, 1):
        for g in range(GROUP):
            query_rows[s, g] = queries[s, :, head_cols(g)].astype(F32).T.astype(BF)
    grads[:, :HD, :] = jnp.zeros((2, HD, GROUP * HALF), BF)
    terms[...] = jnp.zeros(terms.shape, F32)
    sums[...] = jnp.zeros(sums.shape, F32)
    in_turn(c, bulk, True)(*('middle',))
    in_turn(c, bulk, False)(*('start', 'direct'))
    relayed = gather_relay(wires, sends, middle_all, here)
    kept[0].wait()

    own_parts[2].wait()
    shared = out_terms[...].reshape(GROUP * HD, D)

    def attended_rows(i, carry):
        rows = pl.ds(pl.multiple_of(i * ROWS, ROWS), ROWS)
        value = lax.dot_general(
            middle_all[rows, :], shared, (((1,), (1,)), ((), ())), preferred_element_type=F32
        )
        columns[: GROUP * HD, rows] = value.astype(BF).astype(F32).T
        return carry

    lax.fori_loop(0, 4, attended_rows, 0)
    for g in range(GROUP):
        rows = slice(g * HD, (g + 1) * HD)
        grads[0, HD:, head_cols(g)] = columns[rows, :HALF].astype(BF)
        across_grads[:, head_cols(g)] = columns[rows, HALF:].astype(BF)
    grad_at = wires.send(across_grads, grads.at[1, pl.ds(HD, HD)], opposite)

    def prepare(s):
        for g in range(GROUP):
            cols = head_cols(g)
            value = grads[s, :, cols].astype(F32)
            delta[s, :, cols] = jnp.sum(value[HD:] * mixed[s, :, cols], axis=0, keepdims=True)
            grad_rows[s, g] = value.T.astype(BF)

    prepare(0)

    def out_columns(i, carry):
        cols = pl.ds(pl.multiple_of(i * HALF, HALF), HALF)
        value = jnp.dot(attended[...], middle_all[:, cols], preferred_element_type=F32)
        out_terms[:, :, :, cols] = value.astype(BF).reshape(4, 2, PIECE, HALF)
        return carry

    lax.fori_loop(0, D // HALF, out_columns, 0)
    out_sum.start()
    in_turn(c, bulk, False)(*('relay',))
    output_numbers = fold_sends(wires, output_part, output_fold[0], here)

    ends = ends_of(lengths)
    tour = Tour(z * 4 + y, (0, 1))
    heads = range(GROUP)

    def step(s, at, masked):
        slot = key_at(at)
        pairs = keys[slot]
        query_columns = [queries[s, :, head_cols(g)] for g in heads]
        grad_columns = [grads[s, :, head_cols(g)] for g in heads]
        log_rows = [logs[s, :, head_cols(g)] for g in heads]
        deltas = [delta[s, :, head_cols(g)] for g in heads]
        rows = [query_rows[s, g] for g in heads]
        outer = [grad_rows[s, g] for g in heads]
        if not masked:
            fits = in_second(tour.half(s), ends)
            log_rows = [jnp.where(fits, value, -NEVER) for value in log_rows]
        scores = [jnp.dot(pairs, value, preferred_element_type=F32) for value in query_columns]
        prob_grads = [jnp.dot(pairs, value, preferred_element_type=F32) for value in grad_columns]
        probs = [jnp.exp(scores[g] - log_rows[g]) for g in heads]
        if masked:
            allowed = allowed_pairs(at, tour.half(s), ends)
            probs = [jnp.where(allowed, value, 0.0) for value in probs]
        score_grads = [(probs[g] * (prob_grads[g] - deltas[g])).astype(BF) for g in heads]
        probs_low = [value.astype(BF) for value in probs]
        back = [
            lax.dot_general(pairs, value, (((0,), (0,)), ((), ())), preferred_element_type=F32)
            for value in score_grads
        ]
        added = [
            jnp.dot(score_grads[g], rows[g], preferred_element_type=F32)
            + jnp.dot(probs_low[g], outer[g], preferred_element_type=F32)
            for g in heads
        ]
        terms[slot] += (added[0] + added[1]) + (added[2] + added[3])
        for g in heads:
            sums[s, :, head_cols(g)] += back[g]

    def between():
        wires.landed(grad_at, grads.at[1, pl.ds(HD, HD)])
        prepare(1)

    tour.run(step, between, 0, 4)
    tour.run(step, between, 4, 8)
    own_parts[1].wait()
    output_moves = fold_moves(
        wires, output_numbers, output_own, *output_fold[:3], here, output_fold[3]
    )
    out_sum.middle()
    tour.run(step, between, 8, 14)
    tour.run(step, between, 14, 20)
    fold_finish(wires, output_moves, output_fold[2], output_fold[3])
    output[...] = (middle[...] + output_fold[3][...]).astype(BF)
    normed_parts = [
        pltpu.make_async_copy(normed.at[:, pl.ds(n * WIDTH, WIDTH)], value, local_sem.at[46 + n])
        for n, value in enumerate((part_own, output_own))
    ]
    for copy in normed_parts:
        copy.start()
    out_sum.deal()
    in_turn(c, bulk, True)(*('finish',))
    in_turn(c, bulk, False)(*('middle',))
    tour.run(step, between, 20, 26)
    tour.run(step, between, 26, 33)

    for s in (0, 1):
        for i in range(4):
            rounded[s, i] = terms[s, i].astype(BF)
    first = [[], []]
    for k, by in enumerate(OFFSETS):
        first[0].append(
            wires.send(
                rounded.at[0, :, lax.rem(y + by, 4)], key_rec.at[0, k], second_device(here, 0, by)
            )
        )
        first[1].append(
            wires.send(
                rounded.at[1, lax.rem(z + by, 4)], key_rec.at[1, k], second_device(here, 1, by)
            )
        )
    across_back[...] = (sums[1, :HD, :] * HD ** (-0.5)).astype(BF)
    back_at = wires.send(across_back, across, opposite)
    in_turn(c, bulk, False)(*('finish',))
    down_fin = down_buffers[5]
    down_swap = wires.send(
        down_fin.at[:, :, col_span(1 - c)], down_out.at[c], device(z, y, x, 1 - c)
    )
    keep(down_fin.at[:, :, col_span(c)], down_out.at[c])
    up_swap = deal(up_buffers[5], up_out)
    gate_swap = deal(gate_buffers[5], gate_out)

    second = [[], []]
    for s in (0, 1):
        for k in range(3):
            wires.landed(first[s][k], key_rec.at[s, k])
        for i in range(4):
            value = terms[0, i, y] if s == 0 else terms[1, z, i]
            for k in range(3):
                value = value + key_rec[s, k, i].astype(F32)
            key_sums[s, i] = value.astype(BF)
        for k, by in enumerate(OFFSETS):
            second[s].append(
                wires.send(
                    key_sums.at[s, first_at(here, s, by)],
                    key_rec_two.at[s, k],
                    first_device(here, s, by),
                )
            )
    def turn_back(values, tokens, scale):
        for g in range(GROUP):
            turned = rope(values.at[:, head_cols(g)], 0, cosine[:, tokens], -sine[:, tokens])
            for i, value in enumerate(turned):
                at = g * HD + i * (HD // 2)
                columns[at : at + HD // 2, tokens] = value * scale

    turn_back(sums.at[0], slice(0, HALF), HD ** (-0.5))
    wires.landed(back_at, across)
    turn_back(across, slice(HALF, LINE), 1.0)

    def take_rows(cols):
        for r in range(4):
            rows = slice(r * ROWS, (r + 1) * ROWS)
            rows_back[rows, cols] = columns[cols, rows].T.astype(BF)

    def weight_terms(cols, result):
        back_part = rows_back[:, cols]
        for n, half in enumerate((part_own, output_own)):

            def body(i, carry):
                at = pl.ds(pl.multiple_of(i * 256, 256), 256)
                value = lax.dot_general(
                    half[:, at], back_part, (((0,), (0,)), ((), ())), preferred_element_type=F32
                )
                result[n, i] = value.astype(BF).reshape(result.shape[2:])
                return carry

            lax.fori_loop(0, 4, body, 0)

    q_cols, kv_cols = slice(0, GROUP * HD), slice(GROUP * HD, (GROUP + 2) * HD)
    take_rows(q_cols)
    own_parts[3].wait()
    wires.settle(relayed)
    weight = q_terms[...].reshape(D, GROUP * HD)
    for r in range(4):
        rows = slice(r * ROWS, (r + 1) * ROWS)
        middle_all[rows, :] = lax.dot_general(
            rows_back[rows, q_cols], weight, (((1,), (1,)), ((), ())), preferred_element_type=F32
        ).astype(BF)
    for copy in normed_parts:
        copy.wait()
    weight_terms(q_cols, q_terms)
    run_bulk((q_sum,), ('start', 'direct'))
    for s in (0, 1):
        tokens = slice(s * HALF, (s + 1) * HALF)
        value = key_sums[s, first_at(here, s)].astype(F32)
        for k in range(3):
            wires.landed(second[s][k], key_rec_two.at[s, k])
            value = value + key_rec_two[s, k].astype(F32)
        pair_columns = value.T
        turned = rope(pair_columns, 0, cosine[:, tokens], -sine[:, tokens])
        for i, value in enumerate(turned):
            at = GROUP * HD + i * (HD // 2)
            columns[at : at + HD // 2, tokens] = value
        columns[(GROUP + 1) * HD :, tokens] = pair_columns[HD:]

    run_bulk((q_sum,), ('relay',))

    take_rows(kv_cols)
    own_parts[4].wait()
    weight = kv_terms[...].reshape(D, 2 * HD)
    last_numbers = []
    for k, o in enumerate(FOLD_ORDER):
        rows = row_span(lax.rem(x + o, 4))
        value = lax.dot_general(
            rows_back[rows, kv_cols], weight, (((1,), (1,)), ((), ())), preferred_element_type=F32
        )
        middle_all[rows, :] = (middle_all[rows, :].astype(F32) + value).astype(BF)
        last_numbers.append(
            wires.send(
                middle_all.at[rows, col_span(1 - c)], last_fold[0].at[k], device(z, y, x, 1 - c)
            )
        )
    weight_terms(kv_cols, kv_terms)
    run_bulk((kv_sum,), ('start', 'direct'))
    wires.settle(moves)
    last_moves = fold_moves(
        wires, last_numbers, middle_all, *last_fold[:3], here, last_fold[3], col_span(c)
    )

    run_bulk((kv_sum,), ('relay',))
    run_bulk((q_sum,), ('middle',))
    out_sum.finish()
    wires.landed(down_swap, down_out.at[1 - c])
    dealt(up_swap, up_out)
    dealt(gate_swap, gate_out)
    for copy in kept[1:]:
        copy.wait()
    left = lax.broadcasted_iota(jnp.int32, (PIECE, 2 * HD), 1) < HD
    squares = jnp.zeros((PIECE, 2 * HD), F32)
    for u, result in enumerate((gate_out, up_out)):
        for side in (0, 1):
            for j in range(HIDDEN // (2 * HD)):
                cols = slice(j * 2 * HD, (j + 1) * 2 * HD)
                one = result[side * 2, :, cols].astype(F32)
                two = result[side * 2 + 1, :, cols].astype(F32)
                squares = squares + one * one + two * two
                even = jnp.where(left, one, pltpu.roll(two, HD, 1))
                odd = jnp.where(left, pltpu.roll(one, HD, 1), two)
                for i, value in enumerate((even, odd)):
                    at = ((2 * j + i) * 2 + side) * 2 * HD
                    gate_up_grad[:, u, at : at + 2 * HD] = value
    square = jnp.sum(squares)
    for k in range(2):
        for o in range(2):
            value = down_out[k, o].astype(F32)
            down_grad[(2 * k + o) * PIECE : (2 * k + o + 1) * PIECE, :] = value
            square = square + jnp.sum(value * value)
    value = out_out[...].astype(F32)
    out_grad[...] = value
    square = square + jnp.sum(value * value)
    run_bulk((kv_sum,), ('middle',))
    run_bulk((q_sum,), ('finish',))
    q_swap = deal(q_buffers[5], q_out)
    fold_finish(wires, last_moves, last_fold[2], last_fold[3])
    back, gain_one = norm_back(
        wires,
        inputs[...].astype(F32),
        scale_one[:, :1],
        gains[0:1, :],
        last_fold[3][...],
        *last_rows,
        here,
    )
    input_grad[...] = input_grad[...] + back
    run_bulk((kv_sum,), ('finish',))
    kv_swap = deal(kv_buffers[5], kv_out)
    dealt(q_swap, q_out)
    dealt(kv_swap, kv_out)
    for copy in kept[-2:]:
        copy.wait()
    for k in range(4):
        for result, at in ((q_out, 0), (kv_out, GROUP * HD)):
            value = result[k].astype(F32)
            qkv_grad[:, k, at : at + value.shape[1]] = value
            square = square + jnp.sum(value * value)

    for k in range(8):
        cols = slice(k * 128, (k + 1) * 128)
        total_terms[k : k + 1] = gain_one[:, cols]
        total_terms[8 + k : 9 + k] = gain_two[:, cols]
    total_terms[16:] = jnp.broadcast_to(square, (8, 128))
    first = [
        wires.send(total_terms, rec_one.at[k], device(z + a, y + b, x, c))
        for k, (a, b) in enumerate(PLANE)
    ]
    value = total_terms[...]
    for k, at in enumerate(first):
        wires.landed(at, rec_one.at[k])
        value = value + rec_one[k]
    stage[...] = value
    second = [
        wires.send(stage, rec_two.at[k], device(z, y, lax.rem(x + o, 4), lax.rem(c + b, 2)))
        for k, (o, b) in enumerate(line)
    ]
    both = [value, None]
    for k, (o, b) in enumerate(line):
        wires.landed(second[k], rec_two.at[k])
        both[b] = rec_two[k] if both[b] is None else both[b] + rec_two[k]
    totals[:16] = both[0][:16]
    totals[16:] = (
        both[0][16:]
        + both[1][16:]
        + jnp.sum(both[0][:16] * both[0][:16])
        + jnp.sum(both[1][:16] * both[1][:16])
    )
    for member in bulk + (q_sum, kv_sum):
        member.leave()
    wires.close()


def call_backward(*operands):
    vm = pl.BlockSpec(memory_space=pltpu.VMEM)
    hbm = pl.BlockSpec(memory_space=ANY)
    cols = GROUP * HALF
    qkv_cols = (GROUP + 2) * HD
    share = (ROWS, WIDTH)
    outs = [
        (share, F32, vm),
        (share, BF, vm),
        ((PIECE, 4, qkv_cols), F32, vm),
        ((PIECE, 2, 4 * HIDDEN), F32, vm),
        (share, F32, vm),
        ((PIECE, WIDTH), F32, vm),
        ((24, 128), F32, vm),
    ]
    return pl.pallas_call(
        backward_kernel,
        out_shape=tuple(jax.ShapeDtypeStruct(shape, kind) for shape, kind, _ in outs),
        in_specs=[pl.BlockSpec(memory_space=pltpu.SMEM)] + [vm] * 2 + [hbm] * 2 + [vm] * 11 + [hbm] * 6,
        out_specs=tuple(spec for _, _, spec in outs),
        scratch_shapes=[
            pltpu.VMEM((4, PIECE, GROUP * HD), BF),
            pltpu.VMEM((4, PIECE, 2 * HD), BF),
            pltpu.VMEM((4, PIECE, HIDDEN), BF),
            pltpu.VMEM((4, PIECE, HIDDEN), BF),
            pltpu.VMEM((2, 2, PIECE, WIDTH), BF),
            pltpu.VMEM((PIECE, WIDTH), BF),
            pltpu.VMEM((HD, cols), BF),
            pltpu.VMEM((HD, cols), BF),
            pltpu.VMEM((HD, cols), BF),
            pltpu.VMEM((LINE, D), BF),
            pltpu.VMEM((2, 2 * HD, cols), BF),
            pltpu.VMEM((2, 1, cols), F32),
            pltpu.VMEM((2, GROUP, HALF, 2 * HD), BF),
            pltpu.VMEM((2, GROUP, HALF, 2 * HD), BF),
            pltpu.VMEM((4, 2, PIECE, D), BF),
            pltpu.VMEM((2, 4, 4, HALF, 2 * HD), F32),
            pltpu.VMEM((2, 2 * HD, cols), F32),
            pltpu.VMEM((2, 4, 4, HALF, 2 * HD), BF),
            pltpu.VMEM((qkv_cols, LINE), F32),
            pltpu.VMEM((LINE, qkv_cols), BF),
            pltpu.VMEM((2, 4, 4, 2, PIECE, GROUP * HD), BF),
            pltpu.VMEM((2, 4, 4, 2, PIECE, 2 * HD), BF),
            pltpu.VMEM((2, 3, 4, HALF, 2 * HD), BF),
            pltpu.VMEM((2, 4, HALF, 2 * HD), BF),
            pltpu.VMEM((2, 3, HALF, 2 * HD), BF),
        ]
        + fold_scratch() * 2
        + [pltpu.VMEM((LINE, WIDTH), BF)] * 2
        + [pltpu.VMEM((ROWS, 128), F32)] * 4
        + [pltpu.VMEM(share, BF)]
        + sum_buffers((PIECE, D), BF)
        + sum_buffers((2, PIECE, HIDDEN), BF) * 2
        + sum_buffers((2, PIECE, GROUP * HD), BF)
        + sum_buffers((2, PIECE, 2 * HD), BF)
        + [
            pltpu.VMEM((3, 2, PIECE, D), BF),
            pltpu.VMEM((2, PIECE, D), BF),
            pltpu.VMEM((3, 2, PIECE, D), BF),
            pltpu.VMEM((24, 128), F32),
            pltpu.VMEM((24, 128), F32),
            pltpu.VMEM((15, 24, 128), F32),
            pltpu.VMEM((7, 24, 128), F32),
        ]
        + wire_scratch(200)
        + wire_scratch(6)
        + [pltpu.SemaphoreType.DMA((49,))],
        compiler_params=comm_params(2),
        name="backward",
    )(*operands)


CHUNK = 512


def feed_kernel(
    normed_two, cotangent, gate_low, up_low, down_low,
    output_part, back_part, grad_gate, grad_up, grad_down, output_sum, back_sum,
):
    at = pl.program_id(0)

    @pl.when(at == 0)
    def _():
        output_sum[...] = jnp.zeros(output_sum.shape, F32)
        back_sum[...] = jnp.zeros(back_sum.shape, F32)

    inputs, incoming = normed_two[...], cotangent[...]
    gate = jnp.dot(inputs, gate_low[...], preferred_element_type=F32)
    up = jnp.dot(inputs, up_low[...], preferred_element_type=F32)
    hidden_grad = lax.dot_general(
        incoming, down_low[...], (((1,), (1,)), ((), ())), preferred_element_type=F32
    )
    sigmoid = jax.nn.sigmoid(gate)
    silu = gate * sigmoid
    hidden = (silu * up).astype(BF)
    gate_back = (hidden_grad * up * sigmoid * (1.0 + gate * (1.0 - sigmoid))).astype(BF)
    up_back = (hidden_grad * silu).astype(BF)
    both_back = jnp.concatenate([gate_back, up_back], axis=1)
    for k in range(4):
        cols = slice(k * D // 4, (k + 1) * D // 4)
        output_sum[:, cols] += jnp.dot(hidden, down_low[:, cols], preferred_element_type=F32)
        back_sum[:, cols] += lax.dot_general(
            gate_back, gate_low[cols, :], (((1,), (1,)), ((), ())), preferred_element_type=F32
        ) + lax.dot_general(
            up_back, up_low[cols, :], (((1,), (1,)), ((), ())), preferred_element_type=F32
        )
        grad_down[:, cols] = outer_rows(hidden, incoming[:, cols], BF)
        both = outer_rows(inputs[:, cols], both_back, BF)
        grad_gate[cols, :] = both[:, :CHUNK]
        grad_up[cols, :] = both[:, CHUNK:]

    @pl.when(at == HIDDEN // CHUNK - 1)
    def _():
        output_part[...] = output_sum[...].astype(BF)
        back_part[...] = back_sum[...].astype(BF)


def call_feed(normed_two, cotangent, gate_low, up_low, down_low):
    rows = pl.BlockSpec((LINE, D), lambda j: (0, 0))
    tall = pl.BlockSpec((D, CHUNK), lambda j: (0, j))
    wide = pl.BlockSpec((CHUNK, D), lambda j: (j, 0))
    return pl.pallas_call(
        feed_kernel,
        out_shape=(
            jax.ShapeDtypeStruct((LINE, D), BF),
            jax.ShapeDtypeStruct((LINE, D), BF),
            jax.ShapeDtypeStruct((D, HIDDEN), BF),
            jax.ShapeDtypeStruct((D, HIDDEN), BF),
            jax.ShapeDtypeStruct((HIDDEN, D), BF),
        ),
        grid=(HIDDEN // CHUNK,),
        in_specs=[rows, rows, tall, tall, wide],
        out_specs=(rows, rows, tall, tall, wide),
        scratch_shapes=[pltpu.VMEM((LINE, D), F32), pltpu.VMEM((LINE, D), F32)],
        compiler_params=pltpu.CompilerParams(vmem_limit_bytes=VMEM_LIMIT),
        name="feed_forward",
    )(normed_two, cotangent, gate_low, up_low, down_low)


def rope_inverse():
    half_size = HD // 2
    column = np.arange(half_size, dtype=np.float32)
    inverse = np.exp(-(np.float32(2.0) * column / HD) * np.float32(math.log(ROPE_THETA)))
    wavelength = np.float32(2.0 * math.pi) / inverse
    smooth = (np.float32(OLD_CONTEXT) / wavelength - LOW_FREQ) / (HIGH_FREQ - LOW_FREQ)
    blended = (1.0 - smooth) * inverse / ROPE_FACTOR + smooth * inverse
    inverse = np.where(
        wavelength < OLD_CONTEXT / HIGH_FREQ,
        inverse,
        np.where(wavelength > OLD_CONTEXT / LOW_FREQ, inverse / ROPE_FACTOR, blended),
    )
    return np.broadcast_to(inverse.astype(np.float32)[:, None], (half_size, 128))


def outer_rows(left, right, kind):
    return lax.dot_general(
        left, right, (((0,), (0,)), ((), ())), preferred_element_type=F32
    ).astype(kind)


def adam(weight, moment, second, gradient, rate, decay):
    moment_next = BETA_ONE * moment + (1.0 - BETA_ONE) * gradient
    second_next = BETA_TWO * second + (1.0 - BETA_TWO) * gradient * gradient
    unbiased = moment_next / (1.0 - BETA_ONE**ADAM_STEP)
    divisor = jnp.sqrt(second_next / (1.0 - BETA_TWO**ADAM_STEP)) + ADAM_EPS
    return (weight - rate * (unbiased / divisor + decay * weight), moment_next, second_next)


def shards(
    block_input,
    out_grad,
    qkv_weight,
    qkv_moment,
    qkv_second,
    gate_up_weight,
    gate_up_moment,
    gate_up_second,
    out_weight,
    out_moment,
    out_second,
    down_weight,
    down_moment,
    down_second,
    norm_gains,
    gains_moment,
    gains_second,
    doc_lengths,
):
    (
        cosine,
        sine,
        scale_one,
        normed,
        qkv_whole,
        query_columns,
        mixed,
        logs,
        attended,
        keys,
        cotangent_all,
        out_whole,
        gate_whole,
        up_whole,
        down_whole,
        middle,
        scale_two,
        normed_two,
    ) = call_forward(
        doc_lengths,
        jnp.asarray(rope_inverse()),
        block_input,
        qkv_weight,
        gate_up_weight,
        down_weight,
        out_weight,
        norm_gains,
        out_grad,
    )
    output_part, back_part, grad_gate, grad_up, grad_down = call_feed(
        normed_two,
        cotangent_all,
        gate_whole.reshape(D, HIDDEN),
        up_whole.reshape(D, HIDDEN),
        down_whole.reshape(HIDDEN, D),
    )
    input_grad, output, grad_qkv, grad_gate_up, grad_down, grad_out, totals = call_backward(
        doc_lengths,
        cosine,
        sine,
        back_part,
        output_part,
        middle,
        scale_two,
        scale_one,
        norm_gains,
        block_input,
        out_grad,
        query_columns,
        mixed,
        logs,
        attended,
        keys,
        out_whole,
        qkv_whole,
        normed,
        grad_down.reshape(down_whole.shape),
        grad_up.reshape(up_whole.shape),
        grad_gate.reshape(gate_whole.shape),
    )
    shares = (grad_qkv, grad_gate_up, grad_out, grad_down)
    gains_grad = totals[:16].reshape(2, WIDTH)
    grad_norm = jnp.sqrt(totals[16, 0])
    factor = CLIP_NORM / jnp.maximum(grad_norm, CLIP_NORM)
    weights = (qkv_weight, gate_up_weight, out_weight, down_weight)
    moments = (qkv_moment, gate_up_moment, out_moment, down_moment)
    seconds = (qkv_second, gate_up_second, out_second, down_second)
    out_rate = OUTPUT_RATE * (TOKENS / (HQ * HD)) ** 0.5
    down_rate = DOWN_RATE * FF ** (-0.5)
    rates = (MATRIX_RATE, MATRIX_RATE, out_rate, down_rate)
    results = []
    for weight, moment, second, gradient, rate in zip(weights, moments, seconds, shares, rates):
        results.extend(adam(weight, moment, second, gradient * factor, rate, WEIGHT_DECAY))
    gains_new = adam(norm_gains, gains_moment, gains_second, gains_grad * factor, GAIN_RATE, 0.0)
    return (output, input_grad, grad_norm, *results, *gains_new)


def solution(mesh):
    placed = (
        P(("seq", "wide"), "narrow"),
        P(("seq", "wide"), "narrow"),
        P(("narrow", "seq"), "wide", None),
        P(("narrow", "seq"), "wide", None),
        P(("narrow", "seq"), "wide", None),
        P(("narrow", "seq"), None, "wide"),
        P(("narrow", "seq"), None, "wide"),
        P(("narrow", "seq"), None, "wide"),
        P(("wide", "seq"), "narrow"),
        P(("wide", "seq"), "narrow"),
        P(("wide", "seq"), "narrow"),
        P(("wide", "seq"), "narrow"),
        P(("wide", "seq"), "narrow"),
        P(("wide", "seq"), "narrow"),
        P(None, "narrow"),
        P(None, "narrow"),
        P(None, "narrow"),
        P(),
    )
    return jax.shard_map(
        shards,
        mesh=mesh,
        in_specs=placed,
        out_specs=(
            P(("seq", "wide"), "narrow"),
            P(("seq", "wide"), "narrow"),
            P(),
            P(("narrow", "seq"), "wide", None),
            P(("narrow", "seq"), "wide", None),
            P(("narrow", "seq"), "wide", None),
            P(("narrow", "seq"), None, "wide"),
            P(("narrow", "seq"), None, "wide"),
            P(("narrow", "seq"), None, "wide"),
            P(("wide", "seq"), "narrow"),
            P(("wide", "seq"), "narrow"),
            P(("wide", "seq"), "narrow"),
            P(("wide", "seq"), "narrow"),
            P(("wide", "seq"), "narrow"),
            P(("wide", "seq"), "narrow"),
            P(None, "narrow"),
            P(None, "narrow"),
            P(None, "narrow"),
        ),
        check_vma=False,
    )
```

```python
import functools
import math

import jax
import jax.numpy as jnp
import numpy as np
from jax import lax
from jax.experimental import pallas as pl
from jax.experimental.pallas import tpu as pltpu
from jax.sharding import PartitionSpec as P

D = 2048
HQ = 32
HD = 64
FF = 8192
ADAM_STEP = 10


NORM_EPS = 1e-05
ADAM_EPS = 1e-08
BETA_ONE = 0.9
BETA_TWO = 0.95
WEIGHT_DECAY = 0.1
MATRIX_RATE = 0.01
OUTPUT_RATE = 0.9
DOWN_RATE = 3.0
GAIN_RATE = 2.5
CLIP_NORM = 1.0
ROPE_THETA = 500000.0
ROPE_FACTOR = 32.0
LOW_FREQ = 1.0
HIGH_FREQ = 4.0
OLD_CONTEXT = 8192.0

TOKENS = 8192
HALF = 256
HALVES = TOKENS // HALF
ROWS = 128
LINE = 512
WIDTH = 1024
GROUP = 4
PIECE = 32
HIDDEN = 1024
MESH = pl.DeviceIdType.MESH
ANY = pl.ANY
BF = jnp.bfloat16
F32 = jnp.float32
VMEM_LIMIT = 60 * 1024 * 1024
NEVER = -1e30


def place():
    seq = lax.axis_index("seq")
    return (
        seq // 8,
        lax.rem(seq // 2, 4),
        lax.rem(seq, 2),
        lax.axis_index("wide"),
        lax.axis_index("narrow"),
    )


def device(z, y, x, c):
    return (lax.rem(z, 4) * 8 + lax.rem(y, 4) * 2 + lax.rem(x, 2), c, x // 2)


class Wires:
    def __init__(self, send_sem, recv_sem):
        self.send_sem, self.recv_sem, self.used, self.sent = send_sem, recv_sem, 0, []
        self.settled = set()

    def reserve(self):
        self.used += 1
        self.sent.append(None)
        return self.used - 1

    def send(self, src, dst, target, start=True, at=None):
        held = at is None
        if held:
            at = self.reserve()
        copy = pltpu.make_async_remote_copy(
            src_ref=src,
            dst_ref=dst,
            send_sem=self.send_sem.at[at],
            recv_sem=self.recv_sem.at[at],
            device_id=target,
            device_id_type=MESH,
        )
        if start:
            copy.start()
        if held:
            self.sent[at] = copy
        return at

    def left(self, at, region):
        pltpu.make_async_copy(region, region, self.send_sem.at[at]).wait()

    def landed(self, at, region):
        pltpu.make_async_copy(region, region, self.recv_sem.at[at]).wait()

    def settle(self, numbers):
        for at in numbers:
            self.sent[at].wait_send()
            self.settled.add(at)

    def close(self):
        held = [at for at in range(self.used) if self.sent[at] is not None]
        self.settle([at for at in held if at not in self.settled])


def greet(targets):
    barrier = pltpu.get_barrier_semaphore()
    for target in targets:
        pl.semaphore_signal(barrier, inc=1, device_id=target, device_id_type=MESH)
    pl.semaphore_wait(barrier, len(targets))


def line_targets(z, y, x, c):
    return [device(z, y, lax.rem(x + o, 4), c) for o in (1, 2, 3)] + [device(z, y, x, 1 - c)]


def plane_targets(z, y, x, c):
    return [device(z + o, y, x, c) for o in (1, 2, 3)] + [device(z, y + o, x, c) for o in (1, 2, 3)]


def wire_scratch(count):
    return [pltpu.SemaphoreType.DMA((count,)), pltpu.SemaphoreType.DMA((count,))]


def comm_params(number):
    return pltpu.CompilerParams(
        collective_id=number, has_side_effects=True, vmem_limit_bytes=VMEM_LIMIT
    )


def rows_of(x):
    return lax.rem(x, 2) * 2 + x // 2


def row_span(x):
    return pl.ds(pl.multiple_of(rows_of(x) * ROWS, ROWS), ROWS)


def col_span(c):
    return pl.ds(pl.multiple_of(c * WIDTH, WIDTH), WIDTH)


def half_span(x, half):
    return pl.ds(pl.multiple_of(rows_of(x) * ROWS + half * (ROWS // 2), ROWS // 2), ROWS // 2)


def chip(x, by):
    return lax.rem(x + by, 4)


def gather_sends(wires, own, out, here):
    z, y, x, c = here
    numbers = {}
    for first in (0, 1):
        for by, half in ((1, first), (3, 1 - first)):
            src = own.at[pl.ds(half * (ROWS // 2), ROWS // 2)]
            spot = out.at[half_span(x, half), col_span(c)]
            numbers[by, half] = wires.send(src, spot, device(z, y, chip(x, by), c))
    spot = out.at[row_span(x), col_span(c)]
    numbers["core"] = wires.send(own, spot, device(z, y, x, 1 - c))
    return numbers


def gather_hand(wires, numbers, out, here):
    z, y, x, c = here
    for by, half in ((1, 0), (3, 1)):
        spot = out.at[half_span(chip(x, 4 - by), half), col_span(c)]
        wires.landed(numbers[by, half], spot)
        numbers["far", half] = wires.send(spot, spot, device(z, y, chip(x, by), c))
    relays = []
    for by, half in ((1, 1), (3, 0)):
        from_x = chip(x, 4 - by)
        wires.landed(numbers[by, half], out.at[half_span(from_x, half), col_span(c)])
        spot = out.at[row_span(from_x), col_span(c)]
        relays.append((wires.send(spot, spot, device(z, y, x, 1 - c)), from_x))
    return relays


def gather_take(wires, numbers, relays, out, here):
    z, y, x, c = here
    far = chip(x, 2)
    for half in (0, 1):
        wires.landed(numbers["far", half], out.at[half_span(far, half), col_span(c)])
    spot = out.at[row_span(far), col_span(c)]
    relays = relays + [(wires.send(spot, spot, device(z, y, x, 1 - c)), far)]
    wires.landed(numbers["core"], out.at[row_span(x), col_span(1 - c)])
    for at, from_x in relays:
        wires.landed(at, out.at[row_span(from_x), col_span(1 - c)])
    return [at for at, _ in relays] + [numbers["far", 0], numbers["far", 1]]


def gather_relay(wires, numbers, out, here):
    relays = gather_hand(wires, numbers, out, here)
    return gather_take(wires, numbers, relays, out, here)


FOLD_ORDER = (2, 1, 3, 0)
EVERY = slice(None)


def fold_sends(wires, part, folded, here):
    z, y, x, c = here
    return [
        wires.send(
            part.at[row_span(lax.rem(x + o, 4)), col_span(1 - c)],
            folded.at[k],
            device(z, y, x, 1 - c),
        )
        for k, o in enumerate(FOLD_ORDER)
    ]


def fold_moves(wires, numbers, part, folded, leaving, arriving, here, total, cols=EVERY):
    z, y, x, c = here
    halves = [pl.ds(half * (ROWS // 2), ROWS // 2) for half in (0, 1)]
    near = [device(z, y, chip(x, by), c) for by in (1, 3)]
    far, direct, passed = [], [], []
    for k, o in enumerate(FOLD_ORDER):
        wires.landed(numbers[k], folded.at[k])
        both = part[row_span(chip(x, o)), cols].astype(F32) + folded[k].astype(F32)
        if o == 0:
            total[...] = both
            continue
        leaving[k] = both.astype(BF)
        if o == 2:
            for half in (0, 1):
                src = leaving.at[k, halves[half]]
                far.append(wires.send(src, arriving.at[2, halves[half]], near[half]))
        else:
            side = k - 1
            spot = halves[1 - side]
            direct.append(wires.send(leaving.at[k, spot], arriving.at[side, spot], near[side]))
    for side in (0, 1):
        spot = halves[side]
        wires.landed(far[side], arriving.at[2, spot])
        both = leaving[side + 1, spot].astype(F32) + arriving[2, spot].astype(F32)
        leaving[side + 1, spot] = both.astype(BF)
        passed.append(wires.send(leaving.at[side + 1, spot], arriving.at[side, spot], near[side]))
    return direct + passed + far


def fold_finish(wires, moves, arriving, total):
    for side in (0, 1):
        for at, half in ((moves[side], 1 - side), (moves[2 + side], side)):
            wires.landed(at, arriving.at[side, pl.ds(half * (ROWS // 2), ROWS // 2)])
    total[...] = total[...] + arriving[0].astype(F32) + arriving[1].astype(F32)


def fold_scratch():
    return [
        pltpu.VMEM((4, ROWS, WIDTH), BF),
        pltpu.VMEM((3, ROWS, WIDTH), BF),
        pltpu.VMEM((3, ROWS, WIDTH), BF),
        pltpu.VMEM((ROWS, WIDTH), F32),
    ]


def both_cores(wires, mine, theirs, value, here):
    z, y, x, c = here
    mine[...] = jnp.broadcast_to(value, mine.shape)
    at = wires.send(mine, theirs, device(z, y, x, 1 - c))
    wires.landed(at, theirs)
    return value + theirs[:, :1]


def first_device(here, order, by):
    z, y, x, c = here
    return device(z + by, y, x, c) if order == 0 else device(z, y + by, x, c)


def second_device(here, order, by):
    z, y, x, c = here
    return device(z, y + by, x, c) if order == 0 else device(z + by, y, x, c)


def first_at(here, order, by=0):
    return lax.rem((here[0] if order == 0 else here[1]) + by, 4)


def run_of(ref, here, order, by, sub=None):
    z, y, _, _ = here
    zi, yi = (EVERY, lax.rem(y + by, 4)) if order == 0 else (lax.rem(z + by, 4), EVERY)
    if len(ref.shape) > 4:
        return ref.at[order, zi, yi] if sub is None else ref.at[order, zi, yi, sub]
    rows = ref.shape[2] // 2
    if sub is None:
        return ref.at[zi, yi, pl.ds(order * rows, rows)]
    return ref.at[zi, yi, pl.ds(order * rows + sub * (rows // 2), rows // 2)]


def spot_of(ref, here, order, at, sub=None):
    z, y, _, _ = here
    zi, yi = (at, y) if order == 0 else (z, at)
    if len(ref.shape) > 4:
        return ref.at[order, zi, yi] if sub is None else ref.at[order, zi, yi, sub]
    rows = ref.shape[2] // 2
    if sub is None:
        return ref.at[zi, yi, pl.ds(order * rows, rows)]
    return ref.at[zi, yi, pl.ds(order * rows + sub * (rows // 2), rows // 2)]


class PlaneGather:
    def __init__(self, wires, whole, here):
        self.wires, self.whole, self.here, self.numbers = wires, whole, here, {}

    def send(self, key, spot, target):
        if key not in self.numbers:
            self.numbers[key] = self.wires.reserve()
        self.wires.send(spot, spot, target, at=self.numbers[key])

    def start(self, o):
        spot = spot_of(self.whole, self.here, o, first_at(self.here, o))
        for by in (1, 3):
            self.send(("first", o, by), spot, first_device(self.here, o, by))

    def relay(self, o):
        for sub, by in enumerate((1, 3)):
            at = first_at(self.here, o, 4 - by)
            self.wires.landed(self.numbers["first", o, by], spot_of(self.whole, self.here, o, at))
            spot = spot_of(self.whole, self.here, o, at, sub)
            self.send(("onward", o, by), spot, first_device(self.here, o, by))

    def turn(self, o):
        at = first_at(self.here, o, 2)
        for sub, by in enumerate((1, 3)):
            spot = spot_of(self.whole, self.here, o, at, sub)
            self.wires.landed(self.numbers["onward", o, by], spot)
        spot = run_of(self.whole, self.here, o, 0)
        for by in (1, 3):
            self.send(("second", o, by), spot, second_device(self.here, o, by))

    def relay_two(self, o):
        for sub, by in enumerate((1, 3)):
            spot = run_of(self.whole, self.here, o, 4 - by)
            self.wires.landed(self.numbers["second", o, by], spot)
            spot = run_of(self.whole, self.here, o, 4 - by, sub)
            self.send(("last", o, by), spot, second_device(self.here, o, by))

    def finish(self, o):
        for sub, by in enumerate((1, 3)):
            spot = run_of(self.whole, self.here, o, 2, sub)
            self.wires.landed(self.numbers["last", o, by], spot)

    def leave(self):
        for o in (0, 1):
            spot = spot_of(self.whole, self.here, o, first_at(self.here, o))
            half = spot_of(self.whole, self.here, o, first_at(self.here, o), 0)
            for by in (1, 3):
                self.wires.left(self.numbers["first", o, by], spot)
                self.wires.left(self.numbers["onward", o, by], half)
                self.wires.left(self.numbers["second", o, by], run_of(self.whole, self.here, o, 0))
                self.wires.left(self.numbers["last", o, by], run_of(self.whole, self.here, o, 0, 0))


def in_turn(c, members, first):
    def run(*steps):
        for core in (0, 1):

            @pl.when(c == core)
            def _():
                for step in steps:
                    for member in members:
                        getattr(member, step)(core if first else 1 - core)

    return run


OFFSETS = (2, 1, 3)


class DirectGather:
    def __init__(self, wires, whole, here):
        self.wires, self.whole, self.here = wires, whole, here

    def start(self):
        self.numbers = []
        for o in (0, 1):
            spot = spot_of(self.whole, self.here, o, first_at(self.here, o))
            self.numbers.append(
                [self.wires.send(spot, spot, first_device(self.here, o, by)) for by in OFFSETS]
            )

    def turn(self):
        lines = []
        for o in (0, 1):
            for at, by in zip(self.numbers[o], OFFSETS):
                back = first_at(self.here, o, 4 - by)
                self.wires.landed(at, spot_of(self.whole, self.here, o, back))
            spot = run_of(self.whole, self.here, o, 0)
            lines.append(
                [self.wires.send(spot, spot, second_device(self.here, o, by)) for by in OFFSETS]
            )
        self.numbers = lines

    def finish(self):
        for o in (0, 1):
            for at, by in zip(self.numbers[o], OFFSETS):
                self.wires.landed(at, run_of(self.whole, self.here, o, 4 - by))


class PlaneSum:
    def __init__(self, wires, terms, buffers, here, local_sem, at):
        self.wires, self.terms, self.here, self.numbers = wires, terms, here, {}
        self.far, self.joined, self.rec, self.total, self.rec_two, self.fin = buffers
        self.kept, self.added = [], []
        for o in (0, 1):
            self.kept.append(
                pltpu.make_async_copy(
                    run_of(terms, here, o, 0), self.total.at[o], local_sem.at[at + 3 * o]
                )
            )
            self.added.append(
                [
                    pltpu.make_async_copy(
                        run_of(terms, here, o, by, sub),
                        self.joined.at[o, sub],
                        local_sem.at[at + 3 * o + 1 + sub],
                    )
                    for sub, by in enumerate((1, 3))
                ]
            )

    def send(self, key, src, dst, target):
        if key not in self.numbers:
            self.numbers[key] = self.wires.reserve()
        self.wires.send(src, dst, target, at=self.numbers[key])

    def start(self, o):
        for sub, by in enumerate((1, 3)):
            self.send(
                ("far", o, sub),
                run_of(self.terms, self.here, o, 2, sub),
                self.far.at[o, sub],
                second_device(self.here, o, by),
            )
        for copy in self.added[o]:
            copy.start()
        self.kept[o].start()

    def direct(self, o):
        for sub, by in enumerate((1, 3)):
            self.send(
                ("direct", o, sub),
                run_of(self.terms, self.here, o, by, 1 - sub),
                half_of(self.rec.at[o, sub], 1 - sub),
                second_device(self.here, o, by),
            )

    def relay(self, o):
        for sub, by in enumerate((1, 3)):
            self.added[o][sub].wait()
            self.wires.landed(self.numbers["far", o, sub], self.far.at[o, sub])

            def add(i, carry):
                value = self.joined[o, sub, i].astype(F32) + self.far[o, sub, i].astype(F32)
                self.joined[o, sub, i] = value.astype(BF)
                return carry

            lax.fori_loop(0, 4, add, 0)
            self.send(
                ("passed", o, sub),
                self.joined.at[o, sub],
                half_of(self.rec.at[o, sub], sub),
                second_device(self.here, o, by),
            )

    def middle(self, o):
        self.kept[o].wait()
        for sub in (0, 1):
            rec = self.rec.at[o, sub]
            self.wires.landed(self.numbers["direct", o, sub], half_of(rec, 1 - sub))
            self.wires.landed(self.numbers["passed", o, sub], half_of(rec, sub))

        def add(i, carry):
            value = self.total[o, i].astype(F32)
            for sub in (0, 1):
                value = value + self.rec[o, sub, i].astype(F32)
            self.total[o, i] = value.astype(BF)
            return carry

        lax.fori_loop(0, 4, add, 0)
        for k, by in enumerate(OFFSETS):
            self.send(
                ("last", o, k),
                self.total.at[o, first_at(self.here, o, by)],
                self.rec_two.at[o, k],
                first_device(self.here, o, by),
            )

    def finish(self, o):
        value = self.total[o, first_at(self.here, o)].astype(F32)
        for k in range(3):
            self.wires.landed(self.numbers["last", o, k], self.rec_two.at[o, k])
            value = value + self.rec_two[o, k].astype(F32)
        self.fin[o] = value.astype(self.fin.dtype)

    def leave(self):
        for o in (0, 1):
            for sub in (0, 1):
                self.wires.left(self.numbers["far", o, sub], self.far.at[o, sub])
                self.wires.left(self.numbers["passed", o, sub], self.joined.at[o, sub])
                half = half_of(self.rec.at[o, sub], 1 - sub)
                self.wires.left(self.numbers["direct", o, sub], half)
            for k in range(3):
                self.wires.left(self.numbers["last", o, k], self.rec_two.at[o, k])


def run_bulk(members, steps):
    for step in steps:
        for o in (0, 1):
            for member in members:
                getattr(member, step)(o)


def half_of(line, sub):
    if len(line.shape) == 4:
        return line.at[:, sub]
    rows = line.shape[1] // 2
    return line.at[:, pl.ds(sub * rows, rows)]


def sum_buffers(piece, kind):
    half = piece[1:] if len(piece) == 3 else (piece[0] // 2,) + piece[1:]
    return [
        pltpu.VMEM((2, 2, 4) + half, BF),
        pltpu.VMEM((2, 2, 4) + half, BF),
        pltpu.VMEM((2, 2, 4) + piece, BF),
        pltpu.VMEM((2, 4) + piece, BF),
        pltpu.VMEM((2, 3) + piece, BF),
        pltpu.VMEM((2,) + piece, kind),
    ]


class OutGather:
    def __init__(self, wires, stage, whole, here, mine, send_sem, recv_sem, local_sem, at):
        z, y, x, c = here
        self.wires, self.stage, self.whole, self.here = wires, stage, whole, here
        self.off = lax.rem(z - mine + 4, 4)
        self.recv_sem = recv_sem
        spot = whole.at[y]
        self.kept = pltpu.make_async_copy(stage, spot, local_sem.at[at])

        def copy(k, src, dst, by):
            return pltpu.make_async_remote_copy(
                src_ref=src,
                dst_ref=dst,
                send_sem=send_sem.at[k],
                recv_sem=recv_sem.at[k],
                device_id=device(z + by, y, x, c),
                device_id_type=MESH,
            )

        self.first = [copy(0, stage, spot, 1), copy(1, stage, spot, 3)]
        self.onward = [
            copy(2, spot.at[0], spot.at[0], 1),
            copy(3, spot.at[1], spot.at[1], 3),
        ]

    def landed(self, k, region):
        pltpu.make_async_copy(region, region, self.recv_sem.at[k]).wait()

    def start(self):
        @pl.when(self.off == 0)
        def _():
            self.kept.start()
            for copy in self.first:
                copy.start()

    def relay(self):
        spot = self.whole.at[self.here[1]]
        for k, off in ((0, 1), (1, 3)):

            @pl.when(self.off == off)
            def _():
                self.landed(k, spot)
                self.onward[k].start()

    def turn(self):
        z, y, x, c = self.here
        spot = self.whole.at[y]

        @pl.when(self.off == 0)
        def _():
            self.kept.wait()

        @pl.when(self.off == 2)
        def _():
            self.landed(2, spot.at[0])
            self.landed(3, spot.at[1])

        self.numbers = [self.wires.send(spot, spot, device(z, y + by, x, c)) for by in (1, 3)]

    def relay_two(self):
        z, y, x, c = self.here
        relays = []
        for sub, by in enumerate((1, 3)):
            spot = self.whole.at[lax.rem(y + 4 - by, 4)]
            self.wires.landed(self.numbers[sub], spot)
            relays.append(
                self.wires.send(spot.at[sub], spot.at[sub], device(z, y + by, x, c))
            )
        self.numbers = relays

    def finish(self):
        spot = self.whole.at[lax.rem(self.here[1] + 2, 4)]
        for sub in (0, 1):
            self.wires.landed(self.numbers[sub], spot.at[sub])

        @pl.when(self.off == 0)
        def _():
            for copy in self.first:
                copy.wait_send()

        for k, off in ((0, 1), (1, 3)):

            @pl.when(self.off == off)
            def _():
                self.onward[k].wait_send()


class OutSum:
    def __init__(self, wires, terms, buffers, piece, here, mine, quad, sems, local_sem, at):
        self.wires, self.terms, self.here, self.mine, self.quad = wires, terms, here, mine, quad
        self.rec, self.total, self.rec_two = buffers
        self.piece, self.local_sem, self.at = piece, local_sem, at
        self.send_sem, self.recv_sem = sems
        self.off = lax.rem(here[0] - mine + 4, 4)
        self.kept = pltpu.make_async_copy(
            terms.at[here[1]], self.total, local_sem.at[at]
        )

    def start(self):
        z, y, x, c = self.here
        self.kept.start()
        self.numbers = [
            self.wires.send(
                self.terms.at[lax.rem(y + by, 4)], self.rec.at[k], device(z, y + by, x, c)
            )
            for k, by in enumerate(OFFSETS)
        ]

    def copy(self, k, src, dst, target):
        return pltpu.make_async_remote_copy(
            src_ref=src,
            dst_ref=dst,
            send_sem=self.send_sem.at[k],
            recv_sem=self.recv_sem.at[k],
            device_id=target,
            device_id_type=MESH,
        )

    def middle(self):
        z, y, x, c = self.here
        self.kept.wait()
        value = self.total[...].astype(F32)
        for k in range(3):
            self.wires.landed(self.numbers[k], self.rec.at[k])
            value = value + self.rec[k].astype(F32)
        self.total[...] = value.astype(BF)
        self.moves = []
        for off in (1, 2, 3):
            move = self.copy(
                off - 1, self.total, self.rec_two.at[off - 1], device(self.mine, y, x, c)
            )
            self.moves.append(move)

            @pl.when(self.off == off)
            def _():
                move.start()

    def deal(self):
        z, y, x, c = self.here
        self.deals = []
        xl = lax.rem(x, 2)
        for k, (a, b) in enumerate(self.quad):
            self.deals.append(
                self.copy(
                    3 + k, self.total.at[lax.rem(a, 2), :, col_span(b)], self.piece, device(z, y, a, b)
                )
            )

        @pl.when(self.off == 0)
        def _():
            value = self.total[...].astype(F32)
            for k in range(3):
                region = self.rec_two.at[k]
                pltpu.make_async_copy(region, region, self.recv_sem.at[k]).wait()
                value = value + self.rec_two[k].astype(F32)
            self.total[...] = value.astype(BF)
            for copy in self.deals:
                copy.start()
            own = pltpu.make_async_copy(
                self.total.at[xl, :, col_span(c)], self.piece, self.local_sem.at[self.at]
            )
            own.start()
            own.wait()

    def finish(self):
        z, y, x, c = self.here
        xl = lax.rem(x, 2)
        holder_xl, holder_c = z // 2, lax.rem(z, 2)
        for k, (dx, dc) in enumerate(((0, 1), (1, 0), (1, 1))):

            @pl.when(
                (holder_xl == lax.rem(xl + dx, 2)) & (holder_c == lax.rem(c + dc, 2))
            )
            def _():
                pltpu.make_async_copy(self.piece, self.piece, self.recv_sem.at[3 + k]).wait()

        for off in (1, 2, 3):

            @pl.when(self.off == off)
            def _():
                self.moves[off - 1].wait_send()

        @pl.when(self.off == 0)
        def _():
            for copy in self.deals:
                copy.wait_send()


def quad_of(xl, xh, x, c):
    pair = xh * 2 + 1 - xl
    return [(x, 1 - c), (pair, c), (pair, 1 - c)]


def norm_back(wires, values, scale, gain_row, incoming, mine, theirs, here):
    weighted = incoming * gain_row
    inner = both_cores(
        wires, mine, theirs, jnp.sum(weighted * values, axis=1, keepdims=True), here
    )
    inner = inner / D
    back = scale * (incoming * gain_row) - values * (scale * scale * scale * inner)
    return back, jnp.sum(incoming * values * scale, axis=0, keepdims=True)


PLANE = [(a, b) for a in range(4) for b in range(4) if a or b]


def key_at(half):
    at = half // 2
    return lax.rem(half, 2), at // 4, lax.rem(at, 4)


def ends_of(lengths):
    ends = [lengths[0]]
    for k in range(1, 4):
        ends.append(ends[-1] + lengths[k])
    return ends


def allowed_pairs(key_half, query_half, ends):
    keys = key_half * HALF + lax.broadcasted_iota(jnp.int32, (HALF, HALF), 0)
    queries = query_half * HALF + lax.broadcasted_iota(jnp.int32, (HALF, HALF), 1)
    same = keys <= queries
    for k in range(3):
        same = same & ((keys >= ends[k]) == (queries >= ends[k]))
    return same


def in_second(query_half, ends):
    queries = query_half * HALF + lax.broadcasted_iota(jnp.int32, (1, HALF), 1)
    return (queries >= ends[0]) & (queries < ends[1])


class Tour:
    def __init__(self, spot, order):
        self.spot, self.order = spot, order
        halves = [2 * spot, HALVES - 1 - 2 * spot]
        self.first, self.last = halves[order[0]], halves[order[1]]
        self.turn = self.first + 1

    def half(self, s):
        return jnp.where(s == 0, 2 * self.spot, HALVES - 1 - 2 * self.spot)

    def run(self, step, between, start, stop):
        def body(t, carry):
            late = t >= self.turn

            @pl.when(t == self.turn)
            def _():
                between()

            half = jnp.where(late, self.last, self.first)
            s = jnp.where(late, self.order[1], self.order[0])
            u = t - jnp.where(late, self.turn, 0)
            inner = jnp.maximum(half - 1, 0)

            @pl.when(u < inner)
            def _():
                step(s, 1 + u, False)

            @pl.when(u >= inner)
            def _():
                step(s, (u - inner) * half, True)

            return carry

        lax.fori_loop(start, stop, body, 0)


def head_cols(g):
    return slice(g * HALF, (g + 1) * HALF)


def rope(columns, at, cosine, sine):
    first = columns[at : at + HD // 2]
    second = columns[at + HD // 2 : at + HD]
    return first * cosine - second * sine, second * cosine + first * sine


def forward_kernel(
    lengths, inverse, block_input, qkv_weight, gate_up_weight, down_weight, out_weight, gains, out_grad,
    cosine, sine, scale_one, normed_out, qkv_out, queries, mixed_out, log_out, attended_out, keys_out,
    cotangent_all, out_out, gate_all, up_all, down_all, middle_out, scale_two, out,
    qkv_in, gate_in, up_in, down_in, out_in, gain_rows,
    inputs_all, gains_all, qkv_all, normed, columns, across_queries, attended_here, across,
    keys, tops, sums, mixed,
    attended, out_stage, out_all, part, folded, leaving, arriving, total, mine_row, their_row, own,
    send_sem, recv_sem, stage_send, stage_recv, out_send, out_recv, local_sem,
):
    z, y, xl, xh, c = place()
    x = xh * 2 + xl
    here = (z, y, x, c)
    mine = xl * 2 + c
    quad = quad_of(xl, xh, x, c)
    opposite = device(3 - z, 3 - y, x, c)
    greet(
        line_targets(z, y, x, c)
        + [device(z, y, *quad[2]), opposite]
        + plane_targets(z, y, x, c)
    )
    wires = Wires(send_sem, recv_sem)
    kept = {}

    def keep(name, src, dst):
        copy = pltpu.make_async_copy(src, dst, local_sem.at[len(kept)])
        copy.start()
        kept[name] = copy

    def swap(given, whole):
        numbers = [
            wires.send(
                given.at[lax.rem(to, 2) * 2 + core], whole.at[c, z, y, xl], device(z, y, to, core)
            )
            for to, core in quad
        ]
        return numbers

    def swapped(numbers, whole):
        for at, (from_x, from_c) in zip(numbers, quad):
            wires.landed(at, whole.at[from_c, z, y, lax.rem(from_x, 2)])

    keep("inputs", block_input, inputs_all.at[row_span(x), col_span(c)])
    input_numbers = gather_sends(wires, block_input, inputs_all, here)
    for k in range(4):
        qkv_in[k] = qkv_weight[:, k, :].astype(BF)
    qkv_swap = swap(qkv_in, qkv_all)
    qkv_all[c, z, y, xl] = qkv_in[mine]
    gain_rows[...] = jnp.zeros(gain_rows.shape, F32)
    gain_rows[0:2, :] = gains[...]
    gains_all[:, col_span(c)] = gain_rows[...]
    gain_at = wires.send(gain_rows, gains_all.at[:, col_span(c)], device(z, y, x, 1 - c))
    for k in (0, 1):
        down_in[k] = down_weight[k * 2 * PIECE : (k + 1) * 2 * PIECE, :].astype(BF)
    keep("down", down_in.at[c], down_all.at[z, y, :, col_span(c)])
    down_swap = wires.send(
        down_in.at[1 - c], down_all.at[z, y, :, col_span(c)], device(z, y, x, 1 - c)
    )
    out_in[...] = out_weight[...].astype(BF)
    holds = z == mine
    stage_spot = out_stage.at[xl, :, col_span(c)]
    stage_copy = pltpu.make_async_remote_copy(
        src_ref=out_in,
        dst_ref=stage_spot,
        send_sem=stage_send.at[0],
        recv_sem=stage_recv.at[mine],
        device_id=device(z, y, xh * 2 + z // 2, lax.rem(z, 2)),
        device_id_type=MESH,
    )

    @pl.when(jnp.logical_not(holds))
    def _():
        stage_copy.start()

    @pl.when(holds)
    def _():
        pltpu.make_async_copy(out_in, stage_spot, stage_recv.at[mine]).start()

    qkv = DirectGather(wires, qkv_all, here)
    pairs_gather = DirectGather(wires, keys, here)
    gate = PlaneGather(wires, gate_all, here)
    up = PlaneGather(wires, up_all, here)
    down = PlaneGather(wires, down_all, here)
    bulk = (gate, up, down)
    out_gather = OutGather(
        wires, out_stage, out_all, here, mine, out_send, out_recv, local_sem, 12
    )

    def down_ready():
        wires.landed(down_swap, down_all.at[z, y, :, col_span(1 - c)])
        kept["down"].wait()

    swapped(qkv_swap, qkv_all)
    qkv.start()
    down_ready()
    run_bulk((down,), ('start',))
    left = lax.broadcasted_iota(jnp.int32, (PIECE, 2 * HD), 1) < HD
    for u, dealt in enumerate((gate_in, up_in)):
        for side in (0, 1):
            for j in range(HIDDEN // (2 * HD)):
                cols = slice(j * 2 * HD, (j + 1) * 2 * HD)
                even, odd = (
                    gate_up_weight[:, u, ((2 * j + i) * 2 + side) * 2 * HD :][:, : 2 * HD]
                    for i in (0, 1)
                )
                dealt[side * 2, :, cols] = jnp.where(left, even, pltpu.roll(odd, HD, 1)).astype(BF)
                dealt[side * 2 + 1, :, cols] = jnp.where(
                    left, pltpu.roll(even, HD, 1), odd
                ).astype(BF)
    keep("gate", gate_in.at[mine], gate_all.at[c, z, y, xl])
    keep("up", up_in.at[mine], up_all.at[c, z, y, xl])
    gate_swap = swap(gate_in, gate_all)
    up_swap = swap(up_in, up_all)
    ends = ends_of(lengths)
    tokens = (z * 4 + y) * LINE + lax.broadcasted_iota(jnp.int32, (HD // 2, LINE), 1)
    position = tokens
    for k in range(4):
        position = position - jnp.where(tokens >= ends[k], lengths[k], 0)
    angles = position.astype(F32) * inverse[:, :1]
    cosine[...] = jnp.cos(angles)
    sine[...] = jnp.sin(angles)
    input_relays = gather_hand(wires, input_numbers, inputs_all, here)
    qkv.turn()
    run_bulk((down,), ('relay',))
    gather_take(wires, input_numbers, input_relays, inputs_all, here)
    kept["inputs"].wait()
    wires.landed(gain_at, gains_all.at[:, col_span(1 - c)])
    gain_one = gains_all[0:1, :]

    def norm_rows(i, carry):
        rows = pl.ds(pl.multiple_of(i * ROWS, ROWS), ROWS)
        values = inputs_all[rows, :].astype(F32)
        scale = lax.rsqrt(jnp.sum(values * values, axis=1, keepdims=True) / D + NORM_EPS)
        normed[rows, :] = (values * scale * gain_one).astype(BF)

        @pl.when(i == rows_of(x))
        def _():
            scale_one[...] = jnp.broadcast_to(scale, scale_one.shape)

        return carry

    lax.fori_loop(0, 4, norm_rows, 0)
    keep("normed", normed, normed_out)
    swapped(gate_swap, gate_all)
    swapped(up_swap, up_all)
    for name in ("gate", "up"):
        kept[name].wait()
    run_bulk((gate, up), ('start',))
    qkv.finish()
    keep("qkv_out", qkv_all, qkv_out)
    weight = qkv_all[...].reshape(D, columns.shape[0])

    def project(cols):
        def body(i, carry):
            rows = pl.ds(pl.multiple_of(i * ROWS, ROWS), ROWS)
            product = jnp.dot(normed[rows, :], weight[:, cols], preferred_element_type=F32)
            columns[cols, rows] = product.T
            return carry

        lax.fori_loop(0, 4, body, 0)

    project(slice(GROUP * HD, (GROUP + 2) * HD))
    first, second = rope(columns, GROUP * HD, cosine[...], sine[...])
    pair_columns = jnp.concatenate([first, second, columns[(GROUP + 1) * HD :]], axis=0)
    for s in (0, 1):
        keys[s, z, y] = pair_columns[:, s * HALF : (s + 1) * HALF].T.astype(BF)

    pairs_gather.start()
    project(slice(0, GROUP * HD))
    queries[:, HD:, :] = jnp.zeros((2, HD, GROUP * HALF), BF)
    for g in range(GROUP):
        turned = rope(columns, g * HD, cosine[...], sine[...])
        for i, value in enumerate(turned):
            rows = slice(i * (HD // 2), (i + 1) * (HD // 2))
            value = (value * HD ** (-0.5)).astype(BF)
            queries[0, rows, head_cols(g)] = value[:, :HALF]
            across_queries[rows, head_cols(g)] = value[:, HALF:]
    query_at = wires.send(across_queries, queries.at[1, pl.ds(0, HD)], opposite)
    pairs_gather.turn()
    run_bulk((gate, up), ('relay',))

    @pl.when(holds)
    def _():
        for k in range(4):
            spot = out_stage.at[k // 2, :, pl.ds((k % 2) * WIDTH, WIDTH)]
            pltpu.make_async_copy(spot, spot, stage_recv.at[k]).wait()

    out_gather.start()
    keep("cotangent", out_grad, cotangent_all.at[row_span(x), col_span(c)])
    cotangent_numbers = gather_sends(wires, out_grad, cotangent_all, here)
    pairs_gather.finish()
    keep("keys", keys, keys_out)
    out_gather.relay()
    run_bulk((gate,), ('turn',))

    wires.landed(query_at, queries.at[1, pl.ds(0, HD)])
    tour = Tour(z * 4 + y, (1, 0))
    tops[...] = jnp.full(tops.shape, NEVER, F32)
    sums[...] = jnp.zeros(sums.shape, F32)
    mixed[...] = jnp.zeros(mixed.shape, F32)
    heads = range(GROUP)

    def step(s, at, masked):
        pairs = keys[key_at(at)]
        old = [tops[s, :, head_cols(g)] for g in heads]
        old_sums = [sums[s, :, head_cols(g)] for g in heads]
        scores = [
            jnp.dot(pairs, queries[s, :, head_cols(g)], preferred_element_type=F32) for g in heads
        ]
        if masked:
            counts = in_second(tour.half(s), ends) | (at > 0)
            old = [jnp.where(counts, value, NEVER) for value in old]
            old_sums = [jnp.where(counts, value, 0.0) for value in old_sums]
            allowed = allowed_pairs(at, tour.half(s), ends)
            scores = [jnp.where(allowed, value, NEVER) for value in scores]
        top = [jnp.maximum(old[g], jnp.max(scores[g], axis=0, keepdims=True)) for g in heads]
        weights = [jnp.exp(scores[g] - top[g]) for g in heads]
        if masked:
            weights = [jnp.where(allowed, value, 0.0) for value in weights]
        shrink = [jnp.exp(old[g] - top[g]) for g in heads]
        if masked:
            shrink = [jnp.where(counts, value, 0.0) for value in shrink]
        new_sums = [
            old_sums[g] * shrink[g] + jnp.sum(weights[g], axis=0, keepdims=True) for g in heads
        ]
        new = [
            lax.dot_general(
                pairs, weights[g].astype(BF), (((0,), (0,)), ((), ())), preferred_element_type=F32
            )
            for g in heads
        ]
        for g in heads:
            cols = head_cols(g)
            tops[s, :, cols] = top[g]
            sums[s, :, cols] = new_sums[g]
            mixed[s, :, cols] = mixed[s, :, cols] * shrink[g] + new[g]

    def settle(s, rows):
        log_out[s] = tops[s] + jnp.log(sums[s])
        mixed_out[s] = mixed[s, HD:, :] / sums[s]
        for g in heads:
            rows[g * HD : (g + 1) * HD, :] = mixed_out[s, :, head_cols(g)].astype(BF)

    across_at = wires.send(attended_here, across, opposite, start=False)

    def between():
        settle(1, attended_here)
        wires.sent[across_at].start()

    tour.run(step, between, 0, 5)
    out_gather.turn()
    tour.run(step, between, 5, 9)
    gather_relay(wires, cotangent_numbers, cotangent_all, here)
    run_bulk((up,), ('turn',))
    tour.run(step, between, 9, 17)
    out_gather.relay_two()
    run_bulk((gate,), ('relay_two',))
    tour.run(step, between, 17, 21)
    tour.run(step, between, 21, 27)
    run_bulk((down,), ('turn',))
    tour.run(step, between, 27, 33)
    run_bulk((up,), ('relay_two',))
    settle(0, attended_out.at[:, pl.ds(0, HALF)])
    wires.landed(across_at, across)
    attended_out[:, HALF:] = across[...]
    for g in range(0, GROUP, 2):
        rows = slice(g * HD, (g + 2) * HD)
        attended[:, rows] = attended_out[rows, :].astype(F32).T.astype(BF)

    out_gather.finish()
    keep("out", out_all, out_out)
    out_low = out_all[...].reshape(GROUP * HD, D)
    fold_numbers = []
    for k, o in enumerate(FOLD_ORDER):
        rows = row_span(lax.rem(x + o, 4))
        part[rows, :] = jnp.dot(
            attended[rows, :], out_low, preferred_element_type=F32
        ).astype(BF)
        fold_numbers.append(
            wires.send(part.at[rows, col_span(1 - c)], folded.at[k], device(z, y, x, 1 - c))
        )
    moves = fold_moves(
        wires, fold_numbers, part, folded, leaving, arriving, here, total, col_span(c)
    )
    fold_finish(wires, moves, arriving, total)
    run_bulk((down,), ('relay_two',))
    middle = total[...] + block_input[...].astype(F32)
    middle_out[...] = middle
    square = both_cores(
        wires, mine_row, their_row, jnp.sum(middle * middle, axis=1, keepdims=True), here
    )
    scale = lax.rsqrt(square / D + NORM_EPS)
    scale_two[...] = jnp.broadcast_to(scale, scale_two.shape)
    own[...] = (
        middle_out[...] * scale * gains_all[1:2, col_span(c)]
    ).astype(BF)
    keep("own", own, out.at[row_span(x), col_span(c)])
    sends = gather_sends(wires, own, out, here)
    gather_relay(wires, sends, out, here)
    run_bulk(bulk, ('finish',))
    for member in bulk:
        member.leave()
    for name in ("normed", "qkv_out", "cotangent", "keys", "out", "own"):
        kept[name].wait()

    @pl.when(jnp.logical_not(holds))
    def _():
        stage_copy.wait_send()

    wires.close()


def call_forward(*operands):
    vm = pl.BlockSpec(memory_space=pltpu.VMEM)
    hbm = pl.BlockSpec(memory_space=ANY)
    cols = GROUP * HALF
    qkv_cols = (GROUP + 2) * HD
    share = (ROWS, WIDTH)
    whole = (2, 4, 4, 2, PIECE)
    outs = [
        ((HD // 2, LINE), F32, vm),
        ((HD // 2, LINE), F32, vm),
        ((ROWS, 128), F32, vm),
        ((LINE, D), BF, hbm),
        (whole + (qkv_cols,), BF, hbm),
        ((2, 2 * HD, cols), BF, vm),
        ((2, HD, cols), F32, vm),
        ((2, 1, cols), F32, vm),
        ((GROUP * HD, LINE), BF, vm),
        ((2, 4, 4, HALF, 2 * HD), BF, hbm),
        ((LINE, D), BF, hbm),
        ((4, 2, PIECE, D), BF, hbm),
        (whole + (HIDDEN,), BF, hbm),
        (whole + (HIDDEN,), BF, hbm),
        ((4, 4, 2 * PIECE, D), BF, hbm),
        (share, F32, vm),
        ((ROWS, 128), F32, vm),
        ((LINE, D), BF, hbm),
    ]
    return pl.pallas_call(
        forward_kernel,
        out_shape=tuple(jax.ShapeDtypeStruct(shape, kind) for shape, kind, _ in outs),
        in_specs=[pl.BlockSpec(memory_space=pltpu.SMEM)] + [vm] * 7 + [hbm],
        out_specs=tuple(spec for _, _, spec in outs),
        scratch_shapes=[
            pltpu.VMEM((4, PIECE, qkv_cols), BF),
            pltpu.VMEM((4, PIECE, HIDDEN), BF),
            pltpu.VMEM((4, PIECE, HIDDEN), BF),
            pltpu.VMEM((2, ROWS // 2, WIDTH), BF),
            pltpu.VMEM((PIECE, WIDTH), BF),
            pltpu.VMEM((8, WIDTH), F32),
            pltpu.VMEM((LINE, D), BF),
            pltpu.VMEM((8, D), F32),
            pltpu.VMEM(whole + (qkv_cols,), BF),
            pltpu.VMEM((LINE, D), BF),
            pltpu.VMEM((qkv_cols, LINE), F32),
            pltpu.VMEM((HD, cols), BF),
            pltpu.VMEM((GROUP * HD, HALF), BF),
            pltpu.VMEM((GROUP * HD, HALF), BF),
            pltpu.VMEM((2, 4, 4, HALF, 2 * HD), BF),
            pltpu.VMEM((2, 1, cols), F32),
            pltpu.VMEM((2, 1, cols), F32),
            pltpu.VMEM((2, 2 * HD, cols), F32),
            pltpu.VMEM((LINE, GROUP * HD), BF),
            pltpu.VMEM((2, PIECE, D), BF),
            pltpu.VMEM((4, 2, PIECE, D), BF),
            pltpu.VMEM((LINE, D), BF),
        ]
        + fold_scratch()
        + [
            pltpu.VMEM((ROWS, 128), F32),
            pltpu.VMEM((ROWS, 128), F32),
            pltpu.VMEM((ROWS, WIDTH), BF),
        ]
        + wire_scratch(144)
        + wire_scratch(4)
        + wire_scratch(4)
        + [pltpu.SemaphoreType.DMA((13,))],
        compiler_params=comm_params(1),
        name="forward",
    )(*operands)


def backward_kernel(
    lengths, cosine, sine, part, output_part, middle, scale_two, scale_one, gains, inputs, cotangent,
    queries, mixed, logs, attended, keys, out_low, qkv_low, normed, grad_down, grad_up, grad_gate,
    input_grad, output, qkv_grad, gate_up_grad, down_grad, out_grad, totals,
    q_out, kv_out, gate_out, up_out, down_out, out_out, across_grads, across_back, across,
    middle_all, grads, delta, query_rows, grad_rows, out_terms,
    terms, sums, rounded, columns, rows_back, q_terms, kv_terms, key_rec, key_sums, key_rec_two,
    *rest,
):
    rest = list(rest)

    def take(count):
        taken = rest[:count]
        del rest[:count]
        return taken

    first_fold, output_fold, (part_own, output_own) = take(4), take(4), take(2)
    last_fold = first_fold
    first_rows, last_rows, (own,) = take(2), take(2), take(1)
    down_buffers, up_buffers, gate_buffers = take(6), take(6), take(6)
    q_buffers, kv_buffers = take(6), take(6)
    out_buffers, (total_terms, stage, rec_one, rec_two) = take(3), take(4)
    send_sem, recv_sem, out_send, out_recv, local_sem = rest
    z, y, xl, xh, c = place()
    x = xh * 2 + xl
    here = (z, y, x, c)
    mine = xl * 2 + c
    quad = quad_of(xl, xh, x, c)
    line = [(o, b) for b in (0, 1) for o in range(4) if o or b]
    fixed = [device(z + a, y + b, x, c) for a, b in PLANE]
    fixed += [device(z, y, lax.rem(x + o, 4), lax.rem(c + b, 2)) for o, b in line]
    opposite = device(3 - z, 3 - y, x, c)
    greet(fixed)
    wires = Wires(send_sem, recv_sem)
    kept = []

    def keep(src, dst):
        copy = pltpu.make_async_copy(src, dst, local_sem.at[31 + len(kept)])
        copy.start()
        kept.append(copy)

    def deal(fin, result):
        keep(fin.at[c, xl], result.at[mine])
        return [
            wires.send(fin.at[b, lax.rem(a, 2)], result.at[mine], device(z, y, a, b))
            for a, b in quad
        ]

    def dealt(numbers, result):
        for at, (a, b) in zip(numbers, quad):
            wires.landed(at, result.at[lax.rem(a, 2) * 2 + b])

    numbers = fold_sends(wires, part, first_fold[0], here)
    own_parts = [
        pltpu.make_async_copy(part.at[:, col_span(c)], part_own, local_sem.at[42]),
        pltpu.make_async_copy(output_part.at[:, col_span(c)], output_own, local_sem.at[43]),
        pltpu.make_async_copy(out_low, out_terms, local_sem.at[44]),
        pltpu.make_async_copy(
            qkv_low.at[:, :, :, :, :, pl.ds(0, GROUP * HD)], q_terms, local_sem.at[45]
        ),
        pltpu.make_async_copy(
            qkv_low.at[:, :, :, :, :, pl.ds(GROUP * HD, 2 * HD)], kv_terms, local_sem.at[48]
        ),
    ]
    for copy in own_parts:
        copy.start()
    down = PlaneSum(wires, grad_down, down_buffers, here, local_sem, 0)
    up = PlaneSum(wires, grad_up, up_buffers, here, local_sem, 6)
    gate = PlaneSum(wires, grad_gate, gate_buffers, here, local_sem, 12)
    q_sum = PlaneSum(wires, q_terms, q_buffers, here, local_sem, 18)
    kv_sum = PlaneSum(wires, kv_terms, kv_buffers, here, local_sem, 24)
    out_sum = OutSum(
        wires, out_terms, out_buffers, out_out, here, mine, quad, (out_send, out_recv), local_sem, 30
    )
    bulk = (down, up, gate)
    in_turn(c, bulk, True)(*('start', 'direct'))
    own_parts[0].wait()
    moves = fold_moves(wires, numbers, part_own, *first_fold[:3], here, first_fold[3])
    in_turn(c, bulk, True)(*('relay',))
    fold_finish(wires, moves, first_fold[2], first_fold[3])
    back, gain_two = norm_back(
        wires, middle[...], scale_two[:, :1], gains[1:2, :], first_fold[3][...], *first_rows, here
    )
    grad = cotangent[...].astype(F32) + back
    input_grad[...] = grad
    own[...] = grad.astype(BF)
    keep(own, middle_all.at[row_span(x), col_span(c)])
    sends = gather_sends(wires, own, middle_all, here)
    for s in (0, 1):
        for g in range(GROUP):
            query_rows[s, g] = queries[s, :, head_cols(g)].astype(F32).T.astype(BF)
    grads[:, :HD, :] = jnp.zeros((2, HD, GROUP * HALF), BF)
    terms[...] = jnp.zeros(terms.shape, F32)
    sums[...] = jnp.zeros(sums.shape, F32)
    relayed = gather_relay(wires, sends, middle_all, here)
    in_turn(c, bulk, True)(*('middle',))
    in_turn(c, bulk, False)(*('start', 'direct'))
    kept[0].wait()

    own_parts[2].wait()
    shared = out_terms[...].reshape(GROUP * HD, D)

    def attended_rows(i, carry):
        rows = pl.ds(pl.multiple_of(i * ROWS, ROWS), ROWS)
        value = lax.dot_general(
            middle_all[rows, :], shared, (((1,), (1,)), ((), ())), preferred_element_type=F32
        )
        columns[: GROUP * HD, rows] = value.astype(BF).astype(F32).T
        return carry

    lax.fori_loop(0, 4, attended_rows, 0)
    for g in range(GROUP):
        rows = slice(g * HD, (g + 1) * HD)
        grads[0, HD:, head_cols(g)] = columns[rows, :HALF].astype(BF)
        across_grads[:, head_cols(g)] = columns[rows, HALF:].astype(BF)
    grad_at = wires.send(across_grads, grads.at[1, pl.ds(HD, HD)], opposite)

    def prepare(s):
        for g in range(GROUP):
            cols = head_cols(g)
            value = grads[s, :, cols].astype(F32)
            delta[s, :, cols] = jnp.sum(value[HD:] * mixed[s, :, cols], axis=0, keepdims=True)
            grad_rows[s, g] = value.T.astype(BF)

    prepare(0)

    def out_columns(i, carry):
        cols = pl.ds(pl.multiple_of(i * HALF, HALF), HALF)
        value = jnp.dot(attended[...], middle_all[:, cols], preferred_element_type=F32)
        out_terms[:, :, :, cols] = value.astype(BF).reshape(4, 2, PIECE, HALF)
        return carry

    lax.fori_loop(0, D // HALF, out_columns, 0)
    out_sum.start()
    output_numbers = fold_sends(wires, output_part, output_fold[0], here)

    ends = ends_of(lengths)
    tour = Tour(z * 4 + y, (0, 1))
    heads = range(GROUP)

    def step(s, at, masked):
        slot = key_at(at)
        pairs = keys[slot]
        query_columns = [queries[s, :, head_cols(g)] for g in heads]
        grad_columns = [grads[s, :, head_cols(g)] for g in heads]
        log_rows = [logs[s, :, head_cols(g)] for g in heads]
        deltas = [delta[s, :, head_cols(g)] for g in heads]
        rows = [query_rows[s, g] for g in heads]
        outer = [grad_rows[s, g] for g in heads]
        if not masked:
            fits = in_second(tour.half(s), ends)
            log_rows = [jnp.where(fits, value, -NEVER) for value in log_rows]
        scores = [jnp.dot(pairs, value, preferred_element_type=F32) for value in query_columns]
        prob_grads = [jnp.dot(pairs, value, preferred_element_type=F32) for value in grad_columns]
        probs = [jnp.exp(scores[g] - log_rows[g]) for g in heads]
        if masked:
            allowed = allowed_pairs(at, tour.half(s), ends)
            probs = [jnp.where(allowed, value, 0.0) for value in probs]
        score_grads = [(probs[g] * (prob_grads[g] - deltas[g])).astype(BF) for g in heads]
        probs_low = [value.astype(BF) for value in probs]
        back = [
            lax.dot_general(pairs, value, (((0,), (0,)), ((), ())), preferred_element_type=F32)
            for value in score_grads
        ]
        added = [
            jnp.dot(score_grads[g], rows[g], preferred_element_type=F32)
            + jnp.dot(probs_low[g], outer[g], preferred_element_type=F32)
            for g in heads
        ]
        terms[slot] += (added[0] + added[1]) + (added[2] + added[3])
        for g in heads:
            sums[s, :, head_cols(g)] += back[g]

    def between():
        wires.landed(grad_at, grads.at[1, pl.ds(HD, HD)])
        prepare(1)

    tour.run(step, between, 0, 4)
    in_turn(c, bulk, False)(*('relay',))
    tour.run(step, between, 4, 8)
    own_parts[1].wait()
    output_moves = fold_moves(
        wires, output_numbers, output_own, *output_fold[:3], here, output_fold[3]
    )
    out_sum.middle()
    tour.run(step, between, 8, 14)
    tour.run(step, between, 14, 20)
    fold_finish(wires, output_moves, output_fold[2], output_fold[3])
    output[...] = (middle[...] + output_fold[3][...]).astype(BF)
    normed_parts = [
        pltpu.make_async_copy(normed.at[:, pl.ds(n * WIDTH, WIDTH)], value, local_sem.at[46 + n])
        for n, value in enumerate((part_own, output_own))
    ]
    for copy in normed_parts:
        copy.start()
    out_sum.deal()
    in_turn(c, bulk, True)(*('finish',))
    tour.run(step, between, 20, 26)
    in_turn(c, bulk, False)(*('middle',))
    tour.run(step, between, 26, 33)

    for s in (0, 1):
        for i in range(4):
            rounded[s, i] = terms[s, i].astype(BF)
    first = [[], []]
    for k, by in enumerate(OFFSETS):
        first[0].append(
            wires.send(
                rounded.at[0, :, lax.rem(y + by, 4)], key_rec.at[0, k], second_device(here, 0, by)
            )
        )
        first[1].append(
            wires.send(
                rounded.at[1, lax.rem(z + by, 4)], key_rec.at[1, k], second_device(here, 1, by)
            )
        )
    across_back[...] = (sums[1, :HD, :] * HD ** (-0.5)).astype(BF)
    back_at = wires.send(across_back, across, opposite)
    in_turn(c, bulk, False)(*('finish',))
    down_fin = down_buffers[5]
    down_swap = wires.send(
        down_fin.at[:, :, col_span(1 - c)], down_out.at[c], device(z, y, x, 1 - c)
    )
    keep(down_fin.at[:, :, col_span(c)], down_out.at[c])
    up_swap = deal(up_buffers[5], up_out)
    gate_swap = deal(gate_buffers[5], gate_out)

    second = [[], []]
    for s in (0, 1):
        for k in range(3):
            wires.landed(first[s][k], key_rec.at[s, k])
        for i in range(4):
            value = terms[0, i, y] if s == 0 else terms[1, z, i]
            for k in range(3):
                value = value + key_rec[s, k, i].astype(F32)
            key_sums[s, i] = value.astype(BF)
        for k, by in enumerate(OFFSETS):
            second[s].append(
                wires.send(
                    key_sums.at[s, first_at(here, s, by)],
                    key_rec_two.at[s, k],
                    first_device(here, s, by),
                )
            )
    def turn_back(values, tokens, scale):
        for g in range(GROUP):
            turned = rope(values.at[:, head_cols(g)], 0, cosine[:, tokens], -sine[:, tokens])
            for i, value in enumerate(turned):
                at = g * HD + i * (HD // 2)
                columns[at : at + HD // 2, tokens] = value * scale

    turn_back(sums.at[0], slice(0, HALF), HD ** (-0.5))
    wires.landed(back_at, across)
    turn_back(across, slice(HALF, LINE), 1.0)

    def take_rows(cols):
        for r in range(4):
            rows = slice(r * ROWS, (r + 1) * ROWS)
            rows_back[rows, cols] = columns[cols, rows].T.astype(BF)

    def weight_terms(cols, result):
        back_part = rows_back[:, cols]
        for n, half in enumerate((part_own, output_own)):

            def body(i, carry):
                at = pl.ds(pl.multiple_of(i * 256, 256), 256)
                value = lax.dot_general(
                    half[:, at], back_part, (((0,), (0,)), ((), ())), preferred_element_type=F32
                )
                result[n, i] = value.astype(BF).reshape(result.shape[2:])
                return carry

            lax.fori_loop(0, 4, body, 0)

    q_cols, kv_cols = slice(0, GROUP * HD), slice(GROUP * HD, (GROUP + 2) * HD)
    take_rows(q_cols)
    own_parts[3].wait()
    wires.settle(relayed)
    weight = q_terms[...].reshape(D, GROUP * HD)
    for r in range(4):
        rows = slice(r * ROWS, (r + 1) * ROWS)
        middle_all[rows, :] = lax.dot_general(
            rows_back[rows, q_cols], weight, (((1,), (1,)), ((), ())), preferred_element_type=F32
        ).astype(BF)
    for copy in normed_parts:
        copy.wait()
    weight_terms(q_cols, q_terms)
    run_bulk((q_sum,), ('start', 'direct'))
    for s in (0, 1):
        tokens = slice(s * HALF, (s + 1) * HALF)
        value = key_sums[s, first_at(here, s)].astype(F32)
        for k in range(3):
            wires.landed(second[s][k], key_rec_two.at[s, k])
            value = value + key_rec_two[s, k].astype(F32)
        pair_columns = value.T
        turned = rope(pair_columns, 0, cosine[:, tokens], -sine[:, tokens])
        for i, value in enumerate(turned):
            at = GROUP * HD + i * (HD // 2)
            columns[at : at + HD // 2, tokens] = value
        columns[(GROUP + 1) * HD :, tokens] = pair_columns[HD:]

    run_bulk((q_sum,), ('relay',))

    take_rows(kv_cols)
    own_parts[4].wait()
    weight = kv_terms[...].reshape(D, 2 * HD)
    last_numbers = []
    for k, o in enumerate(FOLD_ORDER):
        rows = row_span(lax.rem(x + o, 4))
        value = lax.dot_general(
            rows_back[rows, kv_cols], weight, (((1,), (1,)), ((), ())), preferred_element_type=F32
        )
        middle_all[rows, :] = (middle_all[rows, :].astype(F32) + value).astype(BF)
        last_numbers.append(
            wires.send(
                middle_all.at[rows, col_span(1 - c)], last_fold[0].at[k], device(z, y, x, 1 - c)
            )
        )
    weight_terms(kv_cols, kv_terms)
    run_bulk((kv_sum,), ('start', 'direct'))
    wires.settle(moves)
    last_moves = fold_moves(
        wires, last_numbers, middle_all, *last_fold[:3], here, last_fold[3], col_span(c)
    )

    run_bulk((kv_sum,), ('relay',))
    run_bulk((q_sum,), ('middle',))
    out_sum.finish()
    wires.landed(down_swap, down_out.at[1 - c])
    dealt(up_swap, up_out)
    dealt(gate_swap, gate_out)
    for copy in kept[1:]:
        copy.wait()
    left = lax.broadcasted_iota(jnp.int32, (PIECE, 2 * HD), 1) < HD
    squares = jnp.zeros((PIECE, 2 * HD), F32)
    for u, result in enumerate((gate_out, up_out)):
        for side in (0, 1):
            for j in range(HIDDEN // (2 * HD)):
                cols = slice(j * 2 * HD, (j + 1) * 2 * HD)
                one = result[side * 2, :, cols].astype(F32)
                two = result[side * 2 + 1, :, cols].astype(F32)
                squares = squares + one * one + two * two
                even = jnp.where(left, one, pltpu.roll(two, HD, 1))
                odd = jnp.where(left, pltpu.roll(one, HD, 1), two)
                for i, value in enumerate((even, odd)):
                    at = ((2 * j + i) * 2 + side) * 2 * HD
                    gate_up_grad[:, u, at : at + 2 * HD] = value
    square = jnp.sum(squares)
    for k in range(2):
        for o in range(2):
            value = down_out[k, o].astype(F32)
            down_grad[(2 * k + o) * PIECE : (2 * k + o + 1) * PIECE, :] = value
            square = square + jnp.sum(value * value)
    value = out_out[...].astype(F32)
    out_grad[...] = value
    square = square + jnp.sum(value * value)
    run_bulk((kv_sum,), ('middle',))
    run_bulk((q_sum,), ('finish',))
    q_swap = deal(q_buffers[5], q_out)
    fold_finish(wires, last_moves, last_fold[2], last_fold[3])
    back, gain_one = norm_back(
        wires,
        inputs[...].astype(F32),
        scale_one[:, :1],
        gains[0:1, :],
        last_fold[3][...],
        *last_rows,
        here,
    )
    input_grad[...] = input_grad[...] + back
    run_bulk((kv_sum,), ('finish',))
    kv_swap = deal(kv_buffers[5], kv_out)
    dealt(q_swap, q_out)
    dealt(kv_swap, kv_out)
    for copy in kept[-2:]:
        copy.wait()
    for k in range(4):
        for result, at in ((q_out, 0), (kv_out, GROUP * HD)):
            value = result[k].astype(F32)
            qkv_grad[:, k, at : at + value.shape[1]] = value
            square = square + jnp.sum(value * value)

    for k in range(8):
        cols = slice(k * 128, (k + 1) * 128)
        total_terms[k : k + 1] = gain_one[:, cols]
        total_terms[8 + k : 9 + k] = gain_two[:, cols]
    total_terms[16:] = jnp.broadcast_to(square, (8, 128))
    first = [
        wires.send(total_terms, rec_one.at[k], device(z + a, y + b, x, c))
        for k, (a, b) in enumerate(PLANE)
    ]
    value = total_terms[...]
    for k, at in enumerate(first):
        wires.landed(at, rec_one.at[k])
        value = value + rec_one[k]
    stage[...] = value
    second = [
        wires.send(stage, rec_two.at[k], device(z, y, lax.rem(x + o, 4), lax.rem(c + b, 2)))
        for k, (o, b) in enumerate(line)
    ]
    both = [value, None]
    for k, (o, b) in enumerate(line):
        wires.landed(second[k], rec_two.at[k])
        both[b] = rec_two[k] if both[b] is None else both[b] + rec_two[k]
    totals[:16] = both[0][:16]
    totals[16:] = (
        both[0][16:]
        + both[1][16:]
        + jnp.sum(both[0][:16] * both[0][:16])
        + jnp.sum(both[1][:16] * both[1][:16])
    )
    for member in bulk + (q_sum, kv_sum):
        member.leave()
    wires.close()


def call_backward(*operands):
    vm = pl.BlockSpec(memory_space=pltpu.VMEM)
    hbm = pl.BlockSpec(memory_space=ANY)
    cols = GROUP * HALF
    qkv_cols = (GROUP + 2) * HD
    share = (ROWS, WIDTH)
    outs = [
        (share, F32, vm),
        (share, BF, vm),
        ((PIECE, 4, qkv_cols), F32, vm),
        ((PIECE, 2, 4 * HIDDEN), F32, vm),
        (share, F32, vm),
        ((PIECE, WIDTH), F32, vm),
        ((24, 128), F32, vm),
    ]
    return pl.pallas_call(
        backward_kernel,
        out_shape=tuple(jax.ShapeDtypeStruct(shape, kind) for shape, kind, _ in outs),
        in_specs=[pl.BlockSpec(memory_space=pltpu.SMEM)] + [vm] * 2 + [hbm] * 2 + [vm] * 11 + [hbm] * 6,
        out_specs=tuple(spec for _, _, spec in outs),
        scratch_shapes=[
            pltpu.VMEM((4, PIECE, GROUP * HD), BF),
            pltpu.VMEM((4, PIECE, 2 * HD), BF),
            pltpu.VMEM((4, PIECE, HIDDEN), BF),
            pltpu.VMEM((4, PIECE, HIDDEN), BF),
            pltpu.VMEM((2, 2, PIECE, WIDTH), BF),
            pltpu.VMEM((PIECE, WIDTH), BF),
            pltpu.VMEM((HD, cols), BF),
            pltpu.VMEM((HD, cols), BF),
            pltpu.VMEM((HD, cols), BF),
            pltpu.VMEM((LINE, D), BF),
            pltpu.VMEM((2, 2 * HD, cols), BF),
            pltpu.VMEM((2, 1, cols), F32),
            pltpu.VMEM((2, GROUP, HALF, 2 * HD), BF),
            pltpu.VMEM((2, GROUP, HALF, 2 * HD), BF),
            pltpu.VMEM((4, 2, PIECE, D), BF),
            pltpu.VMEM((2, 4, 4, HALF, 2 * HD), F32),
            pltpu.VMEM((2, 2 * HD, cols), F32),
            pltpu.VMEM((2, 4, 4, HALF, 2 * HD), BF),
            pltpu.VMEM((qkv_cols, LINE), F32),
            pltpu.VMEM((LINE, qkv_cols), BF),
            pltpu.VMEM((2, 4, 4, 2, PIECE, GROUP * HD), BF),
            pltpu.VMEM((2, 4, 4, 2, PIECE, 2 * HD), BF),
            pltpu.VMEM((2, 3, 4, HALF, 2 * HD), BF),
            pltpu.VMEM((2, 4, HALF, 2 * HD), BF),
            pltpu.VMEM((2, 3, HALF, 2 * HD), BF),
        ]
        + fold_scratch() * 2
        + [pltpu.VMEM((LINE, WIDTH), BF)] * 2
        + [pltpu.VMEM((ROWS, 128), F32)] * 4
        + [pltpu.VMEM(share, BF)]
        + sum_buffers((PIECE, D), BF)
        + sum_buffers((2, PIECE, HIDDEN), BF) * 2
        + sum_buffers((2, PIECE, GROUP * HD), BF)
        + sum_buffers((2, PIECE, 2 * HD), BF)
        + [
            pltpu.VMEM((3, 2, PIECE, D), BF),
            pltpu.VMEM((2, PIECE, D), BF),
            pltpu.VMEM((3, 2, PIECE, D), BF),
            pltpu.VMEM((24, 128), F32),
            pltpu.VMEM((24, 128), F32),
            pltpu.VMEM((15, 24, 128), F32),
            pltpu.VMEM((7, 24, 128), F32),
        ]
        + wire_scratch(200)
        + wire_scratch(6)
        + [pltpu.SemaphoreType.DMA((49,))],
        compiler_params=comm_params(2),
        name="backward",
    )(*operands)


CHUNK = 512


def feed_kernel(
    normed_two, cotangent, gate_low, up_low, down_low,
    output_part, back_part, grad_gate, grad_up, grad_down, output_sum, back_sum,
):
    at = pl.program_id(0)

    @pl.when(at == 0)
    def _():
        output_sum[...] = jnp.zeros(output_sum.shape, F32)
        back_sum[...] = jnp.zeros(back_sum.shape, F32)

    inputs, incoming = normed_two[...], cotangent[...]
    gate = jnp.dot(inputs, gate_low[...], preferred_element_type=F32)
    up = jnp.dot(inputs, up_low[...], preferred_element_type=F32)
    hidden_grad = lax.dot_general(
        incoming, down_low[...], (((1,), (1,)), ((), ())), preferred_element_type=F32
    )
    sigmoid = jax.nn.sigmoid(gate)
    silu = gate * sigmoid
    hidden = (silu * up).astype(BF)
    gate_back = (hidden_grad * up * sigmoid * (1.0 + gate * (1.0 - sigmoid))).astype(BF)
    up_back = (hidden_grad * silu).astype(BF)
    both_back = jnp.concatenate([gate_back, up_back], axis=1)
    for k in range(4):
        cols = slice(k * D // 4, (k + 1) * D // 4)
        output_sum[:, cols] += jnp.dot(hidden, down_low[:, cols], preferred_element_type=F32)
        back_sum[:, cols] += lax.dot_general(
            gate_back, gate_low[cols, :], (((1,), (1,)), ((), ())), preferred_element_type=F32
        ) + lax.dot_general(
            up_back, up_low[cols, :], (((1,), (1,)), ((), ())), preferred_element_type=F32
        )
        grad_down[:, cols] = outer_rows(hidden, incoming[:, cols], BF)
        both = outer_rows(inputs[:, cols], both_back, BF)
        grad_gate[cols, :] = both[:, :CHUNK]
        grad_up[cols, :] = both[:, CHUNK:]

    @pl.when(at == HIDDEN // CHUNK - 1)
    def _():
        output_part[...] = output_sum[...].astype(BF)
        back_part[...] = back_sum[...].astype(BF)


def call_feed(normed_two, cotangent, gate_low, up_low, down_low):
    rows = pl.BlockSpec((LINE, D), lambda j: (0, 0))
    tall = pl.BlockSpec((D, CHUNK), lambda j: (0, j))
    wide = pl.BlockSpec((CHUNK, D), lambda j: (j, 0))
    return pl.pallas_call(
        feed_kernel,
        out_shape=(
            jax.ShapeDtypeStruct((LINE, D), BF),
            jax.ShapeDtypeStruct((LINE, D), BF),
            jax.ShapeDtypeStruct((D, HIDDEN), BF),
            jax.ShapeDtypeStruct((D, HIDDEN), BF),
            jax.ShapeDtypeStruct((HIDDEN, D), BF),
        ),
        grid=(HIDDEN // CHUNK,),
        in_specs=[rows, rows, tall, tall, wide],
        out_specs=(rows, rows, tall, tall, wide),
        scratch_shapes=[pltpu.VMEM((LINE, D), F32), pltpu.VMEM((LINE, D), F32)],
        compiler_params=pltpu.CompilerParams(vmem_limit_bytes=VMEM_LIMIT),
        name="feed_forward",
    )(normed_two, cotangent, gate_low, up_low, down_low)


def rope_inverse():
    half_size = HD // 2
    column = np.arange(half_size, dtype=np.float32)
    inverse = np.exp(-(np.float32(2.0) * column / HD) * np.float32(math.log(ROPE_THETA)))
    wavelength = np.float32(2.0 * math.pi) / inverse
    smooth = (np.float32(OLD_CONTEXT) / wavelength - LOW_FREQ) / (HIGH_FREQ - LOW_FREQ)
    blended = (1.0 - smooth) * inverse / ROPE_FACTOR + smooth * inverse
    inverse = np.where(
        wavelength < OLD_CONTEXT / HIGH_FREQ,
        inverse,
        np.where(wavelength > OLD_CONTEXT / LOW_FREQ, inverse / ROPE_FACTOR, blended),
    )
    return np.broadcast_to(inverse.astype(np.float32)[:, None], (half_size, 128))


def outer_rows(left, right, kind):
    return lax.dot_general(
        left, right, (((0,), (0,)), ((), ())), preferred_element_type=F32
    ).astype(kind)


def adam(weight, moment, second, gradient, rate, decay):
    moment_next = BETA_ONE * moment + (1.0 - BETA_ONE) * gradient
    second_next = BETA_TWO * second + (1.0 - BETA_TWO) * gradient * gradient
    unbiased = moment_next / (1.0 - BETA_ONE**ADAM_STEP)
    divisor = jnp.sqrt(second_next / (1.0 - BETA_TWO**ADAM_STEP)) + ADAM_EPS
    return (weight - rate * (unbiased / divisor + decay * weight), moment_next, second_next)


def shards(
    block_input,
    out_grad,
    qkv_weight,
    qkv_moment,
    qkv_second,
    gate_up_weight,
    gate_up_moment,
    gate_up_second,
    out_weight,
    out_moment,
    out_second,
    down_weight,
    down_moment,
    down_second,
    norm_gains,
    gains_moment,
    gains_second,
    doc_lengths,
):
    (
        cosine,
        sine,
        scale_one,
        normed,
        qkv_whole,
        query_columns,
        mixed,
        logs,
        attended,
        keys,
        cotangent_all,
        out_whole,
        gate_whole,
        up_whole,
        down_whole,
        middle,
        scale_two,
        normed_two,
    ) = call_forward(
        doc_lengths,
        jnp.asarray(rope_inverse()),
        block_input,
        qkv_weight,
        gate_up_weight,
        down_weight,
        out_weight,
        norm_gains,
        out_grad,
    )
    output_part, back_part, grad_gate, grad_up, grad_down = call_feed(
        normed_two,
        cotangent_all,
        gate_whole.reshape(D, HIDDEN),
        up_whole.reshape(D, HIDDEN),
        down_whole.reshape(HIDDEN, D),
    )
    input_grad, output, grad_qkv, grad_gate_up, grad_down, grad_out, totals = call_backward(
        doc_lengths,
        cosine,
        sine,
        back_part,
        output_part,
        middle,
        scale_two,
        scale_one,
        norm_gains,
        block_input,
        out_grad,
        query_columns,
        mixed,
        logs,
        attended,
        keys,
        out_whole,
        qkv_whole,
        normed,
        grad_down.reshape(down_whole.shape),
        grad_up.reshape(up_whole.shape),
        grad_gate.reshape(gate_whole.shape),
    )
    shares = (grad_qkv, grad_gate_up, grad_out, grad_down)
    gains_grad = totals[:16].reshape(2, WIDTH)
    grad_norm = jnp.sqrt(totals[16, 0])
    factor = CLIP_NORM / jnp.maximum(grad_norm, CLIP_NORM)
    weights = (qkv_weight, gate_up_weight, out_weight, down_weight)
    moments = (qkv_moment, gate_up_moment, out_moment, down_moment)
    seconds = (qkv_second, gate_up_second, out_second, down_second)
    out_rate = OUTPUT_RATE * (TOKENS / (HQ * HD)) ** 0.5
    down_rate = DOWN_RATE * FF ** (-0.5)
    rates = (MATRIX_RATE, MATRIX_RATE, out_rate, down_rate)
    results = []
    for weight, moment, second, gradient, rate in zip(weights, moments, seconds, shares, rates):
        results.extend(adam(weight, moment, second, gradient * factor, rate, WEIGHT_DECAY))
    gains_new = adam(norm_gains, gains_moment, gains_second, gains_grad * factor, GAIN_RATE, 0.0)
    return (output, input_grad, grad_norm, *results, *gains_new)


def solution(mesh):
    placed = (
        P(("seq", "wide"), "narrow"),
        P(("seq", "wide"), "narrow"),
        P(("narrow", "seq"), "wide", None),
        P(("narrow", "seq"), "wide", None),
        P(("narrow", "seq"), "wide", None),
        P(("narrow", "seq"), None, "wide"),
        P(("narrow", "seq"), None, "wide"),
        P(("narrow", "seq"), None, "wide"),
        P(("wide", "seq"), "narrow"),
        P(("wide", "seq"), "narrow"),
        P(("wide", "seq"), "narrow"),
        P(("wide", "seq"), "narrow"),
        P(("wide", "seq"), "narrow"),
        P(("wide", "seq"), "narrow"),
        P(None, "narrow"),
        P(None, "narrow"),
        P(None, "narrow"),
        P(),
    )
    return jax.shard_map(
        shards,
        mesh=mesh,
        in_specs=placed,
        out_specs=(
            P(("seq", "wide"), "narrow"),
            P(("seq", "wide"), "narrow"),
            P(),
            P(("narrow", "seq"), "wide", None),
            P(("narrow", "seq"), "wide", None),
            P(("narrow", "seq"), "wide", None),
            P(("narrow", "seq"), None, "wide"),
            P(("narrow", "seq"), None, "wide"),
            P(("narrow", "seq"), None, "wide"),
            P(("wide", "seq"), "narrow"),
            P(("wide", "seq"), "narrow"),
            P(("wide", "seq"), "narrow"),
            P(("wide", "seq"), "narrow"),
            P(("wide", "seq"), "narrow"),
            P(("wide", "seq"), "narrow"),
            P(None, "narrow"),
            P(None, "narrow"),
            P(None, "narrow"),
        ),
        check_vma=False,
    )
```
